512 devices in a mesh: wide: 64 (over z, y), narrow: 8 (over x, core).
Axes of the slice: x: 4, y: 4, z: 16, core: 2. Of those that a mesh axis runs over, the one named last changes fastest.
Arguments:
- right_side: float32 [512, 32, 1024], P('wide', None, 'narrow'), may hold values from -8 to 8
- conductivity: float32 [512, 32, 1024], P('wide', None, 'narrow'), may hold values from 0.1 to 10
Outputs:
- solution: float32 [512, 32, 1024], P('wide', None, 'narrow')
The draws below stay inside these ranges and needn't reach their ends.
All inputs are finite; a program needn't handle non-finite values.
Results may differ from the reference program's by a relative error of at most 0.00002.
Values sent between devices are 32-bit elements; how exact they have to be, the bound alone decides.
A program may use at most 128 MiB of HBM per device.

```python
import math
import jax
import jax.numpy as jnp

PRE_SWEEPS = 3
POST_SWEEPS = 3
COARSE_SWEEPS = 4
NX = 512
NY = 32
NZ = 1024


def levels(rng, extent, pieces, low, top_value):
    factor_of = 1.0
    for axis_at, blocks in pieces:
        steps = jax.random.uniform(jax.random.fold_in(jax.random.fold_in(rng, 6), axis_at), (blocks,), jnp.float32, low / len(pieces), top_value / len(pieces))
        factor_of = factor_of * jnp.repeat(jnp.exp(steps), extent[axis_at] // blocks).reshape((-1,) + (1,) * (len(extent) - 1 - axis_at))
    return factor_of


def centred(rng, dims, width, bound, split=(), kind=jnp.bfloat16):
    gain = levels(rng, dims, split, -0.22, 0.18) if split else 1.0
    drawn = jax.random.normal(rng, dims, jnp.float32) * width * gain
    return jnp.minimum(jnp.maximum(drawn, -bound), bound).astype(kind)


def setup_inputs(seed: int = 0) -> dict:
    arg_keys = jax.random.split(jax.random.key(seed), 3)
    return {
        "right_side": centred(arg_keys[0], (NX, NY, NZ), 1.0, 8.0, ((0, 64), (2, 8)), jnp.float32),
        "conductivity": jnp.clip(jnp.exp(math.log(10.0) - 4.6051702 * jax.random.uniform(arg_keys[1], (NX, NY, NZ), jnp.float32) ** levels(arg_keys[1], (NX, NY, NZ), ((0, 64), (2, 8)), -0.2, 0.2)), 0.1, 10.0),
    }


cheb_center = 1.125
cheb_half = 0.875


def beside_cells(padded):
    return (padded[:-2, 1:-1, 1:-1], padded[2:, 1:-1, 1:-1],
            padded[1:-1, :-2, 1:-1], padded[1:-1, 2:, 1:-1],
            padded[1:-1, 1:-1, :-2], padded[1:-1, 1:-1, 2:])


def pad_whole(values):
    return jnp.pad(values, 1)


def face_coefs(coef, h_scale, pad_fn):
    couplings = tuple((0.5 * h_scale) * (coef + other_side) for other_side in beside_cells(pad_fn(coef)))
    diagonal = couplings[0]
    for single in couplings[1:]:
        diagonal = diagonal + single
    return couplings, diagonal


def operate(values, couplings, diagonal, pad_fn):
    beside = beside_cells(pad_fn(values))
    neighbour_sum = couplings[0] * beside[0]
    for single, other_side in zip(couplings[1:], beside[1:]):
        neighbour_sum = neighbour_sum + single * other_side
    return diagonal * values - neighbour_sum


def smooth(field, source, couplings, diagonal, sweeps, pad_fn):
    sigma = cheb_center / cheb_half
    if field is None:
        resid = source
        step_dir = resid / (cheb_center * diagonal)
        field = step_dir
    else:
        resid = source - operate(field, couplings, diagonal, pad_fn)
        step_dir = resid / (cheb_center * diagonal)
        field = field + step_dir
    ratio = 1.0 / sigma
    for _ in range(sweeps - 1):
        ratio_next = 1.0 / (2.0 * sigma - ratio)
        resid = source - operate(field, couplings, diagonal, pad_fn)
        step_dir = (ratio_next * ratio) * step_dir + (2.0 * ratio_next / cheb_half) * (resid / diagonal)
        field = field + step_dir
        ratio = ratio_next
    return field


def restrict(values):
    size_a, size_b, size_c = values.shape
    blocks = values.reshape(size_a // 2, 2, size_b // 2, 2, size_c // 2, 2)
    return jnp.mean(blocks, axis=(1, 3, 5))


def prolong(values):
    return jnp.repeat(jnp.repeat(jnp.repeat(values, 2, 0), 2, 1), 2, 2)


def vcycle(source, coef, level_index, pad_fn):
    couplings, diagonal = face_coefs(coef, 0.25 ** level_index, pad_fn)
    if level_index == 3:
        return smooth(None, source, couplings, diagonal, COARSE_SWEEPS, pad_fn)
    field = smooth(None, source, couplings, diagonal, PRE_SWEEPS, pad_fn)
    resid = source - operate(field, couplings, diagonal, pad_fn)
    error_field = vcycle(restrict(resid), restrict(coef), level_index + 1, pad_fn)
    field = field + prolong(error_field)
    return smooth(field, source, couplings, diagonal, POST_SWEEPS, pad_fn)


def reference(right_side, conductivity):
    return vcycle(right_side, conductivity, 0, pad_whole)
```

```python
import functools

import jax
import jax.numpy as jnp
from jax import lax
from jax.experimental import pallas as pl
from jax.experimental.pallas import tpu as pltpu
from jax.sharding import PartitionSpec as P

CENTER = 1.125
HALF = 0.875
LANES = 128
REACH = 8
F32 = jnp.float32
MESH_ID = pl.DeviceIdType.MESH


def cheb(sweeps):
    sigma = CENTER / HALF
    steps = [(0.0, 1.0 / CENTER)]
    ratio = 1.0 / sigma
    for _ in range(sweeps - 1):
        ratio_next = 1.0 / (2.0 * sigma - ratio)
        steps.append((ratio_next * ratio, 2.0 * ratio_next / HALF))
        ratio = ratio_next
    return steps


def over_layers(low, high, unroll, body):
    count = high - low + 1
    if count == unroll:
        for at in range(low, high + 1):
            body(at)
        return

    def block(step, carry):
        for at in range(unroll):
            body(low + step * unroll + at)
        return carry

    lax.fori_loop(0, count // unroll, block, 0)


class Level:
    def __init__(self, refs, scale, rows, row_step, lane_step, base, extent, lane_mask):
        self.c, self.s, self.cx, self.cy, self.cz, self.iv, self.dg, self.va, self.vb, self.d = refs
        self.tiles = self.c.shape[0]
        self.half = 0.5 * scale
        self.rows, self.row_step, self.lane_step = rows, row_step, lane_step
        self.base, self.extent, self.lane_mask = base, extent, lane_mask

    def inside(self, at):
        where_x = self.base + at
        return jnp.where((where_x >= 0) & (where_x < self.extent), 1.0, 0.0).astype(F32)

    def lane(self):
        return lax.broadcasted_iota(jnp.int32, (self.rows, LANES), 1)

    def row(self):
        return lax.broadcasted_iota(jnp.int32, (self.rows, LANES), 0)

    def y_up(self, tile):
        return pltpu.roll(tile, self.rows - self.row_step, 0)

    def y_down(self, tile):
        return pltpu.roll(tile, self.row_step, 0)

    def z_up(self, tiles):
        turned = [pltpu.roll(t, LANES - self.lane_step, 1) for t in tiles]
        if self.tiles == 1:
            return turned
        edge = self.lane() == LANES - 1
        return [jnp.where(edge, turned[1 - k], turned[k]) for k in range(2)]

    def z_down(self, tiles):
        turned = [pltpu.roll(t, self.lane_step, 1) for t in tiles]
        if self.tiles == 1:
            return turned
        edge = self.lane() == 0
        return [jnp.where(edge, turned[1 - k], turned[k]) for k in range(2)]

    def setup(self, low, high, unroll):
        tiles = range(self.tiles)
        half = self.half

        def masked(at):
            inside = self.inside(at)
            return [
                self.c[k, at] * inside if self.lane_mask[k] is None else self.c[k, at] * (self.lane_mask[k] * inside)
                for k in tiles
            ]

        first, second = masked(low - 1), masked(low)
        for k in tiles:
            self.cx[k, low - 1] = half * (first[k] + second[k])

        def body(at):
            before, here, after = masked(at - 1), masked(at), masked(at + 1)
            inside = self.inside(at)
            top = self.row() >= self.rows - self.row_step
            bottom = self.row() < self.row_step
            z_up, z_down = self.z_up(here), self.z_down(here)
            for k in tiles:
                own = here[k]
                x_low = half * (before[k] + own)
                x_high = half * (own + after[k])
                y_low = half * (own + jnp.where(bottom, 0.0, self.y_down(own)))
                y_high = half * (own + jnp.where(top, 0.0, self.y_up(own)))
                z_low = half * (own + z_down[k])
                z_high = half * (own + z_up[k])
                diagonal = x_low + x_high + y_low + y_high + z_low + z_high
                keep = inside if self.lane_mask[k] is None else self.lane_mask[k] * inside
                self.cx[k, at] = x_high
                self.cy[k, at] = jnp.where(top, 0.0, y_high)
                self.cz[k, at] = z_high
                self.dg[k, at] = diagonal
                self.iv[k, at] = jnp.where(jnp.full_like(own, 0.0) + keep > 0.5, 1.0 / diagonal, 0.0)

        over_layers(low, high, unroll, body)

    def start(self, low, high, unroll, beta):
        def body(at):
            for k in range(self.tiles):
                step = self.s[k, at] * self.iv[k, at] * beta
                self.d[k, at] = step
                self.va[k, at] = step

        over_layers(low, high, unroll, body)

    def around(self, field, at):
        tiles = range(self.tiles)
        here = [field[k, at] for k in tiles]
        cz = [self.cz[k, at] for k in tiles]
        z_up = self.z_up(here)
        z_down = self.z_down([cz[k] * here[k] for k in tiles])
        sums = []
        for k in tiles:
            cy = self.cy[k, at]
            total = self.cx[k, at] * field[k, at + 1] + self.cx[k, at - 1] * field[k, at - 1]
            total = total + (cy * self.y_up(here[k]) + self.y_down(cy * here[k]))
            total = total + (cz[k] * z_up[k] + z_down[k])
            sums.append(total + self.s[k, at])
        return here, sums

    def sweep(self, field, result, low, high, unroll, step):
        alpha, beta = step

        def body(at):
            here, sums = self.around(field, at)
            for k in range(self.tiles):
                change = beta * (sums[k] * self.iv[k, at] - here[k])
                if alpha:
                    change = change + alpha * self.d[k, at]
                self.d[k, at] = change
                result[k, at] = here[k] + change

        over_layers(low, high, unroll, body)

    def residual(self, field, result, low, high, unroll):
        def body(at):
            here, sums = self.around(field, at)
            result[0, at] = sums[0] - self.dg[0, at] * here[0]

        over_layers(low, high, unroll, body)

    def finish(self, field, kept, change_out, low, high, unroll, step):
        alpha, beta = step

        def body(at):
            here, sums = self.around(field, at)
            change = alpha * self.d[0, at] + beta * (sums[0] * self.iv[0, at] - here[0])
            kept[at - low] = here[0]
            change_out[at - low] = change

        over_layers(low, high, unroll, body)


LEVEL_FIELDS = 10
LEVEL_SHAPES = ((2, 16, 32, LANES), (1, 14, 16, LANES), (1, 34, 8, LANES), (1, 15, 8, LANES))


def kernel(wide, narrow, rhs, coef, kept, change, *scratch):
    scratch = list(scratch)
    level_refs = []
    for _ in range(4):
        level_refs.append(scratch[:LEVEL_FIELDS])
        scratch = scratch[LEVEL_FIELDS:]
    (zs, rz, rcn, cm1, rc1, c1o, c2m, rc2, s1o, sm1, rs1, pz1, rz1, rcn1,
     rx1, rx1b, p2, rz2, s2m, rs2, sb0, hx0, p1, p0, local_sem, send_sem, recv_sem) = scratch
    me_w = lax.axis_index("wide")
    me_n = lax.axis_index("narrow")

    def there(dw, dn):
        return (lax.rem(me_w + (dw + wide), wide), lax.rem(me_n + (dn + narrow), narrow))

    partners = [(dw, 0) for dw in range(-REACH, REACH + 1) if dw]
    partners += [(0, -1), (0, 1)] + [(dw, dn) for dw in (-1, 1) for dn in (-1, 1)]
    barrier = pltpu.get_barrier_semaphore()
    for dw, dn in partners:
        pl.semaphore_signal(barrier, inc=1, device_id=there(dw, dn), device_id_type=MESH_ID)

    c0, s0 = level_refs[0][0], level_refs[0][1]
    load_c = pltpu.make_async_copy(coef, c0.at[0, pl.ds(4, 8)], local_sem.at[0])
    load_s = pltpu.make_async_copy(rhs, s0.at[0, pl.ds(4, 8)], local_sem.at[1])
    load_c.start()
    load_s.start()

    left = jnp.where(me_n > 0, 1.0, 0.0).astype(F32)
    right = jnp.where(me_n < narrow - 1, 1.0, 0.0).astype(F32)

    def lanes(rows):
        return lax.broadcasted_iota(jnp.int32, (rows, LANES), 1)

    def mask(rows, own, until, since):
        at = lanes(rows)
        picked = jnp.where(at < until, right, jnp.where(at >= since, left, 0.0))
        return jnp.where(at < own, 1.0, picked)

    level_0 = Level(level_refs[0], 1.0, 32, 1, 1, 8 * me_w - 4, 8 * wide, [None, mask(32, 0, 8, 120)])
    level_1 = Level(level_refs[1], 0.25, 16, 1, 1, 4 * me_w - 5, 4 * wide, [mask(16, 64, 72, 120)])
    level_2 = Level(level_refs[2], 0.0625, 8, 1, 2, 2 * me_w - 16, 2 * wide, [mask(8, 64, 96, 96)])
    level_3 = Level(level_refs[3], 0.015625, 8, 2, 4, me_w - 7, wide, [mask(8, 64, 96, 96)])

    copies = []

    def send(src, dst, dw, dn):
        at = len(copies)
        copy = pltpu.make_async_remote_copy(
            src_ref=src, dst_ref=dst, send_sem=send_sem.at[at], recv_sem=recv_sem.at[at],
            device_id=there(dw, dn), device_id_type=MESH_ID,
        )
        copies.append(copy)
        copy.start()
        return copy

    def receive(group):
        for copy in group:
            copy.wait_recv()

    def pack(tiles):
        rows = tiles[0].shape[0]
        group = lanes(rows) // 16
        packed = jnp.zeros((rows, LANES), F32)
        for at, tile in enumerate(tiles):
            packed = jnp.where(group == at, pltpu.roll(tile, (16 * at + 8) % LANES, 1), packed)
        return packed

    def unpack(packed, at):
        return pltpu.roll(packed, (2 * LANES - (16 * at + 8)) % LANES, 1)

    def merged(from_left, from_right):
        return jnp.where(lanes(from_left.shape[0]) % 16 < 8, from_left, from_right)

    def halves_0(ref, half):
        tiles = []
        for layer in range(4):
            for part in range(2):
                tiles.append(ref[0, 4 + 4 * half + layer, pl.ds(16 * part, 16), :])
        return tiles

    def restrict_0(ref):
        out = []
        for layer in range(4):
            total = None
            for dx in range(2):
                for dy in range(2):
                    term = ref[0, 4 + 2 * layer + dx, pl.ds(dy, 16, stride=2), :]
                    total = term if total is None else total + term
            total = total + pltpu.roll(total, LANES - 1, 1)
            out.append(0.125 * jnp.take_along_axis(total, (2 * lanes(16)) % LANES, axis=1))
        return out

    def pairs_1(ref, base):
        out = []
        for layer in range(2):
            total = None
            for dx in range(2):
                for dy in range(2):
                    term = ref[base + 2 * layer + dx, pl.ds(dy, 8, stride=2), :]
                    total = term if total is None else total + term
            odd = lanes(8) % 2 == 1
            total = total + jnp.where(odd, pltpu.roll(total, 1, 1), pltpu.roll(total, LANES - 1, 1))
            out.append(0.125 * total)
        return out

    def tiles_1(ref):
        return [ref[layer, pl.ds(8 * part, 8), :] for layer in range(4) for part in range(2)]

    def squeeze_1(ref, out):
        for layer in range(2):
            out[layer] = jnp.where(lanes(16) < 64, ref[layer], ref[layer + 2])

    load_c.wait()
    for layer, value in enumerate(restrict_0(c0)):
        c1o[layer] = value
    squeeze_1(c1o, cm1)
    zs[pl.ds(32, 8), :] = pack(tiles_1(c1o))
    own_2 = pairs_1(c1o, 0)
    odd_8 = lanes(8) % 2 == 1
    zs[pl.ds(40, 8), :] = jnp.where(odd_8, own_2[1], own_2[0])
    for half in range(2):
        zs[pl.ds(48 * half, 16), :] = pack(halves_0(c0, half))
    load_s.wait()
    for half in range(2):
        zs[pl.ds(48 * half + 16, 16), :] = pack(halves_0(s0, half))

    pl.semaphore_wait(barrier, len(partners))

    got_c = [
        send(c0.at[0, pl.ds(4, 4)], c0.at[0, pl.ds(12, 4)], -1, 0),
        send(c0.at[0, pl.ds(8, 4)], c0.at[0, pl.ds(0, 4)], 1, 0),
    ]
    got_z = [send(zs, rz.at[1], 0, -1), send(zs, rz.at[0], 0, 1)]
    for dn in (-1, 1):
        slot = 1 if dn < 0 else 0
        got_z.append(send(zs.at[pl.ds(0, 48)], rcn.at[1, slot], -1, dn))
        got_z.append(send(zs.at[pl.ds(32, 48)], rcn.at[0, slot], 1, dn))
    got_s = [
        send(s0.at[0, pl.ds(4, 3)], s0.at[0, pl.ds(12, 3)], -1, 0),
        send(s0.at[0, pl.ds(9, 3)], s0.at[0, pl.ds(1, 3)], 1, 0),
    ]
    got_c1 = [send(cm1, rc1.at[1], -1, 0), send(cm1, rc1.at[0], 1, 0)]

    def fill_0(ref, field):
        for half in range(2):
            row = 48 * half + 16 * field
            packed = merged(rz[0, pl.ds(row, 16), :], rz[1, pl.ds(row, 16), :])
            for layer in range(4):
                for part in range(2):
                    ref[1, 4 + 4 * half + layer, pl.ds(16 * part, 16), :] = unpack(packed, 2 * layer + part)
        for side in range(2):
            row = 16 * field + (16 if side == 0 else 0)
            packed = merged(rcn[side, 0, pl.ds(row, 16), :], rcn[side, 1, pl.ds(row, 16), :])
            for layer in range(4):
                for part in range(2):
                    ref[1, 12 * side + layer, pl.ds(16 * part, 16), :] = unpack(packed, 2 * layer + part)

    receive(got_z)
    fill_0(c0, 0)
    fill_0(s0, 1)
    receive(got_c)
    level_0.setup(1, 14, 2)
    receive(got_s)
    steps = cheb(3)
    level_0.start(1, 14, 2, steps[0][1])
    level_0.sweep(level_0.va, level_0.vb, 2, 13, 2, steps[1])
    level_0.sweep(level_0.vb, level_0.va, 3, 12, 2, steps[2])
    level_0.residual(level_0.va, level_0.vb, 4, 11, 2)

    for layer, value in enumerate(restrict_0(level_0.vb)):
        s1o[layer] = value
    squeeze_1(s1o, sm1)
    pz1[...] = pack(tiles_1(s1o))
    got_s1 = [send(sm1, rs1.at[1], -1, 0), send(sm1, rs1.at[0], 1, 0)]
    got_s1 += [send(pz1, rz1.at[1], 0, -1), send(pz1, rz1.at[0], 0, 1)]
    for dn in (-1, 1):
        slot = 1 if dn < 0 else 0
        got_s1.append(send(pz1, rcn1.at[1, slot], -1, dn))
        got_s1.append(send(pz1, rcn1.at[0, slot], 1, dn))

    low_lanes = lanes(8) < 64
    mid_lanes = lanes(8) < 96
    c2m[...] = jnp.where(low_lanes, zs[pl.ds(40, 8), :],
                         jnp.where(mid_lanes, rz[1, pl.ds(40, 8), :], rz[0, pl.ds(40, 8), :]))
    rc2[REACH] = c2m[...]
    got_c2 = [send(c2m, rc2.at[REACH - dw], dw, 0) for dw in range(-REACH, REACH + 1) if dw]

    def spread_1(ref, own, own_packs, beside, beside_packs):
        def put(at, layer, base, packed):
            for part in range(2):
                window = unpack(packed, 2 * layer + part)
                ref[0, at, pl.ds(8 * part, 8), :] = jnp.where(
                    low_lanes, base[8 * part:8 * part + 8, :],
                    jnp.where(mid_lanes, pltpu.roll(window, 64, 1), window))

        packed = merged(*own_packs)
        for layer in range(4):
            put(5 + layer, layer, own[layer], packed)
        for side in range(2):
            packed = merged(*beside_packs[side])
            for layer in range(4):
                base = beside[side, layer % 2]
                if layer >= 2:
                    base = pltpu.roll(base, 64, 1)
                put((1 if side == 0 else 9) + layer, layer, base, packed)

    receive(got_c1)
    spread_1(
        level_1.c, c1o, (rz[0, pl.ds(32, 8), :], rz[1, pl.ds(32, 8), :]), rc1,
        [(rcn[0, 0, pl.ds(0, 8), :], rcn[0, 1, pl.ds(0, 8), :]),
         (rcn[1, 0, pl.ds(32, 8), :], rcn[1, 1, pl.ds(32, 8), :])],
    )
    got_c1b = [
        send(level_1.c.at[0, 9], level_1.c.at[0, 13], -1, 0),
        send(level_1.c.at[0, 4], level_1.c.at[0, 0], 1, 0),
    ]
    for side in range(2):
        first = 9 if side == 0 else 4
        tiles = []
        for layer in range(3):
            sb0[side, pl.ds(32 * layer, 32), :] = level_0.va[0, first + layer]
            for part in range(2):
                tiles.append(level_0.va[1, first + layer, pl.ds(16 * part, 16), :])
        sb0[side, pl.ds(96, 16), :] = pack(tiles)
    got_x0 = [send(sb0.at[0], hx0.at[0], 1, 0), send(sb0.at[1], hx0.at[1], -1, 0)]

    receive(got_c1b)
    level_1.setup(1, 12, 12)

    receive(got_s1)
    spread_1(
        level_1.s, s1o, (rz1[0], rz1[1]), rs1,
        [(rcn1[0, 0], rcn1[0, 1]), (rcn1[1, 0], rcn1[1, 1])],
    )
    level_1.start(2, 11, 10, steps[0][1])
    level_1.sweep(level_1.va, level_1.vb, 3, 10, 8, steps[1])
    level_1.sweep(level_1.vb, level_1.va, 4, 9, 6, steps[2])
    level_1.residual(level_1.va, level_1.vb, 5, 8, 4)

    own_2 = [jnp.where(low_lanes, t, pltpu.roll(t, 64, 1)) for t in pairs_1(level_1.vb.at[0], 5)]
    p2[...] = jnp.where(odd_8, own_2[1], own_2[0])
    got_z2 = [send(p2, rz2.at[1], 0, -1), send(p2, rz2.at[0], 0, 1)]
    got_x1 = [
        send(level_1.va.at[0, pl.ds(5, 4)], rx1.at[1], -1, 0),
        send(level_1.va.at[0, pl.ds(5, 4)], rx1.at[0], 1, 0),
        send(level_1.va.at[0, 5], rx1b.at[1], -2, 0),
        send(level_1.va.at[0, 8], rx1b.at[0], 2, 0),
    ]

    def spread_2(ref, blocks):
        for block in range(2 * REACH + 1):
            packed = blocks[block]
            ref[0, 2 * block] = jnp.where(odd_8, pltpu.roll(packed, 1, 1), packed)
            ref[0, 2 * block + 1] = jnp.where(odd_8, packed, pltpu.roll(packed, LANES - 1, 1))

    def restrict_2(ref, at):
        total = ref[0, 2 * at + 2] + ref[0, 2 * at + 3]
        odd_row = lax.broadcasted_iota(jnp.int32, (8, LANES), 0) % 2 == 1
        total = total + jnp.where(odd_row, pltpu.roll(total, 1, 0), pltpu.roll(total, 7, 0))
        second = lanes(8) % 4 >= 2
        total = total + jnp.where(second, pltpu.roll(total, 2, 1), pltpu.roll(total, LANES - 2, 1))
        return 0.125 * total

    receive(got_z2)
    s2m[...] = jnp.where(low_lanes, p2[...], jnp.where(mid_lanes, rz2[1], rz2[0]))
    rs2[REACH] = s2m[...]
    got_s2 = [send(s2m, rs2.at[REACH - dw], dw, 0) for dw in range(-REACH, REACH + 1) if dw]

    receive(got_c2)
    spread_2(level_2.c, rc2)
    level_2.setup(1, 32, 8)
    for at in range(15):
        level_3.c[0, at] = restrict_2(level_2.c, at)
    level_3.setup(1, 13, 13)

    receive(got_s2)
    spread_2(level_2.s, rs2)
    level_2.start(1, 32, 32, steps[0][1])
    level_2.sweep(level_2.va, level_2.vb, 2, 31, 15, steps[1])
    level_2.sweep(level_2.vb, level_2.va, 3, 30, 14, steps[2])
    level_2.residual(level_2.va, level_2.vb, 4, 29, 13)

    for at in range(1, 14):
        level_3.s[0, at] = restrict_2(level_2.vb, at)
    coarse = cheb(4)
    level_3.start(1, 13, 13, coarse[0][1])
    level_3.sweep(level_3.va, level_3.vb, 2, 12, 11, coarse[1])
    level_3.sweep(level_3.vb, level_3.va, 3, 11, 9, coarse[2])
    level_3.sweep(level_3.va, level_3.vb, 4, 10, 7, coarse[3])

    for at in range(10, 24):
        level_2.vb[0, at] = level_2.va[0, at] + level_3.vb[0, (at - 2) // 2]
    level_2.sweep(level_2.vb, level_2.va, 11, 22, 12, steps[0])
    level_2.sweep(level_2.va, level_2.vb, 12, 21, 10, steps[1])
    level_2.sweep(level_2.vb, level_2.va, 13, 20, 8, steps[2])

    for at in range(8):
        value = level_2.va[0, 13 + at]
        for part in range(2):
            p1[at, pl.ds(part, 8, stride=2), :] = value
    receive(got_x1)
    for at in range(14):
        if 5 <= at <= 8:
            before = level_1.va[0, at]
        else:
            beside = (rx1b[0] if at == 0 else rx1[0, at - 1] if at < 5 else rx1[1, at - 9] if at < 13 else rx1b[1])
            before = beside * level_1.inside(at)
        level_1.vb[0, at] = before + p1[(at + 1) // 2]
    for copy in got_x1:
        copy.wait_send()
    level_1.sweep(level_1.vb, level_1.va, 1, 12, 12, steps[0])
    level_1.sweep(level_1.va, level_1.vb, 2, 11, 10, steps[1])
    level_1.sweep(level_1.vb, level_1.va, 3, 10, 8, steps[2])

    at_lane = lanes(16)
    for at in range(8):
        value = level_1.va[0, 3 + at]
        for k in range(2):
            fine = jnp.take_along_axis(value, at_lane // 2 + 64 * k, axis=1)
            for part in range(2):
                p0[k, at, pl.ds(part, 16, stride=2), :] = fine
    receive(got_x0)
    for side in range(2):
        packed = hx0[side, pl.ds(96, 16), :]
        for layer in range(3):
            at = (1 if side == 0 else 12) + layer
            inside = level_0.inside(at)
            coarse_at = (at - 4) // 2 + 2
            level_0.vb[0, at] = hx0[side, pl.ds(32 * layer, 32), :] * inside + p0[0, coarse_at]
            for part in range(2):
                rows = pl.ds(16 * part, 16)
                level_0.vb[1, at, rows, :] = (
                    unpack(packed, 2 * layer + part) * (level_0.lane_mask[1][:16] * inside) + p0[1, coarse_at, rows, :]
                )

    def correct(at):
        for k in range(2):
            level_0.vb[k, at] = level_0.va[k, at] + p0[k, at // 2]

    over_layers(4, 11, 2, correct)
    level_0.sweep(level_0.vb, level_0.va, 2, 13, 2, steps[0])
    level_0.sweep(level_0.va, level_0.vb, 3, 12, 2, steps[1])
    level_0.finish(level_0.vb, kept, change, 4, 11, 2, steps[2])

    for copy in copies:
        if not any(copy is other for other in got_x1):
            copy.wait_send()


def per_device(right_side, conductivity, wide, narrow):
    brick = (8, 32, LANES)
    scratch = []
    for shape in LEVEL_SHAPES:
        scratch += [pltpu.VMEM(shape, F32)] * LEVEL_FIELDS
    shapes = [
        (80, LANES), (2, 80, LANES), (2, 2, 48, LANES),
        (2, 16, LANES), (2, 2, 16, LANES), (4, 16, LANES),
        (8, LANES), (2 * REACH + 1, 8, LANES),
        (4, 16, LANES), (2, 16, LANES), (2, 2, 16, LANES),
        (8, LANES), (2, 8, LANES), (2, 2, 8, LANES),
        (2, 4, 16, LANES), (2, 16, LANES),
        (8, LANES), (2, 8, LANES), (8, LANES), (2 * REACH + 1, 8, LANES),
        (2, 112, LANES), (2, 112, LANES),
        (8, 16, LANES), (2, 8, 32, LANES),
    ]
    scratch += [pltpu.VMEM(shape, F32) for shape in shapes]
    scratch += [pltpu.SemaphoreType.DMA((2,)), pltpu.SemaphoreType.DMA((64,)), pltpu.SemaphoreType.DMA((64,))]
    kept, change = pl.pallas_call(
        functools.partial(kernel, wide, narrow),
        out_shape=[jax.ShapeDtypeStruct(brick, F32)] * 2,
        in_specs=[pl.BlockSpec(memory_space=pl.ANY)] * 2,
        out_specs=[pl.BlockSpec(memory_space=pltpu.VMEM)] * 2,
        scratch_shapes=scratch,
        compiler_params=pltpu.CompilerParams(
            collective_id=0, has_side_effects=True, vmem_limit_bytes=32 * 1024 * 1024
        ),
    )(right_side, conductivity)
    return kept + change


def solution(mesh):
    spec = P("wide", None, "narrow")
    body = functools.partial(per_device, wide=mesh.shape["wide"], narrow=mesh.shape["narrow"])
    return jax.shard_map(body, mesh=mesh, in_specs=(spec, spec), out_specs=spec, check_vma=False)
```

```python
import functools

import jax
import jax.numpy as jnp
from jax import lax
from jax.experimental import pallas as pl
from jax.experimental.pallas import tpu as pltpu
from jax.sharding import PartitionSpec as P

CENTER = 1.125
HALF = 0.875
LANES = 128
REACH = 8
F32 = jnp.float32
MESH_ID = pl.DeviceIdType.MESH


def cheb(sweeps):
    sigma = CENTER / HALF
    steps = [(0.0, 1.0 / CENTER)]
    ratio = 1.0 / sigma
    for _ in range(sweeps - 1):
        ratio_next = 1.0 / (2.0 * sigma - ratio)
        steps.append((ratio_next * ratio, 2.0 * ratio_next / HALF))
        ratio = ratio_next
    return steps


def over_sides(first, second, count, body):
    def block(side, carry):
        for at in range(count):
            body(first + side * (second - first) + at)
        return carry

    lax.fori_loop(0, 2, block, 0)


def over_layers(low, high, unroll, body):
    count = high - low + 1
    if count == unroll:
        for at in range(low, high + 1):
            body(at)
        return

    def block(step, carry):
        for at in range(unroll):
            body(low + step * unroll + at)
        return carry

    lax.fori_loop(0, count // unroll, block, 0)


class Level:
    def __init__(self, refs, scale, rows, row_step, lane_step, base, extent, lane_mask):
        self.c, self.s, self.cx, self.cy, self.cz, self.iv, self.dg, self.va, self.vb = refs
        self.half = 0.5 * scale
        self.rows, self.row_step, self.lane_step = rows, row_step, lane_step
        self.base, self.extent, self.lane_mask = base, extent, lane_mask

    def inside(self, at):
        where_x = self.base + at
        return jnp.where((where_x >= 0) & (where_x < self.extent), 1.0, 0.0).astype(F32)

    def lane(self):
        return lax.broadcasted_iota(jnp.int32, (self.rows, LANES), 1)

    def row(self):
        return lax.broadcasted_iota(jnp.int32, (self.rows, LANES), 0)

    def y_up(self, tile):
        return pltpu.roll(tile, self.rows - self.row_step, 0)

    def y_down(self, tile):
        return pltpu.roll(tile, self.row_step, 0)

    def turned(self, tiles, shift, edge, count):
        out = [pltpu.roll(t, shift, 1) for t in tiles]
        if len(tiles) == 1:
            return out
        at_edge = self.lane() == edge
        return [jnp.where(at_edge, out[1 - k], out[k]) for k in range(count)]

    def z_up(self, tiles, count):
        return self.turned(tiles, LANES - self.lane_step, LANES - 1, count)

    def z_down(self, tiles, count):
        return self.turned(tiles, self.lane_step, 0, count)

    def masked(self, at, tiles):
        keep = self.inside(at) * self.half
        out = []
        for k in range(tiles):
            mask = self.lane_mask[k]
            out.append(self.c[k, at] * (keep if mask is None else mask * keep))
        return out

    def setup_below(self, low, tiles):
        first, second = self.masked(low - 1, tiles), self.masked(low, tiles)
        for k in range(tiles):
            self.cx[k, low - 1] = first[k] + second[k]

    def setup_at(self, at, tiles):
        before, here, after = self.masked(at - 1, tiles), self.masked(at, tiles), self.masked(at + 1, tiles)
        inside = self.inside(at)
        top = self.row() >= self.rows - self.row_step
        bottom = self.row() < self.row_step
        z_up, z_down = self.z_up(here, tiles), self.z_down(here, tiles)
        for k in range(tiles):
            own = here[k]
            x_low = before[k] + own
            x_high = own + after[k]
            y_low = own + jnp.where(bottom, 0.0, self.y_down(own))
            y_high = own + jnp.where(top, 0.0, self.y_up(own))
            z_low = own + z_down[k]
            z_high = own + z_up[k]
            diagonal = x_low + x_high + y_low + y_high + z_low + z_high
            keep = inside if self.lane_mask[k] is None else self.lane_mask[k] * inside
            self.cx[k, at] = x_high
            self.cy[k, at] = jnp.where(top, 0.0, y_high)
            self.cz[k, at] = z_high
            self.dg[k, at] = diagonal
            self.iv[k, at] = jnp.where(jnp.full_like(own, 0.0) + keep > 0.5, 1.0 / diagonal, 0.0)

    def setup(self, low, high, unroll, tiles):
        self.setup_below(low, tiles)
        over_layers(low, high, unroll, lambda at: self.setup_at(at, tiles))

    def start_at(self, at, tiles, beta):
        for k in range(tiles):
            self.va[k, at] = self.s[k, at] * self.iv[k, at] * beta

    def start(self, low, high, unroll, tiles, beta):
        over_layers(low, high, unroll, lambda at: self.start_at(at, tiles, beta))

    def around(self, field, at, tiles, count):
        here = [field[k, at] for k in range(tiles)]
        cz = [self.cz[k, at] for k in range(tiles)]
        z_up = self.z_up(here, count)
        z_down = self.z_down([cz[k] * here[k] for k in range(tiles)], count)
        sums = []
        for k in range(count):
            cy = self.cy[k, at]
            total = self.cx[k, at] * field[k, at + 1] + self.cx[k, at - 1] * field[k, at - 1]
            total = total + (cy * self.y_up(here[k]) + self.y_down(cy * here[k]))
            total = total + (cz[k] * z_up[k] + z_down[k])
            sums.append(total + self.s[k, at])
        return here, sums

    def sweep_at(self, at, field, result, tiles, count, step, fresh):
        alpha, beta = step
        here, sums = self.around(field, at, tiles, count)
        for k in range(count):
            kept = (1.0 + alpha - beta) * here[k]
            if not fresh:
                kept = kept - alpha * result[k, at]
            result[k, at] = kept + (beta * self.iv[k, at]) * sums[k]

    def sweep(self, field, result, low, high, unroll, tiles, count, step, fresh=False):
        over_layers(low, high, unroll, lambda at: self.sweep_at(at, field, result, tiles, count, step, fresh))

    def residual(self, field, result, low, high, unroll, tiles):
        def body(at):
            here, sums = self.around(field, at, tiles, 1)
            result[0, at] = sums[0] - self.dg[0, at] * here[0]

        over_layers(low, high, unroll, body)

    def finish(self, field, older, kept_out, added_out, low, high, unroll, step):
        alpha, beta = step

        def body(at):
            here, sums = self.around(field, at, 2, 1)
            kept_out[at - low] = (1.0 + alpha - beta) * here[0] - alpha * older[0, at]
            added_out[at - low] = (beta * self.iv[0, at]) * sums[0]

        over_layers(low, high, unroll, body)


LEVEL_FIELDS = 9
LEVEL_SHAPES = ((2, 16, 32, LANES), (2, 14, 16, LANES), (1, 34, 8, LANES), (1, 15, 8, LANES))
RULER = 1760


def kernel(wide, narrow, rhs, coef, kept, added, *scratch):
    scratch = list(scratch)
    level_refs = []
    for _ in range(4):
        level_refs.append(scratch[:LEVEL_FIELDS])
        scratch = scratch[LEVEL_FIELDS:]
    (zs, rz, rcn, k1c, s1o, sk, k1s, c2m, rc2, s2m, rs2, rx1, rx1b, sb0, hx0, p1, p0, ruler,
     local_sem, send_sem, recv_sem) = scratch
    me_w = lax.axis_index("wide")
    me_n = lax.axis_index("narrow")

    def there(dw, dn):
        return (lax.rem(me_w + (dw + wide), wide), lax.rem(me_n + (dn + narrow), narrow))

    far = [(sign * dw, 0) for dw in range(REACH, 0, -1) for sign in (1, -1)]
    corners = [(dw, dn) for dw in (-1, 1) for dn in (-1, 1)]
    around = [(-1, 0), (1, 0), (0, -1), (0, 1)] + corners
    partners = around + far[:-2]
    barrier = pltpu.get_barrier_semaphore()
    for dw, dn in partners:
        pl.semaphore_signal(barrier, inc=1, device_id=there(dw, dn), device_id_type=MESH_ID)

    c0, s0 = level_refs[0][0], level_refs[0][1]
    load_c = pltpu.make_async_copy(coef, c0.at[0, pl.ds(4, 8)], local_sem.at[0])
    load_s = pltpu.make_async_copy(rhs, s0.at[0, pl.ds(4, 8)], local_sem.at[1])
    load_c.start()
    load_s.start()

    left = jnp.where(me_n > 0, 1.0, 0.0).astype(F32)
    right = jnp.where(me_n < narrow - 1, 1.0, 0.0).astype(F32)

    def lanes(rows):
        return lax.broadcasted_iota(jnp.int32, (rows, LANES), 1)

    def edges(rows, until, low, since, high):
        at = lanes(rows)
        return jnp.where(at < until, low, jnp.where(at >= since, high, 0.0))

    def centred(rows):
        at = lanes(rows)
        return jnp.where((at >= 32) & (at < 96), 1.0, edges(rows, 32, left, 96, right))

    level_0 = Level(level_refs[0], 1.0, 32, 1, 1, 8 * me_w - 4, 8 * wide, [None, edges(32, 8, right, 120, left)])
    level_1 = Level(
        level_refs[1], 0.25, 16, 1, 1, 4 * me_w - 5, 4 * wide, [centred(16), edges(16, 32, right, 96, left)]
    )
    level_2 = Level(level_refs[2], 0.0625, 8, 1, 2, 2 * me_w - 16, 2 * wide, [centred(8)])
    level_3 = Level(level_refs[3], 0.015625, 8, 2, 4, me_w - 7, wide, [centred(8)])

    sent = [0, 0]

    def send(group, src, dst, dw, dn, rows, sender=0):
        sent[sender] += rows
        pltpu.make_async_remote_copy(
            src_ref=src, dst_ref=dst, send_sem=send_sem.at[sender], recv_sem=recv_sem.at[group],
            device_id=there(dw, dn), device_id_type=MESH_ID,
        ).start()

    def ruled(rows, group, sender):
        span = ruler.at[pl.ds(0, rows)]
        return pltpu.make_async_remote_copy(
            src_ref=span, dst_ref=span, send_sem=send_sem.at[sender], recv_sem=recv_sem.at[group],
            device_id=there(1, 0), device_id_type=MESH_ID,
        )

    def receive(group, rows):
        ruled(rows, group, 0).wait_recv()

    def sends_done(sender):
        ruled(sent[sender], 0, sender).wait_send()

    (from_z, from_edge, from_k, from_s1, from_c1b, from_x0, from_c2, from_x1, from_s2) = range(9)

    def pack(tiles):
        rows = tiles[0].shape[0]
        group = lanes(rows) // 16
        packed = jnp.zeros((rows, LANES), F32)
        for at, tile in enumerate(tiles):
            packed = jnp.where(group == at, pltpu.roll(tile, (16 * at + 8) % LANES, 1), packed)
        return packed

    def unpack(packed, at):
        return pltpu.roll(packed, (2 * LANES - (16 * at + 8)) % LANES, 1)

    def merged(from_left, from_right):
        return jnp.where(lanes(from_left.shape[0]) % 16 < 8, from_left, from_right)

    def halves_0(ref, half):
        tiles = []
        for layer in range(4):
            for part in range(2):
                tiles.append(ref[0, 4 + 4 * half + layer, pl.ds(16 * part, 16), :])
        return tiles

    def restrict_0(ref):
        out = []
        for layer in range(4):
            total = None
            for dx in range(2):
                for dy in range(2):
                    term = ref[0, 4 + 2 * layer + dx, pl.ds(dy, 16, stride=2), :]
                    total = term if total is None else total + term
            total = total + pltpu.roll(total, LANES - 1, 1)
            out.append(0.125 * jnp.take_along_axis(total, (2 * lanes(16) + 64) % LANES, axis=1))
        return out

    odd_8 = lanes(8) % 2 == 1

    def pairs_1(ref):
        out = []
        for layer in range(2):
            total = None
            for dx in range(2):
                for dy in range(2):
                    term = ref[0, 5 + 2 * layer + dx, pl.ds(dy, 8, stride=2), :]
                    total = term if total is None else total + term
            total = total + jnp.where(odd_8, pltpu.roll(total, 1, 1), pltpu.roll(total, LANES - 1, 1))
            out.append(0.125 * total)
        return jnp.where(odd_8, out[1], out[0])

    def squeeze_1(layers, ref, row):
        for part in range(2):
            ref[pl.ds(row + 16 * part, 16), :] = jnp.where(lanes(16) < 64, layers[part], layers[part + 2])

    load_c.wait()
    squeeze_1(restrict_0(c0), zs, 32)
    for half in range(2):
        zs[pl.ds(64 * half, 16), :] = pack(halves_0(c0, half))
    load_s.wait()
    for half in range(2):
        zs[pl.ds(64 * half + 16, 16), :] = pack(halves_0(s0, half))

    pl.semaphore_wait(barrier, len(partners))

    send(from_z, zs, rz.at[1], 0, -1, 96)
    send(from_z, zs, rz.at[0], 0, 1, 96)
    send(from_edge, c0.at[0, pl.ds(4, 4)], c0.at[0, pl.ds(12, 4)], -1, 0, 128)
    send(from_edge, c0.at[0, pl.ds(8, 4)], c0.at[0, pl.ds(0, 4)], 1, 0, 128)
    for dw, dn in corners:
        row = 0 if dw < 0 else 64
        send(from_edge, zs.at[pl.ds(row, 32)], rcn.at[(1 - dw) // 2, (1 - dn) // 2], dw, dn, 32)
    send(from_edge, s0.at[0, pl.ds(4, 3)], s0.at[0, pl.ds(12, 3)], -1, 0, 96)
    send(from_edge, s0.at[0, pl.ds(9, 3)], s0.at[0, pl.ds(1, 3)], 1, 0, 96)
    for dw, dn in [(-1, 0), (1, 0)] + corners:
        send(from_k, zs.at[pl.ds(32, 32)], k1c.at[1 - dw, 1 - dn], dw, dn, 32)

    def fill_0(ref, first, packed):
        for layer in range(4):
            for part in range(2):
                ref[1, first + layer, pl.ds(16 * part, 16), :] = unpack(packed, 2 * layer + part)

    steps = cheb(3)
    receive(from_z, 192)
    for field, ref in enumerate((c0, s0)):
        for half in range(2):
            rows = pl.ds(64 * half + 16 * field, 16)
            fill_0(ref, 4 + 4 * half, merged(rz[0, rows, :], rz[1, rows, :]))
    level_0.setup(5, 10, 3, 2)
    level_0.start(5, 10, 6, 2, steps[0][1])
    level_0.sweep(level_0.va, level_0.vb, 6, 9, 4, 2, 2, steps[1], fresh=True)
    level_0.sweep(level_0.vb, level_0.va, 7, 8, 2, 2, 2, steps[2])

    receive(from_edge, 576)
    for field, ref in enumerate((c0, s0)):
        for side in range(2):
            rows = pl.ds(16 * field, 16)
            fill_0(ref, 12 * side, merged(rcn[side, 0, rows, :], rcn[side, 1, rows, :]))
    level_0.setup_below(1, 2)
    over_sides(1, 11, 4, lambda at: level_0.setup_at(at, 2))
    over_sides(1, 11, 4, lambda at: level_0.start_at(at, 2, steps[0][1]))
    over_sides(2, 10, 4, lambda at: level_0.sweep_at(at, level_0.va, level_0.vb, 2, 2, steps[1], True))
    over_sides(3, 9, 4, lambda at: level_0.sweep_at(at, level_0.vb, level_0.va, 2, 2, steps[2], False))
    level_0.residual(level_0.va, level_0.vb, 4, 11, 4, 2)

    squeeze_1(restrict_0(level_0.vb), sk, 0)
    for dw, dn in around:
        send(from_s1, sk, k1s.at[1 - dw, 1 - dn], dw, dn, 32)

    for side in range(2):
        first = 9 if side == 0 else 4
        tiles = []
        for layer in range(3):
            sb0[side, pl.ds(32 * layer, 32), :] = level_0.va[0, first + layer]
            for part in range(2):
                tiles.append(level_0.va[1, first + layer, pl.ds(16 * part, 16), :])
        sb0[side, pl.ds(96, 16), :] = pack(tiles)
        send(from_x0, sb0.at[side], hx0.at[side], 1 - 2 * side, 0, 112)

    def spread_1(ref, block):
        at_lane = lanes(16)
        low_half = at_lane < 64
        low_quarter = at_lane % 64 < 32
        for dx in (-1, 0, 1):
            for part in range(2):
                before, own, after = (block(dx, dz, part) for dz in (-1, 0, 1))
                near = jnp.where(low_quarter, before, after)
                outer = jnp.where(low_quarter, after, before)
                own_r, near_r, outer_r = (pltpu.roll(t, 64, 1) for t in (own, near, outer))
                at = 5 + 4 * dx + part
                for at, own_a, own_b, near_a, near_b, outer_a, outer_b in (
                    (at, own, own_r, near, near_r, outer, outer_r),
                    (at + 2, own_r, own, near_r, near, outer_r, outer),
                ):
                    centre = jnp.where(low_half, own_a, own_b)
                    ref[0, at] = jnp.where(at_lane < 32, near_a, jnp.where(at_lane < 96, centre, near_b))
                    ref[1, at] = jnp.where(low_half, outer_a, outer_b)

    def coef_block(dx, dz, part):
        if dx == 0:
            rows = pl.ds(32 + 16 * part, 16)
            return zs[rows, :] if dz == 0 else rz[(1 + dz) // 2, rows, :]
        return k1c[1 + dx, 1 + dz, pl.ds(16 * part, 16), :]

    def source_block(dx, dz, part):
        rows = pl.ds(16 * part, 16)
        return sk[rows, :] if dx == 0 and dz == 0 else k1s[1 + dx, 1 + dz, rows, :]

    receive(from_k, 192)
    spread_1(level_1.c, coef_block)
    send(from_c1b, level_1.c.at[:, 9], level_1.c.at[:, 13], -1, 0, 32)
    send(from_c1b, level_1.c.at[:, 4], level_1.c.at[:, 0], 1, 0, 32)
    value = pairs_1(level_1.c)
    c2m[...] = value
    rc2[REACH] = value
    for dw, dn in far:
        send(from_c2, c2m, rc2.at[REACH - dw], dw, dn, 8)
    receive(from_c1b, 64)
    level_1.setup(1, 12, 6, 2)

    receive(from_s1, 256)
    spread_1(level_1.s, source_block)
    level_1.start(2, 11, 10, 2, steps[0][1])
    level_1.sweep(level_1.va, level_1.vb, 3, 10, 8, 2, 1, steps[1], fresh=True)
    level_1.sweep(level_1.vb, level_1.va, 4, 9, 6, 1, 1, steps[2])
    level_1.residual(level_1.va, level_1.vb, 5, 8, 4, 1)

    value = pairs_1(level_1.vb)
    s2m[...] = value
    rs2[REACH] = value
    for dw, dn in far:
        send(from_s2, s2m, rs2.at[REACH - dw], dw, dn, 8)

    own_1 = level_1.va.at[0, pl.ds(5, 4)]
    send(from_x1, own_1, rx1.at[1], -1, 0, 64, 1)
    send(from_x1, own_1, rx1.at[0], 1, 0, 64, 1)
    send(from_x1, level_1.va.at[0, 5], rx1b.at[1], -2, 0, 16, 1)
    send(from_x1, level_1.va.at[0, 8], rx1b.at[0], 2, 0, 16, 1)

    def spread_2(ref, blocks):
        for block in range(2 * REACH + 1):
            packed = blocks[block]
            ref[0, 2 * block] = jnp.where(odd_8, pltpu.roll(packed, 1, 1), packed)
            ref[0, 2 * block + 1] = jnp.where(odd_8, packed, pltpu.roll(packed, LANES - 1, 1))

    def restrict_2(ref, at):
        total = ref[0, 2 * at + 2] + ref[0, 2 * at + 3]
        odd_row = lax.broadcasted_iota(jnp.int32, (8, LANES), 0) % 2 == 1
        total = total + jnp.where(odd_row, pltpu.roll(total, 1, 0), pltpu.roll(total, 7, 0))
        second = lanes(8) % 4 >= 2
        total = total + jnp.where(second, pltpu.roll(total, 2, 1), pltpu.roll(total, LANES - 2, 1))
        return 0.125 * total

    receive(from_c2, 128)
    spread_2(level_2.c, rc2)
    level_2.setup(1, 32, 8, 1)
    for at in range(15):
        level_3.c[0, at] = restrict_2(level_2.c, at)
    level_3.setup(1, 13, 13, 1)

    receive(from_s2, 128)
    spread_2(level_2.s, rs2)
    level_2.start(1, 32, 32, 1, steps[0][1])
    level_2.sweep(level_2.va, level_2.vb, 2, 31, 15, 1, 1, steps[1], fresh=True)
    level_2.sweep(level_2.vb, level_2.va, 3, 30, 14, 1, 1, steps[2])
    level_2.residual(level_2.va, level_2.vb, 4, 29, 13, 1)

    for at in range(1, 14):
        level_3.s[0, at] = restrict_2(level_2.vb, at)
    coarse = cheb(4)
    level_3.start(1, 13, 13, 1, coarse[0][1])
    level_3.sweep(level_3.va, level_3.vb, 2, 12, 11, 1, 1, coarse[1], fresh=True)
    level_3.sweep(level_3.vb, level_3.va, 3, 11, 9, 1, 1, coarse[2])
    level_3.sweep(level_3.va, level_3.vb, 4, 10, 7, 1, 1, coarse[3])

    for at in range(10, 24):
        level_2.vb[0, at] = level_2.va[0, at] + level_3.vb[0, (at - 2) // 2]
    level_2.sweep(level_2.vb, level_2.va, 11, 22, 12, 1, 1, steps[0], fresh=True)
    level_2.sweep(level_2.va, level_2.vb, 12, 21, 10, 1, 1, steps[1])
    level_2.sweep(level_2.vb, level_2.va, 13, 20, 8, 1, 1, steps[2])

    for at in range(8):
        value = level_2.va[0, 13 + at]
        for part in range(2):
            p1[at, pl.ds(part, 8, stride=2), :] = value
    receive(from_x1, 160)
    for at in range(14):
        if 5 <= at <= 8:
            before = level_1.va[0, at]
        else:
            beside = (rx1b[0] if at == 0 else rx1[0, at - 1] if at < 5 else rx1[1, at - 9] if at < 13 else rx1b[1])
            before = beside * level_1.inside(at)
        level_1.vb[0, at] = before + p1[(at + 1) // 2]
    sends_done(1)
    level_1.sweep(level_1.vb, level_1.va, 1, 12, 12, 1, 1, steps[0], fresh=True)
    level_1.sweep(level_1.va, level_1.vb, 2, 11, 10, 1, 1, steps[1])
    level_1.sweep(level_1.vb, level_1.va, 3, 10, 8, 1, 1, steps[2])

    fine_lane = lanes(16) // 2
    for at in range(8):
        value = level_1.va[0, 3 + at]
        for k in range(2):
            fine = jnp.take_along_axis(value, (fine_lane + (32 if k == 0 else 96)) % LANES, axis=1)
            for part in range(2):
                p0[k, at, pl.ds(part, 16, stride=2), :] = fine
    receive(from_x0, 224)
    for side in range(2):
        packed = hx0[side, pl.ds(96, 16), :]
        for layer in range(3):
            at = (1 if side == 0 else 12) + layer
            inside = level_0.inside(at)
            coarse_at = (at - 4) // 2 + 2
            level_0.vb[0, at] = hx0[side, pl.ds(32 * layer, 32), :] * inside + p0[0, coarse_at]
            for part in range(2):
                rows = pl.ds(16 * part, 16)
                level_0.vb[1, at, rows, :] = (
                    unpack(packed, 2 * layer + part) * (level_0.lane_mask[1][:16] * inside) + p0[1, coarse_at, rows, :]
                )

    def correct(at):
        for k in range(2):
            level_0.vb[k, at] = level_0.va[k, at] + p0[k, at // 2]

    over_layers(4, 11, 4, correct)
    level_0.sweep(level_0.vb, level_0.va, 2, 13, 4, 2, 2, steps[0], fresh=True)
    level_0.sweep(level_0.va, level_0.vb, 3, 12, 5, 2, 2, steps[1])
    level_0.finish(level_0.vb, level_0.va, kept, added, 4, 11, 4, steps[2])

    sends_done(0)


def per_device(right_side, conductivity, wide, narrow):
    brick = (8, 32, LANES)
    scratch = []
    for shape in LEVEL_SHAPES:
        scratch += [pltpu.VMEM(shape, F32)] * LEVEL_FIELDS
    shapes = [
        (96, LANES), (2, 96, LANES), (2, 2, 32, LANES), (3, 3, 32, LANES),
        (4, 16, LANES), (32, LANES), (3, 3, 32, LANES),
        (8, LANES), (2 * REACH + 1, 8, LANES), (8, LANES), (2 * REACH + 1, 8, LANES),
        (2, 4, 16, LANES), (2, 16, LANES),
        (2, 112, LANES), (2, 112, LANES),
        (8, 16, LANES), (2, 8, 32, LANES),
        (RULER, LANES),
    ]
    scratch += [pltpu.VMEM(shape, F32) for shape in shapes]
    scratch += [pltpu.SemaphoreType.DMA((2,)), pltpu.SemaphoreType.DMA((2,)), pltpu.SemaphoreType.DMA((9,))]
    kept, added = pl.pallas_call(
        functools.partial(kernel, wide, narrow),
        out_shape=[jax.ShapeDtypeStruct(brick, F32)] * 2,
        in_specs=[pl.BlockSpec(memory_space=pltpu.HBM)] * 2,
        out_specs=[pl.BlockSpec(memory_space=pltpu.VMEM)] * 2,
        scratch_shapes=scratch,
        compiler_params=pltpu.CompilerParams(
            collective_id=0, has_side_effects=True, vmem_limit_bytes=32 * 1024 * 1024
        ),
    )(right_side, conductivity)
    return kept + added


def solution(mesh):
    spec = P("wide", None, "narrow")
    body = functools.partial(per_device, wide=mesh.shape["wide"], narrow=mesh.shape["narrow"])
    return jax.shard_map(body, mesh=mesh, in_specs=(spec, spec), out_specs=spec, check_vma=False)
```

```python
import functools

import jax
import jax.numpy as jnp
from jax import lax
from jax.experimental import pallas as pl
from jax.experimental.pallas import tpu as pltpu
from jax.sharding import PartitionSpec as P

CENTER = 1.125
HALF = 0.875
LANES = 128
REACH = 8
F32 = jnp.float32
MESH_ID = pl.DeviceIdType.MESH


def cheb(sweeps):
    sigma = CENTER / HALF
    steps = [(0.0, 1.0 / CENTER)]
    ratio = 1.0 / sigma
    for _ in range(sweeps - 1):
        ratio_next = 1.0 / (2.0 * sigma - ratio)
        steps.append((ratio_next * ratio, 2.0 * ratio_next / HALF))
        ratio = ratio_next
    return steps


def over_sides(first, second, count, body):
    def block(side, carry):
        for at in range(count):
            body(first + side * (second - first) + at)
        return carry

    lax.fori_loop(0, 2, block, 0)


def over_layers(low, high, unroll, body):
    count = high - low + 1
    if count == unroll:
        for at in range(low, high + 1):
            body(at)
        return

    def block(step, carry):
        for at in range(unroll):
            body(low + step * unroll + at)
        return carry

    lax.fori_loop(0, count // unroll, block, 0)


class Level:
    def __init__(self, refs, scale, rows, row_step, lane_step, base, extent, lane_mask):
        self.c, self.s, self.cx, self.cy, self.cz, self.iv, self.dg, self.va, self.vb = refs
        self.half = 0.5 * scale
        self.rows, self.row_step, self.lane_step = rows, row_step, lane_step
        self.base, self.extent, self.lane_mask = base, extent, lane_mask

    def inside(self, at):
        where_x = self.base + at
        return jnp.where((where_x >= 0) & (where_x < self.extent), 1.0, 0.0).astype(F32)

    def lane(self):
        return lax.broadcasted_iota(jnp.int32, (self.rows, LANES), 1)

    def row(self):
        return lax.broadcasted_iota(jnp.int32, (self.rows, LANES), 0)

    def y_up(self, tile):
        return pltpu.roll(tile, self.rows - self.row_step, 0)

    def y_down(self, tile):
        return pltpu.roll(tile, self.row_step, 0)

    def turned(self, tiles, shift, edge, count):
        out = [pltpu.roll(t, shift, 1) for t in tiles]
        if len(tiles) == 1:
            return out
        at_edge = self.lane() == edge
        return [jnp.where(at_edge, out[1 - k], out[k]) for k in range(count)]

    def z_up(self, tiles, count):
        return self.turned(tiles, LANES - self.lane_step, LANES - 1, count)

    def z_down(self, tiles, count):
        return self.turned(tiles, self.lane_step, 0, count)

    def masked(self, at, tiles):
        keep = self.inside(at) * self.half
        out = []
        for k in range(tiles):
            mask = self.lane_mask[k]
            out.append(self.c[k, at] * (keep if mask is None else mask * keep))
        return out

    def setup_below(self, low, tiles):
        first, second = self.masked(low - 1, tiles), self.masked(low, tiles)
        for k in range(tiles):
            self.cx[k, low - 1] = first[k] + second[k]

    def setup_at(self, at, tiles):
        before, here, after = self.masked(at - 1, tiles), self.masked(at, tiles), self.masked(at + 1, tiles)
        inside = self.inside(at)
        top = self.row() >= self.rows - self.row_step
        bottom = self.row() < self.row_step
        z_up, z_down = self.z_up(here, tiles), self.z_down(here, tiles)
        for k in range(tiles):
            own = here[k]
            x_low = before[k] + own
            x_high = own + after[k]
            y_low = own + jnp.where(bottom, 0.0, self.y_down(own))
            y_high = own + jnp.where(top, 0.0, self.y_up(own))
            z_low = own + z_down[k]
            z_high = own + z_up[k]
            diagonal = x_low + x_high + y_low + y_high + z_low + z_high
            keep = inside if self.lane_mask[k] is None else self.lane_mask[k] * inside
            self.cx[k, at] = x_high
            self.cy[k, at] = jnp.where(top, 0.0, y_high)
            self.cz[k, at] = z_high
            if k == 0:
                self.dg[0, at] = diagonal
            self.iv[k, at] = jnp.where(jnp.full_like(own, 0.0) + keep > 0.5, 1.0 / diagonal, 0.0)

    def setup(self, low, high, unroll, tiles):
        self.setup_below(low, tiles)
        over_layers(low, high, unroll, lambda at: self.setup_at(at, tiles))

    def start_at(self, at, tiles, beta):
        for k in range(tiles):
            self.va[k, at] = self.s[k, at] * self.iv[k, at] * beta

    def start(self, low, high, unroll, tiles, beta):
        over_layers(low, high, unroll, lambda at: self.start_at(at, tiles, beta))

    def around(self, field, at, tiles, count):
        here = [field[k, at] for k in range(tiles)]
        cz = [self.cz[k, at] for k in range(tiles)]
        z_up = self.z_up(here, count)
        z_down = self.z_down([cz[k] * here[k] for k in range(tiles)], count)
        sums = []
        for k in range(count):
            cy = self.cy[k, at]
            total = self.cx[k, at] * field[k, at + 1] + self.cx[k, at - 1] * field[k, at - 1]
            total = total + (cy * self.y_up(here[k]) + self.y_down(cy * here[k]))
            total = total + (cz[k] * z_up[k] + z_down[k])
            sums.append(total + self.s[k, at])
        return here, sums

    def sweep_at(self, at, field, result, tiles, count, step, fresh):
        alpha, beta = step
        here, sums = self.around(field, at, tiles, count)
        for k in range(count):
            kept = (1.0 + alpha - beta) * here[k]
            if not fresh:
                kept = kept - alpha * result[k, at]
            result[k, at] = kept + (beta * self.iv[k, at]) * sums[k]

    def sweep(self, field, result, low, high, unroll, tiles, count, step, fresh=False):
        over_layers(low, high, unroll, lambda at: self.sweep_at(at, field, result, tiles, count, step, fresh))

    def residual(self, field, result, low, high, unroll, tiles):
        def body(at):
            here, sums = self.around(field, at, tiles, 1)
            result[0, at] = sums[0] - self.dg[0, at] * here[0]

        over_layers(low, high, unroll, body)

    def finish(self, field, older, kept_out, added_out, low, high, unroll, step):
        alpha, beta = step

        def body(at):
            here, sums = self.around(field, at, 2, 1)
            kept_out[at - low] = (1.0 + alpha - beta) * here[0] - alpha * older[0, at]
            added_out[at - low] = (beta * self.iv[0, at]) * sums[0]

        over_layers(low, high, unroll, body)


LEVEL_FIELDS = 9
LEVEL_SHAPES = ((2, 16, 32, LANES), (2, 14, 16, LANES), (1, 34, 8, LANES), (1, 15, 8, LANES))
RULER = 1760


def kernel(wide, narrow, rhs, coef, kept, added, *scratch):
    scratch = list(scratch)
    level_refs = []
    for _ in range(4):
        level_refs.append(scratch[:LEVEL_FIELDS])
        scratch = scratch[LEVEL_FIELDS:]
    (zs, rz, rcn, k1c, sk, k1s, c2m, rc2, s2m, rs2, rx1, rx1b, sb0, hx0, p1, p0, ruler,
     local_sem, send_sem, recv_sem) = scratch
    me_w = lax.axis_index("wide")
    me_n = lax.axis_index("narrow")

    def there(dw, dn):
        return (lax.rem(me_w + (dw + wide), wide), lax.rem(me_n + (dn + narrow), narrow))

    far = [(sign * dw, 0) for dw in range(REACH, 0, -1) for sign in (1, -1)]
    corners = [(dw, dn) for dw in (-1, 1) for dn in (-1, 1)]
    around = [(-1, 0), (1, 0), (0, -1), (0, 1)] + corners
    partners = around + far[:-2]
    barrier = pltpu.get_barrier_semaphore()
    for dw, dn in around:
        pl.semaphore_signal(barrier, inc=1, device_id=there(dw, dn), device_id_type=MESH_ID)

    c0, s0 = level_refs[0][0], level_refs[0][1]
    load_c = pltpu.make_async_copy(coef, c0.at[0, pl.ds(4, 8)], local_sem.at[0])
    load_s = pltpu.make_async_copy(rhs, s0.at[0, pl.ds(4, 8)], local_sem.at[1])
    load_c.start()
    load_s.start()
    for dw, dn in far[:-2]:
        pl.semaphore_signal(barrier, inc=1, device_id=there(dw, dn), device_id_type=MESH_ID)

    left = jnp.where(me_n > 0, 1.0, 0.0).astype(F32)
    right = jnp.where(me_n < narrow - 1, 1.0, 0.0).astype(F32)

    def lanes(rows):
        return lax.broadcasted_iota(jnp.int32, (rows, LANES), 1)

    def edges(rows, until, low, since, high):
        at = lanes(rows)
        return jnp.where(at < until, low, jnp.where(at >= since, high, 0.0))

    def centred(rows):
        at = lanes(rows)
        return jnp.where((at >= 32) & (at < 96), 1.0, edges(rows, 32, left, 96, right))

    level_0 = Level(level_refs[0], 1.0, 32, 1, 1, 8 * me_w - 4, 8 * wide, [None, edges(32, 8, right, 120, left)])
    level_1 = Level(
        level_refs[1], 0.25, 16, 1, 1, 4 * me_w - 5, 4 * wide, [centred(16), edges(16, 32, right, 96, left)]
    )
    level_2 = Level(level_refs[2], 0.0625, 8, 1, 2, 2 * me_w - 16, 2 * wide, [centred(8)])
    level_3 = Level(level_refs[3], 0.015625, 8, 2, 4, me_w - 7, wide, [centred(8)])

    sent = [0, 0]

    def send(group, src, dst, dw, dn, rows, sender=0):
        sent[sender] += rows
        pltpu.make_async_remote_copy(
            src_ref=src, dst_ref=dst, send_sem=send_sem.at[sender], recv_sem=recv_sem.at[group],
            device_id=there(dw, dn), device_id_type=MESH_ID,
        ).start()

    def ruled(rows, group, sender):
        span = ruler.at[pl.ds(0, rows)]
        return pltpu.make_async_remote_copy(
            src_ref=span, dst_ref=span, send_sem=send_sem.at[sender], recv_sem=recv_sem.at[group],
            device_id=there(1, 0), device_id_type=MESH_ID,
        )

    def receive(group, rows):
        ruled(rows, group, 0).wait_recv()

    def sends_done(sender):
        ruled(sent[sender], 0, sender).wait_send()

    (from_z, from_c, from_s, from_k, from_s1, from_c1b, from_x0, from_c2, from_x1, from_s2) = range(10)

    def pack(tiles):
        rows = tiles[0].shape[0]
        group = lanes(rows) // 16
        packed = jnp.zeros((rows, LANES), F32)
        for at, tile in enumerate(tiles):
            packed = jnp.where(group == at, pltpu.roll(tile, (16 * at + 8) % LANES, 1), packed)
        return packed

    def unpack(packed, at):
        return pltpu.roll(packed, (2 * LANES - (16 * at + 8)) % LANES, 1)

    def pack_side(ref, half, side):
        group = lanes(8) // 8
        packed = None
        for layer in range(4):
            for part in range(4):
                at = 4 * layer + part
                tile = ref[0, 4 + 4 * half + layer, pl.ds(8 * part, 8), :]
                tile = pltpu.roll(tile, (8 * at + 8 * side) % LANES, 1)
                packed = tile if at == 0 else jnp.where(group == at, tile, packed)
        return packed

    def restrict_0(ref):
        out = []
        for layer in range(4):
            total = None
            for dx in range(2):
                for dy in range(2):
                    term = ref[0, 4 + 2 * layer + dx, pl.ds(dy, 16, stride=2), :]
                    total = term if total is None else total + term
            total = total + pltpu.roll(total, LANES - 1, 1)
            out.append(0.125 * jnp.take_along_axis(total, (2 * lanes(16) + 64) % LANES, axis=1))
        return out

    odd_8 = lanes(8) % 2 == 1

    def pairs_1(ref):
        out = []
        for layer in range(2):
            total = None
            for dx in range(2):
                for dy in range(2):
                    term = ref[0, 5 + 2 * layer + dx, pl.ds(dy, 8, stride=2), :]
                    total = term if total is None else total + term
            total = total + jnp.where(odd_8, pltpu.roll(total, 1, 1), pltpu.roll(total, LANES - 1, 1))
            out.append(0.125 * total)
        return jnp.where(odd_8, out[1], out[0])

    def squeeze_1(layers, ref, row):
        for part in range(2):
            ref[pl.ds(row + 16 * part, 16), :] = jnp.where(lanes(16) < 64, layers[part], layers[part + 2])

    load_c.wait()
    own_c1 = restrict_0(c0)
    for side in range(2):
        squeeze_1(own_c1, zs.at[side], 32)
        for half in range(2):
            zs[side, pl.ds(16 * half, 8), :] = pack_side(c0, half, side)
    load_s.wait()
    for side in range(2):
        for half in range(2):
            zs[side, pl.ds(16 * half + 8, 8), :] = pack_side(s0, half, side)

    pl.semaphore_wait(barrier, len(partners))

    send(from_c, c0.at[0, pl.ds(4, 4)], c0.at[0, pl.ds(12, 4)], -1, 0, 128)
    send(from_c, c0.at[0, pl.ds(8, 4)], c0.at[0, pl.ds(0, 4)], 1, 0, 128)
    send(from_z, zs.at[0], rz.at[1], 0, -1, 64)
    send(from_z, zs.at[1], rz.at[0], 0, 1, 64)
    for dw, dn in corners:
        row = 0 if dw < 0 else 16
        span = zs.at[(1 + dn) // 2, pl.ds(row, 16)]
        send(from_c, span, rcn.at[(1 - dw) // 2, (1 - dn) // 2], dw, dn, 16)
    send(from_s, s0.at[0, pl.ds(4, 3)], s0.at[0, pl.ds(12, 3)], -1, 0, 96)
    send(from_s, s0.at[0, pl.ds(9, 3)], s0.at[0, pl.ds(1, 3)], 1, 0, 96)
    for dw, dn in [(-1, 0), (1, 0)] + corners:
        send(from_k, zs.at[0, pl.ds(32, 32)], k1c.at[1 - dw, 1 - dn], dw, dn, 32)

    def fill_0(ref, first, from_left, from_right):
        low = lanes(8) < 64
        for layer in range(4):
            for part in range(4):
                at = 4 * layer + part
                ref[1, first + layer, pl.ds(8 * part, 8), :] = jnp.where(
                    low, pltpu.roll(from_right, (LANES - 8 * at) % LANES, 1), pltpu.roll(from_left, (120 - 8 * at) % LANES, 1)
                )

    steps = cheb(3)
    receive(from_z, 128)
    for field, ref in enumerate((c0, s0)):
        for half in range(2):
            rows = pl.ds(16 * half + 8 * field, 8)
            fill_0(ref, 4 + 4 * half, rz[0, rows, :], rz[1, rows, :])
    level_0.setup(5, 10, 3, 2)
    level_0.start(5, 10, 6, 2, steps[0][1])
    level_0.sweep(level_0.va, level_0.vb, 6, 9, 4, 2, 2, steps[1], fresh=True)
    level_0.sweep(level_0.vb, level_0.va, 7, 8, 2, 2, 2, steps[2])

    receive(from_c, 320)
    for field, ref in enumerate((c0, s0)):
        for side in range(2):
            rows = pl.ds(8 * field, 8)
            fill_0(ref, 12 * side, rcn[side, 0, rows, :], rcn[side, 1, rows, :])
    level_0.setup_below(1, 2)
    over_sides(1, 11, 4, lambda at: level_0.setup_at(at, 2))
    receive(from_s, 192)
    over_sides(1, 11, 4, lambda at: level_0.start_at(at, 2, steps[0][1]))
    over_sides(2, 10, 4, lambda at: level_0.sweep_at(at, level_0.va, level_0.vb, 2, 2, steps[1], True))
    over_sides(3, 9, 4, lambda at: level_0.sweep_at(at, level_0.vb, level_0.va, 2, 2, steps[2], False))
    level_0.residual(level_0.va, level_0.vb, 4, 11, 4, 2)

    squeeze_1(restrict_0(level_0.vb), sk, 0)
    for dw, dn in around:
        send(from_s1, sk, k1s.at[1 - dw, 1 - dn], dw, dn, 32)

    for side in range(2):
        first = 9 if side == 0 else 4
        tiles = []
        for layer in range(3):
            sb0[side, pl.ds(32 * layer, 32), :] = level_0.va[0, first + layer]
            for part in range(2):
                tiles.append(level_0.va[1, first + layer, pl.ds(16 * part, 16), :])
        sb0[side, pl.ds(96, 16), :] = pack(tiles)
        send(from_x0, sb0.at[side], hx0.at[side], 1 - 2 * side, 0, 112)

    def spread_1(ref, block):
        at_lane = lanes(16)
        low_half = at_lane < 64
        low_quarter = at_lane % 64 < 32
        for dx in (-1, 0, 1):
            for part in range(2):
                before, own, after = (block(dx, dz, part) for dz in (-1, 0, 1))
                near = jnp.where(low_quarter, before, after)
                outer = jnp.where(low_quarter, after, before)
                own_r, near_r, outer_r = (pltpu.roll(t, 64, 1) for t in (own, near, outer))
                at = 5 + 4 * dx + part
                for at, own_a, own_b, near_a, near_b, outer_a, outer_b in (
                    (at, own, own_r, near, near_r, outer, outer_r),
                    (at + 2, own_r, own, near_r, near, outer_r, outer),
                ):
                    centre = jnp.where(low_half, own_a, own_b)
                    ref[0, at] = jnp.where(at_lane < 32, near_a, jnp.where(at_lane < 96, centre, near_b))
                    ref[1, at] = jnp.where(low_half, outer_a, outer_b)

    def coef_block(dx, dz, part):
        if dx == 0:
            rows = pl.ds(32 + 16 * part, 16)
            return zs[0, rows, :] if dz == 0 else rz[(1 + dz) // 2, rows, :]
        return k1c[1 + dx, 1 + dz, pl.ds(16 * part, 16), :]

    def source_block(dx, dz, part):
        rows = pl.ds(16 * part, 16)
        return sk[rows, :] if dx == 0 and dz == 0 else k1s[1 + dx, 1 + dz, rows, :]

    receive(from_k, 192)
    spread_1(level_1.c, coef_block)
    send(from_c1b, level_1.c.at[:, 9], level_1.c.at[:, 13], -1, 0, 32)
    send(from_c1b, level_1.c.at[:, 4], level_1.c.at[:, 0], 1, 0, 32)
    value = pairs_1(level_1.c)
    c2m[...] = value
    rc2[REACH] = value
    for dw, dn in far:
        send(from_c2, c2m, rc2.at[REACH - dw], dw, dn, 8)
    receive(from_c1b, 64)
    level_1.setup(1, 12, 6, 2)

    receive(from_s1, 256)
    spread_1(level_1.s, source_block)
    level_1.start(2, 11, 10, 2, steps[0][1])
    level_1.sweep(level_1.va, level_1.vb, 3, 10, 8, 2, 1, steps[1], fresh=True)
    level_1.sweep(level_1.vb, level_1.va, 4, 9, 6, 1, 1, steps[2])
    level_1.residual(level_1.va, level_1.vb, 5, 8, 4, 1)

    value = pairs_1(level_1.vb)
    s2m[...] = value
    rs2[REACH] = value
    for dw, dn in far:
        send(from_s2, s2m, rs2.at[REACH - dw], dw, dn, 8)

    own_1 = level_1.va.at[0, pl.ds(5, 4)]
    send(from_x1, own_1, rx1.at[1], -1, 0, 64, 1)
    send(from_x1, own_1, rx1.at[0], 1, 0, 64, 1)
    send(from_x1, level_1.va.at[0, 5], rx1b.at[1], -2, 0, 16, 1)
    send(from_x1, level_1.va.at[0, 8], rx1b.at[0], 2, 0, 16, 1)

    def spread_2(ref, blocks):
        for block in range(2 * REACH + 1):
            packed = blocks[block]
            ref[0, 2 * block] = jnp.where(odd_8, pltpu.roll(packed, 1, 1), packed)
            ref[0, 2 * block + 1] = jnp.where(odd_8, packed, pltpu.roll(packed, LANES - 1, 1))

    def restrict_2(ref, at):
        total = ref[0, 2 * at + 2] + ref[0, 2 * at + 3]
        odd_row = lax.broadcasted_iota(jnp.int32, (8, LANES), 0) % 2 == 1
        total = total + jnp.where(odd_row, pltpu.roll(total, 1, 0), pltpu.roll(total, 7, 0))
        second = lanes(8) % 4 >= 2
        total = total + jnp.where(second, pltpu.roll(total, 2, 1), pltpu.roll(total, LANES - 2, 1))
        return 0.125 * total

    receive(from_c2, 128)
    spread_2(level_2.c, rc2)
    level_2.setup(1, 32, 8, 1)
    for at in range(15):
        level_3.c[0, at] = restrict_2(level_2.c, at)
    level_3.setup(1, 13, 13, 1)

    receive(from_s2, 128)
    spread_2(level_2.s, rs2)
    level_2.start(1, 32, 32, 1, steps[0][1])
    level_2.sweep(level_2.va, level_2.vb, 2, 31, 15, 1, 1, steps[1], fresh=True)
    level_2.sweep(level_2.vb, level_2.va, 3, 30, 14, 1, 1, steps[2])
    level_2.residual(level_2.va, level_2.vb, 4, 29, 13, 1)

    for at in range(1, 14):
        level_3.s[0, at] = restrict_2(level_2.vb, at)
    coarse = cheb(4)
    level_3.start(1, 13, 13, 1, coarse[0][1])
    level_3.sweep(level_3.va, level_3.vb, 2, 12, 11, 1, 1, coarse[1], fresh=True)
    level_3.sweep(level_3.vb, level_3.va, 3, 11, 9, 1, 1, coarse[2])
    level_3.sweep(level_3.va, level_3.vb, 4, 10, 7, 1, 1, coarse[3])

    for at in range(10, 24):
        level_2.vb[0, at] = level_2.va[0, at] + level_3.vb[0, (at - 2) // 2]
    level_2.sweep(level_2.vb, level_2.va, 11, 22, 12, 1, 1, steps[0], fresh=True)
    level_2.sweep(level_2.va, level_2.vb, 12, 21, 10, 1, 1, steps[1])
    level_2.sweep(level_2.vb, level_2.va, 13, 20, 8, 1, 1, steps[2])

    for at in range(8):
        value = level_2.va[0, 13 + at]
        for part in range(2):
            p1[at, pl.ds(part, 8, stride=2), :] = value
    receive(from_x1, 160)
    for at in range(14):
        if 5 <= at <= 8:
            before = level_1.va[0, at]
        else:
            beside = (rx1b[0] if at == 0 else rx1[0, at - 1] if at < 5 else rx1[1, at - 9] if at < 13 else rx1b[1])
            before = beside * level_1.inside(at)
        level_1.vb[0, at] = before + p1[(at + 1) // 2]
    sends_done(1)
    level_1.sweep(level_1.vb, level_1.va, 1, 12, 12, 1, 1, steps[0], fresh=True)
    level_1.sweep(level_1.va, level_1.vb, 2, 11, 10, 1, 1, steps[1])
    level_1.sweep(level_1.vb, level_1.va, 3, 10, 8, 1, 1, steps[2])

    fine_lane = lanes(16) // 2
    for at in range(8):
        value = level_1.va[0, 3 + at]
        for k in range(2):
            fine = jnp.take_along_axis(value, (fine_lane + (32 if k == 0 else 96)) % LANES, axis=1)
            for part in range(2):
                p0[k, at, pl.ds(part, 16, stride=2), :] = fine
    receive(from_x0, 224)
    for side in range(2):
        packed = hx0[side, pl.ds(96, 16), :]
        for layer in range(3):
            at = (1 if side == 0 else 12) + layer
            inside = level_0.inside(at)
            coarse_at = (at - 4) // 2 + 2
            level_0.vb[0, at] = hx0[side, pl.ds(32 * layer, 32), :] * inside + p0[0, coarse_at]
            for part in range(2):
                rows = pl.ds(16 * part, 16)
                level_0.vb[1, at, rows, :] = (
                    unpack(packed, 2 * layer + part) * (level_0.lane_mask[1][:16] * inside) + p0[1, coarse_at, rows, :]
                )

    def correct(at):
        for k in range(2):
            level_0.vb[k, at] = level_0.va[k, at] + p0[k, at // 2]

    over_layers(4, 11, 4, correct)
    level_0.sweep(level_0.vb, level_0.va, 2, 13, 4, 2, 2, steps[0], fresh=True)
    level_0.sweep(level_0.va, level_0.vb, 3, 12, 5, 2, 2, steps[1])
    level_0.finish(level_0.vb, level_0.va, kept, added, 4, 11, 4, steps[2])

    sends_done(0)


def per_device(right_side, conductivity, wide, narrow):
    brick = (8, 32, LANES)
    scratch = []
    for shape in LEVEL_SHAPES:
        scratch += [pltpu.VMEM(shape, F32)] * LEVEL_FIELDS
    shapes = [
        (2, 64, LANES), (2, 64, LANES), (2, 2, 16, LANES), (3, 3, 32, LANES),
        (32, LANES), (3, 3, 32, LANES),
        (8, LANES), (2 * REACH + 1, 8, LANES), (8, LANES), (2 * REACH + 1, 8, LANES),
        (2, 4, 16, LANES), (2, 16, LANES),
        (2, 112, LANES), (2, 112, LANES),
        (8, 16, LANES), (2, 8, 32, LANES),
        (RULER, LANES),
    ]
    scratch += [pltpu.VMEM(shape, F32) for shape in shapes]
    scratch += [pltpu.SemaphoreType.DMA((2,)), pltpu.SemaphoreType.DMA((2,)), pltpu.SemaphoreType.DMA((10,))]
    kept, added = pl.pallas_call(
        functools.partial(kernel, wide, narrow),
        out_shape=[jax.ShapeDtypeStruct(brick, F32)] * 2,
        in_specs=[pl.BlockSpec(memory_space=pltpu.HBM)] * 2,
        out_specs=[pl.BlockSpec(memory_space=pltpu.VMEM)] * 2,
        scratch_shapes=scratch,
        compiler_params=pltpu.CompilerParams(
            collective_id=0, has_side_effects=True, vmem_limit_bytes=32 * 1024 * 1024
        ),
    )(pltpu.with_memory_space_constraint(right_side, pltpu.HBM), pltpu.with_memory_space_constraint(conductivity, pltpu.HBM))
    return kept + added


def solution(mesh):
    spec = P("wide", None, "narrow")
    body = functools.partial(per_device, wide=mesh.shape["wide"], narrow=mesh.shape["narrow"])
    return jax.shard_map(body, mesh=mesh, in_specs=(spec, spec), out_specs=spec, check_vma=False)
```

```python
import functools

import jax
import jax.numpy as jnp
from jax import lax
from jax.experimental import pallas as pl
from jax.experimental.pallas import tpu as pltpu
from jax.sharding import PartitionSpec as P

CENTER = 1.125
HALF = 0.875
LANES = 128
REACH = 8
F32 = jnp.float32
MESH_ID = pl.DeviceIdType.MESH


def cheb(sweeps):
    sigma = CENTER / HALF
    steps = [(0.0, 1.0 / CENTER)]
    ratio = 1.0 / sigma
    for _ in range(sweeps - 1):
        ratio_next = 1.0 / (2.0 * sigma - ratio)
        steps.append((ratio_next * ratio, 2.0 * ratio_next / HALF))
        ratio = ratio_next
    return steps


def over_sides(first, second, count, body):
    def block(side, carry):
        for at in range(count):
            body(first + side * (second - first) + at)
        return carry

    lax.fori_loop(0, 2, block, 0)


def over_layers(low, high, unroll, body):
    count = high - low + 1
    if count == unroll:
        for at in range(low, high + 1):
            body(at)
        return

    def block(step, carry):
        for at in range(unroll):
            body(low + step * unroll + at)
        return carry

    lax.fori_loop(0, count // unroll, block, 0)


class Level:
    def __init__(self, refs, scale, rows, row_step, lane_step, base, extent, lane_mask):
        self.c, self.s, self.cx, self.cy, self.cz, self.iv, self.dg, self.va, self.vb = refs
        self.half = 0.5 * scale
        self.rows, self.row_step, self.lane_step = rows, row_step, lane_step
        self.base, self.extent, self.lane_mask = base, extent, lane_mask

    def inside(self, at):
        where_x = self.base + at
        return jnp.where((where_x >= 0) & (where_x < self.extent), 1.0, 0.0).astype(F32)

    def lane(self):
        return lax.broadcasted_iota(jnp.int32, (self.rows, LANES), 1)

    def row(self):
        return lax.broadcasted_iota(jnp.int32, (self.rows, LANES), 0)

    def y_up(self, tile):
        return pltpu.roll(tile, self.rows - self.row_step, 0)

    def y_down(self, tile):
        return pltpu.roll(tile, self.row_step, 0)

    def turned(self, tiles, shift, edge, count):
        out = [pltpu.roll(t, shift, 1) for t in tiles]
        if len(tiles) == 1:
            return out
        at_edge = self.lane() == edge
        return [jnp.where(at_edge, out[1 - k], out[k]) for k in range(count)]

    def z_up(self, tiles, count):
        return self.turned(tiles, LANES - self.lane_step, LANES - 1, count)

    def z_down(self, tiles, count):
        return self.turned(tiles, self.lane_step, 0, count)

    def masked(self, at, tiles):
        keep = self.inside(at) * self.half
        out = []
        for k in range(tiles):
            mask = self.lane_mask[k]
            out.append(self.c[k, at] * (keep if mask is None else mask * keep))
        return out

    def setup_below(self, low, tiles):
        first, second = self.masked(low - 1, tiles), self.masked(low, tiles)
        for k in range(tiles):
            self.cx[k, low - 1] = first[k] + second[k]

    def setup_at(self, at, tiles):
        before, here, after = self.masked(at - 1, tiles), self.masked(at, tiles), self.masked(at + 1, tiles)
        inside = self.inside(at)
        top = self.row() >= self.rows - self.row_step
        bottom = self.row() < self.row_step
        z_up, z_down = self.z_up(here, tiles), self.z_down(here, tiles)
        for k in range(tiles):
            own = here[k]
            x_low = before[k] + own
            x_high = own + after[k]
            y_low = own + jnp.where(bottom, 0.0, self.y_down(own))
            y_high = own + jnp.where(top, 0.0, self.y_up(own))
            z_low = own + z_down[k]
            z_high = own + z_up[k]
            diagonal = x_low + x_high + y_low + y_high + z_low + z_high
            keep = inside if self.lane_mask[k] is None else self.lane_mask[k] * inside
            self.cx[k, at] = x_high
            self.cy[k, at] = jnp.where(top, 0.0, y_high)
            self.cz[k, at] = z_high
            if k == 0:
                self.dg[0, at] = diagonal
            self.iv[k, at] = jnp.where(jnp.full_like(own, 0.0) + keep > 0.5, 1.0 / diagonal, 0.0)

    def setup(self, low, high, unroll, tiles):
        self.setup_below(low, tiles)
        over_layers(low, high, unroll, lambda at: self.setup_at(at, tiles))

    def start_at(self, at, tiles, beta):
        for k in range(tiles):
            self.va[k, at] = self.s[k, at] * self.iv[k, at] * beta

    def start(self, low, high, unroll, tiles, beta):
        over_layers(low, high, unroll, lambda at: self.start_at(at, tiles, beta))

    def around(self, field, at, tiles, count):
        here = [field[k, at] for k in range(tiles)]
        cz = [self.cz[k, at] for k in range(tiles)]
        z_up = self.z_up(here, count)
        z_down = self.z_down([cz[k] * here[k] for k in range(tiles)], count)
        sums = []
        for k in range(count):
            cy = self.cy[k, at]
            total = self.cx[k, at] * field[k, at + 1] + self.cx[k, at - 1] * field[k, at - 1]
            total = total + (cy * self.y_up(here[k]) + self.y_down(cy * here[k]))
            total = total + (cz[k] * z_up[k] + z_down[k])
            sums.append(total + self.s[k, at])
        return here, sums

    def sweep_at(self, at, field, result, tiles, count, step, fresh):
        alpha, beta = step
        here, sums = self.around(field, at, tiles, count)
        for k in range(count):
            kept = (1.0 + alpha - beta) * here[k]
            if not fresh:
                kept = kept - alpha * result[k, at]
            result[k, at] = kept + (beta * self.iv[k, at]) * sums[k]

    def sweep(self, field, result, low, high, unroll, tiles, count, step, fresh=False):
        over_layers(low, high, unroll, lambda at: self.sweep_at(at, field, result, tiles, count, step, fresh))

    def residual(self, field, result, low, high, unroll, tiles):
        def body(at):
            here, sums = self.around(field, at, tiles, 1)
            result[0, at] = sums[0] - self.dg[0, at] * here[0]

        over_layers(low, high, unroll, body)

    def finish(self, field, older, kept_out, added_out, low, high, unroll, step):
        alpha, beta = step

        def body(at):
            here, sums = self.around(field, at, 2, 1)
            kept_out[at - low] = (1.0 + alpha - beta) * here[0] - alpha * older[0, at]
            added_out[at - low] = (beta * self.iv[0, at]) * sums[0]

        over_layers(low, high, unroll, body)


LEVEL_FIELDS = 9
LEVEL_SHAPES = ((2, 16, 32, LANES), (2, 14, 16, LANES), (1, 34, 8, LANES), (1, 15, 8, LANES))
RULER = 1760


def kernel(wide, narrow, rhs, coef, kept, added, *scratch):
    scratch = list(scratch)
    level_refs = []
    for _ in range(4):
        level_refs.append(scratch[:LEVEL_FIELDS])
        scratch = scratch[LEVEL_FIELDS:]
    (zs, rz, rcn, sv, k1c, sk, k1s, c2m, rc2, s2m, rs2, rx1, rx1b, sb0, hx0, p1, p0, ruler,
     local_sem, send_sem, recv_sem) = scratch
    me_w = lax.axis_index("wide")
    me_n = lax.axis_index("narrow")

    def there(dw, dn):
        return (lax.rem(me_w + (dw + wide), wide), lax.rem(me_n + (dn + narrow), narrow))

    far = [(sign * dw, 0) for dw in range(REACH, 0, -1) for sign in (1, -1)]
    corners = [(dw, dn) for dw in (-1, 1) for dn in (-1, 1)]
    around = [(-1, 0), (1, 0), (0, -1), (0, 1)] + corners
    partners = around + far[:-2]
    barrier = pltpu.get_barrier_semaphore()
    for dw, dn in around:
        pl.semaphore_signal(barrier, inc=1, device_id=there(dw, dn), device_id_type=MESH_ID)

    c0, s0 = level_refs[0][0], level_refs[0][1]
    load_c = pltpu.make_async_copy(coef, c0.at[0, pl.ds(4, 8)], local_sem.at[0])
    load_s = pltpu.make_async_copy(rhs, s0.at[0, pl.ds(4, 8)], local_sem.at[1])
    load_c.start()
    load_s.start()
    for dw, dn in far[:-2]:
        pl.semaphore_signal(barrier, inc=1, device_id=there(dw, dn), device_id_type=MESH_ID)

    left = jnp.where(me_n > 0, 1.0, 0.0).astype(F32)
    right = jnp.where(me_n < narrow - 1, 1.0, 0.0).astype(F32)

    def lanes(rows):
        return lax.broadcasted_iota(jnp.int32, (rows, LANES), 1)

    def edges(rows, until, low, since, high):
        at = lanes(rows)
        return jnp.where(at < until, low, jnp.where(at >= since, high, 0.0))

    def centred(rows):
        at = lanes(rows)
        return jnp.where((at >= 32) & (at < 96), 1.0, edges(rows, 32, left, 96, right))

    level_0 = Level(level_refs[0], 1.0, 32, 1, 1, 8 * me_w - 4, 8 * wide, [None, edges(32, 8, right, 120, left)])
    level_1 = Level(
        level_refs[1], 0.25, 16, 1, 1, 4 * me_w - 5, 4 * wide, [centred(16), edges(16, 32, right, 96, left)]
    )
    level_2 = Level(level_refs[2], 0.0625, 8, 1, 2, 2 * me_w - 16, 2 * wide, [centred(8)])
    level_3 = Level(level_refs[3], 0.015625, 8, 2, 4, me_w - 7, wide, [centred(8)])

    sent = [0, 0]

    def send(group, src, dst, dw, dn, rows, sender=0):
        sent[sender] += rows
        pltpu.make_async_remote_copy(
            src_ref=src, dst_ref=dst, send_sem=send_sem.at[sender], recv_sem=recv_sem.at[group],
            device_id=there(dw, dn), device_id_type=MESH_ID,
        ).start()

    def ruled(rows, group, sender):
        span = ruler.at[pl.ds(0, rows)]
        return pltpu.make_async_remote_copy(
            src_ref=span, dst_ref=span, send_sem=send_sem.at[sender], recv_sem=recv_sem.at[group],
            device_id=there(1, 0), device_id_type=MESH_ID,
        )

    def receive(group, rows):
        ruled(rows, group, 0).wait_recv()

    def sends_done(sender):
        ruled(sent[sender], 0, sender).wait_send()

    (from_z, from_c, from_s, from_v, from_k, from_s1, from_c1b, from_x0, from_c2, from_x1, from_s2) = range(11)

    def pack(tiles):
        rows = tiles[0].shape[0]
        group = lanes(rows) // 16
        packed = jnp.zeros((rows, LANES), F32)
        for at, tile in enumerate(tiles):
            packed = jnp.where(group == at, pltpu.roll(tile, (16 * at + 8) % LANES, 1), packed)
        return packed

    def unpack(packed, at):
        return pltpu.roll(packed, (2 * LANES - (16 * at + 8)) % LANES, 1)

    def pack_side(ref, half, side):
        group = lanes(8) // 8
        packed = None
        for layer in range(4):
            for part in range(4):
                at = 4 * layer + part
                tile = ref[0, 4 + 4 * half + layer, pl.ds(8 * part, 8), :]
                tile = pltpu.roll(tile, (8 * at + 8 * side) % LANES, 1)
                packed = tile if at == 0 else jnp.where(group == at, tile, packed)
        return packed

    def restrict_0(ref):
        out = []
        for layer in range(4):
            total = None
            for dx in range(2):
                for dy in range(2):
                    term = ref[0, 4 + 2 * layer + dx, pl.ds(dy, 16, stride=2), :]
                    total = term if total is None else total + term
            total = total + pltpu.roll(total, LANES - 1, 1)
            out.append(0.125 * jnp.take_along_axis(total, (2 * lanes(16) + 64) % LANES, axis=1))
        return out

    odd_8 = lanes(8) % 2 == 1

    def pairs_1(ref):
        out = []
        for layer in range(2):
            total = None
            for dx in range(2):
                for dy in range(2):
                    term = ref[0, 5 + 2 * layer + dx, pl.ds(dy, 8, stride=2), :]
                    total = term if total is None else total + term
            total = total + jnp.where(odd_8, pltpu.roll(total, 1, 1), pltpu.roll(total, LANES - 1, 1))
            out.append(0.125 * total)
        return jnp.where(odd_8, out[1], out[0])

    def squeeze_1(layers, ref, row):
        for part in range(2):
            ref[pl.ds(row + 16 * part, 16), :] = jnp.where(lanes(16) < 64, layers[part], layers[part + 2])

    pl.semaphore_wait(barrier, len(partners))
    send(from_c, coef.at[pl.ds(0, 3)], c0.at[0, pl.ds(12, 3)], -1, 0, 96)
    send(from_c, coef.at[pl.ds(5, 3)], c0.at[0, pl.ds(1, 3)], 1, 0, 96)
    send(from_s, rhs.at[pl.ds(0, 2)], s0.at[0, pl.ds(12, 2)], -1, 0, 64)
    send(from_s, rhs.at[pl.ds(6, 2)], s0.at[0, pl.ds(2, 2)], 1, 0, 64)

    load_c.wait()
    own_c1 = restrict_0(c0)
    for side in range(2):
        squeeze_1(own_c1, zs.at[side], 32)
        for half in range(2):
            zs[side, pl.ds(16 * half, 8), :] = pack_side(c0, half, side)
    load_s.wait()
    for side in range(2):
        for half in range(2):
            zs[side, pl.ds(16 * half + 8, 8), :] = pack_side(s0, half, side)

    send(from_z, zs.at[0], rz.at[1], 0, -1, 64)
    send(from_z, zs.at[1], rz.at[0], 0, 1, 64)
    for dw, dn in corners:
        row = 0 if dw < 0 else 16
        span = zs.at[(1 + dn) // 2, pl.ds(row, 16)]
        send(from_c, span, rcn.at[(1 - dw) // 2, (1 - dn) // 2], dw, dn, 16)
    for dw, dn in [(-1, 0), (1, 0)] + corners:
        send(from_k, zs.at[0, pl.ds(32, 32)], k1c.at[1 - dw, 1 - dn], dw, dn, 32)

    def fill_0(ref, first, from_left, from_right):
        low = lanes(8) < 64
        for layer in range(4):
            for part in range(4):
                at = 4 * layer + part
                ref[1, first + layer, pl.ds(8 * part, 8), :] = jnp.where(
                    low, pltpu.roll(from_right, (LANES - 8 * at) % LANES, 1), pltpu.roll(from_left, (120 - 8 * at) % LANES, 1)
                )

    steps = cheb(3)
    receive(from_z, 128)
    for field, ref in enumerate((c0, s0)):
        for half in range(2):
            rows = pl.ds(16 * half + 8 * field, 8)
            fill_0(ref, 4 + 4 * half, rz[0, rows, :], rz[1, rows, :])
    level_0.setup(5, 10, 3, 2)
    level_0.start(5, 10, 6, 2, steps[0][1])
    for side in range(2):
        sv[side] = level_0.va[0, 6 + 3 * side]
        send(from_v, sv.at[side], level_0.va.at[0, 14 - 13 * side], 2 * side - 1, 0, 32)
        level_0.va[1, 1 + 13 * side] = jnp.zeros((32, LANES), F32)
    level_0.sweep(level_0.va, level_0.vb, 6, 9, 4, 2, 2, steps[1], fresh=True)
    level_0.sweep(level_0.vb, level_0.va, 7, 8, 2, 2, 2, steps[2])

    receive(from_c, 256)
    for field, ref in enumerate((c0, s0)):
        for side in range(2):
            rows = pl.ds(8 * field, 8)
            fill_0(ref, 12 * side, rcn[side, 0, rows, :], rcn[side, 1, rows, :])
    level_0.setup_below(2, 2)
    over_sides(2, 11, 3, lambda at: level_0.setup_at(at, 2))
    receive(from_s, 128)
    over_sides(2, 11, 3, lambda at: level_0.start_at(at, 2, steps[0][1]))
    receive(from_v, 64)
    over_sides(2, 10, 4, lambda at: level_0.sweep_at(at, level_0.va, level_0.vb, 2, 2, steps[1], True))
    over_sides(3, 9, 4, lambda at: level_0.sweep_at(at, level_0.vb, level_0.va, 2, 2, steps[2], False))
    level_0.residual(level_0.va, level_0.vb, 4, 11, 4, 2)

    squeeze_1(restrict_0(level_0.vb), sk, 0)
    for dw, dn in around:
        send(from_s1, sk, k1s.at[1 - dw, 1 - dn], dw, dn, 32)

    for side in range(2):
        first = 9 if side == 0 else 4
        tiles = []
        for layer in range(3):
            sb0[side, pl.ds(32 * layer, 32), :] = level_0.va[0, first + layer]
            for part in range(2):
                tiles.append(level_0.va[1, first + layer, pl.ds(16 * part, 16), :])
        sb0[side, pl.ds(96, 16), :] = pack(tiles)
        send(from_x0, sb0.at[side], hx0.at[side], 1 - 2 * side, 0, 112)

    def spread_1(ref, block):
        at_lane = lanes(16)
        low_half = at_lane < 64
        low_quarter = at_lane % 64 < 32
        for dx in (-1, 0, 1):
            for part in range(2):
                before, own, after = (block(dx, dz, part) for dz in (-1, 0, 1))
                near = jnp.where(low_quarter, before, after)
                outer = jnp.where(low_quarter, after, before)
                own_r, near_r, outer_r = (pltpu.roll(t, 64, 1) for t in (own, near, outer))
                at = 5 + 4 * dx + part
                for at, own_a, own_b, near_a, near_b, outer_a, outer_b in (
                    (at, own, own_r, near, near_r, outer, outer_r),
                    (at + 2, own_r, own, near_r, near, outer_r, outer),
                ):
                    centre = jnp.where(low_half, own_a, own_b)
                    ref[0, at] = jnp.where(at_lane < 32, near_a, jnp.where(at_lane < 96, centre, near_b))
                    ref[1, at] = jnp.where(low_half, outer_a, outer_b)

    def coef_block(dx, dz, part):
        if dx == 0:
            rows = pl.ds(32 + 16 * part, 16)
            return zs[0, rows, :] if dz == 0 else rz[(1 + dz) // 2, rows, :]
        return k1c[1 + dx, 1 + dz, pl.ds(16 * part, 16), :]

    def source_block(dx, dz, part):
        rows = pl.ds(16 * part, 16)
        return sk[rows, :] if dx == 0 and dz == 0 else k1s[1 + dx, 1 + dz, rows, :]

    receive(from_k, 192)
    spread_1(level_1.c, coef_block)
    send(from_c1b, level_1.c.at[:, 9], level_1.c.at[:, 13], -1, 0, 32)
    send(from_c1b, level_1.c.at[:, 4], level_1.c.at[:, 0], 1, 0, 32)
    value = pairs_1(level_1.c)
    c2m[...] = value
    rc2[REACH] = value
    for dw, dn in far:
        send(from_c2, c2m, rc2.at[REACH - dw], dw, dn, 8)
    receive(from_c1b, 64)
    level_1.setup(1, 12, 6, 2)

    receive(from_s1, 256)
    spread_1(level_1.s, source_block)
    level_1.start(2, 11, 10, 2, steps[0][1])
    level_1.sweep(level_1.va, level_1.vb, 3, 10, 8, 2, 1, steps[1], fresh=True)
    level_1.sweep(level_1.vb, level_1.va, 4, 9, 6, 1, 1, steps[2])
    level_1.residual(level_1.va, level_1.vb, 5, 8, 4, 1)

    value = pairs_1(level_1.vb)
    s2m[...] = value
    rs2[REACH] = value
    for dw, dn in far:
        send(from_s2, s2m, rs2.at[REACH - dw], dw, dn, 8)

    own_1 = level_1.va.at[0, pl.ds(5, 4)]
    send(from_x1, own_1, rx1.at[1], -1, 0, 64, 1)
    send(from_x1, own_1, rx1.at[0], 1, 0, 64, 1)
    send(from_x1, level_1.va.at[0, 5], rx1b.at[1], -2, 0, 16, 1)
    send(from_x1, level_1.va.at[0, 8], rx1b.at[0], 2, 0, 16, 1)

    def spread_2(ref, blocks):
        for block in range(2 * REACH + 1):
            packed = blocks[block]
            ref[0, 2 * block] = jnp.where(odd_8, pltpu.roll(packed, 1, 1), packed)
            ref[0, 2 * block + 1] = jnp.where(odd_8, packed, pltpu.roll(packed, LANES - 1, 1))

    def restrict_2(ref, at):
        total = ref[0, 2 * at + 2] + ref[0, 2 * at + 3]
        odd_row = lax.broadcasted_iota(jnp.int32, (8, LANES), 0) % 2 == 1
        total = total + jnp.where(odd_row, pltpu.roll(total, 1, 0), pltpu.roll(total, 7, 0))
        second = lanes(8) % 4 >= 2
        total = total + jnp.where(second, pltpu.roll(total, 2, 1), pltpu.roll(total, LANES - 2, 1))
        return 0.125 * total

    receive(from_c2, 128)
    spread_2(level_2.c, rc2)
    level_2.setup(1, 32, 8, 1)
    for at in range(15):
        level_3.c[0, at] = restrict_2(level_2.c, at)
    level_3.setup(1, 13, 13, 1)

    receive(from_s2, 128)
    spread_2(level_2.s, rs2)
    level_2.start(1, 32, 32, 1, steps[0][1])
    level_2.sweep(level_2.va, level_2.vb, 2, 31, 15, 1, 1, steps[1], fresh=True)
    level_2.sweep(level_2.vb, level_2.va, 3, 30, 14, 1, 1, steps[2])
    level_2.residual(level_2.va, level_2.vb, 4, 29, 13, 1)

    for at in range(1, 14):
        level_3.s[0, at] = restrict_2(level_2.vb, at)
    coarse = cheb(4)
    level_3.start(1, 13, 13, 1, coarse[0][1])
    level_3.sweep(level_3.va, level_3.vb, 2, 12, 11, 1, 1, coarse[1], fresh=True)
    level_3.sweep(level_3.vb, level_3.va, 3, 11, 9, 1, 1, coarse[2])
    level_3.sweep(level_3.va, level_3.vb, 4, 10, 7, 1, 1, coarse[3])

    for at in range(10, 24):
        level_2.vb[0, at] = level_2.va[0, at] + level_3.vb[0, (at - 2) // 2]
    level_2.sweep(level_2.vb, level_2.va, 11, 22, 12, 1, 1, steps[0], fresh=True)
    level_2.sweep(level_2.va, level_2.vb, 12, 21, 10, 1, 1, steps[1])
    level_2.sweep(level_2.vb, level_2.va, 13, 20, 8, 1, 1, steps[2])

    for at in range(8):
        value = level_2.va[0, 13 + at]
        for part in range(2):
            p1[at, pl.ds(part, 8, stride=2), :] = value
    receive(from_x1, 160)
    for at in range(14):
        if 5 <= at <= 8:
            before = level_1.va[0, at]
        else:
            beside = (rx1b[0] if at == 0 else rx1[0, at - 1] if at < 5 else rx1[1, at - 9] if at < 13 else rx1b[1])
            before = beside * level_1.inside(at)
        level_1.vb[0, at] = before + p1[(at + 1) // 2]
    sends_done(1)
    level_1.sweep(level_1.vb, level_1.va, 1, 12, 12, 1, 1, steps[0], fresh=True)
    level_1.sweep(level_1.va, level_1.vb, 2, 11, 10, 1, 1, steps[1])
    level_1.sweep(level_1.vb, level_1.va, 3, 10, 8, 1, 1, steps[2])

    fine_lane = lanes(16) // 2
    for at in range(8):
        value = level_1.va[0, 3 + at]
        for k in range(2):
            fine = jnp.take_along_axis(value, (fine_lane + (32 if k == 0 else 96)) % LANES, axis=1)
            for part in range(2):
                p0[k, at, pl.ds(part, 16, stride=2), :] = fine
    receive(from_x0, 224)
    for side in range(2):
        packed = hx0[side, pl.ds(96, 16), :]
        for layer in range(3):
            at = (1 if side == 0 else 12) + layer
            inside = level_0.inside(at)
            coarse_at = (at - 4) // 2 + 2
            level_0.vb[0, at] = hx0[side, pl.ds(32 * layer, 32), :] * inside + p0[0, coarse_at]
            for part in range(2):
                rows = pl.ds(16 * part, 16)
                level_0.vb[1, at, rows, :] = (
                    unpack(packed, 2 * layer + part) * (level_0.lane_mask[1][:16] * inside) + p0[1, coarse_at, rows, :]
                )

    def correct(at):
        for k in range(2):
            level_0.vb[k, at] = level_0.va[k, at] + p0[k, at // 2]

    over_layers(4, 11, 4, correct)
    level_0.sweep(level_0.vb, level_0.va, 2, 13, 4, 2, 2, steps[0], fresh=True)
    level_0.sweep(level_0.va, level_0.vb, 3, 12, 5, 2, 2, steps[1])
    level_0.finish(level_0.vb, level_0.va, kept, added, 4, 11, 4, steps[2])

    sends_done(0)


def per_device(right_side, conductivity, wide, narrow):
    brick = (8, 32, LANES)
    scratch = []
    for shape in LEVEL_SHAPES:
        scratch += [pltpu.VMEM(shape, F32)] * LEVEL_FIELDS
    shapes = [
        (2, 64, LANES), (2, 64, LANES), (2, 2, 16, LANES), (2, 32, LANES), (3, 3, 32, LANES),
        (32, LANES), (3, 3, 32, LANES),
        (8, LANES), (2 * REACH + 1, 8, LANES), (8, LANES), (2 * REACH + 1, 8, LANES),
        (2, 4, 16, LANES), (2, 16, LANES),
        (2, 112, LANES), (2, 112, LANES),
        (8, 16, LANES), (2, 8, 32, LANES),
        (RULER, LANES),
    ]
    scratch += [pltpu.VMEM(shape, F32) for shape in shapes]
    scratch += [pltpu.SemaphoreType.DMA((2,)), pltpu.SemaphoreType.DMA((2,)), pltpu.SemaphoreType.DMA((11,))]
    kept, added = pl.pallas_call(
        functools.partial(kernel, wide, narrow),
        out_shape=[jax.ShapeDtypeStruct(brick, F32)] * 2,
        in_specs=[pl.BlockSpec(memory_space=pltpu.HBM)] * 2,
        out_specs=[pl.BlockSpec(memory_space=pltpu.VMEM)] * 2,
        scratch_shapes=scratch,
        compiler_params=pltpu.CompilerParams(
            collective_id=0, has_side_effects=True, vmem_limit_bytes=32 * 1024 * 1024
        ),
    )(pltpu.with_memory_space_constraint(right_side, pltpu.HBM), pltpu.with_memory_space_constraint(conductivity, pltpu.HBM))
    return kept + added


def solution(mesh):
    spec = P("wide", None, "narrow")
    body = functools.partial(per_device, wide=mesh.shape["wide"], narrow=mesh.shape["narrow"])
    return jax.shard_map(body, mesh=mesh, in_specs=(spec, spec), out_specs=spec, check_vma=False)
```

```python
import functools

import jax
import jax.numpy as jnp
from jax import lax
from jax.experimental import pallas as pl
from jax.experimental.pallas import tpu as pltpu
from jax.sharding import PartitionSpec as P

CENTER = 1.125
HALF = 0.875
LANES = 128
REACH = 8
F32 = jnp.float32
MESH_ID = pl.DeviceIdType.MESH


def cheb(sweeps):
    sigma = CENTER / HALF
    steps = [(0.0, 1.0 / CENTER)]
    ratio = 1.0 / sigma
    for _ in range(sweeps - 1):
        ratio_next = 1.0 / (2.0 * sigma - ratio)
        steps.append((ratio_next * ratio, 2.0 * ratio_next / HALF))
        ratio = ratio_next
    return steps


def over_sides(first, second, count, body):
    def block(side, carry):
        for at in range(count):
            body(first + side * (second - first) + at)
        return carry

    lax.fori_loop(0, 2, block, 0)


def over_layers(low, high, unroll, body):
    count = high - low + 1
    if count == unroll:
        for at in range(low, high + 1):
            body(at)
        return

    def block(step, carry):
        for at in range(unroll):
            body(low + step * unroll + at)
        return carry

    lax.fori_loop(0, count // unroll, block, 0)


class Level:
    def __init__(self, refs, scale, rows, row_step, lane_step, base, extent, lane_mask):
        self.c, self.s, self.cx, self.cy, self.cz, self.iv, self.dg, self.va, self.vb = refs
        self.half = 0.5 * scale
        self.rows, self.row_step, self.lane_step = rows, row_step, lane_step
        self.base, self.extent, self.lane_mask = base, extent, lane_mask

    def inside(self, at):
        where_x = self.base + at
        return jnp.where((where_x >= 0) & (where_x < self.extent), 1.0, 0.0).astype(F32)

    def lane(self):
        return lax.broadcasted_iota(jnp.int32, (self.rows, LANES), 1)

    def row(self):
        return lax.broadcasted_iota(jnp.int32, (self.rows, LANES), 0)

    def y_up(self, tile):
        return pltpu.roll(tile, self.rows - self.row_step, 0)

    def y_down(self, tile):
        return pltpu.roll(tile, self.row_step, 0)

    def turned(self, tiles, shift, edge, count):
        out = [pltpu.roll(t, shift, 1) for t in tiles]
        if len(tiles) == 1:
            return out
        at_edge = self.lane() == edge
        return [jnp.where(at_edge, out[1 - k], out[k]) for k in range(count)]

    def z_up(self, tiles, count):
        return self.turned(tiles, LANES - self.lane_step, LANES - 1, count)

    def z_down(self, tiles, count):
        return self.turned(tiles, self.lane_step, 0, count)

    def masked(self, at, tiles):
        keep = self.inside(at) * self.half
        out = []
        for k in range(tiles):
            mask = self.lane_mask[k]
            out.append(self.c[k, at] * (keep if mask is None else mask * keep))
        return out

    def setup_below(self, low, tiles):
        first, second = self.masked(low - 1, tiles), self.masked(low, tiles)
        for k in range(tiles):
            self.cx[k, low - 1] = first[k] + second[k]

    def setup_at(self, at, tiles):
        before, here, after = self.masked(at - 1, tiles), self.masked(at, tiles), self.masked(at + 1, tiles)
        inside = self.inside(at)
        top = self.row() >= self.rows - self.row_step
        bottom = self.row() < self.row_step
        z_up, z_down = self.z_up(here, tiles), self.z_down(here, tiles)
        for k in range(tiles):
            own = here[k]
            x_low = before[k] + own
            x_high = own + after[k]
            y_low = own + jnp.where(bottom, 0.0, self.y_down(own))
            y_high = own + jnp.where(top, 0.0, self.y_up(own))
            z_low = own + z_down[k]
            z_high = own + z_up[k]
            diagonal = x_low + x_high + y_low + y_high + z_low + z_high
            keep = inside if self.lane_mask[k] is None else self.lane_mask[k] * inside
            self.cx[k, at] = x_high
            self.cy[k, at] = jnp.where(top, 0.0, y_high)
            self.cz[k, at] = z_high
            if k == 0:
                self.dg[0, at] = diagonal
            self.iv[k, at] = jnp.where(jnp.full_like(own, 0.0) + keep > 0.5, 1.0 / diagonal, 0.0)

    def setup(self, low, high, unroll, tiles):
        self.setup_below(low, tiles)
        over_layers(low, high, unroll, lambda at: self.setup_at(at, tiles))

    def start_at(self, at, tiles, beta):
        for k in range(tiles):
            self.va[k, at] = self.s[k, at] * self.iv[k, at] * beta

    def start(self, low, high, unroll, tiles, beta):
        over_layers(low, high, unroll, lambda at: self.start_at(at, tiles, beta))

    def around(self, field, at, tiles, count):
        here = [field[k, at] for k in range(tiles)]
        cz = [self.cz[k, at] for k in range(tiles)]
        z_up = self.z_up(here, count)
        z_down = self.z_down([cz[k] * here[k] for k in range(tiles)], count)
        sums = []
        for k in range(count):
            cy = self.cy[k, at]
            total = self.cx[k, at] * field[k, at + 1] + self.cx[k, at - 1] * field[k, at - 1]
            total = total + (cy * self.y_up(here[k]) + self.y_down(cy * here[k]))
            total = total + (cz[k] * z_up[k] + z_down[k])
            sums.append(total + self.s[k, at])
        return here, sums

    def sweep_at(self, at, field, result, tiles, count, step, fresh):
        alpha, beta = step
        here, sums = self.around(field, at, tiles, count)
        for k in range(count):
            kept = (1.0 + alpha - beta) * here[k]
            if not fresh:
                kept = kept - alpha * result[k, at]
            result[k, at] = kept + (beta * self.iv[k, at]) * sums[k]

    def sweep(self, field, result, low, high, unroll, tiles, count, step, fresh=False):
        over_layers(low, high, unroll, lambda at: self.sweep_at(at, field, result, tiles, count, step, fresh))

    def residual(self, field, result, low, high, unroll, tiles):
        def body(at):
            here, sums = self.around(field, at, tiles, 1)
            result[0, at] = sums[0] - self.dg[0, at] * here[0]

        over_layers(low, high, unroll, body)

    def finish(self, field, older, kept_out, added_out, low, high, unroll, step):
        alpha, beta = step

        def body(at):
            here, sums = self.around(field, at, 2, 1)
            kept_out[at - low] = (1.0 + alpha - beta) * here[0] - alpha * older[0, at]
            added_out[at - low] = (beta * self.iv[0, at]) * sums[0]

        over_layers(low, high, unroll, body)


LEVEL_FIELDS = 9
LEVEL_SHAPES = ((2, 16, 32, LANES), (2, 14, 16, LANES), (1, 34, 8, LANES), (1, 15, 8, LANES))
RULER = 1024
SENDERS = 7 + 2 * REACH + 1
GROUPS = 18 + 2 * (2 * REACH + 1)


def kernel(wide, narrow, rhs, coef, kept, added, *scratch):
    scratch = list(scratch)
    level_refs = []
    for _ in range(4):
        level_refs.append(scratch[:LEVEL_FIELDS])
        scratch = scratch[LEVEL_FIELDS:]
    (zs, rz, rcn, k1c, sk, k1s, c2m, rc2, s2m, rs2, rx1, rx1b, sb0, hx0, p1, p0, ruler,
     local_sem, send_sem, recv_sem) = scratch
    me_w = lax.axis_index("wide")
    me_n = lax.axis_index("narrow")

    def there(dw, dn):
        return (lax.rem(me_w + (dw + wide), wide), lax.rem(me_n + (dn + narrow), narrow))

    has = (me_w > 0, me_w < wide - 1)
    reach = (jnp.minimum(me_w, REACH), jnp.minimum(wide - 1 - me_w, REACH))

    def for_far(first, body):
        for side in range(2):
            sign = 2 * side - 1

            def step(k, carry):
                body(REACH + sign * k, sign * k)
                return carry

            lax.fori_loop(first, reach[side] + 1, step, 0)

    def for_sides(body):
        for side in range(2):
            pl.when(has[side])(functools.partial(body, side, 2 * side - 1))

    @pl.when((me_w < REACH) | (me_w >= wide - REACH))
    def clear():
        def zero(ref):
            ref[...] = jnp.zeros(ref.shape, F32)

        for ref in (rcn, rx1, rx1b, hx0, rc2, rs2):
            zero(ref)
        for side in range(2):
            zero(k1c.at[2 * side])
            zero(k1s.at[2 * side])
            for ref in level_refs[0][:2]:
                zero(ref.at[0, pl.ds(12 * side, 4)])
            zero(level_refs[1][0].at[:, 13 * side])

    barrier = pltpu.get_barrier_semaphore()

    def greet(dw, dn):
        pl.semaphore_signal(barrier, inc=1, device_id=there(dw, dn), device_id_type=MESH_ID)

    @for_sides
    def greet_side(side, dw):
        for dn in (0, -1, 1):
            greet(dw, dn)

    greet(0, -1)
    greet(0, 1)

    c0, s0 = level_refs[0][0], level_refs[0][1]
    load_c = pltpu.make_async_copy(coef, c0.at[0, pl.ds(4, 8)], local_sem.at[0])
    load_s = pltpu.make_async_copy(rhs, s0.at[0, pl.ds(4, 8)], local_sem.at[1])
    load_c.start()
    load_s.start()
    for_far(2, lambda slot, dw: greet(dw, 0))
    greeted = 2
    for side in range(2):
        greeted = greeted + jnp.where(has[side], 2, 0) + reach[side]

    left = jnp.where(me_n > 0, 1.0, 0.0).astype(F32)
    right = jnp.where(me_n < narrow - 1, 1.0, 0.0).astype(F32)

    def lanes(rows):
        return lax.broadcasted_iota(jnp.int32, (rows, LANES), 1)

    def edges(rows, until, low, since, high):
        at = lanes(rows)
        return jnp.where(at < until, low, jnp.where(at >= since, high, 0.0))

    def centred(rows):
        at = lanes(rows)
        return jnp.where((at >= 32) & (at < 96), 1.0, edges(rows, 32, left, 96, right))

    level_0 = Level(level_refs[0], 1.0, 32, 1, 1, 8 * me_w - 4, 8 * wide, [None, edges(32, 8, right, 120, left)])
    level_1 = Level(
        level_refs[1], 0.25, 16, 1, 1, 4 * me_w - 5, 4 * wide, [centred(16), edges(16, 32, right, 96, left)]
    )
    level_2 = Level(level_refs[2], 0.0625, 8, 1, 2, 2 * me_w - 16, 2 * wide, [centred(8)])
    level_3 = Level(level_refs[3], 0.015625, 8, 2, 4, me_w - 7, wide, [centred(8)])

    sent = [0] * SENDERS

    def send(group, src, dst, dw, dn, rows, sender):
        if isinstance(sender, int):
            sent[sender] += rows
        pltpu.make_async_remote_copy(
            src_ref=src, dst_ref=dst, send_sem=send_sem.at[sender], recv_sem=recv_sem.at[group],
            device_id=there(dw, dn), device_id_type=MESH_ID,
        ).start()

    def ruled(rows, group, sender):
        span = ruler.at[pl.ds(0, rows)]
        return pltpu.make_async_remote_copy(
            src_ref=span, dst_ref=span, send_sem=send_sem.at[sender], recv_sem=recv_sem.at[group],
            device_id=there(0, 1), device_id_type=MESH_ID,
        )

    def receive(group, rows):
        ruled(rows, group, 0).wait_recv()

    def receive_sides(group, rows):
        for_sides(lambda side, dw: receive(group + side, rows))

    def receive_far(group):
        for_far(1, lambda slot, dw: receive(group + slot, 8))

    def sends_done(sender):
        ruled(sent[sender], 0, sender).wait_send()

    from_z, from_s1z = 0, 1
    from_c, from_s, from_k, from_s1, from_c1b, from_x0, from_x1, from_x1b = range(2, 18, 2)
    from_c2 = 18
    from_s2 = from_c2 + 2 * REACH + 1
    sender_far = 7

    def pack(tiles):
        rows = tiles[0].shape[0]
        group = lanes(rows) // 16
        packed = jnp.zeros((rows, LANES), F32)
        for at, tile in enumerate(tiles):
            packed = jnp.where(group == at, pltpu.roll(tile, (16 * at + 8) % LANES, 1), packed)
        return packed

    def unpack(packed, at):
        return pltpu.roll(packed, (2 * LANES - (16 * at + 8)) % LANES, 1)

    def pack_side(ref, half, side):
        group = lanes(8) // 8
        packed = None
        for layer in range(4):
            for part in range(4):
                at = 4 * layer + part
                tile = ref[0, 4 + 4 * half + layer, pl.ds(8 * part, 8), :]
                tile = pltpu.roll(tile, (8 * at + 8 * side) % LANES, 1)
                packed = tile if at == 0 else jnp.where(group == at, tile, packed)
        return packed

    def restrict_0(ref):
        out = []
        for layer in range(4):
            total = None
            for dx in range(2):
                for dy in range(2):
                    term = ref[0, 4 + 2 * layer + dx, pl.ds(dy, 16, stride=2), :]
                    total = term if total is None else total + term
            total = total + pltpu.roll(total, LANES - 1, 1)
            out.append(0.125 * jnp.take_along_axis(total, (2 * lanes(16) + 64) % LANES, axis=1))
        return out

    odd_8 = lanes(8) % 2 == 1

    def pairs_1(ref):
        out = []
        for layer in range(2):
            total = None
            for dx in range(2):
                for dy in range(2):
                    term = ref[0, 5 + 2 * layer + dx, pl.ds(dy, 8, stride=2), :]
                    total = term if total is None else total + term
            total = total + jnp.where(odd_8, pltpu.roll(total, 1, 1), pltpu.roll(total, LANES - 1, 1))
            out.append(0.125 * total)
        return jnp.where(odd_8, out[1], out[0])

    def squeeze_1(layers, ref, row):
        for part in range(2):
            ref[pl.ds(row + 16 * part, 16), :] = jnp.where(lanes(16) < 64, layers[part], layers[part + 2])

    pl.semaphore_wait(barrier, greeted)

    @for_sides
    def send_faces(side, dw):
        send(from_c + 1 - side, coef.at[pl.ds(4 * side, 4)], c0.at[0, pl.ds(12 - 12 * side, 4)], dw, 0, 128, 1 + side)
        send(from_s + 1 - side, rhs.at[pl.ds(5 * side, 3)], s0.at[0, pl.ds(12 - 11 * side, 3)], dw, 0, 96, 1 + side)

    load_c.wait()
    own_c1 = restrict_0(c0)
    for side in range(2):
        squeeze_1(own_c1, zs.at[side], 32)
        for half in range(2):
            zs[side, pl.ds(16 * half, 8), :] = pack_side(c0, half, side)
    load_s.wait()
    for side in range(2):
        for half in range(2):
            zs[side, pl.ds(16 * half + 8, 8), :] = pack_side(s0, half, side)

    send(from_z, zs.at[0], rz.at[1], 0, -1, 64, 0)
    send(from_z, zs.at[1], rz.at[0], 0, 1, 64, 0)

    @for_sides
    def send_corners(side, dw):
        for dn in (-1, 1):
            span = zs.at[(1 + dn) // 2, pl.ds(16 * side, 16)]
            send(from_c + 1 - side, span, rcn.at[1 - side, (1 - dn) // 2], dw, dn, 16, 1 + side)
        for dn in (0, -1, 1):
            send(from_k + 1 - side, zs.at[0, pl.ds(32, 32)], k1c.at[1 - dw, 1 - dn], dw, dn, 32, 1 + side)

    def fill_0(ref, first, from_left, from_right):
        low = lanes(8) < 64
        for layer in range(4):
            for part in range(4):
                at = 4 * layer + part
                ref[1, first + layer, pl.ds(8 * part, 8), :] = jnp.where(
                    low, pltpu.roll(from_right, (LANES - 8 * at) % LANES, 1), pltpu.roll(from_left, (120 - 8 * at) % LANES, 1)
                )

    steps = cheb(3)
    receive(from_z, 128)
    for field, ref in enumerate((c0, s0)):
        for half in range(2):
            rows = pl.ds(16 * half + 8 * field, 8)
            fill_0(ref, 4 + 4 * half, rz[0, rows, :], rz[1, rows, :])
    level_0.setup(5, 10, 3, 2)
    level_0.start(5, 10, 6, 2, steps[0][1])
    level_0.sweep(level_0.va, level_0.vb, 6, 9, 4, 2, 2, steps[1], fresh=True)
    level_0.sweep(level_0.vb, level_0.va, 7, 8, 2, 2, 2, steps[2])

    receive_sides(from_c, 160)
    for field, ref in enumerate((c0, s0)):
        for side in range(2):
            rows = pl.ds(8 * field, 8)
            fill_0(ref, 12 * side, rcn[side, 0, rows, :], rcn[side, 1, rows, :])
    level_0.setup_below(1, 2)
    over_sides(1, 11, 4, lambda at: level_0.setup_at(at, 2))
    receive_sides(from_s, 96)
    over_sides(1, 11, 4, lambda at: level_0.start_at(at, 2, steps[0][1]))
    over_sides(2, 10, 4, lambda at: level_0.sweep_at(at, level_0.va, level_0.vb, 2, 2, steps[1], True))
    over_sides(3, 9, 4, lambda at: level_0.sweep_at(at, level_0.vb, level_0.va, 2, 2, steps[2], False))
    level_0.residual(level_0.va, level_0.vb, 4, 11, 4, 2)

    squeeze_1(restrict_0(level_0.vb), sk, 0)

    @for_sides
    def send_source(side, dw):
        for dn in (0, -1, 1):
            send(from_s1 + 1 - side, sk, k1s.at[1 - dw, 1 - dn], dw, dn, 32, 1 + side)

    for dn in (-1, 1):
        send(from_s1z, sk, k1s.at[1, 1 - dn], 0, dn, 32, 0)

    for side in range(2):
        first = 9 if side == 0 else 4
        tiles = []
        for layer in range(3):
            sb0[side, pl.ds(32 * layer, 32), :] = level_0.va[0, first + layer]
            for part in range(2):
                tiles.append(level_0.va[1, first + layer, pl.ds(16 * part, 16), :])
        sb0[side, pl.ds(96, 16), :] = pack(tiles)

    @for_sides
    def send_iterate_0(side, dw):
        send(from_x0 + 1 - side, sb0.at[1 - side], hx0.at[1 - side], dw, 0, 112, 1 + side)

    def spread_1(ref, block):
        at_lane = lanes(16)
        low_half = at_lane < 64
        low_quarter = at_lane % 64 < 32
        for dx in (-1, 0, 1):
            for part in range(2):
                before, own, after = (block(dx, dz, part) for dz in (-1, 0, 1))
                near = jnp.where(low_quarter, before, after)
                outer = jnp.where(low_quarter, after, before)
                own_r, near_r, outer_r = (pltpu.roll(t, 64, 1) for t in (own, near, outer))
                at = 5 + 4 * dx + part
                for at, own_a, own_b, near_a, near_b, outer_a, outer_b in (
                    (at, own, own_r, near, near_r, outer, outer_r),
                    (at + 2, own_r, own, near_r, near, outer_r, outer),
                ):
                    centre = jnp.where(low_half, own_a, own_b)
                    ref[0, at] = jnp.where(at_lane < 32, near_a, jnp.where(at_lane < 96, centre, near_b))
                    ref[1, at] = jnp.where(low_half, outer_a, outer_b)

    def coef_block(dx, dz, part):
        if dx == 0:
            rows = pl.ds(32 + 16 * part, 16)
            return zs[0, rows, :] if dz == 0 else rz[(1 + dz) // 2, rows, :]
        return k1c[1 + dx, 1 + dz, pl.ds(16 * part, 16), :]

    def source_block(dx, dz, part):
        rows = pl.ds(16 * part, 16)
        return sk[rows, :] if dx == 0 and dz == 0 else k1s[1 + dx, 1 + dz, rows, :]

    receive_sides(from_k, 96)
    spread_1(level_1.c, coef_block)

    @for_sides
    def send_coef_1(side, dw):
        send(from_c1b + 1 - side, level_1.c.at[:, 9 - 5 * side], level_1.c.at[:, 13 - 13 * side], dw, 0, 32, 1 + side)

    value = pairs_1(level_1.c)
    c2m[...] = value
    rc2[REACH] = value
    for_far(1, lambda slot, dw: send(from_c2 + 2 * REACH - slot, c2m, rc2.at[2 * REACH - slot], dw, 0, 8, sender_far + slot))
    level_1.setup(2, 11, 5, 2)

    receive(from_s1z, 64)
    receive_sides(from_s1, 96)
    spread_1(level_1.s, source_block)
    level_1.start(2, 11, 10, 2, steps[0][1])
    level_1.sweep(level_1.va, level_1.vb, 3, 10, 8, 2, 1, steps[1], fresh=True)
    level_1.sweep(level_1.vb, level_1.va, 4, 9, 6, 1, 1, steps[2])
    level_1.residual(level_1.va, level_1.vb, 5, 8, 4, 1)

    value = pairs_1(level_1.vb)
    s2m[...] = value
    rs2[REACH] = value
    for_far(1, lambda slot, dw: send(from_s2 + 2 * REACH - slot, s2m, rs2.at[2 * REACH - slot], dw, 0, 8, sender_far + slot))

    @for_sides
    def send_iterate_1(side, dw):
        send(from_x1 + 1 - side, level_1.va.at[0, pl.ds(5, 4)], rx1.at[1 - side], dw, 0, 64, 3 + side)

    for side in range(2):
        @pl.when(reach[side] >= 2)
        def send_next_1():
            layer = level_1.va.at[0, 5 + 3 * side]
            send(from_x1b + 1 - side, layer, rx1b.at[1 - side], 4 * side - 2, 0, 16, 5 + side)

    receive_sides(from_c1b, 32)
    level_1.setup_below(1, 1)
    over_sides(1, 12, 1, lambda at: level_1.setup_at(at, 1))

    def spread_2(ref, blocks):
        for block in range(2 * REACH + 1):
            packed = blocks[block]
            ref[0, 2 * block] = jnp.where(odd_8, pltpu.roll(packed, 1, 1), packed)
            ref[0, 2 * block + 1] = jnp.where(odd_8, packed, pltpu.roll(packed, LANES - 1, 1))

    def restrict_2(ref, at):
        total = ref[0, 2 * at + 2] + ref[0, 2 * at + 3]
        odd_row = lax.broadcasted_iota(jnp.int32, (8, LANES), 0) % 2 == 1
        total = total + jnp.where(odd_row, pltpu.roll(total, 1, 0), pltpu.roll(total, 7, 0))
        second = lanes(8) % 4 >= 2
        total = total + jnp.where(second, pltpu.roll(total, 2, 1), pltpu.roll(total, LANES - 2, 1))
        return 0.125 * total

    receive_far(from_c2)
    spread_2(level_2.c, rc2)
    level_2.setup(1, 32, 8, 1)
    for at in range(15):
        level_3.c[0, at] = restrict_2(level_2.c, at)
    level_3.setup(1, 13, 13, 1)

    receive_far(from_s2)
    spread_2(level_2.s, rs2)
    level_2.start(1, 32, 32, 1, steps[0][1])
    level_2.sweep(level_2.va, level_2.vb, 2, 31, 15, 1, 1, steps[1], fresh=True)
    level_2.sweep(level_2.vb, level_2.va, 3, 30, 14, 1, 1, steps[2])
    level_2.residual(level_2.va, level_2.vb, 4, 29, 13, 1)

    for at in range(1, 14):
        level_3.s[0, at] = restrict_2(level_2.vb, at)
    coarse = cheb(4)
    level_3.start(1, 13, 13, 1, coarse[0][1])
    level_3.sweep(level_3.va, level_3.vb, 2, 12, 11, 1, 1, coarse[1], fresh=True)
    level_3.sweep(level_3.vb, level_3.va, 3, 11, 9, 1, 1, coarse[2])
    level_3.sweep(level_3.va, level_3.vb, 4, 10, 7, 1, 1, coarse[3])

    for at in range(10, 24):
        level_2.vb[0, at] = level_2.va[0, at] + level_3.vb[0, (at - 2) // 2]
    level_2.sweep(level_2.vb, level_2.va, 11, 22, 12, 1, 1, steps[0], fresh=True)
    level_2.sweep(level_2.va, level_2.vb, 12, 21, 10, 1, 1, steps[1])
    level_2.sweep(level_2.vb, level_2.va, 13, 20, 8, 1, 1, steps[2])

    for at in range(8):
        value = level_2.va[0, 13 + at]
        for part in range(2):
            p1[at, pl.ds(part, 8, stride=2), :] = value
    receive_sides(from_x1, 64)
    for side in range(2):
        pl.when(reach[side] >= 2)(functools.partial(receive, from_x1b + side, 16))
    for at in range(14):
        if 5 <= at <= 8:
            before = level_1.va[0, at]
        else:
            beside = (rx1b[0] if at == 0 else rx1[0, at - 1] if at < 5 else rx1[1, at - 9] if at < 13 else rx1b[1])
            before = beside * level_1.inside(at)
        level_1.vb[0, at] = before + p1[(at + 1) // 2]
    for side in range(2):
        pl.when(has[side])(functools.partial(sends_done, 3 + side))
        pl.when(reach[side] >= 2)(functools.partial(sends_done, 5 + side))
    level_1.sweep(level_1.vb, level_1.va, 1, 12, 12, 1, 1, steps[0], fresh=True)
    level_1.sweep(level_1.va, level_1.vb, 2, 11, 10, 1, 1, steps[1])
    level_1.sweep(level_1.vb, level_1.va, 3, 10, 8, 1, 1, steps[2])

    fine_lane = lanes(16) // 2
    for at in range(8):
        value = level_1.va[0, 3 + at]
        for k in range(2):
            fine = jnp.take_along_axis(value, (fine_lane + (32 if k == 0 else 96)) % LANES, axis=1)
            for part in range(2):
                p0[k, at, pl.ds(part, 16, stride=2), :] = fine
    receive_sides(from_x0, 112)
    for side in range(2):
        packed = hx0[side, pl.ds(96, 16), :]
        for layer in range(3):
            at = (1 if side == 0 else 12) + layer
            inside = level_0.inside(at)
            coarse_at = (at - 4) // 2 + 2
            level_0.vb[0, at] = hx0[side, pl.ds(32 * layer, 32), :] * inside + p0[0, coarse_at]
            for part in range(2):
                rows = pl.ds(16 * part, 16)
                level_0.vb[1, at, rows, :] = (
                    unpack(packed, 2 * layer + part) * (level_0.lane_mask[1][:16] * inside) + p0[1, coarse_at, rows, :]
                )

    def correct(at):
        for k in range(2):
            level_0.vb[k, at] = level_0.va[k, at] + p0[k, at // 2]

    over_layers(4, 11, 4, correct)
    level_0.sweep(level_0.vb, level_0.va, 2, 13, 4, 2, 2, steps[0], fresh=True)
    level_0.sweep(level_0.va, level_0.vb, 3, 12, 5, 2, 2, steps[1])
    level_0.finish(level_0.vb, level_0.va, kept, added, 4, 11, 4, steps[2])

    sends_done(0)
    for_sides(lambda side, dw: sends_done(1 + side))
    for_far(1, lambda slot, dw: ruled(16, 0, sender_far + slot).wait_send())


def per_device(right_side, conductivity, wide, narrow):
    brick = (8, 32, LANES)
    scratch = []
    for shape in LEVEL_SHAPES:
        scratch += [pltpu.VMEM(shape, F32)] * LEVEL_FIELDS
    shapes = [
        (2, 64, LANES), (2, 64, LANES), (2, 2, 16, LANES), (3, 3, 32, LANES),
        (32, LANES), (3, 3, 32, LANES),
        (8, LANES), (2 * REACH + 1, 8, LANES), (8, LANES), (2 * REACH + 1, 8, LANES),
        (2, 4, 16, LANES), (2, 16, LANES),
        (2, 112, LANES), (2, 112, LANES),
        (8, 16, LANES), (2, 8, 32, LANES),
        (RULER, LANES),
    ]
    scratch += [pltpu.VMEM(shape, F32) for shape in shapes]
    scratch += [pltpu.SemaphoreType.DMA((2,)), pltpu.SemaphoreType.DMA((SENDERS,)), pltpu.SemaphoreType.DMA((GROUPS,))]
    kept, added = pl.pallas_call(
        functools.partial(kernel, wide, narrow),
        out_shape=[jax.ShapeDtypeStruct(brick, F32)] * 2,
        in_specs=[pl.BlockSpec(memory_space=pltpu.HBM)] * 2,
        out_specs=[pl.BlockSpec(memory_space=pltpu.VMEM)] * 2,
        scratch_shapes=scratch,
        compiler_params=pltpu.CompilerParams(
            collective_id=0, has_side_effects=True, vmem_limit_bytes=32 * 1024 * 1024
        ),
    )(pltpu.with_memory_space_constraint(right_side, pltpu.HBM), pltpu.with_memory_space_constraint(conductivity, pltpu.HBM))
    return kept + added


def solution(mesh):
    spec = P("wide", None, "narrow")
    body = functools.partial(per_device, wide=mesh.shape["wide"], narrow=mesh.shape["narrow"])
    return jax.shard_map(body, mesh=mesh, in_specs=(spec, spec), out_specs=spec, check_vma=False)
```

```python
import functools

import jax
import jax.numpy as jnp
from jax import lax
from jax.experimental import pallas as pl
from jax.experimental.pallas import tpu as pltpu
from jax.sharding import PartitionSpec as P

CENTER = 1.125
HALF = 0.875
LANES = 128
REACH = 8
F32 = jnp.float32
MESH_ID = pl.DeviceIdType.MESH


def cheb(sweeps):
    sigma = CENTER / HALF
    steps = [(0.0, 1.0 / CENTER)]
    ratio = 1.0 / sigma
    for _ in range(sweeps - 1):
        ratio_next = 1.0 / (2.0 * sigma - ratio)
        steps.append((ratio_next * ratio, 2.0 * ratio_next / HALF))
        ratio = ratio_next
    return steps


def over_sides(first, second, count, body):
    def block(side, carry):
        for at in range(count):
            body(first + side * (second - first) + at)
        return carry

    lax.fori_loop(0, 2, block, 0)


def over_layers(low, high, unroll, body):
    count = high - low + 1
    if count == unroll:
        for at in range(low, high + 1):
            body(at)
        return

    def block(step, carry):
        for at in range(unroll):
            body(low + step * unroll + at)
        return carry

    lax.fori_loop(0, count // unroll, block, 0)


class Level:
    def __init__(self, refs, scale, rows, row_step, lane_step, base, extent, lane_mask):
        self.c, self.s, self.cx, self.cy, self.cz, self.iv, self.dg, self.va, self.vb = refs
        self.half = 0.5 * scale
        self.rows, self.row_step, self.lane_step = rows, row_step, lane_step
        self.base, self.extent, self.lane_mask = base, extent, lane_mask

    def inside(self, at):
        where_x = self.base + at
        return jnp.where((where_x >= 0) & (where_x < self.extent), 1.0, 0.0).astype(F32)

    def lane(self):
        return lax.broadcasted_iota(jnp.int32, (self.rows, LANES), 1)

    def row(self):
        return lax.broadcasted_iota(jnp.int32, (self.rows, LANES), 0)

    def y_up(self, tile):
        return pltpu.roll(tile, self.rows - self.row_step, 0)

    def y_down(self, tile):
        return pltpu.roll(tile, self.row_step, 0)

    def turned(self, tiles, shift, edge, count):
        out = [pltpu.roll(t, shift, 1) for t in tiles]
        if len(tiles) == 1:
            return out
        at_edge = self.lane() == edge
        return [jnp.where(at_edge, out[1 - k], out[k]) for k in range(count)]

    def z_up(self, tiles, count):
        return self.turned(tiles, LANES - self.lane_step, LANES - 1, count)

    def z_down(self, tiles, count):
        return self.turned(tiles, self.lane_step, 0, count)

    def masked(self, at, tiles):
        keep = self.inside(at) * self.half
        out = []
        for k in range(tiles):
            mask = self.lane_mask[k]
            out.append(self.c[k, at] * (keep if mask is None else mask * keep))
        return out

    def setup_below(self, low, tiles):
        first, second = self.masked(low - 1, tiles), self.masked(low, tiles)
        for k in range(tiles):
            self.cx[k, low - 1] = first[k] + second[k]

    def setup_at(self, at, tiles):
        before, here, after = self.masked(at - 1, tiles), self.masked(at, tiles), self.masked(at + 1, tiles)
        inside = self.inside(at)
        top = self.row() >= self.rows - self.row_step
        bottom = self.row() < self.row_step
        z_up, z_down = self.z_up(here, tiles), self.z_down(here, tiles)
        for k in range(tiles):
            own = here[k]
            x_low = before[k] + own
            x_high = own + after[k]
            y_low = own + jnp.where(bottom, 0.0, self.y_down(own))
            y_high = own + jnp.where(top, 0.0, self.y_up(own))
            z_low = own + z_down[k]
            z_high = own + z_up[k]
            diagonal = x_low + x_high + y_low + y_high + z_low + z_high
            keep = inside if self.lane_mask[k] is None else self.lane_mask[k] * inside
            self.cx[k, at] = x_high
            self.cy[k, at] = jnp.where(top, 0.0, y_high)
            self.cz[k, at] = z_high
            if k == 0:
                self.dg[0, at] = diagonal
            self.iv[k, at] = jnp.where(jnp.full_like(own, 0.0) + keep > 0.5, 1.0 / diagonal, 0.0)

    def setup(self, low, high, unroll, tiles):
        self.setup_below(low, tiles)
        over_layers(low, high, unroll, lambda at: self.setup_at(at, tiles))

    def start_at(self, at, tiles, beta):
        for k in range(tiles):
            self.va[k, at] = self.s[k, at] * self.iv[k, at] * beta

    def start_outer(self, at, beta):
        self.va[1, at] = self.s[1, at] * self.iv[1, at] * beta

    def start(self, low, high, unroll, tiles, beta):
        over_layers(low, high, unroll, lambda at: self.start_at(at, tiles, beta))

    def around(self, field, at, tiles, count):
        here = [field[k, at] for k in range(tiles)]
        cz = [self.cz[k, at] for k in range(tiles)]
        z_up = self.z_up(here, count)
        z_down = self.z_down([cz[k] * here[k] for k in range(tiles)], count)
        sums = []
        for k in range(count):
            cy = self.cy[k, at]
            total = self.cx[k, at] * field[k, at + 1] + self.cx[k, at - 1] * field[k, at - 1]
            total = total + (cy * self.y_up(here[k]) + self.y_down(cy * here[k]))
            total = total + (cz[k] * z_up[k] + z_down[k])
            sums.append(total + self.s[k, at])
        return here, sums

    def sweep_at(self, at, field, result, tiles, count, step, fresh):
        alpha, beta = step
        here, sums = self.around(field, at, tiles, count)
        for k in range(count):
            kept = (1.0 + alpha - beta) * here[k]
            if not fresh:
                kept = kept - alpha * result[k, at]
            result[k, at] = kept + (beta * self.iv[k, at]) * sums[k]

    def sweep(self, field, result, low, high, unroll, tiles, count, step, fresh=False):
        over_layers(low, high, unroll, lambda at: self.sweep_at(at, field, result, tiles, count, step, fresh))

    def residual(self, field, result, low, high, unroll, tiles):
        def body(at):
            here, sums = self.around(field, at, tiles, 1)
            result[0, at] = sums[0] - self.dg[0, at] * here[0]

        over_layers(low, high, unroll, body)

    def finish(self, field, older, kept_out, added_out, low, high, unroll, step):
        alpha, beta = step

        def body(at):
            here, sums = self.around(field, at, 2, 1)
            kept_out[at - low] = (1.0 + alpha - beta) * here[0] - alpha * older[0, at]
            added_out[at - low] = (beta * self.iv[0, at]) * sums[0]

        over_layers(low, high, unroll, body)


LEVEL_FIELDS = 9
LEVEL_SHAPES = ((2, 16, 32, LANES), (2, 14, 16, LANES), (1, 34, 8, LANES), (1, 15, 8, LANES))
RULER = 1024
SENDERS = 13 + 2 * REACH + 1
GROUPS = 26 + 2 * REACH + 1


def kernel(wide, narrow, rhs, coef, kept, added, *scratch):
    scratch = list(scratch)
    level_refs = []
    for _ in range(4):
        level_refs.append(scratch[:LEVEL_FIELDS])
        scratch = scratch[LEVEL_FIELDS:]
    (zs, rz, rcn, k1c, sk, sp, k1x, k1p, k1z, rc2, s2m, rs2, rx1, rx1b, sb0, hx0, p1, p0, ruler,
     local_sem, send_sem, recv_sem) = scratch
    me_w = lax.axis_index("wide")
    me_n = lax.axis_index("narrow")

    def there(dw, dn):
        return (lax.rem(me_w + (dw + wide), wide), lax.rem(me_n + (dn + narrow), narrow))

    has = (me_w > 0, me_w < wide - 1)
    reach = (jnp.minimum(me_w, REACH), jnp.minimum(wide - 1 - me_w, REACH))

    def for_far(first, body):
        for side in range(2):
            sign = 2 * side - 1

            def step(k, carry):
                body(REACH + sign * k, sign * k)
                return carry

            lax.fori_loop(first, reach[side] + 1, step, 0)

    def for_sides(body):
        for side in range(2):
            pl.when(has[side])(functools.partial(body, side, 2 * side - 1))

    @pl.when((me_w < REACH) | (me_w >= wide - REACH))
    def clear():
        def zero(ref):
            ref[...] = jnp.zeros(ref.shape, F32)

        for ref in (rcn, rx1, rx1b, hx0, rc2, rs2, k1x, k1p):
            zero(ref)
        for side in range(2):
            zero(k1c.at[2 * side])
            for ref in level_refs[0][:2]:
                zero(ref.at[0, pl.ds(12 * side, 4)])
            zero(level_refs[1][0].at[0, 13 * side])

    def if_reach(least, body):
        for side in range(2):
            pl.when(reach[side] >= least)(functools.partial(body, side, 2 * side - 1))

    barrier = pltpu.get_barrier_semaphore()

    def greet(dw, dn):
        pl.semaphore_signal(barrier, inc=1, device_id=there(dw, dn), device_id_type=MESH_ID)

    @for_sides
    def greet_side(side, dw):
        for dn in (0, -1, 1):
            greet(dw, dn)

    greet(0, -1)
    greet(0, 1)

    c0, s0 = level_refs[0][0], level_refs[0][1]
    load_c = pltpu.make_async_copy(coef, c0.at[0, pl.ds(4, 8)], local_sem.at[0])
    load_s = pltpu.make_async_copy(rhs, s0.at[0, pl.ds(4, 8)], local_sem.at[1])
    load_c.start()
    load_s.start()
    greeted = 2 + jnp.where(has[0], 3, 0) + jnp.where(has[1], 3, 0)

    left = jnp.where(me_n > 0, 1.0, 0.0).astype(F32)
    right = jnp.where(me_n < narrow - 1, 1.0, 0.0).astype(F32)

    def lanes(rows):
        return lax.broadcasted_iota(jnp.int32, (rows, LANES), 1)

    def edges(rows, until, low, since, high):
        at = lanes(rows)
        return jnp.where(at < until, low, jnp.where(at >= since, high, 0.0))

    def centred(rows):
        at = lanes(rows)
        return jnp.where((at >= 32) & (at < 96), 1.0, edges(rows, 32, left, 96, right))

    level_0 = Level(level_refs[0], 1.0, 32, 1, 1, 8 * me_w - 4, 8 * wide, [None, edges(32, 8, right, 120, left)])
    level_1 = Level(
        level_refs[1], 0.25, 16, 1, 1, 4 * me_w - 5, 4 * wide, [centred(16), edges(16, 32, right, 96, left)]
    )
    level_2 = Level(level_refs[2], 0.0625, 8, 1, 2, 2 * me_w - 16, 2 * wide, [centred(8)])
    level_3 = Level(level_refs[3], 0.015625, 8, 2, 4, me_w - 7, wide, [centred(8)])

    sent = [0] * SENDERS

    def send(group, src, dst, dw, dn, rows, sender):
        if isinstance(sender, int):
            sent[sender] += rows
        pltpu.make_async_remote_copy(
            src_ref=src, dst_ref=dst, send_sem=send_sem.at[sender], recv_sem=recv_sem.at[group],
            device_id=there(dw, dn), device_id_type=MESH_ID,
        ).start()

    def ruled(rows, group, sender):
        span = ruler.at[pl.ds(0, rows)]
        return pltpu.make_async_remote_copy(
            src_ref=span, dst_ref=span, send_sem=send_sem.at[sender], recv_sem=recv_sem.at[group],
            device_id=there(0, 1), device_id_type=MESH_ID,
        )

    def receive(group, rows):
        ruled(rows, group, 0).wait_recv()

    def receive_sides(group, rows):
        for_sides(lambda side, dw: receive(group + side, rows))

    def receive_far(group):
        for_far(1, lambda slot, dw: receive(group + slot, 8))

    def sends_done(sender):
        ruled(sent[sender], 0, sender).wait_send()

    from_z, from_s1z = 0, 1
    from_c, from_s, from_k, from_s1, from_c1b, from_x0, from_x1, from_x1b = range(2, 18, 2)
    from_near, from_two, from_four, from_eight = range(18, 26, 2)
    from_s2 = 26
    sender_two, sender_four, sender_eight, sender_far = 7, 9, 11, 13

    def pack(tiles):
        rows = tiles[0].shape[0]
        group = lanes(rows) // 16
        packed = jnp.zeros((rows, LANES), F32)
        for at, tile in enumerate(tiles):
            packed = jnp.where(group == at, pltpu.roll(tile, (16 * at + 8) % LANES, 1), packed)
        return packed

    def unpack(packed, at):
        return pltpu.roll(packed, (2 * LANES - (16 * at + 8)) % LANES, 1)

    def pack_side(ref, half, side):
        group = lanes(8) // 8
        packed = None
        for layer in range(4):
            for part in range(4):
                at = 4 * layer + part
                tile = ref[0, 4 + 4 * half + layer, pl.ds(8 * part, 8), :]
                tile = pltpu.roll(tile, (8 * at + 8 * side) % LANES, 1)
                packed = tile if at == 0 else jnp.where(group == at, tile, packed)
        return packed

    def restrict_0(ref):
        out = []
        for layer in range(4):
            total = None
            for dx in range(2):
                for dy in range(2):
                    term = ref[0, 4 + 2 * layer + dx, pl.ds(dy, 16, stride=2), :]
                    total = term if total is None else total + term
            total = total + pltpu.roll(total, LANES - 1, 1)
            out.append(0.125 * jnp.take_along_axis(total, (2 * lanes(16) + 64) % LANES, axis=1))
        return out

    odd_8 = lanes(8) % 2 == 1

    def pairs_1(ref):
        out = []
        for layer in range(2):
            total = None
            for dx in range(2):
                for dy in range(2):
                    term = ref[0, 5 + 2 * layer + dx, pl.ds(dy, 8, stride=2), :]
                    total = term if total is None else total + term
            total = total + jnp.where(odd_8, pltpu.roll(total, 1, 1), pltpu.roll(total, LANES - 1, 1))
            out.append(0.125 * total)
        return jnp.where(odd_8, out[1], out[0])

    def squeeze_1(layers, ref, row):
        for part in range(2):
            ref[pl.ds(row + 16 * part, 16), :] = jnp.where(lanes(16) < 64, layers[part], layers[part + 2])

    pl.semaphore_wait(barrier, greeted)

    @for_sides
    def send_faces(side, dw):
        send(from_c + 1 - side, coef.at[pl.ds(4 * side, 4)], c0.at[0, pl.ds(12 - 12 * side, 4)], dw, 0, 128, 1 + side)
        send(from_s + 1 - side, rhs.at[pl.ds(5 * side, 3)], s0.at[0, pl.ds(12 - 11 * side, 3)], dw, 0, 96, 1 + side)

    load_c.wait()
    own_c1 = restrict_0(c0)
    for side in range(2):
        squeeze_1(own_c1, zs.at[side], 32)
        for half in range(2):
            zs[side, pl.ds(16 * half, 8), :] = pack_side(c0, half, side)
    load_s.wait()
    for side in range(2):
        for half in range(2):
            zs[side, pl.ds(16 * half + 8, 8), :] = pack_side(s0, half, side)

    send(from_z, zs.at[0], rz.at[1], 0, -1, 64, 0)
    send(from_z, zs.at[1], rz.at[0], 0, 1, 64, 0)

    @for_sides
    def send_corners(side, dw):
        for dn in (-1, 1):
            span = zs.at[(1 + dn) // 2, pl.ds(16 * side, 16)]
            send(from_c + 1 - side, span, rcn.at[1 - side, (1 - dn) // 2], dw, dn, 16, 1 + side)

    def fill_0(ref, first, from_left, from_right):
        low = lanes(8) < 64
        for layer in range(4):
            for part in range(4):
                at = 4 * layer + part
                ref[1, first + layer, pl.ds(8 * part, 8), :] = jnp.where(
                    low, pltpu.roll(from_right, (LANES - 8 * at) % LANES, 1), pltpu.roll(from_left, (120 - 8 * at) % LANES, 1)
                )

    steps = cheb(3)
    receive(from_z, 128)
    for field, ref in enumerate((c0, s0)):
        for half in range(2):
            rows = pl.ds(16 * half + 8 * field, 8)
            fill_0(ref, 4 + 4 * half, rz[0, rows, :], rz[1, rows, :])
    level_0.setup(5, 10, 3, 2)
    level_0.start(5, 10, 6, 2, steps[0][1])
    level_0.sweep(level_0.va, level_0.vb, 6, 9, 4, 2, 2, steps[1], fresh=True)
    level_0.sweep(level_0.vb, level_0.va, 7, 8, 2, 2, 2, steps[2])

    @for_sides
    def send_coef(side, dw):
        for dn in (0, -1, 1):
            send(from_k + 1 - side, zs.at[0, pl.ds(32, 32)], k1c.at[1 - dw, 1 - dn], dw, dn, 32, 1 + side)

    def spread_1(ref, block, places):
        at_lane = lanes(16)
        low_half = at_lane < 64
        low_quarter = at_lane % 64 < 32
        for dx in places:
            for part in range(2):
                before, own, after = (block(dx, dz, part) for dz in (-1, 0, 1))
                near = jnp.where(low_quarter, before, after)
                outer = jnp.where(low_quarter, after, before)
                own_r, near_r, outer_r = (pltpu.roll(t, 64, 1) for t in (own, near, outer))
                at = 5 + 4 * dx + part
                for at, own_a, own_b, near_a, near_b, outer_a, outer_b in (
                    (at, own, own_r, near, near_r, outer, outer_r),
                    (at + 2, own_r, own, near_r, near, outer_r, outer),
                ):
                    centre = jnp.where(low_half, own_a, own_b)
                    ref[0, at] = jnp.where(at_lane < 32, near_a, jnp.where(at_lane < 96, centre, near_b))
                    ref[1, at] = jnp.where(low_half, outer_a, outer_b)

    def coef_block(dx, dz, part):
        if dx == 0:
            rows = pl.ds(32 + 16 * part, 16)
            return zs[0, rows, :] if dz == 0 else rz[(1 + dz) // 2, rows, :]
        return k1c[1 + dx, 1 + dz, pl.ds(16 * part, 16), :]

    spread_1(level_1.c, coef_block, (0,))
    rc2[REACH] = pairs_1(level_1.c)

    @for_sides
    def send_near(side, dw):
        send(from_near + 1 - side, rc2.at[REACH], rc2.at[REACH - dw], dw, 0, 8, 1 + side)

    receive_sides(from_c, 160)
    for field, ref in enumerate((c0, s0)):
        for side in range(2):
            rows = pl.ds(8 * field, 8)
            fill_0(ref, 12 * side, rcn[side, 0, rows, :], rcn[side, 1, rows, :])
    level_0.setup_below(1, 2)
    over_sides(1, 11, 4, lambda at: level_0.setup_at(at, 2))
    receive_sides(from_near, 8)

    @functools.partial(if_reach, 2)
    def send_two(side, sign):
        src = rc2.at[pl.ds(REACH - side, 2)] if side == 1 else rc2.at[pl.ds(REACH, 2)]
        dst = rc2.at[pl.ds(REACH - 3, 2)] if side == 1 else rc2.at[pl.ds(REACH + 2, 2)]
        send(from_two + 1 - side, src, dst, 2 * sign, 0, 16, sender_two + side)

    receive_sides(from_s, 96)
    over_sides(1, 11, 4, lambda at: level_0.start_at(at, 2, steps[0][1]))
    over_sides(2, 10, 4, lambda at: level_0.sweep_at(at, level_0.va, level_0.vb, 2, 2, steps[1], True))
    over_sides(3, 9, 4, lambda at: level_0.sweep_at(at, level_0.vb, level_0.va, 2, 2, steps[2], False))
    level_0.residual(level_0.va, level_0.vb, 4, 11, 4, 2)

    squeeze_1(restrict_0(level_0.vb), sk, 0)

    low_quarter = lanes(16) % 64 < 32
    first, second = sk[pl.ds(0, 16), :], sk[pl.ds(16, 16), :]
    sp[0] = jnp.where(low_quarter, pltpu.roll(first, 96, 1), second)
    sp[1] = jnp.where(low_quarter, first, pltpu.roll(second, 32, 1))

    @for_sides
    def send_source(side, dw):
        send(from_s1 + 1 - side, sk, k1x.at[1 - side], dw, 0, 32, 1 + side)
        for dn in (-1, 1):
            send(from_s1 + 1 - side, sp.at[(1 + dn) // 2], k1p.at[1 - side, (1 - dn) // 2], dw, dn, 16, 1 + side)

    for dn in (-1, 1):
        send(from_s1z, sk, k1z.at[(1 - dn) // 2], 0, dn, 32, 0)

    if_reach(2, lambda side, sign: receive(from_two + side, 16))

    @functools.partial(if_reach, 4)
    def send_four(side, sign):
        src = rc2.at[pl.ds(REACH - 3, 4)] if side == 1 else rc2.at[pl.ds(REACH, 4)]
        dst = rc2.at[pl.ds(REACH - 7, 4)] if side == 1 else rc2.at[pl.ds(REACH + 4, 4)]
        send(from_four + 1 - side, src, dst, 4 * sign, 0, 32, sender_four + side)

    for side in range(2):
        first = 9 if side == 0 else 4
        tiles = []
        for layer in range(3):
            sb0[side, pl.ds(32 * layer, 32), :] = level_0.va[0, first + layer]
            for part in range(2):
                tiles.append(level_0.va[1, first + layer, pl.ds(16 * part, 16), :])
        sb0[side, pl.ds(96, 16), :] = pack(tiles)

    @for_sides
    def send_iterate_0(side, dw):
        send(from_x0 + 1 - side, sb0.at[1 - side], hx0.at[1 - side], dw, 0, 112, 1 + side)

    def source_block(dx, dz, part):
        rows = pl.ds(16 * part, 16)
        return sk[rows, :] if dz == 0 else k1z[(1 + dz) // 2, rows, :]

    def spread_beside(ref):
        at_lane = lanes(16)
        low_half = at_lane < 64
        for side in range(2):
            for layer in range(4):
                own = k1x[side, pl.ds(16 * (layer % 2), 16), :]
                other = pltpu.roll(own, 64, 1)
                centre = jnp.where(low_half, own, other) if layer < 2 else jnp.where(low_half, other, own)
                before = pltpu.roll(k1p[side, 0], (LANES - 32 * layer) % LANES, 1)
                after = pltpu.roll(k1p[side, 1], (LANES + 96 - 32 * layer) % LANES, 1)
                ref[0, 1 + 8 * side + layer] = jnp.where(at_lane < 32, before, jnp.where(at_lane < 96, centre, after))

    receive_sides(from_k, 96)
    spread_1(level_1.c, coef_block, (-1, 1))

    @for_sides
    def send_coef_1(side, dw):
        send(from_c1b + 1 - side, level_1.c.at[0, 9 - 5 * side], level_1.c.at[0, 13 - 13 * side], dw, 0, 16, 1 + side)

    level_1.setup_below(2, 1)
    over_sides(2, 10, 2, lambda at: level_1.setup_at(at, 1))
    over_layers(4, 9, 6, lambda at: level_1.setup_at(at, 2))

    receive(from_s1z, 64)
    spread_1(level_1.s, source_block, (0,))
    receive_sides(from_s1, 64)
    spread_beside(level_1.s)
    level_1.start(2, 11, 10, 1, steps[0][1])
    over_layers(5, 8, 4, lambda at: level_1.start_outer(at, steps[0][1]))
    over_sides(3, 9, 2, lambda at: level_1.sweep_at(at, level_1.va, level_1.vb, 1, 1, steps[1], True))
    over_layers(5, 8, 4, lambda at: level_1.sweep_at(at, level_1.va, level_1.vb, 2, 1, steps[1], True))
    level_1.sweep(level_1.vb, level_1.va, 4, 9, 6, 1, 1, steps[2])
    level_1.residual(level_1.va, level_1.vb, 5, 8, 4, 1)

    value = pairs_1(level_1.vb)
    s2m[...] = value
    rs2[REACH] = value
    if_reach(4, lambda side, sign: receive(from_four + side, 32))
    for_far(1, lambda slot, dw: send(from_s2 + 2 * REACH - slot, s2m, rs2.at[2 * REACH - slot], dw, 0, 8, sender_far + slot))

    @functools.partial(if_reach, REACH)
    def send_eight(side, sign):
        send(from_eight + 1 - side, rc2.at[REACH], rc2.at[REACH - sign * REACH], REACH * sign, 0, 8, sender_eight + side)

    @for_sides
    def send_iterate_1(side, dw):
        send(from_x1 + 1 - side, level_1.va.at[0, pl.ds(5, 4)], rx1.at[1 - side], dw, 0, 64, 3 + side)

    for side in range(2):
        @pl.when(reach[side] >= 2)
        def send_next_1():
            layer = level_1.va.at[0, 5 + 3 * side]
            send(from_x1b + 1 - side, layer, rx1b.at[1 - side], 4 * side - 2, 0, 16, 5 + side)

    receive_sides(from_c1b, 16)
    level_1.setup_below(1, 1)
    over_sides(1, 12, 1, lambda at: level_1.setup_at(at, 1))

    def spread_2(ref, blocks):
        for block in range(2 * REACH + 1):
            packed = blocks[block]
            ref[0, 2 * block] = jnp.where(odd_8, pltpu.roll(packed, 1, 1), packed)
            ref[0, 2 * block + 1] = jnp.where(odd_8, packed, pltpu.roll(packed, LANES - 1, 1))

    def restrict_2(ref, at):
        total = ref[0, 2 * at + 2] + ref[0, 2 * at + 3]
        odd_row = lax.broadcasted_iota(jnp.int32, (8, LANES), 0) % 2 == 1
        total = total + jnp.where(odd_row, pltpu.roll(total, 1, 0), pltpu.roll(total, 7, 0))
        second = lanes(8) % 4 >= 2
        total = total + jnp.where(second, pltpu.roll(total, 2, 1), pltpu.roll(total, LANES - 2, 1))
        return 0.125 * total

    if_reach(REACH, lambda side, sign: receive(from_eight + side, 8))
    spread_2(level_2.c, rc2)
    level_2.setup(1, 32, 8, 1)
    for at in range(15):
        level_3.c[0, at] = restrict_2(level_2.c, at)
    level_3.setup(1, 13, 13, 1)

    receive_far(from_s2)
    spread_2(level_2.s, rs2)
    level_2.start(1, 32, 32, 1, steps[0][1])
    level_2.sweep(level_2.va, level_2.vb, 2, 31, 15, 1, 1, steps[1], fresh=True)
    level_2.sweep(level_2.vb, level_2.va, 3, 30, 14, 1, 1, steps[2])
    level_2.residual(level_2.va, level_2.vb, 4, 29, 13, 1)

    for at in range(1, 14):
        level_3.s[0, at] = restrict_2(level_2.vb, at)
    coarse = cheb(4)
    level_3.start(1, 13, 13, 1, coarse[0][1])
    level_3.sweep(level_3.va, level_3.vb, 2, 12, 11, 1, 1, coarse[1], fresh=True)
    level_3.sweep(level_3.vb, level_3.va, 3, 11, 9, 1, 1, coarse[2])
    level_3.sweep(level_3.va, level_3.vb, 4, 10, 7, 1, 1, coarse[3])

    for at in range(10, 24):
        level_2.vb[0, at] = level_2.va[0, at] + level_3.vb[0, (at - 2) // 2]
    level_2.sweep(level_2.vb, level_2.va, 11, 22, 12, 1, 1, steps[0], fresh=True)
    level_2.sweep(level_2.va, level_2.vb, 12, 21, 10, 1, 1, steps[1])
    level_2.sweep(level_2.vb, level_2.va, 13, 20, 8, 1, 1, steps[2])

    for at in range(8):
        value = level_2.va[0, 13 + at]
        for part in range(2):
            p1[at, pl.ds(part, 8, stride=2), :] = value
    receive_sides(from_x1, 64)
    for side in range(2):
        pl.when(reach[side] >= 2)(functools.partial(receive, from_x1b + side, 16))
    for at in range(14):
        if 5 <= at <= 8:
            before = level_1.va[0, at]
        else:
            beside = (rx1b[0] if at == 0 else rx1[0, at - 1] if at < 5 else rx1[1, at - 9] if at < 13 else rx1b[1])
            before = beside * level_1.inside(at)
        level_1.vb[0, at] = before + p1[(at + 1) // 2]
    for side in range(2):
        pl.when(has[side])(functools.partial(sends_done, 3 + side))
        pl.when(reach[side] >= 2)(functools.partial(sends_done, 5 + side))
    level_1.sweep(level_1.vb, level_1.va, 1, 12, 12, 1, 1, steps[0], fresh=True)
    level_1.sweep(level_1.va, level_1.vb, 2, 11, 10, 1, 1, steps[1])
    level_1.sweep(level_1.vb, level_1.va, 3, 10, 8, 1, 1, steps[2])

    fine_lane = lanes(16) // 2
    for at in range(8):
        value = level_1.va[0, 3 + at]
        for k in range(2):
            fine = jnp.take_along_axis(value, (fine_lane + (32 if k == 0 else 96)) % LANES, axis=1)
            for part in range(2):
                p0[k, at, pl.ds(part, 16, stride=2), :] = fine
    receive_sides(from_x0, 112)
    for side in range(2):
        packed = hx0[side, pl.ds(96, 16), :]
        for layer in range(3):
            at = (1 if side == 0 else 12) + layer
            inside = level_0.inside(at)
            coarse_at = (at - 4) // 2 + 2
            level_0.vb[0, at] = hx0[side, pl.ds(32 * layer, 32), :] * inside + p0[0, coarse_at]
            for part in range(2):
                rows = pl.ds(16 * part, 16)
                level_0.vb[1, at, rows, :] = (
                    unpack(packed, 2 * layer + part) * (level_0.lane_mask[1][:16] * inside) + p0[1, coarse_at, rows, :]
                )

    def correct(at):
        for k in range(2):
            level_0.vb[k, at] = level_0.va[k, at] + p0[k, at // 2]

    over_layers(4, 11, 4, correct)
    level_0.sweep(level_0.vb, level_0.va, 2, 13, 4, 2, 2, steps[0], fresh=True)
    level_0.sweep(level_0.va, level_0.vb, 3, 12, 5, 2, 2, steps[1])
    level_0.finish(level_0.vb, level_0.va, kept, added, 4, 11, 4, steps[2])

    sends_done(0)
    for_sides(lambda side, dw: sends_done(1 + side))
    if_reach(2, lambda side, sign: sends_done(sender_two + side))
    if_reach(4, lambda side, sign: sends_done(sender_four + side))
    if_reach(REACH, lambda side, sign: sends_done(sender_eight + side))
    for_far(1, lambda slot, dw: ruled(8, 0, sender_far + slot).wait_send())


def per_device(right_side, conductivity, wide, narrow):
    brick = (8, 32, LANES)
    scratch = []
    for shape in LEVEL_SHAPES:
        scratch += [pltpu.VMEM(shape, F32)] * LEVEL_FIELDS
    shapes = [
        (2, 64, LANES), (2, 64, LANES), (2, 2, 16, LANES), (3, 3, 32, LANES),
        (32, LANES), (2, 16, LANES), (2, 32, LANES), (2, 2, 16, LANES), (2, 32, LANES),
        (2 * REACH + 1, 8, LANES), (8, LANES), (2 * REACH + 1, 8, LANES),
        (2, 4, 16, LANES), (2, 16, LANES),
        (2, 112, LANES), (2, 112, LANES),
        (8, 16, LANES), (2, 8, 32, LANES),
        (RULER, LANES),
    ]
    scratch += [pltpu.VMEM(shape, F32) for shape in shapes]
    scratch += [pltpu.SemaphoreType.DMA((2,)), pltpu.SemaphoreType.DMA((SENDERS,)), pltpu.SemaphoreType.DMA((GROUPS,))]
    kept, added = pl.pallas_call(
        functools.partial(kernel, wide, narrow),
        out_shape=[jax.ShapeDtypeStruct(brick, F32)] * 2,
        in_specs=[pl.BlockSpec(memory_space=pltpu.HBM)] * 2,
        out_specs=[pl.BlockSpec(memory_space=pltpu.VMEM)] * 2,
        scratch_shapes=scratch,
        compiler_params=pltpu.CompilerParams(
            collective_id=0, has_side_effects=True, vmem_limit_bytes=32 * 1024 * 1024
        ),
    )(pltpu.with_memory_space_constraint(right_side, pltpu.HBM), pltpu.with_memory_space_constraint(conductivity, pltpu.HBM))
    return kept + added


def solution(mesh):
    spec = P("wide", None, "narrow")
    body = functools.partial(per_device, wide=mesh.shape["wide"], narrow=mesh.shape["narrow"])
    return jax.shard_map(body, mesh=mesh, in_specs=(spec, spec), out_specs=spec, check_vma=False)
```

```python
import functools

import jax
import jax.numpy as jnp
from jax import lax
from jax.experimental import pallas as pl
from jax.experimental.pallas import tpu as pltpu
from jax.sharding import PartitionSpec as P

CENTER = 1.125
HALF = 0.875
LANES = 128
REACH = 8
F32 = jnp.float32
MESH_ID = pl.DeviceIdType.MESH


def cheb(sweeps):
    sigma = CENTER / HALF
    steps = [(0.0, 1.0 / CENTER)]
    ratio = 1.0 / sigma
    for _ in range(sweeps - 1):
        ratio_next = 1.0 / (2.0 * sigma - ratio)
        steps.append((ratio_next * ratio, 2.0 * ratio_next / HALF))
        ratio = ratio_next
    return steps


def over_sides(first, second, count, body):
    def block(side, carry):
        for at in range(count):
            body(first + side * (second - first) + at)
        return carry

    lax.fori_loop(0, 2, block, 0)


def over_layers(low, high, unroll, body):
    count = high - low + 1
    if count == unroll:
        for at in range(low, high + 1):
            body(at)
        return

    def block(step, carry):
        for at in range(unroll):
            body(low + step * unroll + at)
        return carry

    lax.fori_loop(0, count // unroll, block, 0)


class Level:
    def __init__(self, refs, scale, rows, row_step, lane_step, base, extent, lane_mask):
        self.c, self.s, self.cx, self.cy, self.cz, self.iv, self.dg, self.va, self.vb = refs
        self.half = 0.5 * scale
        self.rows, self.row_step, self.lane_step = rows, row_step, lane_step
        self.base, self.extent, self.lane_mask = base, extent, lane_mask

    def inside(self, at):
        where_x = self.base + at
        return jnp.where((where_x >= 0) & (where_x < self.extent), 1.0, 0.0).astype(F32)

    def lane(self):
        return lax.broadcasted_iota(jnp.int32, (self.rows, LANES), 1)

    def row(self):
        return lax.broadcasted_iota(jnp.int32, (self.rows, LANES), 0)

    def y_up(self, tile):
        return pltpu.roll(tile, self.rows - self.row_step, 0)

    def y_down(self, tile):
        return pltpu.roll(tile, self.row_step, 0)

    def turned(self, tiles, shift, edge, count):
        out = [pltpu.roll(t, shift, 1) for t in tiles]
        if len(tiles) == 1:
            return out
        at_edge = self.lane() == edge
        return [jnp.where(at_edge, out[1 - k], out[k]) for k in range(count)]

    def z_up(self, tiles, count):
        return self.turned(tiles, LANES - self.lane_step, LANES - 1, count)

    def z_down(self, tiles, count):
        return self.turned(tiles, self.lane_step, 0, count)

    def masked(self, at, tiles):
        keep = self.inside(at) * self.half
        out = []
        for k in range(tiles):
            mask = self.lane_mask[k]
            out.append(self.c[k, at] * (keep if mask is None else mask * keep))
        return out

    def setup_below(self, low, tiles):
        first, second = self.masked(low - 1, tiles), self.masked(low, tiles)
        for k in range(tiles):
            self.cx[k, low - 1] = first[k] + second[k]

    def setup_at(self, at, tiles):
        before, here, after = self.masked(at - 1, tiles), self.masked(at, tiles), self.masked(at + 1, tiles)
        inside = self.inside(at)
        top = self.row() >= self.rows - self.row_step
        bottom = self.row() < self.row_step
        z_up, z_down = self.z_up(here, tiles), self.z_down(here, tiles)
        for k in range(tiles):
            own = here[k]
            x_low = before[k] + own
            x_high = own + after[k]
            y_low = own + jnp.where(bottom, 0.0, self.y_down(own))
            y_high = own + jnp.where(top, 0.0, self.y_up(own))
            z_low = own + z_down[k]
            z_high = own + z_up[k]
            diagonal = x_low + x_high + y_low + y_high + z_low + z_high
            keep = inside if self.lane_mask[k] is None else self.lane_mask[k] * inside
            self.cx[k, at] = x_high
            self.cy[k, at] = jnp.where(top, 0.0, y_high)
            self.cz[k, at] = z_high
            if k == 0:
                self.dg[0, at] = diagonal
            self.iv[k, at] = jnp.where(jnp.full_like(own, 0.0) + keep > 0.5, 1.0 / diagonal, 0.0)

    def setup(self, low, high, unroll, tiles):
        self.setup_below(low, tiles)
        over_layers(low, high, unroll, lambda at: self.setup_at(at, tiles))

    def start_at(self, at, tiles, beta):
        for k in range(tiles):
            self.va[k, at] = self.s[k, at] * self.iv[k, at] * beta

    def start_outer(self, at, beta):
        self.va[1, at] = self.s[1, at] * self.iv[1, at] * beta

    def start(self, low, high, unroll, tiles, beta):
        over_layers(low, high, unroll, lambda at: self.start_at(at, tiles, beta))

    def around(self, field, at, tiles, count):
        here = [field[k, at] for k in range(tiles)]
        cz = [self.cz[k, at] for k in range(tiles)]
        z_up = self.z_up(here, count)
        z_down = self.z_down([cz[k] * here[k] for k in range(tiles)], count)
        sums = []
        for k in range(count):
            cy = self.cy[k, at]
            total = self.cx[k, at] * field[k, at + 1] + self.cx[k, at - 1] * field[k, at - 1]
            total = total + (cy * self.y_up(here[k]) + self.y_down(cy * here[k]))
            total = total + (cz[k] * z_up[k] + z_down[k])
            sums.append(total + self.s[k, at])
        return here, sums

    def sweep_at(self, at, field, result, tiles, count, step, fresh):
        alpha, beta = step
        here, sums = self.around(field, at, tiles, count)
        for k in range(count):
            kept = (1.0 + alpha - beta) * here[k]
            if not fresh:
                kept = kept - alpha * result[k, at]
            result[k, at] = kept + (beta * self.iv[k, at]) * sums[k]

    def sweep(self, field, result, low, high, unroll, tiles, count, step, fresh=False):
        over_layers(low, high, unroll, lambda at: self.sweep_at(at, field, result, tiles, count, step, fresh))

    def residual(self, field, result, low, high, unroll, tiles):
        def body(at):
            here, sums = self.around(field, at, tiles, 1)
            result[0, at] = sums[0] - self.dg[0, at] * here[0]

        over_layers(low, high, unroll, body)

    def finish(self, field, older, kept_out, added_out, low, high, unroll, step):
        alpha, beta = step

        def body(at):
            here, sums = self.around(field, at, 2, 1)
            kept_out[at - low] = (1.0 + alpha - beta) * here[0] - alpha * older[0, at]
            added_out[at - low] = (beta * self.iv[0, at]) * sums[0]

        over_layers(low, high, unroll, body)


LEVEL_FIELDS = 9
LEVEL_SHAPES = ((2, 16, 32, LANES), (2, 14, 16, LANES), (1, 34, 8, LANES), (1, 15, 8, LANES))
RULER = 1024
SENDERS = 13 + 2 * REACH + 1
GROUPS = 26 + 2 * REACH + 1


def kernel(wide, narrow, rhs, coef, kept, added, *scratch):
    scratch = list(scratch)
    level_refs = []
    for _ in range(4):
        level_refs.append(scratch[:LEVEL_FIELDS])
        scratch = scratch[LEVEL_FIELDS:]
    (zs, rz, rcn, k1c, sk, sp, k1x, k1p, k1z, rc2, s2m, rs2, rx1, rx1b, sb0, hx0, p1, p0, ruler,
     local_sem, send_sem, recv_sem) = scratch
    me_w = lax.axis_index("wide")
    me_n = lax.axis_index("narrow")

    def there(dw, dn):
        return (lax.rem(me_w + (dw + wide), wide), lax.rem(me_n + (dn + narrow), narrow))

    has = (me_w > 0, me_w < wide - 1)
    reach = (jnp.minimum(me_w, REACH), jnp.minimum(wide - 1 - me_w, REACH))

    def for_far(first, body):
        for side in range(2):
            sign = 2 * side - 1

            def step(k, carry):
                body(REACH + sign * k, sign * k)
                return carry

            lax.fori_loop(first, reach[side] + 1, step, 0)

    def for_sides(body):
        for side in range(2):
            pl.when(has[side])(functools.partial(body, side, 2 * side - 1))

    @pl.when((me_w < REACH) | (me_w >= wide - REACH))
    def clear():
        def zero(ref):
            ref[...] = jnp.zeros(ref.shape, F32)

        for ref in (rcn, rx1, rx1b, hx0, rc2, rs2, k1x, k1p):
            zero(ref)
        for side in range(2):
            zero(k1c.at[2 * side])
            for ref in level_refs[0][:2]:
                zero(ref.at[0, pl.ds(12 * side, 4)])
            zero(level_refs[1][0].at[0, 13 * side])

    def if_reach(least, body):
        for side in range(2):
            pl.when(reach[side] >= least)(functools.partial(body, side, 2 * side - 1))

    barrier = pltpu.get_barrier_semaphore()

    def greet(dw, dn):
        pl.semaphore_signal(barrier, inc=1, device_id=there(dw, dn), device_id_type=MESH_ID)

    @for_sides
    def greet_side(side, dw):
        for dn in (0, -1, 1):
            greet(dw, dn)

    greet(0, -1)
    greet(0, 1)

    c0, s0 = level_refs[0][0], level_refs[0][1]
    load_c = pltpu.make_async_copy(coef, c0.at[0, pl.ds(4, 8)], local_sem.at[0])
    load_s = pltpu.make_async_copy(rhs, s0.at[0, pl.ds(4, 8)], local_sem.at[1])
    load_c.start()
    load_s.start()
    greeted = 2 + jnp.where(has[0], 3, 0) + jnp.where(has[1], 3, 0)

    left = jnp.where(me_n > 0, 1.0, 0.0).astype(F32)
    right = jnp.where(me_n < narrow - 1, 1.0, 0.0).astype(F32)

    def lanes(rows):
        return lax.broadcasted_iota(jnp.int32, (rows, LANES), 1)

    def edges(rows, until, low, since, high):
        at = lanes(rows)
        return jnp.where(at < until, low, jnp.where(at >= since, high, 0.0))

    def centred(rows):
        at = lanes(rows)
        return jnp.where((at >= 32) & (at < 96), 1.0, edges(rows, 32, left, 96, right))

    level_0 = Level(level_refs[0], 1.0, 32, 1, 1, 8 * me_w - 4, 8 * wide, [None, edges(32, 8, right, 120, left)])
    level_1 = Level(
        level_refs[1], 0.25, 16, 1, 1, 4 * me_w - 5, 4 * wide, [centred(16), edges(16, 32, right, 96, left)]
    )
    level_2 = Level(level_refs[2], 0.0625, 8, 1, 2, 2 * me_w - 16, 2 * wide, [centred(8)])
    level_3 = Level(level_refs[3], 0.015625, 8, 2, 4, me_w - 7, wide, [centred(8)])

    sent = [0] * SENDERS

    def send(group, src, dst, dw, dn, rows, sender):
        if isinstance(sender, int):
            sent[sender] += rows
        pltpu.make_async_remote_copy(
            src_ref=src, dst_ref=dst, send_sem=send_sem.at[sender], recv_sem=recv_sem.at[group],
            device_id=there(dw, dn), device_id_type=MESH_ID,
        ).start()

    def ruled(rows, group, sender):
        span = ruler.at[pl.ds(0, rows)]
        return pltpu.make_async_remote_copy(
            src_ref=span, dst_ref=span, send_sem=send_sem.at[sender], recv_sem=recv_sem.at[group],
            device_id=there(0, 1), device_id_type=MESH_ID,
        )

    def receive(group, rows):
        ruled(rows, group, 0).wait_recv()

    def receive_sides(group, rows):
        for_sides(lambda side, dw: receive(group + side, rows))

    def receive_far(group):
        for_far(1, lambda slot, dw: receive(group + slot, 8))

    def sends_done(sender):
        ruled(sent[sender], 0, sender).wait_send()

    from_z, from_s1z = 0, 1
    from_c, from_s, from_k, from_s1, from_c1b, from_x0, from_x1, from_x1b = range(2, 18, 2)
    from_near, from_two, from_four, from_eight = range(18, 26, 2)
    from_s2 = 26
    sender_two, sender_four, sender_eight, sender_far = 7, 9, 11, 13

    def pack(tiles):
        rows = tiles[0].shape[0]
        group = lanes(rows) // 16
        packed = jnp.zeros((rows, LANES), F32)
        for at, tile in enumerate(tiles):
            packed = jnp.where(group == at, pltpu.roll(tile, (16 * at + 8) % LANES, 1), packed)
        return packed

    def unpack(packed, at):
        return pltpu.roll(packed, (2 * LANES - (16 * at + 8)) % LANES, 1)

    def pack_side(ref, half, side):
        group = lanes(8) // 8
        packed = None
        for layer in range(4):
            for part in range(4):
                at = 4 * layer + part
                tile = ref[0, 4 + 4 * half + layer, pl.ds(8 * part, 8), :]
                tile = pltpu.roll(tile, (8 * at + 8 * side) % LANES, 1)
                packed = tile if at == 0 else jnp.where(group == at, tile, packed)
        return packed

    def restrict_0(ref):
        out = []
        for layer in range(4):
            total = None
            for dx in range(2):
                for dy in range(2):
                    term = ref[0, 4 + 2 * layer + dx, pl.ds(dy, 16, stride=2), :]
                    total = term if total is None else total + term
            total = total + pltpu.roll(total, LANES - 1, 1)
            out.append(0.125 * jnp.take_along_axis(total, (2 * lanes(16) + 64) % LANES, axis=1))
        return out

    odd_8 = lanes(8) % 2 == 1

    def pairs_1(ref):
        out = []
        for layer in range(2):
            total = None
            for dx in range(2):
                for dy in range(2):
                    term = ref[0, 5 + 2 * layer + dx, pl.ds(dy, 8, stride=2), :]
                    total = term if total is None else total + term
            total = total + jnp.where(odd_8, pltpu.roll(total, 1, 1), pltpu.roll(total, LANES - 1, 1))
            out.append(0.125 * total)
        return jnp.where(odd_8, out[1], out[0])

    def squeeze_1(layers, ref, row):
        for part in range(2):
            ref[pl.ds(row + 16 * part, 16), :] = jnp.where(lanes(16) < 64, layers[part], layers[part + 2])

    pl.semaphore_wait(barrier, greeted)

    @for_sides
    def send_faces(side, dw):
        send(from_c + 1 - side, coef.at[pl.ds(4 * side, 4)], c0.at[0, pl.ds(12 - 12 * side, 4)], dw, 0, 128, 1 + side)

    load_c.wait()
    own_c1 = restrict_0(c0)
    for side in range(2):
        squeeze_1(own_c1, zs.at[side], 32)
        for half in range(2):
            zs[side, pl.ds(16 * half, 8), :] = pack_side(c0, half, side)
    load_s.wait()
    for side in range(2):
        for half in range(2):
            zs[side, pl.ds(16 * half + 8, 8), :] = pack_side(s0, half, side)

    send(from_z, zs.at[0], rz.at[1], 0, -1, 64, 0)
    send(from_z, zs.at[1], rz.at[0], 0, 1, 64, 0)

    @for_sides
    def send_corners(side, dw):
        for dn in (-1, 1):
            span = zs.at[(1 + dn) // 2, pl.ds(16 * side, 16)]
            send(from_c + 1 - side, span, rcn.at[1 - side, (1 - dn) // 2], dw, dn, 16, 1 + side)
        send(from_s + 1 - side, rhs.at[pl.ds(5 * side, 3)], s0.at[0, pl.ds(12 - 11 * side, 3)], dw, 0, 96, 1 + side)

    def fill_0(ref, first, from_left, from_right):
        low = lanes(8) < 64
        for layer in range(4):
            for part in range(4):
                at = 4 * layer + part
                ref[1, first + layer, pl.ds(8 * part, 8), :] = jnp.where(
                    low, pltpu.roll(from_right, (LANES - 8 * at) % LANES, 1), pltpu.roll(from_left, (120 - 8 * at) % LANES, 1)
                )

    steps = cheb(3)
    receive(from_z, 128)
    for field, ref in enumerate((c0, s0)):
        for half in range(2):
            rows = pl.ds(16 * half + 8 * field, 8)
            fill_0(ref, 4 + 4 * half, rz[0, rows, :], rz[1, rows, :])
    level_0.setup(5, 10, 3, 2)
    level_0.start(5, 10, 6, 2, steps[0][1])
    level_0.sweep(level_0.va, level_0.vb, 6, 9, 4, 2, 2, steps[1], fresh=True)
    level_0.sweep(level_0.vb, level_0.va, 7, 8, 2, 2, 2, steps[2])

    @for_sides
    def send_coef(side, dw):
        for dn in (0, -1, 1):
            send(from_k + 1 - side, zs.at[0, pl.ds(32, 32)], k1c.at[1 - dw, 1 - dn], dw, dn, 32, 1 + side)

    def spread_1(ref, block, places):
        at_lane = lanes(16)
        low_half = at_lane < 64
        low_quarter = at_lane % 64 < 32
        for dx in places:
            for part in range(2):
                before, own, after = (block(dx, dz, part) for dz in (-1, 0, 1))
                near = jnp.where(low_quarter, before, after)
                outer = jnp.where(low_quarter, after, before)
                own_r, near_r, outer_r = (pltpu.roll(t, 64, 1) for t in (own, near, outer))
                at = 5 + 4 * dx + part
                for at, own_a, own_b, near_a, near_b, outer_a, outer_b in (
                    (at, own, own_r, near, near_r, outer, outer_r),
                    (at + 2, own_r, own, near_r, near, outer_r, outer),
                ):
                    centre = jnp.where(low_half, own_a, own_b)
                    ref[0, at] = jnp.where(at_lane < 32, near_a, jnp.where(at_lane < 96, centre, near_b))
                    ref[1, at] = jnp.where(low_half, outer_a, outer_b)

    def coef_block(dx, dz, part):
        if dx == 0:
            rows = pl.ds(32 + 16 * part, 16)
            return zs[0, rows, :] if dz == 0 else rz[(1 + dz) // 2, rows, :]
        return k1c[1 + dx, 1 + dz, pl.ds(16 * part, 16), :]

    spread_1(level_1.c, coef_block, (0,))
    rc2[REACH] = pairs_1(level_1.c)

    @for_sides
    def send_near(side, dw):
        send(from_near + 1 - side, rc2.at[REACH], rc2.at[REACH - dw], dw, 0, 8, 1 + side)

    receive_sides(from_c, 160)
    for field, ref in enumerate((c0, s0)):
        for side in range(2):
            rows = pl.ds(8 * field, 8)
            fill_0(ref, 12 * side, rcn[side, 0, rows, :], rcn[side, 1, rows, :])
    level_0.setup_below(1, 2)
    over_sides(1, 11, 4, lambda at: level_0.setup_at(at, 2))
    receive_sides(from_near, 8)

    @functools.partial(if_reach, 2)
    def send_two(side, sign):
        src = rc2.at[pl.ds(REACH - side, 2)] if side == 1 else rc2.at[pl.ds(REACH, 2)]
        dst = rc2.at[pl.ds(REACH - 3, 2)] if side == 1 else rc2.at[pl.ds(REACH + 2, 2)]
        send(from_two + 1 - side, src, dst, 2 * sign, 0, 16, sender_two + side)

    receive_sides(from_s, 96)
    over_sides(1, 11, 4, lambda at: level_0.start_at(at, 2, steps[0][1]))
    over_sides(2, 10, 4, lambda at: level_0.sweep_at(at, level_0.va, level_0.vb, 2, 2, steps[1], True))
    over_sides(3, 9, 4, lambda at: level_0.sweep_at(at, level_0.vb, level_0.va, 2, 2, steps[2], False))
    level_0.residual(level_0.va, level_0.vb, 4, 11, 4, 2)

    squeeze_1(restrict_0(level_0.vb), sk, 0)

    low_quarter = lanes(16) % 64 < 32
    first, second = sk[pl.ds(0, 16), :], sk[pl.ds(16, 16), :]
    sp[0] = jnp.where(low_quarter, pltpu.roll(first, 96, 1), second)
    sp[1] = jnp.where(low_quarter, first, pltpu.roll(second, 32, 1))

    @for_sides
    def send_source(side, dw):
        send(from_s1 + 1 - side, sk, k1x.at[1 - side], dw, 0, 32, 1 + side)
        for dn in (-1, 1):
            send(from_s1 + 1 - side, sp.at[(1 + dn) // 2], k1p.at[1 - side, (1 - dn) // 2], dw, dn, 16, 1 + side)

    for dn in (-1, 1):
        send(from_s1z, sk, k1z.at[(1 - dn) // 2], 0, dn, 32, 0)

    if_reach(2, lambda side, sign: receive(from_two + side, 16))

    @functools.partial(if_reach, 4)
    def send_four(side, sign):
        src = rc2.at[pl.ds(REACH - 3, 4)] if side == 1 else rc2.at[pl.ds(REACH, 4)]
        dst = rc2.at[pl.ds(REACH - 7, 4)] if side == 1 else rc2.at[pl.ds(REACH + 4, 4)]
        send(from_four + 1 - side, src, dst, 4 * sign, 0, 32, sender_four + side)

    for side in range(2):
        first = 9 if side == 0 else 4
        tiles = []
        for layer in range(3):
            sb0[side, pl.ds(32 * layer, 32), :] = level_0.va[0, first + layer]
            for part in range(2):
                tiles.append(level_0.va[1, first + layer, pl.ds(16 * part, 16), :])
        sb0[side, pl.ds(96, 16), :] = pack(tiles)

    def source_block(dx, dz, part):
        rows = pl.ds(16 * part, 16)
        return sk[rows, :] if dz == 0 else k1z[(1 + dz) // 2, rows, :]

    def spread_beside(ref):
        at_lane = lanes(16)
        low_half = at_lane < 64
        for side in range(2):
            for layer in range(4):
                own = k1x[side, pl.ds(16 * (layer % 2), 16), :]
                other = pltpu.roll(own, 64, 1)
                centre = jnp.where(low_half, own, other) if layer < 2 else jnp.where(low_half, other, own)
                before = pltpu.roll(k1p[side, 0], (LANES - 32 * layer) % LANES, 1)
                after = pltpu.roll(k1p[side, 1], (LANES + 96 - 32 * layer) % LANES, 1)
                ref[0, 1 + 8 * side + layer] = jnp.where(at_lane < 32, before, jnp.where(at_lane < 96, centre, after))

    receive_sides(from_k, 96)
    spread_1(level_1.c, coef_block, (-1, 1))

    @for_sides
    def send_coef_1(side, dw):
        send(from_c1b + 1 - side, level_1.c.at[0, 9 - 5 * side], level_1.c.at[0, 13 - 13 * side], dw, 0, 16, 1 + side)

    level_1.setup_below(2, 1)
    over_sides(2, 10, 2, lambda at: level_1.setup_at(at, 1))
    over_layers(4, 9, 6, lambda at: level_1.setup_at(at, 2))

    receive(from_s1z, 64)
    spread_1(level_1.s, source_block, (0,))
    receive_sides(from_s1, 64)
    spread_beside(level_1.s)
    level_1.start(2, 11, 10, 1, steps[0][1])
    over_layers(5, 8, 4, lambda at: level_1.start_outer(at, steps[0][1]))
    over_sides(3, 9, 2, lambda at: level_1.sweep_at(at, level_1.va, level_1.vb, 1, 1, steps[1], True))
    over_layers(5, 8, 4, lambda at: level_1.sweep_at(at, level_1.va, level_1.vb, 2, 1, steps[1], True))
    level_1.sweep(level_1.vb, level_1.va, 4, 9, 6, 1, 1, steps[2])
    level_1.residual(level_1.va, level_1.vb, 5, 8, 4, 1)

    value = pairs_1(level_1.vb)
    s2m[...] = value
    rs2[REACH] = value
    if_reach(4, lambda side, sign: receive(from_four + side, 32))
    for_far(1, lambda slot, dw: send(from_s2 + 2 * REACH - slot, s2m, rs2.at[2 * REACH - slot], dw, 0, 8, sender_far + slot))

    @functools.partial(if_reach, REACH)
    def send_eight(side, sign):
        send(from_eight + 1 - side, rc2.at[REACH], rc2.at[REACH - sign * REACH], REACH * sign, 0, 8, sender_eight + side)

    @for_sides
    def send_iterate_1(side, dw):
        send(from_x1 + 1 - side, level_1.va.at[0, pl.ds(5, 4)], rx1.at[1 - side], dw, 0, 64, 3 + side)

    for side in range(2):
        @pl.when(reach[side] >= 2)
        def send_next_1():
            layer = level_1.va.at[0, 5 + 3 * side]
            send(from_x1b + 1 - side, layer, rx1b.at[1 - side], 4 * side - 2, 0, 16, 5 + side)

    receive_sides(from_c1b, 16)
    level_1.setup_below(1, 1)
    over_sides(1, 12, 1, lambda at: level_1.setup_at(at, 1))

    def spread_2(ref, blocks):
        for block in range(2 * REACH + 1):
            packed = blocks[block]
            ref[0, 2 * block] = jnp.where(odd_8, pltpu.roll(packed, 1, 1), packed)
            ref[0, 2 * block + 1] = jnp.where(odd_8, packed, pltpu.roll(packed, LANES - 1, 1))

    def restrict_2(ref, at):
        total = ref[0, 2 * at + 2] + ref[0, 2 * at + 3]
        odd_row = lax.broadcasted_iota(jnp.int32, (8, LANES), 0) % 2 == 1
        total = total + jnp.where(odd_row, pltpu.roll(total, 1, 0), pltpu.roll(total, 7, 0))
        second = lanes(8) % 4 >= 2
        total = total + jnp.where(second, pltpu.roll(total, 2, 1), pltpu.roll(total, LANES - 2, 1))
        return 0.125 * total

    if_reach(REACH, lambda side, sign: receive(from_eight + side, 8))
    spread_2(level_2.c, rc2)
    level_2.setup(1, 32, 8, 1)
    for at in range(15):
        level_3.c[0, at] = restrict_2(level_2.c, at)
    level_3.setup(1, 13, 13, 1)

    receive_far(from_s2)

    @for_sides
    def send_iterate_0(side, dw):
        send(from_x0 + 1 - side, sb0.at[1 - side], hx0.at[1 - side], dw, 0, 112, 1 + side)

    spread_2(level_2.s, rs2)
    level_2.start(1, 32, 32, 1, steps[0][1])
    level_2.sweep(level_2.va, level_2.vb, 2, 31, 15, 1, 1, steps[1], fresh=True)
    level_2.sweep(level_2.vb, level_2.va, 3, 30, 14, 1, 1, steps[2])
    level_2.residual(level_2.va, level_2.vb, 4, 29, 13, 1)

    for at in range(1, 14):
        level_3.s[0, at] = restrict_2(level_2.vb, at)
    coarse = cheb(4)
    level_3.start(1, 13, 13, 1, coarse[0][1])
    level_3.sweep(level_3.va, level_3.vb, 2, 12, 11, 1, 1, coarse[1], fresh=True)
    level_3.sweep(level_3.vb, level_3.va, 3, 11, 9, 1, 1, coarse[2])
    level_3.sweep(level_3.va, level_3.vb, 4, 10, 7, 1, 1, coarse[3])

    for at in range(10, 24):
        level_2.vb[0, at] = level_2.va[0, at] + level_3.vb[0, (at - 2) // 2]
    level_2.sweep(level_2.vb, level_2.va, 11, 22, 12, 1, 1, steps[0], fresh=True)
    level_2.sweep(level_2.va, level_2.vb, 12, 21, 10, 1, 1, steps[1])
    level_2.sweep(level_2.vb, level_2.va, 13, 20, 8, 1, 1, steps[2])

    for at in range(8):
        value = level_2.va[0, 13 + at]
        for part in range(2):
            p1[at, pl.ds(part, 8, stride=2), :] = value
    receive_sides(from_x1, 64)
    for side in range(2):
        pl.when(reach[side] >= 2)(functools.partial(receive, from_x1b + side, 16))
    for at in range(14):
        if 5 <= at <= 8:
            before = level_1.va[0, at]
        else:
            beside = (rx1b[0] if at == 0 else rx1[0, at - 1] if at < 5 else rx1[1, at - 9] if at < 13 else rx1b[1])
            before = beside * level_1.inside(at)
        level_1.vb[0, at] = before + p1[(at + 1) // 2]
    for side in range(2):
        pl.when(has[side])(functools.partial(sends_done, 3 + side))
        pl.when(reach[side] >= 2)(functools.partial(sends_done, 5 + side))
    level_1.sweep(level_1.vb, level_1.va, 1, 12, 12, 1, 1, steps[0], fresh=True)
    level_1.sweep(level_1.va, level_1.vb, 2, 11, 10, 1, 1, steps[1])
    level_1.sweep(level_1.vb, level_1.va, 3, 10, 8, 1, 1, steps[2])

    fine_lane = lanes(16) // 2
    for at in range(8):
        value = level_1.va[0, 3 + at]
        for k in range(2):
            fine = jnp.take_along_axis(value, (fine_lane + (32 if k == 0 else 96)) % LANES, axis=1)
            for part in range(2):
                p0[k, at, pl.ds(part, 16, stride=2), :] = fine
    receive_sides(from_x0, 112)
    for side in range(2):
        packed = hx0[side, pl.ds(96, 16), :]
        for layer in range(3):
            at = (1 if side == 0 else 12) + layer
            inside = level_0.inside(at)
            coarse_at = (at - 4) // 2 + 2
            level_0.vb[0, at] = hx0[side, pl.ds(32 * layer, 32), :] * inside + p0[0, coarse_at]
            for part in range(2):
                rows = pl.ds(16 * part, 16)
                level_0.vb[1, at, rows, :] = (
                    unpack(packed, 2 * layer + part) * (level_0.lane_mask[1][:16] * inside) + p0[1, coarse_at, rows, :]
                )

    def correct(at):
        for k in range(2):
            level_0.vb[k, at] = level_0.va[k, at] + p0[k, at // 2]

    over_layers(4, 11, 4, correct)
    level_0.sweep(level_0.vb, level_0.va, 2, 13, 4, 2, 2, steps[0], fresh=True)
    level_0.sweep(level_0.va, level_0.vb, 3, 12, 5, 2, 2, steps[1])
    level_0.finish(level_0.vb, level_0.va, kept, added, 4, 11, 4, steps[2])

    sends_done(0)
    for_sides(lambda side, dw: sends_done(1 + side))
    if_reach(2, lambda side, sign: sends_done(sender_two + side))
    if_reach(4, lambda side, sign: sends_done(sender_four + side))
    if_reach(REACH, lambda side, sign: sends_done(sender_eight + side))
    for_far(1, lambda slot, dw: ruled(8, 0, sender_far + slot).wait_send())


def per_device(right_side, conductivity, wide, narrow):
    brick = (8, 32, LANES)
    scratch = []
    for shape in LEVEL_SHAPES:
        scratch += [pltpu.VMEM(shape, F32)] * LEVEL_FIELDS
    shapes = [
        (2, 64, LANES), (2, 64, LANES), (2, 2, 16, LANES), (3, 3, 32, LANES),
        (32, LANES), (2, 16, LANES), (2, 32, LANES), (2, 2, 16, LANES), (2, 32, LANES),
        (2 * REACH + 1, 8, LANES), (8, LANES), (2 * REACH + 1, 8, LANES),
        (2, 4, 16, LANES), (2, 16, LANES),
        (2, 112, LANES), (2, 112, LANES),
        (8, 16, LANES), (2, 8, 32, LANES),
        (RULER, LANES),
    ]
    scratch += [pltpu.VMEM(shape, F32) for shape in shapes]
    scratch += [pltpu.SemaphoreType.DMA((2,)), pltpu.SemaphoreType.DMA((SENDERS,)), pltpu.SemaphoreType.DMA((GROUPS,))]
    kept, added = pl.pallas_call(
        functools.partial(kernel, wide, narrow),
        out_shape=[jax.ShapeDtypeStruct(brick, F32)] * 2,
        in_specs=[pl.BlockSpec(memory_space=pltpu.HBM)] * 2,
        out_specs=[pl.BlockSpec(memory_space=pltpu.VMEM)] * 2,
        scratch_shapes=scratch,
        compiler_params=pltpu.CompilerParams(
            collective_id=0, has_side_effects=True, vmem_limit_bytes=32 * 1024 * 1024
        ),
    )(pltpu.with_memory_space_constraint(right_side, pltpu.HBM), pltpu.with_memory_space_constraint(conductivity, pltpu.HBM))
    return kept + added


def solution(mesh):
    spec = P("wide", None, "narrow")
    body = functools.partial(per_device, wide=mesh.shape["wide"], narrow=mesh.shape["narrow"])
    return jax.shard_map(body, mesh=mesh, in_specs=(spec, spec), out_specs=spec, check_vma=False)
```

```python
import functools

import jax
import jax.numpy as jnp
from jax import lax
from jax.experimental import pallas as pl
from jax.experimental.pallas import tpu as pltpu
from jax.sharding import PartitionSpec as P

CENTER = 1.125
HALF = 0.875
LANES = 128
REACH = 8
F32 = jnp.float32
MESH_ID = pl.DeviceIdType.MESH


def cheb(sweeps):
    sigma = CENTER / HALF
    steps = [(0.0, 1.0 / CENTER)]
    ratio = 1.0 / sigma
    for _ in range(sweeps - 1):
        ratio_next = 1.0 / (2.0 * sigma - ratio)
        steps.append((ratio_next * ratio, 2.0 * ratio_next / HALF))
        ratio = ratio_next
    return steps


def over_sides(first, second, count, body):
    def block(side, carry):
        for at in range(count):
            body(first + side * (second - first) + at)
        return carry

    lax.fori_loop(0, 2, block, 0)


def over_layers(low, high, unroll, body):
    count = high - low + 1
    if count == unroll:
        for at in range(low, high + 1):
            body(at)
        return

    def block(step, carry):
        for at in range(unroll):
            body(low + step * unroll + at)
        return carry

    lax.fori_loop(0, count // unroll, block, 0)


class Level:
    def __init__(self, refs, scale, rows, row_step, lane_step, base, extent, lane_mask):
        self.c, self.s, self.cx, self.cy, self.cz, self.iv, self.dg, self.va, self.vb = refs
        self.half = 0.5 * scale
        self.rows, self.row_step, self.lane_step = rows, row_step, lane_step
        self.base, self.extent, self.lane_mask = base, extent, lane_mask

    def inside(self, at):
        where_x = self.base + at
        return jnp.where((where_x >= 0) & (where_x < self.extent), 1.0, 0.0).astype(F32)

    def lane(self):
        return lax.broadcasted_iota(jnp.int32, (self.rows, LANES), 1)

    def row(self):
        return lax.broadcasted_iota(jnp.int32, (self.rows, LANES), 0)

    def y_up(self, tile):
        return pltpu.roll(tile, self.rows - self.row_step, 0)

    def y_down(self, tile):
        return pltpu.roll(tile, self.row_step, 0)

    def turned(self, tiles, shift, edge, count):
        out = [pltpu.roll(t, shift, 1) for t in tiles]
        if len(tiles) == 1:
            return out
        at_edge = self.lane() == edge
        return [jnp.where(at_edge, out[1 - k], out[k]) for k in range(count)]

    def z_up(self, tiles, count):
        return self.turned(tiles, LANES - self.lane_step, LANES - 1, count)

    def z_down(self, tiles, count):
        return self.turned(tiles, self.lane_step, 0, count)

    def masked(self, at, tiles):
        keep = self.inside(at) * self.half
        out = []
        for k in range(tiles):
            mask = self.lane_mask[k]
            out.append(self.c[k, at] * (keep if mask is None else mask * keep))
        return out

    def setup_below(self, low, tiles):
        first, second = self.masked(low - 1, tiles), self.masked(low, tiles)
        for k in range(tiles):
            self.cx[k, low - 1] = first[k] + second[k]

    def setup_at(self, at, tiles):
        before, here, after = self.masked(at - 1, tiles), self.masked(at, tiles), self.masked(at + 1, tiles)
        inside = self.inside(at)
        top = self.row() >= self.rows - self.row_step
        bottom = self.row() < self.row_step
        z_up, z_down = self.z_up(here, tiles), self.z_down(here, tiles)
        for k in range(tiles):
            own = here[k]
            x_low = before[k] + own
            x_high = own + after[k]
            y_low = own + jnp.where(bottom, 0.0, self.y_down(own))
            y_high = own + jnp.where(top, 0.0, self.y_up(own))
            z_low = own + z_down[k]
            z_high = own + z_up[k]
            diagonal = x_low + x_high + y_low + y_high + z_low + z_high
            keep = inside if self.lane_mask[k] is None else self.lane_mask[k] * inside
            self.cx[k, at] = x_high
            self.cy[k, at] = jnp.where(top, 0.0, y_high)
            self.cz[k, at] = z_high
            if k == 0:
                self.dg[0, at] = diagonal
            self.iv[k, at] = jnp.where(jnp.full_like(own, 0.0) + keep > 0.5, 1.0 / diagonal, 0.0)

    def setup(self, low, high, unroll, tiles):
        self.setup_below(low, tiles)
        over_layers(low, high, unroll, lambda at: self.setup_at(at, tiles))

    def start_at(self, at, tiles, beta):
        for k in range(tiles):
            self.va[k, at] = self.s[k, at] * self.iv[k, at] * beta

    def start_outer(self, at, beta):
        self.va[1, at] = self.s[1, at] * self.iv[1, at] * beta

    def start(self, low, high, unroll, tiles, beta):
        over_layers(low, high, unroll, lambda at: self.start_at(at, tiles, beta))

    def around(self, field, at, tiles, count):
        here = [field[k, at] for k in range(tiles)]
        cz = [self.cz[k, at] for k in range(tiles)]
        z_up = self.z_up(here, count)
        z_down = self.z_down([cz[k] * here[k] for k in range(tiles)], count)
        sums = []
        for k in range(count):
            cy = self.cy[k, at]
            total = self.cx[k, at] * field[k, at + 1] + self.cx[k, at - 1] * field[k, at - 1]
            total = total + (cy * self.y_up(here[k]) + self.y_down(cy * here[k]))
            total = total + (cz[k] * z_up[k] + z_down[k])
            sums.append(total + self.s[k, at])
        return here, sums

    def sweep_at(self, at, field, result, tiles, count, step, fresh):
        alpha, beta = step
        here, sums = self.around(field, at, tiles, count)
        for k in range(count):
            kept = (1.0 + alpha - beta) * here[k]
            if not fresh:
                kept = kept - alpha * result[k, at]
            result[k, at] = kept + (beta * self.iv[k, at]) * sums[k]

    def sweep(self, field, result, low, high, unroll, tiles, count, step, fresh=False):
        over_layers(low, high, unroll, lambda at: self.sweep_at(at, field, result, tiles, count, step, fresh))

    def residual_at(self, at, field, result, tiles):
        here, sums = self.around(field, at, tiles, 1)
        result[0, at] = sums[0] - self.dg[0, at] * here[0]

    def residual(self, field, result, low, high, unroll, tiles):
        over_layers(low, high, unroll, lambda at: self.residual_at(at, field, result, tiles))

    def finish(self, field, older, kept_out, added_out, low, high, unroll, step):
        alpha, beta = step

        def body(at):
            here, sums = self.around(field, at, 2, 1)
            kept_out[at - low] = (1.0 + alpha - beta) * here[0] - alpha * older[0, at]
            added_out[at - low] = (beta * self.iv[0, at]) * sums[0]

        over_layers(low, high, unroll, body)


LEVEL_FIELDS = 9
LEVEL_SHAPES = ((2, 16, 32, LANES), (2, 14, 16, LANES), (1, 34, 8, LANES), (1, 15, 8, LANES))
RULER = 1024
SENDERS = 13 + 2 * REACH + 1
GROUPS = 28 + 2 * REACH + 1


def kernel(wide, narrow, rhs, coef, kept, added, *scratch):
    scratch = list(scratch)
    level_refs = []
    for _ in range(4):
        level_refs.append(scratch[:LEVEL_FIELDS])
        scratch = scratch[LEVEL_FIELDS:]
    (zs, rz, rcn, k1c, sk, sp, k1x, k1p, k1z, rc2, s2m, rs2, rx1, rx1b, sb0, hx0, p1, p0, ruler,
     local_sem, send_sem, recv_sem) = scratch
    me_w = lax.axis_index("wide")
    me_n = lax.axis_index("narrow")

    def there(dw, dn):
        return (lax.rem(me_w + (dw + wide), wide), lax.rem(me_n + (dn + narrow), narrow))

    has = (me_w > 0, me_w < wide - 1)
    reach = (jnp.minimum(me_w, REACH), jnp.minimum(wide - 1 - me_w, REACH))

    def for_far(first, body):
        for side in range(2):
            sign = 2 * side - 1

            def step(k, carry):
                body(REACH + sign * k, sign * k)
                return carry

            lax.fori_loop(first, reach[side] + 1, step, 0)

    def for_sides(body):
        for side in range(2):
            pl.when(has[side])(functools.partial(body, side, 2 * side - 1))

    @pl.when((me_w < REACH) | (me_w >= wide - REACH))
    def clear():
        def zero(ref):
            ref[...] = jnp.zeros(ref.shape, F32)

        for ref in (rcn, rx1, rx1b, hx0, rc2, rs2, k1x, k1p):
            zero(ref)
        for side in range(2):
            zero(k1c.at[2 * side])
            for ref in level_refs[0][:2]:
                zero(ref.at[0, pl.ds(12 * side, 4)])
            zero(level_refs[1][0].at[0, 13 * side])

    def if_reach(least, body):
        for side in range(2):
            pl.when(reach[side] >= least)(functools.partial(body, side, 2 * side - 1))

    barrier = pltpu.get_barrier_semaphore()

    def greet(dw, dn):
        pl.semaphore_signal(barrier, inc=1, device_id=there(dw, dn), device_id_type=MESH_ID)

    @for_sides
    def greet_side(side, dw):
        for dn in (0, -1, 1):
            greet(dw, dn)

    greet(0, -1)
    greet(0, 1)

    c0, s0 = level_refs[0][0], level_refs[0][1]
    load_c = pltpu.make_async_copy(coef, c0.at[0, pl.ds(4, 8)], local_sem.at[0])
    load_s = pltpu.make_async_copy(rhs, s0.at[0, pl.ds(4, 8)], local_sem.at[1])
    load_c.start()
    load_s.start()
    greeted = 2 + jnp.where(has[0], 3, 0) + jnp.where(has[1], 3, 0)

    left = jnp.where(me_n > 0, 1.0, 0.0).astype(F32)
    right = jnp.where(me_n < narrow - 1, 1.0, 0.0).astype(F32)

    def lanes(rows):
        return lax.broadcasted_iota(jnp.int32, (rows, LANES), 1)

    def edges(rows, until, low, since, high):
        at = lanes(rows)
        return jnp.where(at < until, low, jnp.where(at >= since, high, 0.0))

    def centred(rows):
        at = lanes(rows)
        return jnp.where((at >= 32) & (at < 96), 1.0, edges(rows, 32, left, 96, right))

    level_0 = Level(level_refs[0], 1.0, 32, 1, 1, 8 * me_w - 4, 8 * wide, [None, edges(32, 8, right, 120, left)])
    level_1 = Level(
        level_refs[1], 0.25, 16, 1, 1, 4 * me_w - 5, 4 * wide, [centred(16), edges(16, 32, right, 96, left)]
    )
    level_2 = Level(level_refs[2], 0.0625, 8, 1, 2, 2 * me_w - 16, 2 * wide, [centred(8)])
    level_3 = Level(level_refs[3], 0.015625, 8, 2, 4, me_w - 7, wide, [centred(8)])

    sent = [0] * SENDERS

    def send(group, src, dst, dw, dn, rows, sender):
        if isinstance(sender, int):
            sent[sender] += rows
        pltpu.make_async_remote_copy(
            src_ref=src, dst_ref=dst, send_sem=send_sem.at[sender], recv_sem=recv_sem.at[group],
            device_id=there(dw, dn), device_id_type=MESH_ID,
        ).start()

    def ruled(rows, group, sender):
        span = ruler.at[pl.ds(0, rows)]
        return pltpu.make_async_remote_copy(
            src_ref=span, dst_ref=span, send_sem=send_sem.at[sender], recv_sem=recv_sem.at[group],
            device_id=there(0, 1), device_id_type=MESH_ID,
        )

    def receive(group, rows):
        ruled(rows, group, 0).wait_recv()

    def receive_sides(group, rows):
        for_sides(lambda side, dw: receive(group + side, rows))

    def receive_far(group):
        for_far(1, lambda slot, dw: receive(group + slot, 8))

    def sends_done(sender):
        ruled(sent[sender], 0, sender).wait_send()

    from_z, from_s1z = 0, 1
    from_c, from_s, from_k, from_s1, from_c1b, from_x0, from_x1, from_x1b = range(2, 18, 2)
    from_s_next = 26
    from_near, from_two, from_four, from_eight = range(18, 26, 2)
    from_s2 = 28
    sender_two, sender_four, sender_eight, sender_far = 7, 9, 11, 13

    def pack(tiles):
        rows = tiles[0].shape[0]
        group = lanes(rows) // 16
        packed = jnp.zeros((rows, LANES), F32)
        for at, tile in enumerate(tiles):
            packed = jnp.where(group == at, pltpu.roll(tile, (16 * at + 8) % LANES, 1), packed)
        return packed

    def unpack(packed, at):
        return pltpu.roll(packed, (2 * LANES - (16 * at + 8)) % LANES, 1)

    def pack_side(ref, half, side):
        group = lanes(8) // 8
        packed = None
        for layer in range(4):
            for part in range(4):
                at = 4 * layer + part
                tile = ref[0, 4 + 4 * half + layer, pl.ds(8 * part, 8), :]
                tile = pltpu.roll(tile, (8 * at + 8 * side) % LANES, 1)
                packed = tile if at == 0 else jnp.where(group == at, tile, packed)
        return packed

    def restrict_0(ref):
        out = []
        for layer in range(4):
            total = None
            for dx in range(2):
                for dy in range(2):
                    term = ref[0, 4 + 2 * layer + dx, pl.ds(dy, 16, stride=2), :]
                    total = term if total is None else total + term
            total = total + pltpu.roll(total, LANES - 1, 1)
            out.append(0.125 * jnp.take_along_axis(total, (2 * lanes(16) + 64) % LANES, axis=1))
        return out

    odd_8 = lanes(8) % 2 == 1

    def pairs_1(ref):
        out = []
        for layer in range(2):
            total = None
            for dx in range(2):
                for dy in range(2):
                    term = ref[0, 5 + 2 * layer + dx, pl.ds(dy, 8, stride=2), :]
                    total = term if total is None else total + term
            total = total + jnp.where(odd_8, pltpu.roll(total, 1, 1), pltpu.roll(total, LANES - 1, 1))
            out.append(0.125 * total)
        return jnp.where(odd_8, out[1], out[0])

    def squeeze_1(layers, ref, row):
        for part in range(2):
            ref[pl.ds(row + 16 * part, 16), :] = jnp.where(lanes(16) < 64, layers[part], layers[part + 2])

    pl.semaphore_wait(barrier, greeted)

    @for_sides
    def send_faces(side, dw):
        send(from_c + 1 - side, coef.at[pl.ds(4 * side, 4)], c0.at[0, pl.ds(12 - 12 * side, 4)], dw, 0, 128, 1 + side)
        send(from_s + 1 - side, rhs.at[7 * side], s0.at[0, 12 - 9 * side], dw, 0, 32, 1 + side)

    load_c.wait()
    own_c1 = restrict_0(c0)
    for side in range(2):
        squeeze_1(own_c1, zs.at[side], 32)
        for half in range(2):
            zs[side, pl.ds(16 * half, 8), :] = pack_side(c0, half, side)
    load_s.wait()
    for side in range(2):
        for half in range(2):
            zs[side, pl.ds(16 * half + 8, 8), :] = pack_side(s0, half, side)

    send(from_z, zs.at[0], rz.at[1], 0, -1, 64, 0)
    send(from_z, zs.at[1], rz.at[0], 0, 1, 64, 0)

    @for_sides
    def send_corners(side, dw):
        for dn in (-1, 1):
            span = zs.at[(1 + dn) // 2, pl.ds(16 * side, 16)]
            send(from_c + 1 - side, span, rcn.at[1 - side, (1 - dn) // 2], dw, dn, 16, 1 + side)
        src = rhs.at[pl.ds(1 + 4 * side, 2)]
        send(from_s_next + 1 - side, src, s0.at[0, pl.ds(13 - 12 * side, 2)], dw, 0, 64, 1 + side)

    def fill_0(ref, first, from_left, from_right):
        low = lanes(8) < 64
        for layer in range(4):
            for part in range(4):
                at = 4 * layer + part
                ref[1, first + layer, pl.ds(8 * part, 8), :] = jnp.where(
                    low, pltpu.roll(from_right, (LANES - 8 * at) % LANES, 1), pltpu.roll(from_left, (120 - 8 * at) % LANES, 1)
                )

    steps = cheb(3)
    receive(from_z, 128)
    for field, ref in enumerate((c0, s0)):
        for half in range(2):
            rows = pl.ds(16 * half + 8 * field, 8)
            fill_0(ref, 4 + 4 * half, rz[0, rows, :], rz[1, rows, :])
    level_0.setup(5, 10, 3, 2)
    level_0.start(5, 10, 6, 2, steps[0][1])
    level_0.sweep(level_0.va, level_0.vb, 6, 9, 4, 2, 2, steps[1], fresh=True)
    level_0.sweep(level_0.vb, level_0.va, 7, 8, 2, 2, 2, steps[2])

    def spread_1(ref, block, places):
        at_lane = lanes(16)
        low_half = at_lane < 64
        low_quarter = at_lane % 64 < 32
        for dx in places:
            for part in range(2):
                before, own, after = (block(dx, dz, part) for dz in (-1, 0, 1))
                near = jnp.where(low_quarter, before, after)
                outer = jnp.where(low_quarter, after, before)
                own_r, near_r, outer_r = (pltpu.roll(t, 64, 1) for t in (own, near, outer))
                at = 5 + 4 * dx + part
                for at, own_a, own_b, near_a, near_b, outer_a, outer_b in (
                    (at, own, own_r, near, near_r, outer, outer_r),
                    (at + 2, own_r, own, near_r, near, outer_r, outer),
                ):
                    centre = jnp.where(low_half, own_a, own_b)
                    ref[0, at] = jnp.where(at_lane < 32, near_a, jnp.where(at_lane < 96, centre, near_b))
                    ref[1, at] = jnp.where(low_half, outer_a, outer_b)

    def coef_block(dx, dz, part):
        if dx == 0:
            rows = pl.ds(32 + 16 * part, 16)
            return zs[0, rows, :] if dz == 0 else rz[(1 + dz) // 2, rows, :]
        return k1c[1 + dx, 1 + dz, pl.ds(16 * part, 16), :]

    spread_1(level_1.c, coef_block, (0,))
    rc2[REACH] = pairs_1(level_1.c)

    @for_sides
    def send_near(side, dw):
        send(from_near + 1 - side, rc2.at[REACH], rc2.at[REACH - dw], dw, 0, 8, 1 + side)

    @for_sides
    def send_coef(side, dw):
        for dn in (0, -1, 1):
            send(from_k + 1 - side, zs.at[0, pl.ds(32, 32)], k1c.at[1 - dw, 1 - dn], dw, dn, 32, 1 + side)

    receive_sides(from_c, 160)
    for field, ref in enumerate((c0, s0)):
        for side in range(2):
            rows = pl.ds(8 * field, 8)
            fill_0(ref, 12 * side, rcn[side, 0, rows, :], rcn[side, 1, rows, :])
    level_0.setup_below(1, 2)
    over_sides(1, 11, 4, lambda at: level_0.setup_at(at, 2))
    receive_sides(from_s, 32)
    sweep_a = (level_0.va, level_0.vb, 2, 2, steps[1], True)
    sweep_b = (level_0.vb, level_0.va, 2, 2, steps[2], False)
    over_sides(3, 11, 2, lambda at: level_0.start_at(at, 2, steps[0][1]))
    over_sides(4, 10, 2, lambda at: level_0.sweep_at(at, *sweep_a))
    over_sides(5, 9, 2, lambda at: level_0.sweep_at(at, *sweep_b))
    level_0.residual(level_0.va, level_0.vb, 6, 9, 4, 2)
    receive_sides(from_near, 8)

    @functools.partial(if_reach, 2)
    def send_two(side, sign):
        src = rc2.at[pl.ds(REACH - side, 2)] if side == 1 else rc2.at[pl.ds(REACH, 2)]
        dst = rc2.at[pl.ds(REACH - 3, 2)] if side == 1 else rc2.at[pl.ds(REACH + 2, 2)]
        send(from_two + 1 - side, src, dst, 2 * sign, 0, 16, sender_two + side)

    receive_sides(from_s_next, 64)
    over_sides(1, 13, 2, lambda at: level_0.start_at(at, 2, steps[0][1]))
    over_sides(2, 12, 2, lambda at: level_0.sweep_at(at, *sweep_a))
    over_sides(3, 11, 2, lambda at: level_0.sweep_at(at, *sweep_b))
    over_sides(4, 10, 2, lambda at: level_0.residual_at(at, level_0.va, level_0.vb, 2))

    squeeze_1(restrict_0(level_0.vb), sk, 0)

    low_quarter = lanes(16) % 64 < 32
    first, second = sk[pl.ds(0, 16), :], sk[pl.ds(16, 16), :]
    sp[0] = jnp.where(low_quarter, pltpu.roll(first, 96, 1), second)
    sp[1] = jnp.where(low_quarter, first, pltpu.roll(second, 32, 1))

    @for_sides
    def send_source(side, dw):
        send(from_s1 + 1 - side, sk, k1x.at[1 - side], dw, 0, 32, 1 + side)
        for dn in (-1, 1):
            send(from_s1 + 1 - side, sp.at[(1 + dn) // 2], k1p.at[1 - side, (1 - dn) // 2], dw, dn, 16, 1 + side)

    for dn in (-1, 1):
        send(from_s1z, sk, k1z.at[(1 - dn) // 2], 0, dn, 32, 0)

    if_reach(2, lambda side, sign: receive(from_two + side, 16))

    @functools.partial(if_reach, 4)
    def send_four(side, sign):
        src = rc2.at[pl.ds(REACH - 3, 4)] if side == 1 else rc2.at[pl.ds(REACH, 4)]
        dst = rc2.at[pl.ds(REACH - 7, 4)] if side == 1 else rc2.at[pl.ds(REACH + 4, 4)]
        send(from_four + 1 - side, src, dst, 4 * sign, 0, 32, sender_four + side)

    for side in range(2):
        first = 9 if side == 0 else 5
        tiles = []
        for layer in range(2):
            sb0[side, pl.ds(32 * layer, 32), :] = level_0.va[0, first + layer]
            for part in range(4):
                tiles.append(level_0.va[1, first + layer, pl.ds(8 * part, 8), :])
        sb0[side, pl.ds(64, 8), :] = pack(tiles)

    @for_sides
    def send_iterate_0(side, dw):
        send(from_x0 + 1 - side, sb0.at[1 - side], hx0.at[1 - side], dw, 0, 72, 1 + side)

    def source_block(dx, dz, part):
        rows = pl.ds(16 * part, 16)
        return sk[rows, :] if dz == 0 else k1z[(1 + dz) // 2, rows, :]

    def spread_beside(ref):
        at_lane = lanes(16)
        low_half = at_lane < 64
        for side in range(2):
            for layer in range(4):
                own = k1x[side, pl.ds(16 * (layer % 2), 16), :]
                other = pltpu.roll(own, 64, 1)
                centre = jnp.where(low_half, own, other) if layer < 2 else jnp.where(low_half, other, own)
                before = pltpu.roll(k1p[side, 0], (LANES - 32 * layer) % LANES, 1)
                after = pltpu.roll(k1p[side, 1], (LANES + 96 - 32 * layer) % LANES, 1)
                ref[0, 1 + 8 * side + layer] = jnp.where(at_lane < 32, before, jnp.where(at_lane < 96, centre, after))

    receive_sides(from_k, 96)
    spread_1(level_1.c, coef_block, (-1, 1))

    @for_sides
    def send_coef_1(side, dw):
        send(from_c1b + 1 - side, level_1.c.at[0, 9 - 5 * side], level_1.c.at[0, 13 - 13 * side], dw, 0, 16, 1 + side)

    level_1.setup_below(2, 1)
    over_sides(2, 10, 2, lambda at: level_1.setup_at(at, 1))
    over_layers(4, 9, 6, lambda at: level_1.setup_at(at, 2))

    receive(from_s1z, 64)
    spread_1(level_1.s, source_block, (0,))
    receive_sides(from_s1, 64)
    spread_beside(level_1.s)
    level_1.start(2, 11, 10, 1, steps[0][1])
    over_layers(5, 8, 4, lambda at: level_1.start_outer(at, steps[0][1]))
    over_sides(3, 9, 2, lambda at: level_1.sweep_at(at, level_1.va, level_1.vb, 1, 1, steps[1], True))
    over_layers(5, 8, 4, lambda at: level_1.sweep_at(at, level_1.va, level_1.vb, 2, 1, steps[1], True))
    level_1.sweep(level_1.vb, level_1.va, 4, 9, 6, 1, 1, steps[2])
    level_1.residual(level_1.va, level_1.vb, 5, 8, 4, 1)

    value = pairs_1(level_1.vb)
    s2m[...] = value
    rs2[REACH] = value
    if_reach(4, lambda side, sign: receive(from_four + side, 32))
    for_far(1, lambda slot, dw: send(from_s2 + 2 * REACH - slot, s2m, rs2.at[2 * REACH - slot], dw, 0, 8, sender_far + slot))

    @functools.partial(if_reach, REACH)
    def send_eight(side, sign):
        send(from_eight + 1 - side, rc2.at[REACH], rc2.at[REACH - sign * REACH], REACH * sign, 0, 8, sender_eight + side)

    @for_sides
    def send_iterate_1(side, dw):
        send(from_x1 + 1 - side, level_1.va.at[0, pl.ds(6 - side, 3)], rx1.at[1 - side], dw, 0, 48, 3 + side)

    for side in range(2):
        @pl.when(reach[side] >= 2)
        def send_next_1():
            layer = level_1.va.at[0, 5 + 3 * side]
            send(from_x1b + 1 - side, layer, rx1b.at[1 - side], 4 * side - 2, 0, 16, 5 + side)

    receive_sides(from_c1b, 16)
    level_1.setup_below(1, 1)
    over_sides(1, 12, 1, lambda at: level_1.setup_at(at, 1))

    def spread_2(ref, blocks):
        for block in range(2 * REACH + 1):
            packed = blocks[block]
            ref[0, 2 * block] = jnp.where(odd_8, pltpu.roll(packed, 1, 1), packed)
            ref[0, 2 * block + 1] = jnp.where(odd_8, packed, pltpu.roll(packed, LANES - 1, 1))

    def restrict_2(ref, at):
        total = ref[0, 2 * at + 2] + ref[0, 2 * at + 3]
        odd_row = lax.broadcasted_iota(jnp.int32, (8, LANES), 0) % 2 == 1
        total = total + jnp.where(odd_row, pltpu.roll(total, 1, 0), pltpu.roll(total, 7, 0))
        second = lanes(8) % 4 >= 2
        total = total + jnp.where(second, pltpu.roll(total, 2, 1), pltpu.roll(total, LANES - 2, 1))
        return 0.125 * total

    if_reach(REACH, lambda side, sign: receive(from_eight + side, 8))
    spread_2(level_2.c, rc2)
    level_2.setup(1, 32, 8, 1)
    for at in range(15):
        level_3.c[0, at] = restrict_2(level_2.c, at)
    level_3.setup(1, 13, 13, 1)

    receive_far(from_s2)
    spread_2(level_2.s, rs2)
    level_2.start(1, 32, 32, 1, steps[0][1])
    level_2.sweep(level_2.va, level_2.vb, 2, 31, 15, 1, 1, steps[1], fresh=True)
    level_2.sweep(level_2.vb, level_2.va, 3, 30, 14, 1, 1, steps[2])
    level_2.residual(level_2.va, level_2.vb, 4, 29, 13, 1)

    for at in range(1, 14):
        level_3.s[0, at] = restrict_2(level_2.vb, at)
    coarse = cheb(4)
    level_3.start(1, 13, 13, 1, coarse[0][1])
    level_3.sweep(level_3.va, level_3.vb, 2, 12, 11, 1, 1, coarse[1], fresh=True)
    level_3.sweep(level_3.vb, level_3.va, 3, 11, 9, 1, 1, coarse[2])
    level_3.sweep(level_3.va, level_3.vb, 4, 10, 7, 1, 1, coarse[3])

    for at in range(10, 24):
        level_2.vb[0, at] = level_2.va[0, at] + level_3.vb[0, (at - 2) // 2]
    level_2.sweep(level_2.vb, level_2.va, 11, 22, 12, 1, 1, steps[0], fresh=True)
    level_2.sweep(level_2.va, level_2.vb, 12, 21, 10, 1, 1, steps[1])
    level_2.sweep(level_2.vb, level_2.va, 13, 20, 8, 1, 1, steps[2])

    for at in range(8):
        value = level_2.va[0, 13 + at]
        for part in range(2):
            p1[at, pl.ds(part, 8, stride=2), :] = value
    receive_sides(from_x1, 48)
    for side in range(2):
        pl.when(reach[side] >= 2)(functools.partial(receive, from_x1b + side, 16))
    for at in range(14):
        if 4 <= at <= 9:
            before = level_1.va[0, at]
        else:
            before = rx1b[0] if at == 0 else rx1[0, at - 1] if at < 4 else rx1[1, at - 10] if at < 13 else rx1b[1]
        level_1.vb[0, at] = before + p1[(at + 1) // 2]
    for side in range(2):
        pl.when(has[side])(functools.partial(sends_done, 3 + side))
        pl.when(reach[side] >= 2)(functools.partial(sends_done, 5 + side))
    level_1.sweep(level_1.vb, level_1.va, 1, 12, 12, 1, 1, steps[0], fresh=True)
    level_1.sweep(level_1.va, level_1.vb, 2, 11, 10, 1, 1, steps[1])
    level_1.sweep(level_1.vb, level_1.va, 3, 10, 8, 1, 1, steps[2])

    fine_lane = lanes(16) // 2
    for at in range(8):
        value = level_1.va[0, 3 + at]
        for k in range(2):
            fine = jnp.take_along_axis(value, (fine_lane + (32 if k == 0 else 96)) % LANES, axis=1)
            for part in range(2):
                p0[k, at, pl.ds(part, 16, stride=2), :] = fine
    receive_sides(from_x0, 72)
    for side in range(2):
        packed = hx0[side, pl.ds(64, 8), :]
        for layer in range(2):
            at = (1 if side == 0 else 13) + layer
            coarse_at = (at - 4) // 2 + 2
            level_0.vb[0, at] = hx0[side, pl.ds(32 * layer, 32), :] + p0[0, coarse_at]
            for part in range(4):
                rows = pl.ds(8 * part, 8)
                level_0.vb[1, at, rows, :] = (
                    unpack(packed, 4 * layer + part) * level_0.lane_mask[1][:8] + p0[1, coarse_at, rows, :]
                )

    def correct(at):
        for k in range(2):
            level_0.vb[k, at] = level_0.va[k, at] + p0[k, at // 2]

    over_layers(3, 12, 5, correct)
    level_0.sweep(level_0.vb, level_0.va, 2, 13, 4, 2, 2, steps[0], fresh=True)
    level_0.sweep(level_0.va, level_0.vb, 3, 12, 5, 2, 2, steps[1])
    level_0.finish(level_0.vb, level_0.va, kept, added, 4, 11, 4, steps[2])

    sends_done(0)
    for_sides(lambda side, dw: sends_done(1 + side))
    if_reach(2, lambda side, sign: sends_done(sender_two + side))
    if_reach(4, lambda side, sign: sends_done(sender_four + side))
    if_reach(REACH, lambda side, sign: sends_done(sender_eight + side))
    for_far(1, lambda slot, dw: ruled(8, 0, sender_far + slot).wait_send())


def per_device(right_side, conductivity, wide, narrow):
    brick = (8, 32, LANES)
    scratch = []
    for shape in LEVEL_SHAPES:
        scratch += [pltpu.VMEM(shape, F32)] * LEVEL_FIELDS
    shapes = [
        (2, 64, LANES), (2, 64, LANES), (2, 2, 16, LANES), (3, 3, 32, LANES),
        (32, LANES), (2, 16, LANES), (2, 32, LANES), (2, 2, 16, LANES), (2, 32, LANES),
        (2 * REACH + 1, 8, LANES), (8, LANES), (2 * REACH + 1, 8, LANES),
        (2, 3, 16, LANES), (2, 16, LANES),
        (2, 72, LANES), (2, 72, LANES),
        (8, 16, LANES), (2, 8, 32, LANES),
        (RULER, LANES),
    ]
    scratch += [pltpu.VMEM(shape, F32) for shape in shapes]
    scratch += [pltpu.SemaphoreType.DMA((2,)), pltpu.SemaphoreType.DMA((SENDERS,)), pltpu.SemaphoreType.DMA((GROUPS,))]
    kept, added = pl.pallas_call(
        functools.partial(kernel, wide, narrow),
        out_shape=[jax.ShapeDtypeStruct(brick, F32)] * 2,
        in_specs=[pl.BlockSpec(memory_space=pltpu.HBM)] * 2,
        out_specs=[pl.BlockSpec(memory_space=pltpu.VMEM)] * 2,
        scratch_shapes=scratch,
        compiler_params=pltpu.CompilerParams(
            collective_id=0, has_side_effects=True, vmem_limit_bytes=32 * 1024 * 1024
        ),
    )(pltpu.with_memory_space_constraint(right_side, pltpu.HBM), pltpu.with_memory_space_constraint(conductivity, pltpu.HBM))
    return kept + added


def solution(mesh):
    spec = P("wide", None, "narrow")
    body = functools.partial(per_device, wide=mesh.shape["wide"], narrow=mesh.shape["narrow"])
    return jax.shard_map(body, mesh=mesh, in_specs=(spec, spec), out_specs=spec, check_vma=False)
```

```python
import functools

import jax
import jax.numpy as jnp
from jax import lax
from jax.experimental import pallas as pl
from jax.experimental.pallas import tpu as pltpu
from jax.sharding import PartitionSpec as P

CENTER = 1.125
HALF = 0.875
LANES = 128
REACH = 8
F32 = jnp.float32
MESH_ID = pl.DeviceIdType.MESH


def cheb(sweeps):
    sigma = CENTER / HALF
    steps = [(0.0, 1.0 / CENTER)]
    ratio = 1.0 / sigma
    for _ in range(sweeps - 1):
        ratio_next = 1.0 / (2.0 * sigma - ratio)
        steps.append((ratio_next * ratio, 2.0 * ratio_next / HALF))
        ratio = ratio_next
    return steps


def over_sides(first, second, count, body):
    def block(side, carry):
        for at in range(count):
            body(first + side * (second - first) + at)
        return carry

    lax.fori_loop(0, 2, block, 0)


def over_layers(low, high, unroll, body):
    count = high - low + 1
    if count == unroll:
        for at in range(low, high + 1):
            body(at)
        return

    def block(step, carry):
        for at in range(unroll):
            body(low + step * unroll + at)
        return carry

    lax.fori_loop(0, count // unroll, block, 0)


class Level:
    def __init__(self, refs, scale, rows, row_step, lane_step, base, extent, lane_mask):
        self.c, self.s, self.cx, self.cy, self.cz, self.iv, self.dg, self.va, self.vb = refs
        self.half = 0.5 * scale
        self.rows, self.row_step, self.lane_step = rows, row_step, lane_step
        self.base, self.extent, self.lane_mask = base, extent, lane_mask

    def inside(self, at):
        where_x = self.base + at
        return jnp.where((where_x >= 0) & (where_x < self.extent), 1.0, 0.0).astype(F32)

    def lane(self):
        return lax.broadcasted_iota(jnp.int32, (self.rows, LANES), 1)

    def row(self):
        return lax.broadcasted_iota(jnp.int32, (self.rows, LANES), 0)

    def y_up(self, tile):
        return pltpu.roll(tile, self.rows - self.row_step, 0)

    def y_down(self, tile):
        return pltpu.roll(tile, self.row_step, 0)

    def turned(self, tiles, shift, edge, count):
        out = [pltpu.roll(t, shift, 1) for t in tiles]
        if len(tiles) == 1:
            return out
        at_edge = self.lane() == edge
        return [jnp.where(at_edge, out[1 - k], out[k]) for k in range(count)]

    def z_up(self, tiles, count):
        return self.turned(tiles, LANES - self.lane_step, LANES - 1, count)

    def z_down(self, tiles, count):
        return self.turned(tiles, self.lane_step, 0, count)

    def masked(self, at, tiles):
        keep = self.inside(at) * self.half
        out = []
        for k in range(tiles):
            mask = self.lane_mask[k]
            out.append(self.c[k, at] * (keep if mask is None else mask * keep))
        return out

    def setup_below(self, low, tiles):
        first, second = self.masked(low - 1, tiles), self.masked(low, tiles)
        for k in range(tiles):
            self.cx[k, low - 1] = first[k] + second[k]

    def setup_at(self, at, tiles):
        before, here, after = self.masked(at - 1, tiles), self.masked(at, tiles), self.masked(at + 1, tiles)
        inside = self.inside(at)
        top = self.row() >= self.rows - self.row_step
        bottom = self.row() < self.row_step
        z_up, z_down = self.z_up(here, tiles), self.z_down(here, tiles)
        for k in range(tiles):
            own = here[k]
            x_low = before[k] + own
            x_high = own + after[k]
            y_low = own + jnp.where(bottom, 0.0, self.y_down(own))
            y_high = own + jnp.where(top, 0.0, self.y_up(own))
            z_low = own + z_down[k]
            z_high = own + z_up[k]
            diagonal = x_low + x_high + y_low + y_high + z_low + z_high
            keep = inside if self.lane_mask[k] is None else self.lane_mask[k] * inside
            self.cx[k, at] = x_high
            self.cy[k, at] = jnp.where(top, 0.0, y_high)
            self.cz[k, at] = z_high
            if k == 0:
                self.dg[0, at] = diagonal
            self.iv[k, at] = jnp.where(jnp.full_like(own, 0.0) + keep > 0.5, 1.0 / diagonal, 0.0)

    def setup(self, low, high, unroll, tiles):
        self.setup_below(low, tiles)
        over_layers(low, high, unroll, lambda at: self.setup_at(at, tiles))

    def start_at(self, at, tiles, beta):
        for k in range(tiles):
            self.va[k, at] = self.s[k, at] * self.iv[k, at] * beta

    def start_outer(self, at, beta):
        self.va[1, at] = self.s[1, at] * self.iv[1, at] * beta

    def start(self, low, high, unroll, tiles, beta):
        over_layers(low, high, unroll, lambda at: self.start_at(at, tiles, beta))

    def around(self, field, at, tiles, count):
        here = [field[k, at] for k in range(tiles)]
        cz = [self.cz[k, at] for k in range(tiles)]
        z_up = self.z_up(here, count)
        z_down = self.z_down([cz[k] * here[k] for k in range(tiles)], count)
        sums = []
        for k in range(count):
            cy = self.cy[k, at]
            total = self.cx[k, at] * field[k, at + 1] + self.cx[k, at - 1] * field[k, at - 1]
            total = total + (cy * self.y_up(here[k]) + self.y_down(cy * here[k]))
            total = total + (cz[k] * z_up[k] + z_down[k])
            sums.append(total + self.s[k, at])
        return here, sums

    def sweep_at(self, at, field, result, tiles, count, step, fresh):
        alpha, beta = step
        here, sums = self.around(field, at, tiles, count)
        for k in range(count):
            kept = (1.0 + alpha - beta) * here[k]
            if not fresh:
                kept = kept - alpha * result[k, at]
            result[k, at] = kept + (beta * self.iv[k, at]) * sums[k]

    def sweep(self, field, result, low, high, unroll, tiles, count, step, fresh=False):
        over_layers(low, high, unroll, lambda at: self.sweep_at(at, field, result, tiles, count, step, fresh))

    def residual_at(self, at, field, result, tiles):
        here, sums = self.around(field, at, tiles, 1)
        result[0, at] = sums[0] - self.dg[0, at] * here[0]

    def residual(self, field, result, low, high, unroll, tiles):
        over_layers(low, high, unroll, lambda at: self.residual_at(at, field, result, tiles))

    def finish(self, field, older, kept_out, added_out, low, high, unroll, step):
        alpha, beta = step

        def body(at):
            here, sums = self.around(field, at, 2, 1)
            kept_out[at - low] = (1.0 + alpha - beta) * here[0] - alpha * older[0, at]
            added_out[at - low] = (beta * self.iv[0, at]) * sums[0]

        over_layers(low, high, unroll, body)


LEVEL_FIELDS = 9
LEVEL_SHAPES = ((2, 16, 32, LANES), (2, 14, 16, LANES), (1, 34, 8, LANES), (1, 15, 8, LANES))
RULER = 1024
SENDERS = 18 + 2 * REACH + 1
GROUPS = 42 + 2 * REACH + 1


def kernel(wide, narrow, rhs, coef, kept, added, *scratch):
    scratch = list(scratch)
    level_refs = []
    for _ in range(4):
        level_refs.append(scratch[:LEVEL_FIELDS])
        scratch = scratch[LEVEL_FIELDS:]
    (zs, rz, rcn, k1c, sk, sp, k1x, k1p, k1z, rc2, s2m, rs2, rx1, rx1b, sb0, hx0, p1, p0, ruler,
     local_sem, send_sem, recv_sem) = scratch
    me_w = lax.axis_index("wide")
    me_n = lax.axis_index("narrow")

    def there(dw, dn):
        return (lax.rem(me_w + (dw + wide), wide), lax.rem(me_n + (dn + narrow), narrow))

    has = (me_w > 0, me_w < wide - 1)
    has_z = (me_n > 0, me_n < narrow - 1)
    reach = (jnp.minimum(me_w, REACH), jnp.minimum(wide - 1 - me_w, REACH))

    def for_far(first, body):
        for side in range(2):
            sign = 2 * side - 1

            def step(k, carry):
                body(REACH + sign * k, sign * k)
                return carry

            lax.fori_loop(first, reach[side] + 1, step, 0)

    def for_sides(body):
        for side in range(2):
            pl.when(has[side])(functools.partial(body, side, 2 * side - 1))

    def for_sides_z(body):
        for side in range(2):
            pl.when(has_z[side])(functools.partial(body, side, 2 * side - 1))

    def for_corners(body):
        for side in range(2):
            for side_z in range(2):
                pl.when(has[side] & has_z[side_z])(
                    functools.partial(body, side, side_z, 2 * side - 1, 2 * side_z - 1)
                )

    @pl.when((me_n == 0) | (me_n == narrow - 1))
    def clear_z():
        for ref in (rz, rcn, k1z, k1p):
            ref[...] = jnp.zeros(ref.shape, F32)
        for side in range(2):
            for side_z in range(2):
                k1c[2 * side, 2 * side_z] = jnp.zeros((32, LANES), F32)

    @pl.when((me_w < REACH) | (me_w >= wide - REACH))
    def clear():
        def zero(ref):
            ref[...] = jnp.zeros(ref.shape, F32)

        for ref in (rcn, rx1, rx1b, hx0, rc2, rs2, k1x, k1p):
            zero(ref)
        for side in range(2):
            zero(k1c.at[2 * side])
            for ref in level_refs[0][:2]:
                zero(ref.at[0, pl.ds(12 * side, 4)])
            zero(level_refs[1][0].at[0, 13 * side])

    def if_reach(least, body):
        for side in range(2):
            pl.when(reach[side] >= least)(functools.partial(body, side, 2 * side - 1))

    barrier = pltpu.get_barrier_semaphore()

    def greet(dw, dn):
        pl.semaphore_signal(barrier, inc=1, device_id=there(dw, dn), device_id_type=MESH_ID)

    for_sides(lambda side, dw: greet(dw, 0))
    for_sides_z(lambda side, dn: greet(0, dn))
    for_corners(lambda side, side_z, dw, dn: greet(dw, dn))

    c0, s0 = level_refs[0][0], level_refs[0][1]
    load_c = pltpu.make_async_copy(coef, c0.at[0, pl.ds(4, 8)], local_sem.at[0])
    load_s = pltpu.make_async_copy(rhs, s0.at[0, pl.ds(4, 8)], local_sem.at[1])
    load_c.start()
    load_s.start()
    beside_x = jnp.where(has[0], 1, 0) + jnp.where(has[1], 1, 0)
    beside_z = jnp.where(has_z[0], 1, 0) + jnp.where(has_z[1], 1, 0)
    greeted = beside_x + beside_z + beside_x * beside_z

    left = jnp.where(me_n > 0, 1.0, 0.0).astype(F32)
    right = jnp.where(me_n < narrow - 1, 1.0, 0.0).astype(F32)

    def lanes(rows):
        return lax.broadcasted_iota(jnp.int32, (rows, LANES), 1)

    def edges(rows, until, low, since, high):
        at = lanes(rows)
        return jnp.where(at < until, low, jnp.where(at >= since, high, 0.0))

    def centred(rows):
        at = lanes(rows)
        return jnp.where((at >= 32) & (at < 96), 1.0, edges(rows, 32, left, 96, right))

    level_0 = Level(level_refs[0], 1.0, 32, 1, 1, 8 * me_w - 4, 8 * wide, [None, edges(32, 8, right, 120, left)])
    level_1 = Level(
        level_refs[1], 0.25, 16, 1, 1, 4 * me_w - 5, 4 * wide, [centred(16), edges(16, 32, right, 96, left)]
    )
    level_2 = Level(level_refs[2], 0.0625, 8, 1, 2, 2 * me_w - 16, 2 * wide, [centred(8)])
    level_3 = Level(level_refs[3], 0.015625, 8, 2, 4, me_w - 7, wide, [centred(8)])

    sent = [0] * SENDERS

    def send(group, src, dst, dw, dn, rows, sender):
        if isinstance(sender, int):
            sent[sender] += rows
        pltpu.make_async_remote_copy(
            src_ref=src, dst_ref=dst, send_sem=send_sem.at[sender], recv_sem=recv_sem.at[group],
            device_id=there(dw, dn), device_id_type=MESH_ID,
        ).start()

    def ruled(rows, group, sender):
        span = ruler.at[pl.ds(0, rows)]
        return pltpu.make_async_remote_copy(
            src_ref=span, dst_ref=span, send_sem=send_sem.at[sender], recv_sem=recv_sem.at[group],
            device_id=there(0, 1), device_id_type=MESH_ID,
        )

    def receive(group, rows):
        ruled(rows, group, 0).wait_recv()

    def receive_sides(group, rows):
        for_sides(lambda side, dw: receive(group + side, rows))

    def receive_sides_z(group, rows):
        for_sides_z(lambda side, dn: receive(group + side, rows))

    def receive_corners(group, rows):
        for_corners(lambda side, side_z, dw, dn: receive(group + 2 * side + side_z, rows))

    def receive_far(group):
        for_far(1, lambda slot, dw: receive(group + slot, 8))

    def sends_done(sender):
        ruled(sent[sender], 0, sender).wait_send()

    from_z, from_s1z = 0, 2
    from_c_corner, from_k_corner, from_s1_corner = 4, 8, 12
    from_c, from_s, from_s_next, from_k, from_s1, from_c1b, from_x0, from_x1, from_x1b = range(16, 34, 2)
    from_near, from_two, from_four, from_eight = range(34, 42, 2)
    from_s2 = 42
    sender_x, sender_x1, sender_x1b, sender_two, sender_four, sender_eight, sender_z = range(0, 14, 2)
    sender_corner, sender_far = 14, 18

    def pack(tiles):
        rows = tiles[0].shape[0]
        group = lanes(rows) // 16
        packed = jnp.zeros((rows, LANES), F32)
        for at, tile in enumerate(tiles):
            packed = jnp.where(group == at, pltpu.roll(tile, (16 * at + 8) % LANES, 1), packed)
        return packed

    def unpack(packed, at):
        return pltpu.roll(packed, (2 * LANES - (16 * at + 8)) % LANES, 1)

    def pack_side(ref, half, side):
        group = lanes(8) // 8
        packed = None
        for layer in range(4):
            for part in range(4):
                at = 4 * layer + part
                tile = ref[0, 4 + 4 * half + layer, pl.ds(8 * part, 8), :]
                tile = pltpu.roll(tile, (8 * at + 8 * side) % LANES, 1)
                packed = tile if at == 0 else jnp.where(group == at, tile, packed)
        return packed

    def restrict_0(ref):
        out = []
        for layer in range(4):
            total = None
            for dx in range(2):
                for dy in range(2):
                    term = ref[0, 4 + 2 * layer + dx, pl.ds(dy, 16, stride=2), :]
                    total = term if total is None else total + term
            total = total + pltpu.roll(total, LANES - 1, 1)
            out.append(0.125 * jnp.take_along_axis(total, (2 * lanes(16) + 64) % LANES, axis=1))
        return out

    odd_8 = lanes(8) % 2 == 1

    def pairs_1(ref):
        out = []
        for layer in range(2):
            total = None
            for dx in range(2):
                for dy in range(2):
                    term = ref[0, 5 + 2 * layer + dx, pl.ds(dy, 8, stride=2), :]
                    total = term if total is None else total + term
            total = total + jnp.where(odd_8, pltpu.roll(total, 1, 1), pltpu.roll(total, LANES - 1, 1))
            out.append(0.125 * total)
        return jnp.where(odd_8, out[1], out[0])

    def squeeze_1(layers, ref, row):
        for part in range(2):
            ref[pl.ds(row + 16 * part, 16), :] = jnp.where(lanes(16) < 64, layers[part], layers[part + 2])

    pl.semaphore_wait(barrier, greeted)

    @for_sides
    def send_faces(side, dw):
        send(from_c + 1 - side, coef.at[pl.ds(4 * side, 4)], c0.at[0, pl.ds(12 - 12 * side, 4)], dw, 0, 128, sender_x + side)
        send(from_s + 1 - side, rhs.at[7 * side], s0.at[0, 12 - 9 * side], dw, 0, 32, sender_x + side)

    load_c.wait()
    own_c1 = restrict_0(c0)
    for side in range(2):
        squeeze_1(own_c1, zs.at[side], 32)
        for half in range(2):
            zs[side, pl.ds(16 * half, 8), :] = pack_side(c0, half, side)
    load_s.wait()
    for side in range(2):
        for half in range(2):
            zs[side, pl.ds(16 * half + 8, 8), :] = pack_side(s0, half, side)

    for_sides_z(
        lambda side, dn: send(from_z + 1 - side, zs.at[side], rz.at[1 - side], 0, dn, 64, sender_z + side)
    )

    def send_corner(group, src, dst, rows, side, side_z):
        at = 2 * side + side_z
        send(group + 3 - at, src, dst, 2 * side - 1, 2 * side_z - 1, rows, sender_corner + at)

    @for_corners
    def send_c_corner(side, side_z, dw, dn):
        src = zs.at[side_z, pl.ds(16 * side, 16)]
        send_corner(from_c_corner, src, rcn.at[1 - side, 1 - side_z], 16, side, side_z)

    @for_sides
    def send_s_next(side, dw):
        src = rhs.at[pl.ds(1 + 4 * side, 2)]
        send(from_s_next + 1 - side, src, s0.at[0, pl.ds(13 - 12 * side, 2)], dw, 0, 64, sender_x + side)

    def fill_0(ref, first, from_left, from_right):
        low = lanes(8) < 64
        for layer in range(4):
            for part in range(4):
                at = 4 * layer + part
                ref[1, first + layer, pl.ds(8 * part, 8), :] = jnp.where(
                    low, pltpu.roll(from_right, (LANES - 8 * at) % LANES, 1), pltpu.roll(from_left, (120 - 8 * at) % LANES, 1)
                )

    steps = cheb(3)
    receive_sides_z(from_z, 64)
    for field, ref in enumerate((c0, s0)):
        for half in range(2):
            rows = pl.ds(16 * half + 8 * field, 8)
            fill_0(ref, 4 + 4 * half, rz[0, rows, :], rz[1, rows, :])
    level_0.setup(5, 10, 3, 2)
    level_0.start(5, 10, 6, 2, steps[0][1])
    level_0.sweep(level_0.va, level_0.vb, 6, 9, 4, 2, 2, steps[1], fresh=True)
    level_0.sweep(level_0.vb, level_0.va, 7, 8, 2, 2, 2, steps[2])

    def spread_1(ref, block, places):
        at_lane = lanes(16)
        low_half = at_lane < 64
        low_quarter = at_lane % 64 < 32
        for dx in places:
            for part in range(2):
                before, own, after = (block(dx, dz, part) for dz in (-1, 0, 1))
                near = jnp.where(low_quarter, before, after)
                outer = jnp.where(low_quarter, after, before)
                own_r, near_r, outer_r = (pltpu.roll(t, 64, 1) for t in (own, near, outer))
                at = 5 + 4 * dx + part
                for at, own_a, own_b, near_a, near_b, outer_a, outer_b in (
                    (at, own, own_r, near, near_r, outer, outer_r),
                    (at + 2, own_r, own, near_r, near, outer_r, outer),
                ):
                    centre = jnp.where(low_half, own_a, own_b)
                    ref[0, at] = jnp.where(at_lane < 32, near_a, jnp.where(at_lane < 96, centre, near_b))
                    ref[1, at] = jnp.where(low_half, outer_a, outer_b)

    def coef_block(dx, dz, part):
        if dx == 0:
            rows = pl.ds(32 + 16 * part, 16)
            return zs[0, rows, :] if dz == 0 else rz[(1 + dz) // 2, rows, :]
        return k1c[1 + dx, 1 + dz, pl.ds(16 * part, 16), :]

    spread_1(level_1.c, coef_block, (0,))
    rc2[REACH] = pairs_1(level_1.c)

    @for_sides
    def send_near(side, dw):
        send(from_near + 1 - side, rc2.at[REACH], rc2.at[REACH - dw], dw, 0, 8, sender_x + side)

    k1_own = zs.at[0, pl.ds(32, 32)]
    for_sides(
        lambda side, dw: send(from_k + 1 - side, k1_own, k1c.at[1 - dw, 1], dw, 0, 32, sender_x + side)
    )
    for_corners(
        lambda side, side_z, dw, dn: send_corner(from_k_corner, k1_own, k1c.at[1 - dw, 1 - dn], 32, side, side_z)
    )

    receive_sides(from_c, 128)
    receive_corners(from_c_corner, 16)
    for field, ref in enumerate((c0, s0)):
        for side in range(2):
            rows = pl.ds(8 * field, 8)
            fill_0(ref, 12 * side, rcn[side, 0, rows, :], rcn[side, 1, rows, :])
    level_0.setup_below(1, 2)
    over_sides(1, 11, 4, lambda at: level_0.setup_at(at, 2))
    receive_sides(from_s, 32)
    sweep_a = (level_0.va, level_0.vb, 2, 2, steps[1], True)
    sweep_b = (level_0.vb, level_0.va, 2, 2, steps[2], False)
    over_sides(3, 11, 2, lambda at: level_0.start_at(at, 2, steps[0][1]))
    over_sides(4, 10, 2, lambda at: level_0.sweep_at(at, *sweep_a))
    over_sides(5, 9, 2, lambda at: level_0.sweep_at(at, *sweep_b))
    level_0.residual(level_0.va, level_0.vb, 6, 9, 4, 2)
    receive_sides(from_near, 8)

    @functools.partial(if_reach, 2)
    def send_two(side, sign):
        src = rc2.at[pl.ds(REACH - side, 2)] if side == 1 else rc2.at[pl.ds(REACH, 2)]
        dst = rc2.at[pl.ds(REACH - 3, 2)] if side == 1 else rc2.at[pl.ds(REACH + 2, 2)]
        send(from_two + 1 - side, src, dst, 2 * sign, 0, 16, sender_two + side)

    receive_sides(from_s_next, 64)
    over_sides(1, 13, 2, lambda at: level_0.start_at(at, 2, steps[0][1]))
    over_sides(2, 12, 2, lambda at: level_0.sweep_at(at, *sweep_a))
    over_sides(3, 11, 2, lambda at: level_0.sweep_at(at, *sweep_b))
    over_sides(4, 10, 2, lambda at: level_0.residual_at(at, level_0.va, level_0.vb, 2))

    squeeze_1(restrict_0(level_0.vb), sk, 0)

    low_quarter = lanes(16) % 64 < 32
    first, second = sk[pl.ds(0, 16), :], sk[pl.ds(16, 16), :]
    sp[0] = jnp.where(low_quarter, pltpu.roll(first, 96, 1), second)
    sp[1] = jnp.where(low_quarter, first, pltpu.roll(second, 32, 1))

    for_sides(lambda side, dw: send(from_s1 + 1 - side, sk, k1x.at[1 - side], dw, 0, 32, sender_x + side))
    for_corners(
        lambda side, side_z, dw, dn: send_corner(
            from_s1_corner, sp.at[side_z], k1p.at[1 - side, 1 - side_z], 16, side, side_z
        )
    )
    for_sides_z(lambda side, dn: send(from_s1z + 1 - side, sk, k1z.at[1 - side], 0, dn, 32, sender_z + side))

    if_reach(2, lambda side, sign: receive(from_two + side, 16))

    @functools.partial(if_reach, 4)
    def send_four(side, sign):
        src = rc2.at[pl.ds(REACH - 3, 4)] if side == 1 else rc2.at[pl.ds(REACH, 4)]
        dst = rc2.at[pl.ds(REACH - 7, 4)] if side == 1 else rc2.at[pl.ds(REACH + 4, 4)]
        send(from_four + 1 - side, src, dst, 4 * sign, 0, 32, sender_four + side)

    for side in range(2):
        first = 9 if side == 0 else 5
        tiles = []
        for layer in range(2):
            sb0[side, pl.ds(32 * layer, 32), :] = level_0.va[0, first + layer]
            for part in range(4):
                tiles.append(level_0.va[1, first + layer, pl.ds(8 * part, 8), :])
        sb0[side, pl.ds(64, 8), :] = pack(tiles)

    @for_sides
    def send_iterate_0(side, dw):
        send(from_x0 + 1 - side, sb0.at[1 - side], hx0.at[1 - side], dw, 0, 72, sender_x + side)

    def source_block(dx, dz, part):
        rows = pl.ds(16 * part, 16)
        return sk[rows, :] if dz == 0 else k1z[(1 + dz) // 2, rows, :]

    def spread_beside(ref):
        at_lane = lanes(16)
        low_half = at_lane < 64
        for side in range(2):
            for layer in range(4):
                own = k1x[side, pl.ds(16 * (layer % 2), 16), :]
                other = pltpu.roll(own, 64, 1)
                centre = jnp.where(low_half, own, other) if layer < 2 else jnp.where(low_half, other, own)
                before = pltpu.roll(k1p[side, 0], (LANES - 32 * layer) % LANES, 1)
                after = pltpu.roll(k1p[side, 1], (LANES + 96 - 32 * layer) % LANES, 1)
                ref[0, 1 + 8 * side + layer] = jnp.where(at_lane < 32, before, jnp.where(at_lane < 96, centre, after))

    receive_sides(from_k, 32)
    receive_corners(from_k_corner, 32)
    spread_1(level_1.c, coef_block, (-1, 1))

    @for_sides
    def send_coef_1(side, dw):
        send(from_c1b + 1 - side, level_1.c.at[0, 9 - 5 * side], level_1.c.at[0, 13 - 13 * side], dw, 0, 16, sender_x + side)

    level_1.setup_below(2, 1)
    over_sides(2, 10, 2, lambda at: level_1.setup_at(at, 1))
    over_layers(4, 9, 6, lambda at: level_1.setup_at(at, 2))

    receive_sides_z(from_s1z, 32)
    spread_1(level_1.s, source_block, (0,))
    receive_sides(from_s1, 32)
    receive_corners(from_s1_corner, 16)
    spread_beside(level_1.s)
    level_1.start(2, 11, 10, 1, steps[0][1])
    over_layers(5, 8, 4, lambda at: level_1.start_outer(at, steps[0][1]))
    over_sides(3, 9, 2, lambda at: level_1.sweep_at(at, level_1.va, level_1.vb, 1, 1, steps[1], True))
    over_layers(5, 8, 4, lambda at: level_1.sweep_at(at, level_1.va, level_1.vb, 2, 1, steps[1], True))
    level_1.sweep(level_1.vb, level_1.va, 4, 9, 6, 1, 1, steps[2])
    level_1.residual(level_1.va, level_1.vb, 5, 8, 4, 1)

    value = pairs_1(level_1.vb)
    s2m[...] = value
    rs2[REACH] = value
    if_reach(4, lambda side, sign: receive(from_four + side, 32))
    for_far(1, lambda slot, dw: send(from_s2 + 2 * REACH - slot, s2m, rs2.at[2 * REACH - slot], dw, 0, 8, sender_far + slot))

    @functools.partial(if_reach, REACH)
    def send_eight(side, sign):
        send(from_eight + 1 - side, rc2.at[REACH], rc2.at[REACH - sign * REACH], REACH * sign, 0, 8, sender_eight + side)

    @for_sides
    def send_iterate_1(side, dw):
        send(from_x1 + 1 - side, level_1.va.at[0, pl.ds(6 - side, 3)], rx1.at[1 - side], dw, 0, 48, sender_x1 + side)

    for side in range(2):
        @pl.when(reach[side] >= 2)
        def send_next_1():
            layer = level_1.va.at[0, 5 + 3 * side]
            send(from_x1b + 1 - side, layer, rx1b.at[1 - side], 4 * side - 2, 0, 16, sender_x1b + side)

    receive_sides(from_c1b, 16)
    level_1.setup_below(1, 1)
    over_sides(1, 12, 1, lambda at: level_1.setup_at(at, 1))

    def spread_2(ref, blocks):
        for block in range(2 * REACH + 1):
            packed = blocks[block]
            ref[0, 2 * block] = jnp.where(odd_8, pltpu.roll(packed, 1, 1), packed)
            ref[0, 2 * block + 1] = jnp.where(odd_8, packed, pltpu.roll(packed, LANES - 1, 1))

    def restrict_2(ref, at):
        total = ref[0, 2 * at + 2] + ref[0, 2 * at + 3]
        odd_row = lax.broadcasted_iota(jnp.int32, (8, LANES), 0) % 2 == 1
        total = total + jnp.where(odd_row, pltpu.roll(total, 1, 0), pltpu.roll(total, 7, 0))
        second = lanes(8) % 4 >= 2
        total = total + jnp.where(second, pltpu.roll(total, 2, 1), pltpu.roll(total, LANES - 2, 1))
        return 0.125 * total

    if_reach(REACH, lambda side, sign: receive(from_eight + side, 8))
    spread_2(level_2.c, rc2)
    level_2.setup(1, 32, 8, 1)
    for at in range(15):
        level_3.c[0, at] = restrict_2(level_2.c, at)
    level_3.setup(1, 13, 13, 1)

    receive_far(from_s2)
    spread_2(level_2.s, rs2)
    level_2.start(1, 32, 32, 1, steps[0][1])
    level_2.sweep(level_2.va, level_2.vb, 2, 31, 15, 1, 1, steps[1], fresh=True)
    level_2.sweep(level_2.vb, level_2.va, 3, 30, 14, 1, 1, steps[2])
    level_2.residual(level_2.va, level_2.vb, 4, 29, 13, 1)

    for at in range(1, 14):
        level_3.s[0, at] = restrict_2(level_2.vb, at)
    coarse = cheb(4)
    level_3.start(1, 13, 13, 1, coarse[0][1])
    level_3.sweep(level_3.va, level_3.vb, 2, 12, 11, 1, 1, coarse[1], fresh=True)
    level_3.sweep(level_3.vb, level_3.va, 3, 11, 9, 1, 1, coarse[2])
    level_3.sweep(level_3.va, level_3.vb, 4, 10, 7, 1, 1, coarse[3])

    for at in range(10, 24):
        level_2.vb[0, at] = level_2.va[0, at] + level_3.vb[0, (at - 2) // 2]
    level_2.sweep(level_2.vb, level_2.va, 11, 22, 12, 1, 1, steps[0], fresh=True)
    level_2.sweep(level_2.va, level_2.vb, 12, 21, 10, 1, 1, steps[1])
    level_2.sweep(level_2.vb, level_2.va, 13, 20, 8, 1, 1, steps[2])

    for at in range(8):
        value = level_2.va[0, 13 + at]
        for part in range(2):
            p1[at, pl.ds(part, 8, stride=2), :] = value
    receive_sides(from_x1, 48)
    for side in range(2):
        pl.when(reach[side] >= 2)(functools.partial(receive, from_x1b + side, 16))
    for at in range(14):
        if 4 <= at <= 9:
            before = level_1.va[0, at]
        else:
            before = rx1b[0] if at == 0 else rx1[0, at - 1] if at < 4 else rx1[1, at - 10] if at < 13 else rx1b[1]
        level_1.vb[0, at] = before + p1[(at + 1) // 2]
    for side in range(2):
        pl.when(has[side])(functools.partial(sends_done, sender_x1 + side))
        pl.when(reach[side] >= 2)(functools.partial(sends_done, sender_x1b + side))
    level_1.sweep(level_1.vb, level_1.va, 1, 12, 12, 1, 1, steps[0], fresh=True)
    level_1.sweep(level_1.va, level_1.vb, 2, 11, 10, 1, 1, steps[1])
    level_1.sweep(level_1.vb, level_1.va, 3, 10, 8, 1, 1, steps[2])

    fine_lane = lanes(16) // 2
    for at in range(8):
        value = level_1.va[0, 3 + at]
        for k in range(2):
            fine = jnp.take_along_axis(value, (fine_lane + (32 if k == 0 else 96)) % LANES, axis=1)
            for part in range(2):
                p0[k, at, pl.ds(part, 16, stride=2), :] = fine
    receive_sides(from_x0, 72)
    for side in range(2):
        packed = hx0[side, pl.ds(64, 8), :]
        for layer in range(2):
            at = (1 if side == 0 else 13) + layer
            coarse_at = (at - 4) // 2 + 2
            level_0.vb[0, at] = hx0[side, pl.ds(32 * layer, 32), :] + p0[0, coarse_at]
            for part in range(4):
                rows = pl.ds(8 * part, 8)
                level_0.vb[1, at, rows, :] = (
                    unpack(packed, 4 * layer + part) * level_0.lane_mask[1][:8] + p0[1, coarse_at, rows, :]
                )

    def correct(at):
        for k in range(2):
            level_0.vb[k, at] = level_0.va[k, at] + p0[k, at // 2]

    over_layers(3, 12, 5, correct)
    level_0.sweep(level_0.vb, level_0.va, 2, 13, 4, 2, 2, steps[0], fresh=True)
    level_0.sweep(level_0.va, level_0.vb, 3, 12, 5, 2, 2, steps[1])
    level_0.finish(level_0.vb, level_0.va, kept, added, 4, 11, 4, steps[2])

    for_sides(lambda side, dw: sends_done(sender_x + side))
    for_sides_z(lambda side, dn: sends_done(sender_z + side))
    for_corners(lambda side, side_z, dw, dn: sends_done(sender_corner + 2 * side + side_z))
    if_reach(2, lambda side, sign: sends_done(sender_two + side))
    if_reach(4, lambda side, sign: sends_done(sender_four + side))
    if_reach(REACH, lambda side, sign: sends_done(sender_eight + side))
    for_far(1, lambda slot, dw: ruled(8, 0, sender_far + slot).wait_send())


def per_device(right_side, conductivity, wide, narrow):
    brick = (8, 32, LANES)
    scratch = []
    for shape in LEVEL_SHAPES:
        scratch += [pltpu.VMEM(shape, F32)] * LEVEL_FIELDS
    shapes = [
        (2, 64, LANES), (2, 64, LANES), (2, 2, 16, LANES), (3, 3, 32, LANES),
        (32, LANES), (2, 16, LANES), (2, 32, LANES), (2, 2, 16, LANES), (2, 32, LANES),
        (2 * REACH + 1, 8, LANES), (8, LANES), (2 * REACH + 1, 8, LANES),
        (2, 3, 16, LANES), (2, 16, LANES),
        (2, 72, LANES), (2, 72, LANES),
        (8, 16, LANES), (2, 8, 32, LANES),
        (RULER, LANES),
    ]
    scratch += [pltpu.VMEM(shape, F32) for shape in shapes]
    scratch += [pltpu.SemaphoreType.DMA((2,)), pltpu.SemaphoreType.DMA((SENDERS,)), pltpu.SemaphoreType.DMA((GROUPS,))]
    kept, added = pl.pallas_call(
        functools.partial(kernel, wide, narrow),
        out_shape=[jax.ShapeDtypeStruct(brick, F32)] * 2,
        in_specs=[pl.BlockSpec(memory_space=pltpu.HBM)] * 2,
        out_specs=[pl.BlockSpec(memory_space=pltpu.VMEM)] * 2,
        scratch_shapes=scratch,
        compiler_params=pltpu.CompilerParams(
            collective_id=0, has_side_effects=True, vmem_limit_bytes=32 * 1024 * 1024
        ),
    )(pltpu.with_memory_space_constraint(right_side, pltpu.HBM), pltpu.with_memory_space_constraint(conductivity, pltpu.HBM))
    return kept + added


def solution(mesh):
    spec = P("wide", None, "narrow")
    body = functools.partial(per_device, wide=mesh.shape["wide"], narrow=mesh.shape["narrow"])
    return jax.shard_map(body, mesh=mesh, in_specs=(spec, spec), out_specs=spec, check_vma=False)
```

```python
import functools

import jax
import jax.numpy as jnp
from jax import lax
from jax.experimental import pallas as pl
from jax.experimental.pallas import tpu as pltpu
from jax.sharding import PartitionSpec as P

CENTER = 1.125
HALF = 0.875
LANES = 128
REACH = 8
F32 = jnp.float32
MESH_ID = pl.DeviceIdType.MESH


def cheb(sweeps):
    sigma = CENTER / HALF
    steps = [(0.0, 1.0 / CENTER)]
    ratio = 1.0 / sigma
    for _ in range(sweeps - 1):
        ratio_next = 1.0 / (2.0 * sigma - ratio)
        steps.append((ratio_next * ratio, 2.0 * ratio_next / HALF))
        ratio = ratio_next
    return steps


def over_sides(first, second, count, body):
    for base in (first, second):
        for at in range(count):
            body(base + at)


def over_layers(low, high, unroll, body):
    count = high - low + 1
    if count == unroll:
        for at in range(low, high + 1):
            body(at)
        return

    def block(step, carry):
        for at in range(unroll):
            body(low + step * unroll + at)
        return carry

    lax.fori_loop(0, count // unroll, block, 0)


class Level:
    def __init__(self, refs, scale, rows, row_step, lane_step, base, extent, lane_mask):
        self.c, self.s, self.cx, self.cy, self.cz, self.iv, self.dg, self.va, self.vb = refs
        self.half = 0.5 * scale
        self.rows, self.row_step, self.lane_step = rows, row_step, lane_step
        self.base, self.extent, self.lane_mask = base, extent, lane_mask

    def inside(self, at):
        where_x = self.base + at
        return jnp.where((where_x >= 0) & (where_x < self.extent), 1.0, 0.0).astype(F32)

    def lane(self):
        return lax.broadcasted_iota(jnp.int32, (self.rows, LANES), 1)

    def row(self):
        return lax.broadcasted_iota(jnp.int32, (self.rows, LANES), 0)

    def y_up(self, tile):
        return pltpu.roll(tile, self.rows - self.row_step, 0)

    def y_down(self, tile):
        return pltpu.roll(tile, self.row_step, 0)

    def turned(self, tiles, shift, edge, count):
        out = [pltpu.roll(t, shift, 1) for t in tiles]
        if len(tiles) == 1:
            return out
        at_edge = self.lane() == edge
        return [jnp.where(at_edge, out[1 - k], out[k]) for k in range(count)]

    def z_up(self, tiles, count):
        return self.turned(tiles, LANES - self.lane_step, LANES - 1, count)

    def z_down(self, tiles, count):
        return self.turned(tiles, self.lane_step, 0, count)

    def masked(self, at, tiles):
        keep = self.inside(at) * self.half
        out = []
        for k in range(tiles):
            mask = self.lane_mask[k]
            out.append(self.c[k, at] * (keep if mask is None else mask * keep))
        return out

    def setup_below(self, low, tiles):
        first, second = self.masked(low - 1, tiles), self.masked(low, tiles)
        for k in range(tiles):
            self.cx[k, low - 1] = first[k] + second[k]

    def setup_at(self, at, tiles):
        before, here, after = self.masked(at - 1, tiles), self.masked(at, tiles), self.masked(at + 1, tiles)
        inside = self.inside(at)
        top = self.row() >= self.rows - self.row_step
        bottom = self.row() < self.row_step
        z_up, z_down = self.z_up(here, tiles), self.z_down(here, tiles)
        for k in range(tiles):
            own = here[k]
            x_low = before[k] + own
            x_high = own + after[k]
            y_low = own + jnp.where(bottom, 0.0, self.y_down(own))
            y_high = own + jnp.where(top, 0.0, self.y_up(own))
            z_low = own + z_down[k]
            z_high = own + z_up[k]
            diagonal = x_low + x_high + y_low + y_high + z_low + z_high
            keep = inside if self.lane_mask[k] is None else self.lane_mask[k] * inside
            self.cx[k, at] = x_high
            self.cy[k, at] = jnp.where(top, 0.0, y_high)
            self.cz[k, at] = z_high
            if k == 0:
                self.dg[0, at] = diagonal
            self.iv[k, at] = jnp.where(jnp.full_like(own, 0.0) + keep > 0.5, 1.0 / diagonal, 0.0)

    def setup(self, low, high, unroll, tiles):
        self.setup_below(low, tiles)
        over_layers(low, high, unroll, lambda at: self.setup_at(at, tiles))

    def start_at(self, at, tiles, beta):
        for k in range(tiles):
            self.va[k, at] = self.s[k, at] * self.iv[k, at] * beta

    def start_outer(self, at, beta):
        self.va[1, at] = self.s[1, at] * self.iv[1, at] * beta

    def start(self, low, high, unroll, tiles, beta):
        over_layers(low, high, unroll, lambda at: self.start_at(at, tiles, beta))

    def around(self, field, at, tiles, count):
        here = [field[k, at] for k in range(tiles)]
        cz = [self.cz[k, at] for k in range(tiles)]
        z_up = self.z_up(here, count)
        z_down = self.z_down([cz[k] * here[k] for k in range(tiles)], count)
        sums = []
        for k in range(count):
            cy = self.cy[k, at]
            total = self.cx[k, at] * field[k, at + 1] + self.cx[k, at - 1] * field[k, at - 1]
            total = total + (cy * self.y_up(here[k]) + self.y_down(cy * here[k]))
            total = total + (cz[k] * z_up[k] + z_down[k])
            sums.append(total + self.s[k, at])
        return here, sums

    def sweep_at(self, at, field, result, tiles, count, step, fresh):
        alpha, beta = step
        here, sums = self.around(field, at, tiles, count)
        for k in range(count):
            kept = (1.0 + alpha - beta) * here[k]
            if not fresh:
                kept = kept - alpha * result[k, at]
            result[k, at] = kept + (beta * self.iv[k, at]) * sums[k]

    def sweep(self, field, result, low, high, unroll, tiles, count, step, fresh=False):
        over_layers(low, high, unroll, lambda at: self.sweep_at(at, field, result, tiles, count, step, fresh))

    def residual_at(self, at, field, result, tiles):
        here, sums = self.around(field, at, tiles, 1)
        result[0, at] = sums[0] - self.dg[0, at] * here[0]

    def residual(self, field, result, low, high, unroll, tiles):
        over_layers(low, high, unroll, lambda at: self.residual_at(at, field, result, tiles))

    def finish(self, field, older, kept_out, added_out, low, high, unroll, step):
        alpha, beta = step

        def body(at):
            here, sums = self.around(field, at, 2, 1)
            kept_out[at - low] = (1.0 + alpha - beta) * here[0] - alpha * older[0, at]
            added_out[at - low] = (beta * self.iv[0, at]) * sums[0]

        over_layers(low, high, unroll, body)


LEVEL_FIELDS = 9
LEVEL_SHAPES = ((2, 16, 32, LANES), (2, 14, 16, LANES), (1, 34, 8, LANES), (1, 15, 8, LANES))
RULER = 1024
SENDERS = 18 + 2 * REACH + 1
GROUPS = 42 + 2 * REACH + 1


def kernel(wide, narrow, rhs, coef, kept, added, *scratch):
    scratch = list(scratch)
    level_refs = []
    for _ in range(4):
        level_refs.append(scratch[:LEVEL_FIELDS])
        scratch = scratch[LEVEL_FIELDS:]
    (zs, rz, rcn, kp, k1cx, k1c, sk, sp, k1x, k1p, k1z, rc2, s2m, rs2, rx1, rx1b, sb0, hx0, p1, p0, ruler,
     local_sem, send_sem, recv_sem) = scratch
    me_w = lax.axis_index("wide")
    me_n = lax.axis_index("narrow")

    def there(dw, dn):
        return (lax.rem(me_w + (dw + wide), wide), lax.rem(me_n + (dn + narrow), narrow))

    has = (me_w > 0, me_w < wide - 1)
    has_z = (me_n > 0, me_n < narrow - 1)
    reach = (jnp.minimum(me_w, REACH), jnp.minimum(wide - 1 - me_w, REACH))

    def for_far(first, body):
        for side in range(2):
            sign = 2 * side - 1

            def step(k, carry):
                body(REACH + sign * k, sign * k)
                return carry

            lax.fori_loop(first, reach[side] + 1, step, 0)

    def for_sides(body):
        for side in range(2):
            pl.when(has[side])(functools.partial(body, side, 2 * side - 1))

    def for_sides_z(body):
        for side in range(2):
            pl.when(has_z[side])(functools.partial(body, side, 2 * side - 1))

    def for_corners(body):
        for side in range(2):
            for side_z in range(2):
                pl.when(has[side] & has_z[side_z])(
                    functools.partial(body, side, side_z, 2 * side - 1, 2 * side_z - 1)
                )

    @pl.when((me_n == 0) | (me_n == narrow - 1))
    def clear_z():
        for ref in (rz, rcn, k1c, k1z, k1p):
            ref[...] = jnp.zeros(ref.shape, F32)

    @pl.when((me_w < REACH) | (me_w >= wide - REACH))
    def clear():
        def zero(ref):
            ref[...] = jnp.zeros(ref.shape, F32)

        for ref in (rcn, rx1, rx1b, hx0, rc2, rs2, k1cx, k1c, k1x, k1p):
            zero(ref)
        for side in range(2):
            for ref in level_refs[0][:2]:
                zero(ref.at[0, pl.ds(12 * side, 4)])
            zero(level_refs[1][0].at[0, 13 * side])

    def if_reach(least, body):
        for side in range(2):
            pl.when(reach[side] >= least)(functools.partial(body, side, 2 * side - 1))

    barrier = pltpu.get_barrier_semaphore()

    def greet(dw, dn):
        pl.semaphore_signal(barrier, inc=1, device_id=there(dw, dn), device_id_type=MESH_ID)

    for_sides(lambda side, dw: greet(dw, 0))
    for_sides_z(lambda side, dn: greet(0, dn))
    for_corners(lambda side, side_z, dw, dn: greet(dw, dn))

    c0, s0 = level_refs[0][0], level_refs[0][1]
    load_c = pltpu.make_async_copy(coef, c0.at[0, pl.ds(4, 8)], local_sem.at[0])
    load_s = pltpu.make_async_copy(rhs, s0.at[0, pl.ds(4, 8)], local_sem.at[1])
    load_c.start()
    load_s.start()
    beside_x = jnp.where(has[0], 1, 0) + jnp.where(has[1], 1, 0)
    beside_z = jnp.where(has_z[0], 1, 0) + jnp.where(has_z[1], 1, 0)
    greeted = beside_x + beside_z + beside_x * beside_z

    left = jnp.where(me_n > 0, 1.0, 0.0).astype(F32)
    right = jnp.where(me_n < narrow - 1, 1.0, 0.0).astype(F32)

    def lanes(rows):
        return lax.broadcasted_iota(jnp.int32, (rows, LANES), 1)

    def edges(rows, until, low, since, high):
        at = lanes(rows)
        return jnp.where(at < until, low, jnp.where(at >= since, high, 0.0))

    def centred(rows):
        at = lanes(rows)
        return jnp.where((at >= 32) & (at < 96), 1.0, edges(rows, 32, left, 96, right))

    level_0 = Level(level_refs[0], 1.0, 32, 1, 1, 8 * me_w - 4, 8 * wide, [None, edges(32, 8, right, 120, left)])
    level_1 = Level(
        level_refs[1], 0.25, 16, 1, 1, 4 * me_w - 5, 4 * wide, [centred(16), edges(16, 32, right, 96, left)]
    )
    level_2 = Level(level_refs[2], 0.0625, 8, 1, 2, 2 * me_w - 16, 2 * wide, [centred(8)])
    level_3 = Level(level_refs[3], 0.015625, 8, 2, 4, me_w - 7, wide, [centred(8)])

    sent = [0] * SENDERS

    def send(group, src, dst, dw, dn, rows, sender):
        if isinstance(sender, int):
            sent[sender] += rows
        pltpu.make_async_remote_copy(
            src_ref=src, dst_ref=dst, send_sem=send_sem.at[sender], recv_sem=recv_sem.at[group],
            device_id=there(dw, dn), device_id_type=MESH_ID,
        ).start()

    def ruled(rows, group, sender):
        span = ruler.at[pl.ds(0, rows)]
        return pltpu.make_async_remote_copy(
            src_ref=span, dst_ref=span, send_sem=send_sem.at[sender], recv_sem=recv_sem.at[group],
            device_id=there(0, 1), device_id_type=MESH_ID,
        )

    def receive(group, rows):
        ruled(rows, group, 0).wait_recv()

    def receive_sides(group, rows):
        for_sides(lambda side, dw: receive(group + side, rows))

    def receive_sides_z(group, rows):
        for_sides_z(lambda side, dn: receive(group + side, rows))

    def receive_corners(group, rows):
        for_corners(lambda side, side_z, dw, dn: receive(group + 2 * side + side_z, rows))

    def receive_far(group):
        for_far(1, lambda slot, dw: receive(group + slot, 8))

    def sends_done(sender):
        ruled(sent[sender], 0, sender).wait_send()

    from_z, from_s1z = 0, 2
    from_c_corner, from_k_corner, from_s1_corner = 4, 8, 12
    from_c, from_s, from_s_next, from_k, from_s1, from_c1b, from_x0, from_x1, from_x1b = range(16, 34, 2)
    from_near, from_two, from_four, from_eight = range(34, 42, 2)
    from_s2 = 42
    sender_x, sender_x1, sender_x1b, sender_two, sender_four, sender_eight, sender_z = range(0, 14, 2)
    sender_corner, sender_far = 14, 18

    def pack(tiles):
        rows = tiles[0].shape[0]
        group = lanes(rows) // 16
        packed = jnp.zeros((rows, LANES), F32)
        for at, tile in enumerate(tiles):
            packed = jnp.where(group == at, pltpu.roll(tile, (16 * at + 8) % LANES, 1), packed)
        return packed

    def unpack(packed, at):
        return pltpu.roll(packed, (2 * LANES - (16 * at + 8)) % LANES, 1)

    def pack_side(ref, half, side):
        group = lanes(8) // 8
        packed = None
        for layer in range(4):
            for part in range(4):
                at = 4 * layer + part
                tile = ref[0, 4 + 4 * half + layer, pl.ds(8 * part, 8), :]
                tile = pltpu.roll(tile, (8 * at + 8 * side) % LANES, 1)
                packed = tile if at == 0 else jnp.where(group == at, tile, packed)
        return packed

    def restrict_0(ref):
        out = []
        for layer in range(4):
            total = None
            for dx in range(2):
                for dy in range(2):
                    term = ref[0, 4 + 2 * layer + dx, pl.ds(dy, 16, stride=2), :]
                    total = term if total is None else total + term
            total = total + pltpu.roll(total, LANES - 1, 1)
            out.append(0.125 * jnp.take_along_axis(total, (2 * lanes(16) + 64) % LANES, axis=1))
        return out

    odd_8 = lanes(8) % 2 == 1

    def pairs_1(ref):
        out = []
        for layer in range(2):
            total = None
            for dx in range(2):
                for dy in range(2):
                    term = ref[0, 5 + 2 * layer + dx, pl.ds(dy, 8, stride=2), :]
                    total = term if total is None else total + term
            total = total + jnp.where(odd_8, pltpu.roll(total, 1, 1), pltpu.roll(total, LANES - 1, 1))
            out.append(0.125 * total)
        return jnp.where(odd_8, out[1], out[0])

    def squeeze_1(layers, ref, row):
        for part in range(2):
            ref[pl.ds(row + 16 * part, 16), :] = jnp.where(lanes(16) < 64, layers[part], layers[part + 2])

    pl.semaphore_wait(barrier, greeted)

    @for_sides
    def send_faces(side, dw):
        send(from_c + 1 - side, coef.at[pl.ds(4 * side, 4)], c0.at[0, pl.ds(12 - 12 * side, 4)], dw, 0, 128, sender_x + side)
        send(from_s + 1 - side, rhs.at[7 * side], s0.at[0, 12 - 9 * side], dw, 0, 32, sender_x + side)

    def squeeze_halves(first, second):
        low_quarter = lanes(16) % 64 < 32
        return (
            jnp.where(low_quarter, pltpu.roll(first, 96, 1), second),
            jnp.where(low_quarter, first, pltpu.roll(second, 32, 1)),
        )

    load_c.wait()
    own_c1 = restrict_0(c0)
    for side in range(2):
        squeeze_1(own_c1, zs.at[side], 32)
        for half in range(2):
            zs[side, pl.ds(16 * half, 8), :] = pack_side(c0, half, side)
    load_s.wait()
    for side in range(2):
        for half in range(2):
            zs[side, pl.ds(16 * half + 8, 8), :] = pack_side(s0, half, side)

    for_sides_z(
        lambda side, dn: send(from_z + 1 - side, zs.at[side], rz.at[1 - side], 0, dn, 64, sender_z + side)
    )

    def send_corner(group, src, dst, rows, side, side_z):
        at = 2 * side + side_z
        send(group + 3 - at, src, dst, 2 * side - 1, 2 * side_z - 1, rows, sender_corner + at)

    @for_corners
    def send_c_corner(side, side_z, dw, dn):
        src = zs.at[side_z, pl.ds(16 * side, 16)]
        send_corner(from_c_corner, src, rcn.at[1 - side, 1 - side_z], 16, side, side_z)

    @for_sides
    def send_s_next(side, dw):
        src = rhs.at[pl.ds(1 + 4 * side, 2)]
        send(from_s_next + 1 - side, src, s0.at[0, pl.ds(13 - 12 * side, 2)], dw, 0, 64, sender_x + side)

    def fill_0(ref, first, from_left, from_right):
        low = lanes(8) < 64
        for layer in range(4):
            for part in range(4):
                at = 4 * layer + part
                ref[1, first + layer, pl.ds(8 * part, 8), :] = jnp.where(
                    low, pltpu.roll(from_right, (LANES - 8 * at) % LANES, 1), pltpu.roll(from_left, (120 - 8 * at) % LANES, 1)
                )

    steps = cheb(3)
    receive_sides_z(from_z, 64)
    for field, ref in enumerate((c0, s0)):
        for half in range(2):
            rows = pl.ds(16 * half + 8 * field, 8)
            fill_0(ref, 4 + 4 * half, rz[0, rows, :], rz[1, rows, :])
    level_0.setup(5, 10, 3, 2)
    level_0.start(5, 10, 6, 2, steps[0][1])
    level_0.sweep(level_0.va, level_0.vb, 6, 9, 4, 2, 2, steps[1], fresh=True)
    level_0.sweep(level_0.vb, level_0.va, 7, 8, 2, 2, 2, steps[2])

    def spread_1(ref, block):
        at_lane = lanes(16)
        low_half = at_lane < 64
        low_quarter = at_lane % 64 < 32
        for part in range(2):
            before, own, after = (block(dz, part) for dz in (-1, 0, 1))
            near = jnp.where(low_quarter, before, after)
            outer = jnp.where(low_quarter, after, before)
            own_r, near_r, outer_r = (pltpu.roll(t, 64, 1) for t in (own, near, outer))
            at = 5 + part
            for at, own_a, own_b, near_a, near_b, outer_a, outer_b in (
                (at, own, own_r, near, near_r, outer, outer_r),
                (at + 2, own_r, own, near_r, near, outer_r, outer),
            ):
                centre = jnp.where(low_half, own_a, own_b)
                ref[0, at] = jnp.where(at_lane < 32, near_a, jnp.where(at_lane < 96, centre, near_b))
                ref[1, at] = jnp.where(low_half, outer_a, outer_b)

    def coef_block(dz, part):
        rows = pl.ds(32 + 16 * part, 16)
        return zs[0, rows, :] if dz == 0 else rz[(1 + dz) // 2, rows, :]

    spread_1(level_1.c, coef_block)
    rc2[REACH] = pairs_1(level_1.c)

    @for_sides
    def send_near(side, dw):
        send(from_near + 1 - side, rc2.at[REACH], rc2.at[REACH - dw], dw, 0, 8, sender_x + side)

    k1_own = zs.at[0, pl.ds(32, 32)]
    halves = squeeze_halves(zs[0, pl.ds(32, 16), :], zs[0, pl.ds(48, 16), :])
    at_lane = lanes(16)
    for side in range(2):
        near, far = (0, 3) if side == 0 else (3, 0)
        full = level_1.c[0, 5 + near]
        place = (32 * far + 31, 32 * far)
        cell = (64, 63)
        for side_z in range(2):
            moved = pltpu.roll(full, (place[side_z] - cell[side_z]) % LANES, 1)
            kp[side, side_z] = jnp.where(at_lane == place[side_z], moved, halves[side_z])
    for_sides(
        lambda side, dw: send(from_k + 1 - side, k1_own, k1cx.at[1 - side], dw, 0, 32, sender_x + side)
    )
    for_corners(
        lambda side, side_z, dw, dn: send_corner(
            from_k_corner, kp.at[side, side_z], k1c.at[1 - side, 1 - side_z], 16, side, side_z
        )
    )

    receive_sides(from_c, 128)
    receive_corners(from_c_corner, 16)
    for field, ref in enumerate((c0, s0)):
        for side in range(2):
            rows = pl.ds(8 * field, 8)
            fill_0(ref, 12 * side, rcn[side, 0, rows, :], rcn[side, 1, rows, :])
    level_0.setup_below(1, 2)
    over_sides(1, 11, 4, lambda at: level_0.setup_at(at, 2))
    receive_sides(from_s, 32)
    sweep_a = (level_0.va, level_0.vb, 2, 2, steps[1], True)
    sweep_b = (level_0.vb, level_0.va, 2, 2, steps[2], False)
    over_sides(3, 11, 2, lambda at: level_0.start_at(at, 2, steps[0][1]))
    over_sides(4, 10, 2, lambda at: level_0.sweep_at(at, *sweep_a))
    over_sides(5, 9, 2, lambda at: level_0.sweep_at(at, *sweep_b))
    level_0.residual(level_0.va, level_0.vb, 6, 9, 4, 2)
    receive_sides(from_near, 8)

    @functools.partial(if_reach, 2)
    def send_two(side, sign):
        src = rc2.at[pl.ds(REACH - side, 2)] if side == 1 else rc2.at[pl.ds(REACH, 2)]
        dst = rc2.at[pl.ds(REACH - 3, 2)] if side == 1 else rc2.at[pl.ds(REACH + 2, 2)]
        send(from_two + 1 - side, src, dst, 2 * sign, 0, 16, sender_two + side)

    receive_sides(from_s_next, 64)
    over_sides(1, 13, 2, lambda at: level_0.start_at(at, 2, steps[0][1]))
    over_sides(2, 12, 2, lambda at: level_0.sweep_at(at, *sweep_a))
    over_sides(3, 11, 2, lambda at: level_0.sweep_at(at, *sweep_b))
    over_sides(4, 10, 2, lambda at: level_0.residual_at(at, level_0.va, level_0.vb, 2))

    squeeze_1(restrict_0(level_0.vb), sk, 0)

    sp[0], sp[1] = squeeze_halves(sk[pl.ds(0, 16), :], sk[pl.ds(16, 16), :])

    for_sides(lambda side, dw: send(from_s1 + 1 - side, sk, k1x.at[1 - side], dw, 0, 32, sender_x + side))
    for_corners(
        lambda side, side_z, dw, dn: send_corner(
            from_s1_corner, sp.at[side_z], k1p.at[1 - side, 1 - side_z], 16, side, side_z
        )
    )
    for_sides_z(lambda side, dn: send(from_s1z + 1 - side, sk, k1z.at[1 - side], 0, dn, 32, sender_z + side))

    if_reach(2, lambda side, sign: receive(from_two + side, 16))

    @functools.partial(if_reach, 4)
    def send_four(side, sign):
        src = rc2.at[pl.ds(REACH - 3, 4)] if side == 1 else rc2.at[pl.ds(REACH, 4)]
        dst = rc2.at[pl.ds(REACH - 7, 4)] if side == 1 else rc2.at[pl.ds(REACH + 4, 4)]
        send(from_four + 1 - side, src, dst, 4 * sign, 0, 32, sender_four + side)

    for side in range(2):
        first = 9 if side == 0 else 5
        tiles = []
        for layer in range(2):
            sb0[side, pl.ds(32 * layer, 32), :] = level_0.va[0, first + layer]
            for part in range(4):
                tiles.append(level_0.va[1, first + layer, pl.ds(8 * part, 8), :])
        sb0[side, pl.ds(64, 8), :] = pack(tiles)

    @for_sides
    def send_iterate_0(side, dw):
        send(from_x0 + 1 - side, sb0.at[1 - side], hx0.at[1 - side], dw, 0, 72, sender_x + side)

    def source_block(dz, part):
        rows = pl.ds(16 * part, 16)
        return sk[rows, :] if dz == 0 else k1z[(1 + dz) // 2, rows, :]

    def spread_beside(ref, blocks, packs):
        at_lane = lanes(16)
        low_half = at_lane < 64
        for side in range(2):
            for layer in range(4):
                own = blocks[side, pl.ds(16 * (layer % 2), 16), :]
                other = pltpu.roll(own, 64, 1)
                centre = jnp.where(low_half, own, other) if layer < 2 else jnp.where(low_half, other, own)
                before = pltpu.roll(packs[side, 0], (LANES - 32 * layer) % LANES, 1)
                after = pltpu.roll(packs[side, 1], (LANES + 96 - 32 * layer) % LANES, 1)
                ref[0, 1 + 8 * side + layer] = jnp.where(at_lane < 32, before, jnp.where(at_lane < 96, centre, after))

    receive_sides(from_k, 32)
    receive_corners(from_k_corner, 16)
    spread_beside(level_1.c, k1cx, k1c)
    for side in range(2):
        far = 3 if side == 1 else 0
        below, above = (pltpu.roll(k1c[side, side_z], (shift - 32 * far) % LANES, 1)
                        for side_z, shift in ((0, 127), (1, -31)))
        level_1.c[1, 4 + 5 * side] = jnp.where(lanes(16) < 64, above, below)

    @for_sides
    def send_coef_1(side, dw):
        send(from_c1b + 1 - side, level_1.c.at[0, 9 - 5 * side], level_1.c.at[0, 13 - 13 * side], dw, 0, 16, sender_x + side)

    level_1.setup_below(2, 1)
    over_sides(2, 10, 2, lambda at: level_1.setup_at(at, 1))
    over_layers(4, 9, 6, lambda at: level_1.setup_at(at, 2))

    receive_sides_z(from_s1z, 32)
    spread_1(level_1.s, source_block)
    receive_sides(from_s1, 32)
    receive_corners(from_s1_corner, 16)
    spread_beside(level_1.s, k1x, k1p)
    level_1.start(2, 11, 10, 1, steps[0][1])
    over_layers(5, 8, 4, lambda at: level_1.start_outer(at, steps[0][1]))
    over_sides(3, 9, 2, lambda at: level_1.sweep_at(at, level_1.va, level_1.vb, 1, 1, steps[1], True))
    over_layers(5, 8, 4, lambda at: level_1.sweep_at(at, level_1.va, level_1.vb, 2, 1, steps[1], True))
    level_1.sweep(level_1.vb, level_1.va, 4, 9, 6, 1, 1, steps[2])
    level_1.residual(level_1.va, level_1.vb, 5, 8, 4, 1)

    value = pairs_1(level_1.vb)
    s2m[...] = value
    rs2[REACH] = value
    if_reach(4, lambda side, sign: receive(from_four + side, 32))
    for_far(1, lambda slot, dw: send(from_s2 + 2 * REACH - slot, s2m, rs2.at[2 * REACH - slot], dw, 0, 8, sender_far + slot))

    @functools.partial(if_reach, REACH)
    def send_eight(side, sign):
        send(from_eight + 1 - side, rc2.at[REACH], rc2.at[REACH - sign * REACH], REACH * sign, 0, 8, sender_eight + side)

    @for_sides
    def send_iterate_1(side, dw):
        send(from_x1 + 1 - side, level_1.va.at[0, pl.ds(6 - side, 3)], rx1.at[1 - side], dw, 0, 48, sender_x1 + side)

    for side in range(2):
        @pl.when(reach[side] >= 2)
        def send_next_1():
            layer = level_1.va.at[0, 5 + 3 * side]
            send(from_x1b + 1 - side, layer, rx1b.at[1 - side], 4 * side - 2, 0, 16, sender_x1b + side)

    receive_sides(from_c1b, 16)
    level_1.setup_below(1, 1)
    over_sides(1, 12, 1, lambda at: level_1.setup_at(at, 1))

    def spread_2(ref, blocks):
        for block in range(2 * REACH + 1):
            packed = blocks[block]
            ref[0, 2 * block] = jnp.where(odd_8, pltpu.roll(packed, 1, 1), packed)
            ref[0, 2 * block + 1] = jnp.where(odd_8, packed, pltpu.roll(packed, LANES - 1, 1))

    def restrict_2(ref, at):
        total = ref[0, 2 * at + 2] + ref[0, 2 * at + 3]
        odd_row = lax.broadcasted_iota(jnp.int32, (8, LANES), 0) % 2 == 1
        total = total + jnp.where(odd_row, pltpu.roll(total, 1, 0), pltpu.roll(total, 7, 0))
        second = lanes(8) % 4 >= 2
        total = total + jnp.where(second, pltpu.roll(total, 2, 1), pltpu.roll(total, LANES - 2, 1))
        return 0.125 * total

    if_reach(REACH, lambda side, sign: receive(from_eight + side, 8))
    spread_2(level_2.c, rc2)
    level_2.setup(1, 32, 8, 1)
    for at in range(15):
        level_3.c[0, at] = restrict_2(level_2.c, at)
    level_3.setup(1, 13, 13, 1)

    receive_far(from_s2)
    spread_2(level_2.s, rs2)
    level_2.start(1, 32, 32, 1, steps[0][1])
    level_2.sweep(level_2.va, level_2.vb, 2, 31, 15, 1, 1, steps[1], fresh=True)
    level_2.sweep(level_2.vb, level_2.va, 3, 30, 14, 1, 1, steps[2])
    level_2.residual(level_2.va, level_2.vb, 4, 29, 13, 1)

    for at in range(1, 14):
        level_3.s[0, at] = restrict_2(level_2.vb, at)
    coarse = cheb(4)
    level_3.start(1, 13, 13, 1, coarse[0][1])
    level_3.sweep(level_3.va, level_3.vb, 2, 12, 11, 1, 1, coarse[1], fresh=True)
    level_3.sweep(level_3.vb, level_3.va, 3, 11, 9, 1, 1, coarse[2])
    level_3.sweep(level_3.va, level_3.vb, 4, 10, 7, 1, 1, coarse[3])

    for at in range(10, 24):
        level_2.vb[0, at] = level_2.va[0, at] + level_3.vb[0, (at - 2) // 2]
    level_2.sweep(level_2.vb, level_2.va, 11, 22, 12, 1, 1, steps[0], fresh=True)
    level_2.sweep(level_2.va, level_2.vb, 12, 21, 10, 1, 1, steps[1])
    level_2.sweep(level_2.vb, level_2.va, 13, 20, 8, 1, 1, steps[2])

    for at in range(8):
        value = level_2.va[0, 13 + at]
        for part in range(2):
            p1[at, pl.ds(part, 8, stride=2), :] = value
    receive_sides(from_x1, 48)
    for side in range(2):
        pl.when(reach[side] >= 2)(functools.partial(receive, from_x1b + side, 16))
    for at in range(14):
        if 4 <= at <= 9:
            before = level_1.va[0, at]
        else:
            before = rx1b[0] if at == 0 else rx1[0, at - 1] if at < 4 else rx1[1, at - 10] if at < 13 else rx1b[1]
        level_1.vb[0, at] = before + p1[(at + 1) // 2]
    for side in range(2):
        pl.when(has[side])(functools.partial(sends_done, sender_x1 + side))
        pl.when(reach[side] >= 2)(functools.partial(sends_done, sender_x1b + side))
    level_1.sweep(level_1.vb, level_1.va, 1, 12, 12, 1, 1, steps[0], fresh=True)
    level_1.sweep(level_1.va, level_1.vb, 2, 11, 10, 1, 1, steps[1])
    level_1.sweep(level_1.vb, level_1.va, 3, 10, 8, 1, 1, steps[2])

    fine_lane = lanes(16) // 2
    for at in range(8):
        value = level_1.va[0, 3 + at]
        for k in range(2):
            fine = jnp.take_along_axis(value, (fine_lane + (32 if k == 0 else 96)) % LANES, axis=1)
            for part in range(2):
                p0[k, at, pl.ds(part, 16, stride=2), :] = fine
    receive_sides(from_x0, 72)
    for side in range(2):
        packed = hx0[side, pl.ds(64, 8), :]
        for layer in range(2):
            at = (1 if side == 0 else 13) + layer
            coarse_at = (at - 4) // 2 + 2
            level_0.vb[0, at] = hx0[side, pl.ds(32 * layer, 32), :] + p0[0, coarse_at]
            for part in range(4):
                rows = pl.ds(8 * part, 8)
                level_0.vb[1, at, rows, :] = (
                    unpack(packed, 4 * layer + part) * level_0.lane_mask[1][:8] + p0[1, coarse_at, rows, :]
                )

    def correct(at):
        for k in range(2):
            level_0.vb[k, at] = level_0.va[k, at] + p0[k, at // 2]

    over_layers(3, 12, 5, correct)
    level_0.sweep(level_0.vb, level_0.va, 2, 13, 4, 2, 2, steps[0], fresh=True)
    level_0.sweep(level_0.va, level_0.vb, 3, 12, 5, 2, 2, steps[1])
    level_0.finish(level_0.vb, level_0.va, kept, added, 4, 11, 4, steps[2])

    for_sides(lambda side, dw: sends_done(sender_x + side))
    for_sides_z(lambda side, dn: sends_done(sender_z + side))
    for_corners(lambda side, side_z, dw, dn: sends_done(sender_corner + 2 * side + side_z))
    if_reach(2, lambda side, sign: sends_done(sender_two + side))
    if_reach(4, lambda side, sign: sends_done(sender_four + side))
    if_reach(REACH, lambda side, sign: sends_done(sender_eight + side))
    for_far(1, lambda slot, dw: ruled(8, 0, sender_far + slot).wait_send())


def per_device(right_side, conductivity, wide, narrow):
    brick = (8, 32, LANES)
    scratch = []
    for shape in LEVEL_SHAPES:
        scratch += [pltpu.VMEM(shape, F32)] * LEVEL_FIELDS
    shapes = [
        (2, 64, LANES), (2, 64, LANES), (2, 2, 16, LANES),
        (2, 2, 16, LANES), (2, 32, LANES), (2, 2, 16, LANES),
        (32, LANES), (2, 16, LANES), (2, 32, LANES), (2, 2, 16, LANES), (2, 32, LANES),
        (2 * REACH + 1, 8, LANES), (8, LANES), (2 * REACH + 1, 8, LANES),
        (2, 3, 16, LANES), (2, 16, LANES),
        (2, 72, LANES), (2, 72, LANES),
        (8, 16, LANES), (2, 8, 32, LANES),
        (RULER, LANES),
    ]
    scratch += [pltpu.VMEM(shape, F32) for shape in shapes]
    scratch += [pltpu.SemaphoreType.DMA((2,)), pltpu.SemaphoreType.DMA((SENDERS,)), pltpu.SemaphoreType.DMA((GROUPS,))]
    kept, added = pl.pallas_call(
        functools.partial(kernel, wide, narrow),
        out_shape=[jax.ShapeDtypeStruct(brick, F32)] * 2,
        in_specs=[pl.BlockSpec(memory_space=pltpu.HBM)] * 2,
        out_specs=[pl.BlockSpec(memory_space=pltpu.VMEM)] * 2,
        scratch_shapes=scratch,
        compiler_params=pltpu.CompilerParams(
            collective_id=0, has_side_effects=True, vmem_limit_bytes=32 * 1024 * 1024
        ),
    )(pltpu.with_memory_space_constraint(right_side, pltpu.HBM), pltpu.with_memory_space_constraint(conductivity, pltpu.HBM))
    return kept + added


def solution(mesh):
    spec = P("wide", None, "narrow")
    body = functools.partial(per_device, wide=mesh.shape["wide"], narrow=mesh.shape["narrow"])
    return jax.shard_map(body, mesh=mesh, in_specs=(spec, spec), out_specs=spec, check_vma=False)
```

```python
import functools

import jax
import jax.numpy as jnp
from jax import lax
from jax.experimental import pallas as pl
from jax.experimental.pallas import tpu as pltpu
from jax.sharding import PartitionSpec as P

CENTER = 1.125
HALF = 0.875
LANES = 128
REACH = 8
HALF_REACH = 4
F32 = jnp.float32
MESH_ID = pl.DeviceIdType.MESH


def cheb(sweeps):
    sigma = CENTER / HALF
    steps = [(0.0, 1.0 / CENTER)]
    ratio = 1.0 / sigma
    for _ in range(sweeps - 1):
        ratio_next = 1.0 / (2.0 * sigma - ratio)
        steps.append((ratio_next * ratio, 2.0 * ratio_next / HALF))
        ratio = ratio_next
    return steps


def over_sides(first, second, count, body):
    for base in (first, second):
        for at in range(count):
            body(base + at)


def over_layers(low, high, unroll, body):
    count = high - low + 1
    if count == unroll:
        for at in range(low, high + 1):
            body(at)
        return

    def block(step, carry):
        for at in range(unroll):
            body(low + step * unroll + at)
        return carry

    lax.fori_loop(0, count // unroll, block, 0)


class Level:
    def __init__(self, refs, scale, rows, row_step, lane_step, base, extent, lane_mask):
        self.c, self.s, self.cx, self.cy, self.cz, self.iv, self.dg, self.va, self.vb = refs
        self.half = 0.5 * scale
        self.rows, self.row_step, self.lane_step = rows, row_step, lane_step
        self.base, self.extent, self.lane_mask = base, extent, lane_mask

    def inside(self, at):
        where_x = self.base + at
        return jnp.where((where_x >= 0) & (where_x < self.extent), 1.0, 0.0).astype(F32)

    def lane(self):
        return lax.broadcasted_iota(jnp.int32, (self.rows, LANES), 1)

    def row(self):
        return lax.broadcasted_iota(jnp.int32, (self.rows, LANES), 0)

    def y_up(self, tile):
        return pltpu.roll(tile, self.rows - self.row_step, 0)

    def y_down(self, tile):
        return pltpu.roll(tile, self.row_step, 0)

    def turned(self, tiles, shift, edge, count):
        out = [pltpu.roll(t, shift, 1) for t in tiles]
        if len(tiles) == 1:
            return out
        at_edge = self.lane() == edge
        return [jnp.where(at_edge, out[1 - k], out[k]) for k in range(count)]

    def z_up(self, tiles, count):
        return self.turned(tiles, LANES - self.lane_step, LANES - 1, count)

    def z_down(self, tiles, count):
        return self.turned(tiles, self.lane_step, 0, count)

    def masked(self, at, tiles):
        keep = self.inside(at) * self.half
        out = []
        for k in range(tiles):
            mask = self.lane_mask[k]
            out.append(self.c[k, at] * (keep if mask is None else mask * keep))
        return out

    def setup_below(self, low, tiles):
        first, second = self.masked(low - 1, tiles), self.masked(low, tiles)
        for k in range(tiles):
            self.cx[k, low - 1] = first[k] + second[k]

    def setup_at(self, at, tiles):
        before, here, after = self.masked(at - 1, tiles), self.masked(at, tiles), self.masked(at + 1, tiles)
        inside = self.inside(at)
        top = self.row() >= self.rows - self.row_step
        bottom = self.row() < self.row_step
        z_up, z_down = self.z_up(here, tiles), self.z_down(here, tiles)
        for k in range(tiles):
            own = here[k]
            x_low = before[k] + own
            x_high = own + after[k]
            y_low = own + jnp.where(bottom, 0.0, self.y_down(own))
            y_high = own + jnp.where(top, 0.0, self.y_up(own))
            z_low = own + z_down[k]
            z_high = own + z_up[k]
            diagonal = x_low + x_high + y_low + y_high + z_low + z_high
            keep = inside if self.lane_mask[k] is None else self.lane_mask[k] * inside
            self.cx[k, at] = x_high
            self.cy[k, at] = jnp.where(top, 0.0, y_high)
            self.cz[k, at] = z_high
            if k == 0:
                self.dg[0, at] = diagonal
            self.iv[k, at] = jnp.where(jnp.full_like(own, 0.0) + keep > 0.5, 1.0 / diagonal, 0.0)

    def setup(self, low, high, unroll, tiles):
        self.setup_below(low, tiles)
        over_layers(low, high, unroll, lambda at: self.setup_at(at, tiles))

    def start_at(self, at, tiles, beta):
        for k in range(tiles):
            self.va[k, at] = self.s[k, at] * self.iv[k, at] * beta

    def start_outer(self, at, beta):
        self.va[1, at] = self.s[1, at] * self.iv[1, at] * beta

    def start(self, low, high, unroll, tiles, beta):
        over_layers(low, high, unroll, lambda at: self.start_at(at, tiles, beta))

    def around(self, field, at, tiles, count):
        here = [field[k, at] for k in range(tiles)]
        cz = [self.cz[k, at] for k in range(tiles)]
        z_up = self.z_up(here, count)
        z_down = self.z_down([cz[k] * here[k] for k in range(tiles)], count)
        sums = []
        for k in range(count):
            cy = self.cy[k, at]
            total = self.cx[k, at] * field[k, at + 1] + self.cx[k, at - 1] * field[k, at - 1]
            total = total + (cy * self.y_up(here[k]) + self.y_down(cy * here[k]))
            total = total + (cz[k] * z_up[k] + z_down[k])
            sums.append(total + self.s[k, at])
        return here, sums

    def sweep_at(self, at, field, result, tiles, count, step, fresh):
        alpha, beta = step
        here, sums = self.around(field, at, tiles, count)
        for k in range(count):
            kept = (1.0 + alpha - beta) * here[k]
            if not fresh:
                kept = kept - alpha * result[k, at]
            result[k, at] = kept + (beta * self.iv[k, at]) * sums[k]

    def sweep(self, field, result, low, high, unroll, tiles, count, step, fresh=False):
        over_layers(low, high, unroll, lambda at: self.sweep_at(at, field, result, tiles, count, step, fresh))

    def residual_at(self, at, field, result, tiles):
        here, sums = self.around(field, at, tiles, 1)
        result[0, at] = sums[0] - self.dg[0, at] * here[0]

    def residual(self, field, result, low, high, unroll, tiles):
        over_layers(low, high, unroll, lambda at: self.residual_at(at, field, result, tiles))

    def finish(self, field, older, kept_out, added_out, low, high, unroll, step):
        alpha, beta = step

        def body(at):
            here, sums = self.around(field, at, 2, 1)
            kept_out[at - low] = (1.0 + alpha - beta) * here[0] - alpha * older[0, at]
            added_out[at - low] = (beta * self.iv[0, at]) * sums[0]

        over_layers(low, high, unroll, body)


LEVEL_FIELDS = 9
LEVEL_SHAPES = ((2, 16, 32, LANES), (2, 14, 16, LANES), (1, 34, 8, LANES), (1, 15, 8, LANES))
RULER = 1024
SENDERS = 14 + 2 * (2 * REACH + 1)
GROUPS = 36 + 2 * (2 * REACH + 1)


def kernel(wide, narrow, rhs, coef, kept, added, *scratch):
    scratch = list(scratch)
    level_refs = []
    for _ in range(4):
        level_refs.append(scratch[:LEVEL_FIELDS])
        scratch = scratch[LEVEL_FIELDS:]
    (zs, rz, rcn, kp, k1cx, k1c, sk, sp, k1x, k1p, k1z, rc2, s2m, rs2, rx1, rx1b, sb0, hx0, p1, p0, ruler,
     local_sem, send_sem, recv_sem) = scratch
    me_w = lax.axis_index("wide")
    me_n = lax.axis_index("narrow")

    def there(dw, dn):
        return (lax.rem(me_w + (dw + wide), wide), lax.rem(me_n + (dn + narrow), narrow))

    has = (me_w > 0, me_w < wide - 1)
    has_z = (me_n > 0, me_n < narrow - 1)
    reach = (jnp.minimum(me_w, REACH), jnp.minimum(wide - 1 - me_w, REACH))

    def for_far(first, body, last=REACH):
        for side in range(2):
            sign = 2 * side - 1

            def step(k, carry):
                body(REACH + sign * k, sign * k)
                return carry

            lax.fori_loop(first, jnp.minimum(reach[side], last) + 1, step, 0)

    def for_sides(body):
        for side in range(2):
            pl.when(has[side])(functools.partial(body, side, 2 * side - 1))

    def for_sides_z(body):
        for side in range(2):
            pl.when(has_z[side])(functools.partial(body, side, 2 * side - 1))

    def for_corners(body):
        for side in range(2):
            for side_z in range(2):
                pl.when(has[side] & has_z[side_z])(
                    functools.partial(body, side, side_z, 2 * side - 1, 2 * side_z - 1)
                )

    @pl.when((me_n == 0) | (me_n == narrow - 1))
    def clear_z():
        for ref in (rz, rcn, k1c, k1z, k1p):
            ref[...] = jnp.zeros(ref.shape, F32)

    @pl.when((me_w < REACH) | (me_w >= wide - REACH))
    def clear():
        def zero(ref):
            ref[...] = jnp.zeros(ref.shape, F32)

        for ref in (rcn, rx1, rx1b, hx0, rc2, rs2, k1cx, k1c, k1x, k1p):
            zero(ref)
        for side in range(2):
            for ref in level_refs[0][:2]:
                zero(ref.at[0, pl.ds(12 * side, 4)])
            zero(level_refs[1][0].at[0, 13 * side])

    def if_reach(least, body):
        for side in range(2):
            pl.when(reach[side] >= least)(functools.partial(body, side, 2 * side - 1))

    barrier = pltpu.get_barrier_semaphore()

    def greet(dw, dn):
        pl.semaphore_signal(barrier, inc=1, device_id=there(dw, dn), device_id_type=MESH_ID)

    for_far(1, lambda slot, dw: greet(dw, 0), HALF_REACH)
    for_sides_z(lambda side, dn: greet(0, dn))
    for_corners(lambda side, side_z, dw, dn: greet(dw, dn))

    c0, s0 = level_refs[0][0], level_refs[0][1]
    load_c = pltpu.make_async_copy(coef, c0.at[0, pl.ds(4, 8)], local_sem.at[0])
    load_s = pltpu.make_async_copy(rhs, s0.at[0, pl.ds(4, 8)], local_sem.at[1])
    load_c.start()
    load_s.start()
    beside_x = jnp.where(has[0], 1, 0) + jnp.where(has[1], 1, 0)
    beside_z = jnp.where(has_z[0], 1, 0) + jnp.where(has_z[1], 1, 0)
    greeted = beside_z + beside_x * beside_z
    for side in range(2):
        greeted = greeted + jnp.minimum(reach[side], HALF_REACH)

    left = jnp.where(me_n > 0, 1.0, 0.0).astype(F32)
    right = jnp.where(me_n < narrow - 1, 1.0, 0.0).astype(F32)

    def lanes(rows):
        return lax.broadcasted_iota(jnp.int32, (rows, LANES), 1)

    def edges(rows, until, low, since, high):
        at = lanes(rows)
        return jnp.where(at < until, low, jnp.where(at >= since, high, 0.0))

    def centred(rows):
        at = lanes(rows)
        return jnp.where((at >= 32) & (at < 96), 1.0, edges(rows, 32, left, 96, right))

    level_0 = Level(level_refs[0], 1.0, 32, 1, 1, 8 * me_w - 4, 8 * wide, [None, edges(32, 8, right, 120, left)])
    level_1 = Level(
        level_refs[1], 0.25, 16, 1, 1, 4 * me_w - 5, 4 * wide, [centred(16), edges(16, 32, right, 96, left)]
    )
    level_2 = Level(level_refs[2], 0.0625, 8, 1, 2, 2 * me_w - 16, 2 * wide, [centred(8)])
    level_3 = Level(level_refs[3], 0.015625, 8, 2, 4, me_w - 7, wide, [centred(8)])

    sent = [0] * SENDERS

    def send(group, src, dst, dw, dn, rows, sender):
        if isinstance(sender, int):
            sent[sender] += rows
        pltpu.make_async_remote_copy(
            src_ref=src, dst_ref=dst, send_sem=send_sem.at[sender], recv_sem=recv_sem.at[group],
            device_id=there(dw, dn), device_id_type=MESH_ID,
        ).start()

    def ruled(rows, group, sender):
        span = ruler.at[pl.ds(0, rows)]
        return pltpu.make_async_remote_copy(
            src_ref=span, dst_ref=span, send_sem=send_sem.at[sender], recv_sem=recv_sem.at[group],
            device_id=there(0, 1), device_id_type=MESH_ID,
        )

    def receive(group, rows):
        ruled(rows, group, 0).wait_recv()

    def receive_sides(group, rows):
        for_sides(lambda side, dw: receive(group + side, rows))

    def receive_sides_z(group, rows):
        for_sides_z(lambda side, dn: receive(group + side, rows))

    def receive_corners(group, rows):
        for_corners(lambda side, side_z, dw, dn: receive(group + 2 * side + side_z, rows))

    def receive_far(group, last=REACH):
        for_far(1, lambda slot, dw: receive(group + slot, 8), last)

    def sends_done(sender):
        ruled(sent[sender], 0, sender).wait_send()

    from_z, from_s1z = 0, 2
    from_c_corner, from_k_corner, from_s1_corner = 4, 8, 12
    from_c, from_s, from_s_next, from_k, from_s1, from_c1b, from_x0, from_x1, from_x1b = range(16, 34, 2)
    from_four = 34
    from_c2 = 36
    from_s2 = from_c2 + 2 * REACH + 1
    sender_x, sender_x1, sender_x1b, sender_four, sender_z = range(0, 10, 2)
    sender_corner, sender_c2, sender_far = 10, 14, 14 + 2 * REACH + 1

    def pack(tiles):
        rows = tiles[0].shape[0]
        group = lanes(rows) // 16
        packed = jnp.zeros((rows, LANES), F32)
        for at, tile in enumerate(tiles):
            packed = jnp.where(group == at, pltpu.roll(tile, (16 * at + 8) % LANES, 1), packed)
        return packed

    def unpack(packed, at):
        return pltpu.roll(packed, (2 * LANES - (16 * at + 8)) % LANES, 1)

    def pack_side(ref, half, side):
        group = lanes(8) // 8
        packed = None
        for layer in range(4):
            for part in range(4):
                at = 4 * layer + part
                tile = ref[0, 4 + 4 * half + layer, pl.ds(8 * part, 8), :]
                tile = pltpu.roll(tile, (8 * at + 8 * side) % LANES, 1)
                packed = tile if at == 0 else jnp.where(group == at, tile, packed)
        return packed

    def restrict_0(ref):
        out = []
        for layer in range(4):
            total = None
            for dx in range(2):
                for dy in range(2):
                    term = ref[0, 4 + 2 * layer + dx, pl.ds(dy, 16, stride=2), :]
                    total = term if total is None else total + term
            total = total + pltpu.roll(total, LANES - 1, 1)
            out.append(0.125 * jnp.take_along_axis(total, (2 * lanes(16) + 64) % LANES, axis=1))
        return out

    odd_8 = lanes(8) % 2 == 1

    def pairs_1(ref):
        out = []
        for layer in range(2):
            total = None
            for dx in range(2):
                for dy in range(2):
                    term = ref[0, 5 + 2 * layer + dx, pl.ds(dy, 8, stride=2), :]
                    total = term if total is None else total + term
            total = total + jnp.where(odd_8, pltpu.roll(total, 1, 1), pltpu.roll(total, LANES - 1, 1))
            out.append(0.125 * total)
        return jnp.where(odd_8, out[1], out[0])

    def squeeze_1(layers, ref, row):
        for part in range(2):
            ref[pl.ds(row + 16 * part, 16), :] = jnp.where(lanes(16) < 64, layers[part], layers[part + 2])

    pl.semaphore_wait(barrier, greeted)

    @for_sides
    def send_faces(side, dw):
        send(from_c + 1 - side, coef.at[pl.ds(4 * side, 4)], c0.at[0, pl.ds(12 - 12 * side, 4)], dw, 0, 128, sender_x + side)
        send(from_s + 1 - side, rhs.at[7 * side], s0.at[0, 12 - 9 * side], dw, 0, 32, sender_x + side)

    def squeeze_halves(first, second):
        low_quarter = lanes(16) % 64 < 32
        return (
            jnp.where(low_quarter, pltpu.roll(first, 96, 1), second),
            jnp.where(low_quarter, first, pltpu.roll(second, 32, 1)),
        )

    load_c.wait()
    own_c1 = restrict_0(c0)
    for side in range(2):
        squeeze_1(own_c1, zs.at[side], 32)
        for half in range(2):
            zs[side, pl.ds(16 * half, 8), :] = pack_side(c0, half, side)
    load_s.wait()
    for side in range(2):
        for half in range(2):
            zs[side, pl.ds(16 * half + 8, 8), :] = pack_side(s0, half, side)

    for_sides_z(
        lambda side, dn: send(from_z + 1 - side, zs.at[side], rz.at[1 - side], 0, dn, 64, sender_z + side)
    )

    def send_corner(group, src, dst, rows, side, side_z):
        at = 2 * side + side_z
        send(group + 3 - at, src, dst, 2 * side - 1, 2 * side_z - 1, rows, sender_corner + at)

    @for_corners
    def send_c_corner(side, side_z, dw, dn):
        src = zs.at[side_z, pl.ds(16 * side, 16)]
        send_corner(from_c_corner, src, rcn.at[1 - side, 1 - side_z], 16, side, side_z)

    @for_sides
    def send_s_next(side, dw):
        src = rhs.at[pl.ds(1 + 4 * side, 2)]
        send(from_s_next + 1 - side, src, s0.at[0, pl.ds(13 - 12 * side, 2)], dw, 0, 64, sender_x + side)

    def fill_0(ref, first, from_left, from_right):
        low = lanes(8) < 64
        for layer in range(4):
            for part in range(4):
                at = 4 * layer + part
                ref[1, first + layer, pl.ds(8 * part, 8), :] = jnp.where(
                    low, pltpu.roll(from_right, (LANES - 8 * at) % LANES, 1), pltpu.roll(from_left, (120 - 8 * at) % LANES, 1)
                )

    steps = cheb(3)
    receive_sides_z(from_z, 64)
    for field, ref in enumerate((c0, s0)):
        for half in range(2):
            rows = pl.ds(16 * half + 8 * field, 8)
            fill_0(ref, 4 + 4 * half, rz[0, rows, :], rz[1, rows, :])
    level_0.setup(5, 10, 3, 2)
    level_0.start(5, 10, 6, 2, steps[0][1])
    level_0.sweep(level_0.va, level_0.vb, 6, 9, 4, 2, 2, steps[1], fresh=True)
    level_0.sweep(level_0.vb, level_0.va, 7, 8, 2, 2, 2, steps[2])

    def spread_1(ref, block):
        at_lane = lanes(16)
        low_half = at_lane < 64
        low_quarter = at_lane % 64 < 32
        for part in range(2):
            before, own, after = (block(dz, part) for dz in (-1, 0, 1))
            near = jnp.where(low_quarter, before, after)
            outer = jnp.where(low_quarter, after, before)
            own_r, near_r, outer_r = (pltpu.roll(t, 64, 1) for t in (own, near, outer))
            at = 5 + part
            for at, own_a, own_b, near_a, near_b, outer_a, outer_b in (
                (at, own, own_r, near, near_r, outer, outer_r),
                (at + 2, own_r, own, near_r, near, outer_r, outer),
            ):
                centre = jnp.where(low_half, own_a, own_b)
                ref[0, at] = jnp.where(at_lane < 32, near_a, jnp.where(at_lane < 96, centre, near_b))
                ref[1, at] = jnp.where(low_half, outer_a, outer_b)

    def coef_block(dz, part):
        rows = pl.ds(32 + 16 * part, 16)
        return zs[0, rows, :] if dz == 0 else rz[(1 + dz) // 2, rows, :]

    spread_1(level_1.c, coef_block)
    rc2[REACH] = pairs_1(level_1.c)

    for_far(
        1,
        lambda slot, dw: send(
            from_c2 + 2 * REACH - slot, rc2.at[REACH], rc2.at[2 * REACH - slot], dw, 0, 8, sender_c2 + slot
        ),
        HALF_REACH,
    )
    k1_own = zs.at[0, pl.ds(32, 32)]
    halves = squeeze_halves(zs[0, pl.ds(32, 16), :], zs[0, pl.ds(48, 16), :])
    at_lane = lanes(16)
    for side in range(2):
        near, far = (0, 3) if side == 0 else (3, 0)
        full = level_1.c[0, 5 + near]
        place = (32 * far + 31, 32 * far)
        cell = (64, 63)
        for side_z in range(2):
            moved = pltpu.roll(full, (place[side_z] - cell[side_z]) % LANES, 1)
            kp[side, side_z] = jnp.where(at_lane == place[side_z], moved, halves[side_z])
    for_sides(
        lambda side, dw: send(from_k + 1 - side, k1_own, k1cx.at[1 - side], dw, 0, 32, sender_x + side)
    )
    for_corners(
        lambda side, side_z, dw, dn: send_corner(
            from_k_corner, kp.at[side, side_z], k1c.at[1 - side, 1 - side_z], 16, side, side_z
        )
    )

    receive_sides(from_c, 128)
    receive_corners(from_c_corner, 16)
    for field, ref in enumerate((c0, s0)):
        for side in range(2):
            rows = pl.ds(8 * field, 8)
            fill_0(ref, 12 * side, rcn[side, 0, rows, :], rcn[side, 1, rows, :])
    level_0.setup_below(1, 2)
    over_sides(1, 11, 4, lambda at: level_0.setup_at(at, 2))
    receive_sides(from_s, 32)
    sweep_a = (level_0.va, level_0.vb, 2, 2, steps[1], True)
    sweep_b = (level_0.vb, level_0.va, 2, 2, steps[2], False)
    over_sides(3, 11, 2, lambda at: level_0.start_at(at, 2, steps[0][1]))
    over_sides(4, 10, 2, lambda at: level_0.sweep_at(at, *sweep_a))
    over_sides(5, 9, 2, lambda at: level_0.sweep_at(at, *sweep_b))
    level_0.residual(level_0.va, level_0.vb, 6, 9, 4, 2)
    receive_sides(from_s_next, 64)
    over_sides(1, 13, 2, lambda at: level_0.start_at(at, 2, steps[0][1]))
    over_sides(2, 12, 2, lambda at: level_0.sweep_at(at, *sweep_a))
    over_sides(3, 11, 2, lambda at: level_0.sweep_at(at, *sweep_b))
    over_sides(4, 10, 2, lambda at: level_0.residual_at(at, level_0.va, level_0.vb, 2))

    squeeze_1(restrict_0(level_0.vb), sk, 0)

    sp[0], sp[1] = squeeze_halves(sk[pl.ds(0, 16), :], sk[pl.ds(16, 16), :])

    for_sides(lambda side, dw: send(from_s1 + 1 - side, sk, k1x.at[1 - side], dw, 0, 32, sender_x + side))
    for_corners(
        lambda side, side_z, dw, dn: send_corner(
            from_s1_corner, sp.at[side_z], k1p.at[1 - side, 1 - side_z], 16, side, side_z
        )
    )
    for_sides_z(lambda side, dn: send(from_s1z + 1 - side, sk, k1z.at[1 - side], 0, dn, 32, sender_z + side))

    receive_far(from_c2, HALF_REACH)

    @functools.partial(if_reach, HALF_REACH)
    def send_four(side, sign):
        src, dst = rc2.at[pl.ds(9 - 5 * side, 4)], rc2.at[pl.ds(13 - 13 * side, 4)]
        send(from_four + 1 - side, src, dst, HALF_REACH * sign, 0, 32, sender_four + side)

    for side in range(2):
        first = 9 if side == 0 else 5
        tiles = []
        for layer in range(2):
            sb0[side, pl.ds(32 * layer, 32), :] = level_0.va[0, first + layer]
            for part in range(4):
                tiles.append(level_0.va[1, first + layer, pl.ds(8 * part, 8), :])
        sb0[side, pl.ds(64, 8), :] = pack(tiles)

    @for_sides
    def send_iterate_0(side, dw):
        send(from_x0 + 1 - side, sb0.at[1 - side], hx0.at[1 - side], dw, 0, 72, sender_x + side)

    def source_block(dz, part):
        rows = pl.ds(16 * part, 16)
        return sk[rows, :] if dz == 0 else k1z[(1 + dz) // 2, rows, :]

    def spread_beside(ref, blocks, packs):
        at_lane = lanes(16)
        low_half = at_lane < 64
        for side in range(2):
            for layer in range(4):
                own = blocks[side, pl.ds(16 * (layer % 2), 16), :]
                other = pltpu.roll(own, 64, 1)
                centre = jnp.where(low_half, own, other) if layer < 2 else jnp.where(low_half, other, own)
                before = pltpu.roll(packs[side, 0], (LANES - 32 * layer) % LANES, 1)
                after = pltpu.roll(packs[side, 1], (LANES + 96 - 32 * layer) % LANES, 1)
                ref[0, 1 + 8 * side + layer] = jnp.where(at_lane < 32, before, jnp.where(at_lane < 96, centre, after))

    receive_sides(from_k, 32)
    receive_corners(from_k_corner, 16)
    spread_beside(level_1.c, k1cx, k1c)
    for side in range(2):
        far = 3 if side == 1 else 0
        below, above = (pltpu.roll(k1c[side, side_z], (shift - 32 * far) % LANES, 1)
                        for side_z, shift in ((0, 127), (1, -31)))
        level_1.c[1, 4 + 5 * side] = jnp.where(lanes(16) < 64, above, below)

    @for_sides
    def send_coef_1(side, dw):
        send(from_c1b + 1 - side, level_1.c.at[0, 9 - 5 * side], level_1.c.at[0, 13 - 13 * side], dw, 0, 16, sender_x + side)

    level_1.setup_below(2, 1)
    over_sides(2, 10, 2, lambda at: level_1.setup_at(at, 1))
    over_layers(4, 9, 6, lambda at: level_1.setup_at(at, 2))

    receive_sides_z(from_s1z, 32)
    spread_1(level_1.s, source_block)
    receive_sides(from_s1, 32)
    receive_corners(from_s1_corner, 16)
    spread_beside(level_1.s, k1x, k1p)
    level_1.start(2, 11, 10, 1, steps[0][1])
    over_layers(5, 8, 4, lambda at: level_1.start_outer(at, steps[0][1]))
    over_sides(3, 9, 2, lambda at: level_1.sweep_at(at, level_1.va, level_1.vb, 1, 1, steps[1], True))
    over_layers(5, 8, 4, lambda at: level_1.sweep_at(at, level_1.va, level_1.vb, 2, 1, steps[1], True))
    level_1.sweep(level_1.vb, level_1.va, 4, 9, 6, 1, 1, steps[2])
    level_1.residual(level_1.va, level_1.vb, 5, 8, 4, 1)

    value = pairs_1(level_1.vb)
    s2m[...] = value
    rs2[REACH] = value
    for_far(1, lambda slot, dw: send(from_s2 + 2 * REACH - slot, s2m, rs2.at[2 * REACH - slot], dw, 0, 8, sender_far + slot))

    @for_sides
    def send_iterate_1(side, dw):
        send(from_x1 + 1 - side, level_1.va.at[0, pl.ds(6 - side, 3)], rx1.at[1 - side], dw, 0, 48, sender_x1 + side)

    for side in range(2):
        @pl.when(reach[side] >= 2)
        def send_next_1():
            layer = level_1.va.at[0, 5 + 3 * side]
            send(from_x1b + 1 - side, layer, rx1b.at[1 - side], 4 * side - 2, 0, 16, sender_x1b + side)

    receive_sides(from_c1b, 16)
    level_1.setup_below(1, 1)
    over_sides(1, 12, 1, lambda at: level_1.setup_at(at, 1))

    def spread_2(ref, blocks):
        for block in range(2 * REACH + 1):
            packed = blocks[block]
            ref[0, 2 * block] = jnp.where(odd_8, pltpu.roll(packed, 1, 1), packed)
            ref[0, 2 * block + 1] = jnp.where(odd_8, packed, pltpu.roll(packed, LANES - 1, 1))

    def restrict_2(ref, at):
        total = ref[0, 2 * at + 2] + ref[0, 2 * at + 3]
        odd_row = lax.broadcasted_iota(jnp.int32, (8, LANES), 0) % 2 == 1
        total = total + jnp.where(odd_row, pltpu.roll(total, 1, 0), pltpu.roll(total, 7, 0))
        second = lanes(8) % 4 >= 2
        total = total + jnp.where(second, pltpu.roll(total, 2, 1), pltpu.roll(total, LANES - 2, 1))
        return 0.125 * total

    if_reach(HALF_REACH, lambda side, sign: receive(from_four + side, 32))
    spread_2(level_2.c, rc2)
    level_2.setup(1, 32, 8, 1)
    for at in range(15):
        level_3.c[0, at] = restrict_2(level_2.c, at)
    level_3.setup(1, 13, 13, 1)

    receive_far(from_s2)
    spread_2(level_2.s, rs2)
    level_2.start(1, 32, 32, 1, steps[0][1])
    level_2.sweep(level_2.va, level_2.vb, 2, 31, 15, 1, 1, steps[1], fresh=True)
    level_2.sweep(level_2.vb, level_2.va, 3, 30, 14, 1, 1, steps[2])
    level_2.residual(level_2.va, level_2.vb, 4, 29, 13, 1)

    for at in range(1, 14):
        level_3.s[0, at] = restrict_2(level_2.vb, at)
    coarse = cheb(4)
    level_3.start(1, 13, 13, 1, coarse[0][1])
    level_3.sweep(level_3.va, level_3.vb, 2, 12, 11, 1, 1, coarse[1], fresh=True)
    level_3.sweep(level_3.vb, level_3.va, 3, 11, 9, 1, 1, coarse[2])
    level_3.sweep(level_3.va, level_3.vb, 4, 10, 7, 1, 1, coarse[3])

    for at in range(10, 24):
        level_2.vb[0, at] = level_2.va[0, at] + level_3.vb[0, (at - 2) // 2]
    level_2.sweep(level_2.vb, level_2.va, 11, 22, 12, 1, 1, steps[0], fresh=True)
    level_2.sweep(level_2.va, level_2.vb, 12, 21, 10, 1, 1, steps[1])
    level_2.sweep(level_2.vb, level_2.va, 13, 20, 8, 1, 1, steps[2])

    for at in range(8):
        value = level_2.va[0, 13 + at]
        for part in range(2):
            p1[at, pl.ds(part, 8, stride=2), :] = value
    receive_sides(from_x1, 48)
    for side in range(2):
        pl.when(reach[side] >= 2)(functools.partial(receive, from_x1b + side, 16))
    for at in range(14):
        if 4 <= at <= 9:
            before = level_1.va[0, at]
        else:
            before = rx1b[0] if at == 0 else rx1[0, at - 1] if at < 4 else rx1[1, at - 10] if at < 13 else rx1b[1]
        level_1.vb[0, at] = before + p1[(at + 1) // 2]
    for side in range(2):
        pl.when(has[side])(functools.partial(sends_done, sender_x1 + side))
        pl.when(reach[side] >= 2)(functools.partial(sends_done, sender_x1b + side))
    level_1.sweep(level_1.vb, level_1.va, 1, 12, 12, 1, 1, steps[0], fresh=True)
    level_1.sweep(level_1.va, level_1.vb, 2, 11, 10, 1, 1, steps[1])
    level_1.sweep(level_1.vb, level_1.va, 3, 10, 8, 1, 1, steps[2])

    fine_lane = lanes(16) // 2
    for at in range(8):
        value = level_1.va[0, 3 + at]
        for k in range(2):
            fine = jnp.take_along_axis(value, (fine_lane + (32 if k == 0 else 96)) % LANES, axis=1)
            for part in range(2):
                p0[k, at, pl.ds(part, 16, stride=2), :] = fine
    receive_sides(from_x0, 72)
    for side in range(2):
        packed = hx0[side, pl.ds(64, 8), :]
        for layer in range(2):
            at = (1 if side == 0 else 13) + layer
            coarse_at = (at - 4) // 2 + 2
            level_0.vb[0, at] = hx0[side, pl.ds(32 * layer, 32), :] + p0[0, coarse_at]
            for part in range(4):
                rows = pl.ds(8 * part, 8)
                level_0.vb[1, at, rows, :] = (
                    unpack(packed, 4 * layer + part) * level_0.lane_mask[1][:8] + p0[1, coarse_at, rows, :]
                )

    def correct(at):
        for k in range(2):
            level_0.vb[k, at] = level_0.va[k, at] + p0[k, at // 2]

    over_layers(3, 12, 5, correct)
    level_0.sweep(level_0.vb, level_0.va, 2, 13, 4, 2, 2, steps[0], fresh=True)
    level_0.sweep(level_0.va, level_0.vb, 3, 12, 5, 2, 2, steps[1])
    level_0.finish(level_0.vb, level_0.va, kept, added, 4, 11, 4, steps[2])

    for_sides(lambda side, dw: sends_done(sender_x + side))
    for_sides_z(lambda side, dn: sends_done(sender_z + side))
    for_corners(lambda side, side_z, dw, dn: sends_done(sender_corner + 2 * side + side_z))
    if_reach(HALF_REACH, lambda side, sign: sends_done(sender_four + side))
    for_far(1, lambda slot, dw: ruled(8, 0, sender_c2 + slot).wait_send(), HALF_REACH)
    for_far(1, lambda slot, dw: ruled(8, 0, sender_far + slot).wait_send())


def per_device(right_side, conductivity, wide, narrow):
    brick = (8, 32, LANES)
    scratch = []
    for shape in LEVEL_SHAPES:
        scratch += [pltpu.VMEM(shape, F32)] * LEVEL_FIELDS
    shapes = [
        (2, 64, LANES), (2, 64, LANES), (2, 2, 16, LANES),
        (2, 2, 16, LANES), (2, 32, LANES), (2, 2, 16, LANES),
        (32, LANES), (2, 16, LANES), (2, 32, LANES), (2, 2, 16, LANES), (2, 32, LANES),
        (2 * REACH + 1, 8, LANES), (8, LANES), (2 * REACH + 1, 8, LANES),
        (2, 3, 16, LANES), (2, 16, LANES),
        (2, 72, LANES), (2, 72, LANES),
        (8, 16, LANES), (2, 8, 32, LANES),
        (RULER, LANES),
    ]
    scratch += [pltpu.VMEM(shape, F32) for shape in shapes]
    scratch += [pltpu.SemaphoreType.DMA((2,)), pltpu.SemaphoreType.DMA((SENDERS,)), pltpu.SemaphoreType.DMA((GROUPS,))]
    kept, added = pl.pallas_call(
        functools.partial(kernel, wide, narrow),
        out_shape=[jax.ShapeDtypeStruct(brick, F32)] * 2,
        in_specs=[pl.BlockSpec(memory_space=pltpu.HBM)] * 2,
        out_specs=[pl.BlockSpec(memory_space=pltpu.VMEM)] * 2,
        scratch_shapes=scratch,
        compiler_params=pltpu.CompilerParams(
            collective_id=0, has_side_effects=True, vmem_limit_bytes=32 * 1024 * 1024
        ),
    )(pltpu.with_memory_space_constraint(right_side, pltpu.HBM), pltpu.with_memory_space_constraint(conductivity, pltpu.HBM))
    return kept + added


def solution(mesh):
    spec = P("wide", None, "narrow")
    body = functools.partial(per_device, wide=mesh.shape["wide"], narrow=mesh.shape["narrow"])
    return jax.shard_map(body, mesh=mesh, in_specs=(spec, spec), out_specs=spec, check_vma=False)
```

```python
import functools

import jax
import jax.numpy as jnp
from jax import lax
from jax.experimental import pallas as pl
from jax.experimental.pallas import tpu as pltpu
from jax.sharding import PartitionSpec as P

CENTER = 1.125
HALF = 0.875
LANES = 128
REACH = 8
HALF_REACH = 4
F32 = jnp.float32
MESH_ID = pl.DeviceIdType.MESH


def cheb(sweeps):
    sigma = CENTER / HALF
    steps = [(0.0, 1.0 / CENTER)]
    ratio = 1.0 / sigma
    for _ in range(sweeps - 1):
        ratio_next = 1.0 / (2.0 * sigma - ratio)
        steps.append((ratio_next * ratio, 2.0 * ratio_next / HALF))
        ratio = ratio_next
    return steps


def over_sides(first, second, count, body):
    for base in (first, second):
        for at in range(count):
            body(base + at)


def over_layers(low, high, unroll, body):
    count = high - low + 1
    if count == unroll:
        for at in range(low, high + 1):
            body(at)
        return

    def block(step, carry):
        for at in range(unroll):
            body(low + step * unroll + at)
        return carry

    lax.fori_loop(0, count // unroll, block, 0)


class Level:
    def __init__(self, refs, scale, rows, row_step, lane_step, base, extent, lane_mask):
        self.c, self.s, self.cx, self.cy, self.cz, self.iv, self.dg, self.va, self.vb = refs
        self.half = 0.5 * scale
        self.rows, self.row_step, self.lane_step = rows, row_step, lane_step
        self.base, self.extent, self.lane_mask = base, extent, lane_mask

    def inside(self, at):
        where_x = self.base + at
        return jnp.where((where_x >= 0) & (where_x < self.extent), 1.0, 0.0).astype(F32)

    def lane(self):
        return lax.broadcasted_iota(jnp.int32, (self.rows, LANES), 1)

    def row(self):
        return lax.broadcasted_iota(jnp.int32, (self.rows, LANES), 0)

    def y_up(self, tile):
        return pltpu.roll(tile, self.rows - self.row_step, 0)

    def y_down(self, tile):
        return pltpu.roll(tile, self.row_step, 0)

    def turned(self, tiles, shift, edge, count):
        out = [pltpu.roll(t, shift, 1) for t in tiles]
        if len(tiles) == 1:
            return out
        at_edge = self.lane() == edge
        return [jnp.where(at_edge, out[1 - k], out[k]) for k in range(count)]

    def z_up(self, tiles, count):
        return self.turned(tiles, LANES - self.lane_step, LANES - 1, count)

    def z_down(self, tiles, count):
        return self.turned(tiles, self.lane_step, 0, count)

    def masked(self, at, tiles):
        keep = self.inside(at) * self.half
        out = []
        for k in range(tiles):
            mask = self.lane_mask[k]
            out.append(self.c[k, at] * (keep if mask is None else mask * keep))
        return out

    def setup_below(self, low, tiles):
        first, second = self.masked(low - 1, tiles), self.masked(low, tiles)
        for k in range(tiles):
            self.cx[k, low - 1] = first[k] + second[k]

    def setup_at(self, at, tiles):
        before, here, after = self.masked(at - 1, tiles), self.masked(at, tiles), self.masked(at + 1, tiles)
        inside = self.inside(at)
        top = self.row() >= self.rows - self.row_step
        bottom = self.row() < self.row_step
        z_up, z_down = self.z_up(here, tiles), self.z_down(here, tiles)
        for k in range(tiles):
            own = here[k]
            x_low = before[k] + own
            x_high = own + after[k]
            y_low = own + jnp.where(bottom, 0.0, self.y_down(own))
            y_high = own + jnp.where(top, 0.0, self.y_up(own))
            z_low = own + z_down[k]
            z_high = own + z_up[k]
            diagonal = x_low + x_high + y_low + y_high + z_low + z_high
            keep = inside if self.lane_mask[k] is None else self.lane_mask[k] * inside
            self.cx[k, at] = x_high
            self.cy[k, at] = jnp.where(top, 0.0, y_high)
            self.cz[k, at] = z_high
            if k == 0:
                self.dg[0, at] = diagonal
            self.iv[k, at] = jnp.where(jnp.full_like(own, 0.0) + keep > 0.5, 1.0 / diagonal, 0.0)

    def setup(self, low, high, unroll, tiles):
        self.setup_below(low, tiles)
        over_layers(low, high, unroll, lambda at: self.setup_at(at, tiles))

    def start_at(self, at, tiles, beta):
        for k in range(tiles):
            self.va[k, at] = self.s[k, at] * self.iv[k, at] * beta

    def start_outer(self, at, beta):
        self.va[1, at] = self.s[1, at] * self.iv[1, at] * beta

    def start(self, low, high, unroll, tiles, beta):
        over_layers(low, high, unroll, lambda at: self.start_at(at, tiles, beta))

    def around(self, field, at, tiles, count):
        here = [field[k, at] for k in range(tiles)]
        cz = [self.cz[k, at] for k in range(tiles)]
        z_up = self.z_up(here, count)
        z_down = self.z_down([cz[k] * here[k] for k in range(tiles)], count)
        sums = []
        for k in range(count):
            cy = self.cy[k, at]
            total = self.cx[k, at] * field[k, at + 1] + self.cx[k, at - 1] * field[k, at - 1]
            total = total + (cy * self.y_up(here[k]) + self.y_down(cy * here[k]))
            total = total + (cz[k] * z_up[k] + z_down[k])
            sums.append(total + self.s[k, at])
        return here, sums

    def sweep_at(self, at, field, result, tiles, count, step, fresh):
        alpha, beta = step
        here, sums = self.around(field, at, tiles, count)
        for k in range(count):
            kept = (1.0 + alpha - beta) * here[k]
            if not fresh:
                kept = kept - alpha * result[k, at]
            result[k, at] = kept + (beta * self.iv[k, at]) * sums[k]

    def sweep(self, field, result, low, high, unroll, tiles, count, step, fresh=False):
        over_layers(low, high, unroll, lambda at: self.sweep_at(at, field, result, tiles, count, step, fresh))

    def residual_at(self, at, field, result, tiles):
        here, sums = self.around(field, at, tiles, 1)
        result[0, at] = sums[0] - self.dg[0, at] * here[0]

    def residual(self, field, result, low, high, unroll, tiles):
        over_layers(low, high, unroll, lambda at: self.residual_at(at, field, result, tiles))

    def finish(self, field, older, kept_out, added_out, low, high, unroll, step):
        alpha, beta = step

        def body(at):
            here, sums = self.around(field, at, 2, 1)
            kept_out[at - low] = (1.0 + alpha - beta) * here[0] - alpha * older[0, at]
            added_out[at - low] = (beta * self.iv[0, at]) * sums[0]

        over_layers(low, high, unroll, body)


LEVEL_FIELDS = 9
LEVEL_SHAPES = ((2, 16, 32, LANES), (2, 14, 16, LANES), (1, 34, 8, LANES), (1, 15, 8, LANES))
RULER = 1024
SENDERS = 14 + 2 * (2 * REACH + 1)
GROUPS = 36 + 2 * (2 * REACH + 1)


def kernel(wide, narrow, rhs, coef, kept, added, *scratch):
    scratch = list(scratch)
    level_refs = []
    for _ in range(4):
        level_refs.append(scratch[:LEVEL_FIELDS])
        scratch = scratch[LEVEL_FIELDS:]
    (zs, rz, rcn, kp, k1cx, k1c, sk, sp, k1x, k1p, k1z, rc2, s2m, rs2, rx1, rx1b, sb0, hx0, p1, p0, ruler,
     local_sem, send_sem, recv_sem) = scratch
    me_w = lax.axis_index("wide")
    me_n = lax.axis_index("narrow")

    def there(dw, dn):
        return (lax.rem(me_w + (dw + wide), wide), lax.rem(me_n + (dn + narrow), narrow))

    has = (me_w > 0, me_w < wide - 1)
    has_z = (me_n > 0, me_n < narrow - 1)
    reach = (jnp.minimum(me_w, REACH), jnp.minimum(wide - 1 - me_w, REACH))

    def for_far(first, body, last=REACH):
        for side in range(2):
            sign = 2 * side - 1

            def step(k, carry):
                body(REACH + sign * k, sign * k)
                return carry

            lax.fori_loop(first, jnp.minimum(reach[side], last) + 1, step, 0)

    def for_sides(body):
        for side in range(2):
            pl.when(has[side])(functools.partial(body, side, 2 * side - 1))

    def for_sides_z(body):
        for side in range(2):
            pl.when(has_z[side])(functools.partial(body, side, 2 * side - 1))

    def for_corners(body):
        for side in range(2):
            for side_z in range(2):
                pl.when(has[side] & has_z[side_z])(
                    functools.partial(body, side, side_z, 2 * side - 1, 2 * side_z - 1)
                )

    @pl.when((me_n == 0) | (me_n == narrow - 1))
    def clear_z():
        for ref in (rz, rcn, k1c, k1z, k1p):
            ref[...] = jnp.zeros(ref.shape, F32)

    @pl.when((me_w < REACH) | (me_w >= wide - REACH))
    def clear():
        def zero(ref):
            ref[...] = jnp.zeros(ref.shape, F32)

        for ref in (rcn, rx1, rx1b, hx0, rc2, rs2, k1cx, k1c, k1x, k1p):
            zero(ref)
        for side in range(2):
            for ref in level_refs[0][:2]:
                zero(ref.at[0, pl.ds(12 * side, 4)])
            zero(level_refs[1][0].at[0, 13 * side])

    def if_reach(least, body):
        for side in range(2):
            pl.when(reach[side] >= least)(functools.partial(body, side, 2 * side - 1))

    barrier = pltpu.get_barrier_semaphore()

    def greet(dw, dn):
        pl.semaphore_signal(barrier, inc=1, device_id=there(dw, dn), device_id_type=MESH_ID)

    for_far(1, lambda slot, dw: greet(dw, 0), HALF_REACH)
    for_sides_z(lambda side, dn: greet(0, dn))
    for_corners(lambda side, side_z, dw, dn: greet(dw, dn))

    c0, s0 = level_refs[0][0], level_refs[0][1]
    load_c = pltpu.make_async_copy(coef, c0.at[0, pl.ds(4, 8)], local_sem.at[0])
    load_s = pltpu.make_async_copy(rhs, s0.at[0, pl.ds(4, 8)], local_sem.at[1])
    load_c.start()
    load_s.start()
    beside_x = jnp.where(has[0], 1, 0) + jnp.where(has[1], 1, 0)
    beside_z = jnp.where(has_z[0], 1, 0) + jnp.where(has_z[1], 1, 0)
    greeted = beside_z + beside_x * beside_z
    for side in range(2):
        greeted = greeted + jnp.minimum(reach[side], HALF_REACH)

    left = jnp.where(me_n > 0, 1.0, 0.0).astype(F32)
    right = jnp.where(me_n < narrow - 1, 1.0, 0.0).astype(F32)

    def lanes(rows):
        return lax.broadcasted_iota(jnp.int32, (rows, LANES), 1)

    def edges(rows, until, low, since, high):
        at = lanes(rows)
        return jnp.where(at < until, low, jnp.where(at >= since, high, 0.0))

    def centred(rows):
        at = lanes(rows)
        return jnp.where((at >= 32) & (at < 96), 1.0, edges(rows, 32, left, 96, right))

    level_0 = Level(level_refs[0], 1.0, 32, 1, 1, 8 * me_w - 4, 8 * wide, [None, edges(32, 8, right, 120, left)])
    level_1 = Level(
        level_refs[1], 0.25, 16, 1, 1, 4 * me_w - 5, 4 * wide, [centred(16), edges(16, 32, right, 96, left)]
    )
    level_2 = Level(level_refs[2], 0.0625, 8, 1, 2, 2 * me_w - 16, 2 * wide, [centred(8)])
    level_3 = Level(level_refs[3], 0.015625, 8, 2, 4, me_w - 7, wide, [centred(8)])

    sent = [0] * SENDERS

    def send(group, src, dst, dw, dn, rows, sender):
        if isinstance(sender, int):
            sent[sender] += rows
        pltpu.make_async_remote_copy(
            src_ref=src, dst_ref=dst, send_sem=send_sem.at[sender], recv_sem=recv_sem.at[group],
            device_id=there(dw, dn), device_id_type=MESH_ID,
        ).start()

    def ruled(rows, group, sender):
        span = ruler.at[pl.ds(0, rows)]
        return pltpu.make_async_remote_copy(
            src_ref=span, dst_ref=span, send_sem=send_sem.at[sender], recv_sem=recv_sem.at[group],
            device_id=there(0, 1), device_id_type=MESH_ID,
        )

    def receive(group, rows):
        ruled(rows, group, 0).wait_recv()

    def receive_sides(group, rows):
        for_sides(lambda side, dw: receive(group + side, rows))

    def receive_sides_z(group, rows):
        for_sides_z(lambda side, dn: receive(group + side, rows))

    def receive_corners(group, rows):
        for_corners(lambda side, side_z, dw, dn: receive(group + 2 * side + side_z, rows))

    def receive_far(group, last=REACH):
        for_far(1, lambda slot, dw: receive(group + slot, 8), last)

    def sends_done(sender):
        ruled(sent[sender], 0, sender).wait_send()

    from_z, from_s1z = 0, 2
    from_c_corner, from_k_corner, from_s1_corner = 4, 8, 12
    from_c, from_s, from_s_next, from_k, from_s1, from_c1b, from_x0, from_x1, from_x1b = range(16, 34, 2)
    from_four = 34
    from_c2 = 36
    from_s2 = from_c2 + 2 * REACH + 1
    sender_x, sender_x1, sender_x1b, sender_four, sender_z = range(0, 10, 2)
    sender_corner, sender_c2, sender_far = 10, 14, 14 + 2 * REACH + 1

    def pack(tiles):
        rows = tiles[0].shape[0]
        group = lanes(rows) // 16
        packed = jnp.zeros((rows, LANES), F32)
        for at, tile in enumerate(tiles):
            packed = jnp.where(group == at, pltpu.roll(tile, (16 * at + 8) % LANES, 1), packed)
        return packed

    def unpack(packed, at):
        return pltpu.roll(packed, (2 * LANES - (16 * at + 8)) % LANES, 1)

    def pack_side(ref, half, side):
        group = lanes(8) // 8
        packed = None
        for layer in range(4):
            for part in range(4):
                at = 4 * layer + part
                tile = ref[0, 4 + 4 * half + layer, pl.ds(8 * part, 8), :]
                tile = pltpu.roll(tile, (8 * at + 8 * side) % LANES, 1)
                packed = tile if at == 0 else jnp.where(group == at, tile, packed)
        return packed

    def restrict_0(ref):
        out = []
        for layer in range(4):
            total = None
            for dx in range(2):
                for dy in range(2):
                    term = ref[0, 4 + 2 * layer + dx, pl.ds(dy, 16, stride=2), :]
                    total = term if total is None else total + term
            total = total + pltpu.roll(total, LANES - 1, 1)
            out.append(0.125 * jnp.take_along_axis(total, (2 * lanes(16) + 64) % LANES, axis=1))
        return out

    odd_8 = lanes(8) % 2 == 1

    def pairs_1(ref):
        out = []
        for layer in range(2):
            total = None
            for dx in range(2):
                for dy in range(2):
                    term = ref[0, 5 + 2 * layer + dx, pl.ds(dy, 8, stride=2), :]
                    total = term if total is None else total + term
            total = total + jnp.where(odd_8, pltpu.roll(total, 1, 1), pltpu.roll(total, LANES - 1, 1))
            out.append(0.125 * total)
        return jnp.where(odd_8, out[1], out[0])

    def squeeze_1(layers, ref, row):
        for part in range(2):
            ref[pl.ds(row + 16 * part, 16), :] = jnp.where(lanes(16) < 64, layers[part], layers[part + 2])

    pl.semaphore_wait(barrier, greeted)

    @for_sides
    def send_faces(side, dw):
        send(from_c + 1 - side, coef.at[pl.ds(4 * side, 4)], c0.at[0, pl.ds(12 - 12 * side, 4)], dw, 0, 128, sender_x + side)
        send(from_s + 1 - side, rhs.at[7 * side], s0.at[0, 12 - 9 * side], dw, 0, 32, sender_x + side)

    def squeeze_halves(first, second):
        low_quarter = lanes(16) % 64 < 32
        return (
            jnp.where(low_quarter, pltpu.roll(first, 96, 1), second),
            jnp.where(low_quarter, first, pltpu.roll(second, 32, 1)),
        )

    load_c.wait()
    own_c1 = restrict_0(c0)
    for side in range(2):
        squeeze_1(own_c1, zs.at[side], 32)
        for half in range(2):
            zs[side, pl.ds(16 * half, 8), :] = pack_side(c0, half, side)
    load_s.wait()
    for side in range(2):
        for half in range(2):
            zs[side, pl.ds(16 * half + 8, 8), :] = pack_side(s0, half, side)

    for_sides_z(
        lambda side, dn: send(from_z + 1 - side, zs.at[side], rz.at[1 - side], 0, dn, 64, sender_z + side)
    )

    def send_corner(group, src, dst, rows, side, side_z):
        at = 2 * side + side_z
        send(group + 3 - at, src, dst, 2 * side - 1, 2 * side_z - 1, rows, sender_corner + at)

    @for_corners
    def send_c_corner(side, side_z, dw, dn):
        src = zs.at[side_z, pl.ds(16 * side, 16)]
        send_corner(from_c_corner, src, rcn.at[1 - side, 1 - side_z], 16, side, side_z)

    @for_sides
    def send_s_next(side, dw):
        src = rhs.at[pl.ds(1 + 4 * side, 2)]
        send(from_s_next + 1 - side, src, s0.at[0, pl.ds(13 - 12 * side, 2)], dw, 0, 64, sender_x + side)

    def fill_0(ref, first, from_left, from_right):
        low = lanes(8) < 64
        for layer in range(4):
            for part in range(4):
                at = 4 * layer + part
                ref[1, first + layer, pl.ds(8 * part, 8), :] = jnp.where(
                    low, pltpu.roll(from_right, (LANES - 8 * at) % LANES, 1), pltpu.roll(from_left, (120 - 8 * at) % LANES, 1)
                )

    steps = cheb(3)
    receive_sides_z(from_z, 64)
    for field, ref in enumerate((c0, s0)):
        for half in range(2):
            rows = pl.ds(16 * half + 8 * field, 8)
            fill_0(ref, 4 + 4 * half, rz[0, rows, :], rz[1, rows, :])
    level_0.setup(5, 10, 3, 2)
    level_0.start(5, 10, 6, 2, steps[0][1])
    level_0.sweep(level_0.va, level_0.vb, 6, 9, 4, 2, 2, steps[1], fresh=True)
    level_0.sweep(level_0.vb, level_0.va, 7, 8, 2, 2, 2, steps[2])

    def spread_1(ref, block):
        at_lane = lanes(16)
        low_half = at_lane < 64
        low_quarter = at_lane % 64 < 32
        for part in range(2):
            before, own, after = (block(dz, part) for dz in (-1, 0, 1))
            near = jnp.where(low_quarter, before, after)
            outer = jnp.where(low_quarter, after, before)
            own_r, near_r, outer_r = (pltpu.roll(t, 64, 1) for t in (own, near, outer))
            at = 5 + part
            for at, own_a, own_b, near_a, near_b, outer_a, outer_b in (
                (at, own, own_r, near, near_r, outer, outer_r),
                (at + 2, own_r, own, near_r, near, outer_r, outer),
            ):
                centre = jnp.where(low_half, own_a, own_b)
                ref[0, at] = jnp.where(at_lane < 32, near_a, jnp.where(at_lane < 96, centre, near_b))
                ref[1, at] = jnp.where(low_half, outer_a, outer_b)

    def coef_block(dz, part):
        rows = pl.ds(32 + 16 * part, 16)
        return zs[0, rows, :] if dz == 0 else rz[(1 + dz) // 2, rows, :]

    spread_1(level_1.c, coef_block)
    rc2[REACH] = pairs_1(level_1.c)

    for_far(
        1,
        lambda slot, dw: send(
            from_c2 + 2 * REACH - slot, rc2.at[REACH], rc2.at[2 * REACH - slot], dw, 0, 8, sender_c2 + slot
        ),
        HALF_REACH,
    )
    k1_own = zs.at[0, pl.ds(32, 32)]
    halves = squeeze_halves(zs[0, pl.ds(32, 16), :], zs[0, pl.ds(48, 16), :])
    at_lane = lanes(16)
    for side in range(2):
        near, far = (0, 3) if side == 0 else (3, 0)
        full = level_1.c[0, 5 + near]
        place = (32 * far + 31, 32 * far)
        cell = (64, 63)
        for side_z in range(2):
            moved = pltpu.roll(full, (place[side_z] - cell[side_z]) % LANES, 1)
            kp[side, side_z] = jnp.where(at_lane == place[side_z], moved, halves[side_z])
    for_sides(
        lambda side, dw: send(from_k + 1 - side, k1_own, k1cx.at[1 - side], dw, 0, 32, sender_x + side)
    )
    for_corners(
        lambda side, side_z, dw, dn: send_corner(
            from_k_corner, kp.at[side, side_z], k1c.at[1 - side, 1 - side_z], 16, side, side_z
        )
    )

    receive_sides(from_c, 128)
    receive_corners(from_c_corner, 16)
    for field, ref in enumerate((c0, s0)):
        for side in range(2):
            rows = pl.ds(8 * field, 8)
            fill_0(ref, 12 * side, rcn[side, 0, rows, :], rcn[side, 1, rows, :])
    level_0.setup_below(1, 2)
    over_sides(1, 11, 4, lambda at: level_0.setup_at(at, 2))
    receive_sides(from_s, 32)
    sweep_a = (level_0.va, level_0.vb, 2, 2, steps[1], True)
    sweep_b = (level_0.vb, level_0.va, 2, 2, steps[2], False)
    over_sides(3, 11, 2, lambda at: level_0.start_at(at, 2, steps[0][1]))
    over_sides(4, 10, 2, lambda at: level_0.sweep_at(at, *sweep_a))
    over_sides(5, 9, 2, lambda at: level_0.sweep_at(at, *sweep_b))
    level_0.residual(level_0.va, level_0.vb, 6, 9, 4, 2)
    receive_sides(from_s_next, 64)
    over_sides(1, 13, 2, lambda at: level_0.start_at(at, 2, steps[0][1]))
    over_sides(2, 12, 2, lambda at: level_0.sweep_at(at, *sweep_a))
    over_sides(3, 11, 2, lambda at: level_0.sweep_at(at, *sweep_b))
    over_sides(4, 10, 2, lambda at: level_0.residual_at(at, level_0.va, level_0.vb, 2))

    squeeze_1(restrict_0(level_0.vb), sk, 0)

    sp[0], sp[1] = squeeze_halves(sk[pl.ds(0, 16), :], sk[pl.ds(16, 16), :])

    for_sides(lambda side, dw: send(from_s1 + 1 - side, sk, k1x.at[1 - side], dw, 0, 32, sender_x + side))
    for_corners(
        lambda side, side_z, dw, dn: send_corner(
            from_s1_corner, sp.at[side_z], k1p.at[1 - side, 1 - side_z], 16, side, side_z
        )
    )
    for_sides_z(lambda side, dn: send(from_s1z + 1 - side, sk, k1z.at[1 - side], 0, dn, 32, sender_z + side))

    receive_far(from_c2, HALF_REACH)

    @functools.partial(if_reach, HALF_REACH)
    def send_four(side, sign):
        src, dst = rc2.at[pl.ds(9 - 5 * side, 4)], rc2.at[pl.ds(13 - 13 * side, 4)]
        send(from_four + 1 - side, src, dst, HALF_REACH * sign, 0, 32, sender_four + side)

    for side in range(2):
        first = 9 if side == 0 else 5
        tiles = []
        for layer in range(2):
            sb0[side, pl.ds(32 * layer, 32), :] = level_0.va[0, first + layer]
            for part in range(4):
                tiles.append(level_0.va[1, first + layer, pl.ds(8 * part, 8), :])
        sb0[side, pl.ds(64, 8), :] = pack(tiles)

    @for_sides
    def send_iterate_0(side, dw):
        send(from_x0 + 1 - side, sb0.at[1 - side], hx0.at[1 - side], dw, 0, 72, sender_x + side)

    def source_block(dz, part):
        rows = pl.ds(16 * part, 16)
        return sk[rows, :] if dz == 0 else k1z[(1 + dz) // 2, rows, :]

    def spread_beside(ref, blocks, packs):
        at_lane = lanes(16)
        low_half = at_lane < 64
        for side in range(2):
            for layer in range(4):
                own = blocks[side, pl.ds(16 * (layer % 2), 16), :]
                other = pltpu.roll(own, 64, 1)
                centre = jnp.where(low_half, own, other) if layer < 2 else jnp.where(low_half, other, own)
                before = pltpu.roll(packs[side, 0], (LANES - 32 * layer) % LANES, 1)
                after = pltpu.roll(packs[side, 1], (LANES + 96 - 32 * layer) % LANES, 1)
                ref[0, 1 + 8 * side + layer] = jnp.where(at_lane < 32, before, jnp.where(at_lane < 96, centre, after))

    receive_sides(from_k, 32)
    receive_corners(from_k_corner, 16)
    spread_beside(level_1.c, k1cx, k1c)
    for side in range(2):
        far = 3 if side == 1 else 0
        below, above = (pltpu.roll(k1c[side, side_z], (shift - 32 * far) % LANES, 1)
                        for side_z, shift in ((0, 127), (1, -31)))
        level_1.c[1, 4 + 5 * side] = jnp.where(lanes(16) < 64, above, below)

    @for_sides
    def send_coef_1(side, dw):
        send(from_c1b + 1 - side, level_1.c.at[0, 9 - 5 * side], level_1.c.at[0, 13 - 13 * side], dw, 0, 16, sender_x + side)

    level_1.setup_below(2, 1)
    over_sides(2, 10, 2, lambda at: level_1.setup_at(at, 1))
    over_layers(4, 9, 6, lambda at: level_1.setup_at(at, 2))

    receive_sides_z(from_s1z, 32)
    spread_1(level_1.s, source_block)
    receive_sides(from_s1, 32)
    receive_corners(from_s1_corner, 16)
    spread_beside(level_1.s, k1x, k1p)
    level_1.start(2, 11, 10, 1, steps[0][1])
    over_layers(5, 8, 4, lambda at: level_1.start_outer(at, steps[0][1]))
    over_sides(3, 9, 2, lambda at: level_1.sweep_at(at, level_1.va, level_1.vb, 1, 1, steps[1], True))
    over_layers(5, 8, 4, lambda at: level_1.sweep_at(at, level_1.va, level_1.vb, 2, 1, steps[1], True))
    level_1.sweep(level_1.vb, level_1.va, 4, 9, 6, 1, 1, steps[2])
    level_1.residual(level_1.va, level_1.vb, 5, 8, 4, 1)

    value = pairs_1(level_1.vb)
    s2m[...] = value
    rs2[REACH] = value
    for_far(1, lambda slot, dw: send(from_s2 + 2 * REACH - slot, s2m, rs2.at[2 * REACH - slot], dw, 0, 8, sender_far + slot))

    @for_sides
    def send_iterate_1(side, dw):
        send(from_x1 + 1 - side, level_1.va.at[0, pl.ds(6 - side, 3)], rx1.at[1 - side], dw, 0, 48, sender_x1 + side)

    for side in range(2):
        @pl.when(reach[side] >= 2)
        def send_next_1():
            layer = level_1.va.at[0, 5 + 3 * side]
            send(from_x1b + 1 - side, layer, rx1b.at[1 - side], 4 * side - 2, 0, 16, sender_x1b + side)

    receive_sides(from_c1b, 16)
    level_1.setup_below(1, 1)
    over_sides(1, 12, 1, lambda at: level_1.setup_at(at, 1))

    def spread_2(ref, blocks):
        for block in range(2 * REACH + 1):
            packed = blocks[block]
            ref[0, 2 * block] = jnp.where(odd_8, pltpu.roll(packed, 1, 1), packed)
            ref[0, 2 * block + 1] = jnp.where(odd_8, packed, pltpu.roll(packed, LANES - 1, 1))

    def restrict_2(ref, at):
        total = ref[0, 2 * at + 2] + ref[0, 2 * at + 3]
        odd_row = lax.broadcasted_iota(jnp.int32, (8, LANES), 0) % 2 == 1
        total = total + jnp.where(odd_row, pltpu.roll(total, 1, 0), pltpu.roll(total, 7, 0))
        second = lanes(8) % 4 >= 2
        total = total + jnp.where(second, pltpu.roll(total, 2, 1), pltpu.roll(total, LANES - 2, 1))
        return 0.125 * total

    if_reach(HALF_REACH, lambda side, sign: receive(from_four + side, 32))
    spread_2(level_2.c, rc2)
    level_2.setup(1, 32, 16, 1)
    for at in range(15):
        level_3.c[0, at] = restrict_2(level_2.c, at)
    level_3.setup(1, 13, 13, 1)

    for_sides(lambda side, dw: sends_done(sender_x + side))
    for_sides_z(lambda side, dn: sends_done(sender_z + side))
    for_corners(lambda side, side_z, dw, dn: sends_done(sender_corner + 2 * side + side_z))
    if_reach(HALF_REACH, lambda side, sign: sends_done(sender_four + side))
    for_far(1, lambda slot, dw: ruled(8, 0, sender_c2 + slot).wait_send(), HALF_REACH)
    for_far(1, lambda slot, dw: ruled(8, 0, sender_far + slot).wait_send())
    for side in range(2):
        pl.when(has[side])(functools.partial(sends_done, sender_x1 + side))
        pl.when(reach[side] >= 2)(functools.partial(sends_done, sender_x1b + side))

    receive_far(from_s2)
    spread_2(level_2.s, rs2)
    level_2.start(1, 32, 32, 1, steps[0][1])
    level_2.sweep(level_2.va, level_2.vb, 2, 31, 30, 1, 1, steps[1], fresh=True)
    level_2.sweep(level_2.vb, level_2.va, 3, 30, 28, 1, 1, steps[2])
    level_2.residual(level_2.va, level_2.vb, 4, 29, 26, 1)

    for at in range(1, 14):
        level_3.s[0, at] = restrict_2(level_2.vb, at)
    coarse = cheb(4)
    level_3.start(1, 13, 13, 1, coarse[0][1])
    level_3.sweep(level_3.va, level_3.vb, 2, 12, 11, 1, 1, coarse[1], fresh=True)
    level_3.sweep(level_3.vb, level_3.va, 3, 11, 9, 1, 1, coarse[2])
    level_3.sweep(level_3.va, level_3.vb, 4, 10, 7, 1, 1, coarse[3])

    for at in range(10, 24):
        level_2.vb[0, at] = level_2.va[0, at] + level_3.vb[0, (at - 2) // 2]
    level_2.sweep(level_2.vb, level_2.va, 11, 22, 12, 1, 1, steps[0], fresh=True)
    level_2.sweep(level_2.va, level_2.vb, 12, 21, 10, 1, 1, steps[1])
    level_2.sweep(level_2.vb, level_2.va, 13, 20, 8, 1, 1, steps[2])

    for at in range(8):
        value = level_2.va[0, 13 + at]
        for part in range(2):
            p1[at, pl.ds(part, 8, stride=2), :] = value
    receive_sides(from_x1, 48)
    for side in range(2):
        pl.when(reach[side] >= 2)(functools.partial(receive, from_x1b + side, 16))
    for at in range(14):
        if 4 <= at <= 9:
            before = level_1.va[0, at]
        else:
            before = rx1b[0] if at == 0 else rx1[0, at - 1] if at < 4 else rx1[1, at - 10] if at < 13 else rx1b[1]
        level_1.vb[0, at] = before + p1[(at + 1) // 2]
    level_1.sweep(level_1.vb, level_1.va, 1, 12, 12, 1, 1, steps[0], fresh=True)
    level_1.sweep(level_1.va, level_1.vb, 2, 11, 10, 1, 1, steps[1])
    level_1.sweep(level_1.vb, level_1.va, 3, 10, 8, 1, 1, steps[2])

    fine_lane = lanes(16) // 2
    for at in range(8):
        value = level_1.va[0, 3 + at]
        for k in range(2):
            fine = jnp.take_along_axis(value, (fine_lane + (32 if k == 0 else 96)) % LANES, axis=1)
            for part in range(2):
                p0[k, at, pl.ds(part, 16, stride=2), :] = fine
    receive_sides(from_x0, 72)
    for side in range(2):
        packed = hx0[side, pl.ds(64, 8), :]
        for layer in range(2):
            at = (1 if side == 0 else 13) + layer
            coarse_at = (at - 4) // 2 + 2
            level_0.vb[0, at] = hx0[side, pl.ds(32 * layer, 32), :] + p0[0, coarse_at]
            for part in range(4):
                rows = pl.ds(8 * part, 8)
                level_0.vb[1, at, rows, :] = (
                    unpack(packed, 4 * layer + part) * level_0.lane_mask[1][:8] + p0[1, coarse_at, rows, :]
                )

    def correct(at):
        for k in range(2):
            level_0.vb[k, at] = level_0.va[k, at] + p0[k, at // 2]

    over_layers(3, 12, 5, correct)
    level_0.sweep(level_0.vb, level_0.va, 2, 13, 6, 2, 2, steps[0], fresh=True)
    level_0.sweep(level_0.va, level_0.vb, 3, 12, 5, 2, 2, steps[1])
    level_0.finish(level_0.vb, level_0.va, kept, added, 4, 11, 8, steps[2])


def per_device(right_side, conductivity, wide, narrow):
    brick = (8, 32, LANES)
    scratch = []
    for shape in LEVEL_SHAPES:
        scratch += [pltpu.VMEM(shape, F32)] * LEVEL_FIELDS
    shapes = [
        (2, 64, LANES), (2, 64, LANES), (2, 2, 16, LANES),
        (2, 2, 16, LANES), (2, 32, LANES), (2, 2, 16, LANES),
        (32, LANES), (2, 16, LANES), (2, 32, LANES), (2, 2, 16, LANES), (2, 32, LANES),
        (2 * REACH + 1, 8, LANES), (8, LANES), (2 * REACH + 1, 8, LANES),
        (2, 3, 16, LANES), (2, 16, LANES),
        (2, 72, LANES), (2, 72, LANES),
        (8, 16, LANES), (2, 8, 32, LANES),
        (RULER, LANES),
    ]
    scratch += [pltpu.VMEM(shape, F32) for shape in shapes]
    scratch += [pltpu.SemaphoreType.DMA((2,)), pltpu.SemaphoreType.DMA((SENDERS,)), pltpu.SemaphoreType.DMA((GROUPS,))]
    kept, added = pl.pallas_call(
        functools.partial(kernel, wide, narrow),
        out_shape=[jax.ShapeDtypeStruct(brick, F32)] * 2,
        in_specs=[pl.BlockSpec(memory_space=pltpu.HBM)] * 2,
        out_specs=[pl.BlockSpec(memory_space=pltpu.VMEM)] * 2,
        scratch_shapes=scratch,
        compiler_params=pltpu.CompilerParams(
            collective_id=0, has_side_effects=True, vmem_limit_bytes=32 * 1024 * 1024
        ),
    )(pltpu.with_memory_space_constraint(right_side, pltpu.HBM), pltpu.with_memory_space_constraint(conductivity, pltpu.HBM))
    return kept + added


def solution(mesh):
    spec = P("wide", None, "narrow")
    body = functools.partial(per_device, wide=mesh.shape["wide"], narrow=mesh.shape["narrow"])
    return jax.shard_map(body, mesh=mesh, in_specs=(spec, spec), out_specs=spec, check_vma=False)
```

```python
import functools

import jax
import jax.numpy as jnp
from jax import lax
from jax.experimental import pallas as pl
from jax.experimental.pallas import tpu as pltpu
from jax.sharding import PartitionSpec as P

CENTER = 1.125
HALF = 0.875
LANES = 128
REACH = 8
HALF_REACH = 4
F32 = jnp.float32
MESH_ID = pl.DeviceIdType.MESH


def cheb(sweeps):
    sigma = CENTER / HALF
    steps = [(0.0, 1.0 / CENTER)]
    ratio = 1.0 / sigma
    for _ in range(sweeps - 1):
        ratio_next = 1.0 / (2.0 * sigma - ratio)
        steps.append((ratio_next * ratio, 2.0 * ratio_next / HALF))
        ratio = ratio_next
    return steps


def over_sides(first, second, count, body):
    for base in (first, second):
        for at in range(count):
            body(base + at)


def over_layers(low, high, unroll, body):
    count = high - low + 1
    if count == unroll:
        for at in range(low, high + 1):
            body(at)
        return

    def block(step, carry):
        for at in range(unroll):
            body(low + step * unroll + at)
        return carry

    lax.fori_loop(0, count // unroll, block, 0)


class Level:
    def __init__(self, refs, scale, rows, row_step, lane_step, base, extent, lane_mask):
        self.c, self.s, self.cx, self.cy, self.cz, self.iv, self.dg, self.va, self.vb = refs
        self.half = 0.5 * scale
        self.rows, self.row_step, self.lane_step = rows, row_step, lane_step
        self.base, self.extent, self.lane_mask = base, extent, lane_mask

    def inside(self, at):
        where_x = self.base + at
        return jnp.where((where_x >= 0) & (where_x < self.extent), 1.0, 0.0).astype(F32)

    def lane(self):
        return lax.broadcasted_iota(jnp.int32, (self.rows, LANES), 1)

    def row(self):
        return lax.broadcasted_iota(jnp.int32, (self.rows, LANES), 0)

    def y_up(self, tile):
        return pltpu.roll(tile, self.rows - self.row_step, 0)

    def y_down(self, tile):
        return pltpu.roll(tile, self.row_step, 0)

    def turned(self, tiles, shift, edge, count):
        out = [pltpu.roll(t, shift, 1) for t in tiles]
        if len(tiles) == 1:
            return out
        at_edge = self.lane() == edge
        return [jnp.where(at_edge, out[1 - k], out[k]) for k in range(count)]

    def z_up(self, tiles, count):
        return self.turned(tiles, LANES - self.lane_step, LANES - 1, count)

    def z_down(self, tiles, count):
        return self.turned(tiles, self.lane_step, 0, count)

    def masked(self, at, tiles):
        keep = self.inside(at) * self.half
        out = []
        for k in range(tiles):
            mask = self.lane_mask[k]
            out.append(self.c[k, at] * (keep if mask is None else mask * keep))
        return out

    def setup_below(self, low, tiles):
        first, second = self.masked(low - 1, tiles), self.masked(low, tiles)
        for k in range(tiles):
            self.cx[k, low - 1] = first[k] + second[k]

    def setup_at(self, at, tiles):
        before, here, after = self.masked(at - 1, tiles), self.masked(at, tiles), self.masked(at + 1, tiles)
        inside = self.inside(at)
        top = self.row() >= self.rows - self.row_step
        bottom = self.row() < self.row_step
        z_up, z_down = self.z_up(here, tiles), self.z_down(here, tiles)
        for k in range(tiles):
            own = here[k]
            x_low = before[k] + own
            x_high = own + after[k]
            y_low = own + jnp.where(bottom, 0.0, self.y_down(own))
            y_high = own + jnp.where(top, 0.0, self.y_up(own))
            z_low = own + z_down[k]
            z_high = own + z_up[k]
            diagonal = x_low + x_high + y_low + y_high + z_low + z_high
            keep = inside if self.lane_mask[k] is None else self.lane_mask[k] * inside
            self.cx[k, at] = x_high
            self.cy[k, at] = jnp.where(top, 0.0, y_high)
            self.cz[k, at] = z_high
            if k == 0:
                self.dg[0, at] = diagonal
            self.iv[k, at] = jnp.where(jnp.full_like(own, 0.0) + keep > 0.5, 1.0 / diagonal, 0.0)

    def setup(self, low, high, unroll, tiles):
        self.setup_below(low, tiles)
        over_layers(low, high, unroll, lambda at: self.setup_at(at, tiles))

    def start_at(self, at, tiles, beta):
        for k in range(tiles):
            self.va[k, at] = self.s[k, at] * self.iv[k, at] * beta

    def start_outer(self, at, beta):
        self.va[1, at] = self.s[1, at] * self.iv[1, at] * beta

    def start(self, low, high, unroll, tiles, beta):
        over_layers(low, high, unroll, lambda at: self.start_at(at, tiles, beta))

    def around(self, field, at, tiles, count):
        here = [field[k, at] for k in range(tiles)]
        cz = [self.cz[k, at] for k in range(tiles)]
        z_up = self.z_up(here, count)
        z_down = self.z_down([cz[k] * here[k] for k in range(tiles)], count)
        sums = []
        for k in range(count):
            cy = self.cy[k, at]
            total = self.cx[k, at] * field[k, at + 1] + self.cx[k, at - 1] * field[k, at - 1]
            total = total + (cy * self.y_up(here[k]) + self.y_down(cy * here[k]))
            total = total + (cz[k] * z_up[k] + z_down[k])
            sums.append(total + self.s[k, at])
        return here, sums

    def sweep_at(self, at, field, result, tiles, count, step, fresh):
        alpha, beta = step
        here, sums = self.around(field, at, tiles, count)
        for k in range(count):
            kept = (1.0 + alpha - beta) * here[k]
            if not fresh:
                kept = kept - alpha * result[k, at]
            result[k, at] = kept + (beta * self.iv[k, at]) * sums[k]

    def sweep(self, field, result, low, high, unroll, tiles, count, step, fresh=False):
        over_layers(low, high, unroll, lambda at: self.sweep_at(at, field, result, tiles, count, step, fresh))

    def residual_at(self, at, field, result, tiles):
        here, sums = self.around(field, at, tiles, 1)
        result[0, at] = sums[0] - self.dg[0, at] * here[0]

    def residual(self, field, result, low, high, unroll, tiles):
        over_layers(low, high, unroll, lambda at: self.residual_at(at, field, result, tiles))

    def last_at(self, at, field, older, step):
        alpha, beta = step
        here, sums = self.around(field, at, 1, 1)
        return (1.0 + alpha - beta) * here[0] - alpha * older[0, at], (beta * self.iv[0, at]) * sums[0]


class Strips:
    def __init__(self, refs, base, extent, left, right):
        self.c, self.s, self.cx, self.cy, self.cz, self.iv, self.dg, self.va, self.vb = refs
        self.base, self.extent, self.left, self.right = base, extent, left, right

    def lane(self):
        return lax.broadcasted_iota(jnp.int32, (32, LANES), 1)

    def mask(self, pack):
        where_x = self.base + 4 * pack + self.lane() // 32
        cell = self.lane() % 32
        keep = jnp.where(cell < 8, self.left, jnp.where(cell >= 24, self.right, 1.0))
        return jnp.where((where_x >= 0) & (where_x < self.extent), keep, 0.0)

    def x_up(self, tiles):
        turned = [pltpu.roll(t, LANES - 32, 1) for t in tiles]
        return [jnp.where(self.lane() < LANES - 32, turned[p], turned[min(p + 1, 3)]) for p in range(4)]

    def x_down(self, tiles):
        turned = [pltpu.roll(t, 32, 1) for t in tiles]
        return [jnp.where(self.lane() >= 32, turned[p], turned[max(p - 1, 0)]) for p in range(4)]

    def setup(self):
        row = lax.broadcasted_iota(jnp.int32, (32, LANES), 0)
        top, bottom = row == 31, row == 0
        masks = [self.mask(p) for p in range(4)]
        own = [self.c[p] * (0.5 * masks[p]) for p in range(4)]
        above = self.x_up(own)
        x_high = [own[p] + above[p] for p in range(4)]
        x_low = self.x_down(x_high)
        for p in range(4):
            y_high = own[p] + jnp.where(top, 0.0, pltpu.roll(own[p], 31, 0))
            y_low = jnp.where(bottom, own[p], pltpu.roll(y_high, 1, 0))
            z_high = own[p] + pltpu.roll(own[p], LANES - 1, 1)
            z_low = pltpu.roll(z_high, 1, 1)
            diagonal = x_low[p] + x_high[p] + y_low + y_high + z_low + z_high
            self.cx[p] = x_high[p]
            self.cy[p] = jnp.where(top, 0.0, y_high)
            self.cz[p] = z_high
            self.dg[p] = diagonal
            self.iv[p] = jnp.where(masks[p] > 0.5, 1.0 / diagonal, 0.0)

    def start(self, beta):
        for p in range(4):
            self.va[p] = self.s[p] * self.iv[p] * beta

    def around(self, field):
        here = [field[p] for p in range(4)]
        cx = [self.cx[p] for p in range(4)]
        x_up = self.x_up(here)
        x_down = self.x_down([cx[p] * here[p] for p in range(4)])
        sums = []
        for p in range(4):
            cy, cz = self.cy[p], self.cz[p]
            total = cx[p] * x_up[p] + x_down[p]
            total = total + (cy * pltpu.roll(here[p], 31, 0) + pltpu.roll(cy * here[p], 1, 0))
            total = total + (cz * pltpu.roll(here[p], LANES - 1, 1) + pltpu.roll(cz * here[p], 1, 1))
            sums.append(total + self.s[p])
        return here, sums

    def sweep(self, field, result, step, fresh=False):
        alpha, beta = step
        here, sums = self.around(field)
        for p in range(4):
            kept = (1.0 + alpha - beta) * here[p]
            if not fresh:
                kept = kept - alpha * result[p]
            result[p] = kept + (beta * self.iv[p]) * sums[p]

    def residual(self, field, result):
        here, sums = self.around(field)
        for p in range(4):
            result[p] = sums[p] - self.dg[p] * here[p]

    def own(self, ref, pack, layers=range(4)):
        cell = self.lane() % 32
        packed = jnp.zeros((32, LANES), F32)
        for layer in layers:
            tile = ref[0, 4 * pack + layer]
            first = pltpu.roll(tile, 32 * layer + 8, 1)
            last = pltpu.roll(tile, (32 * layer + 24) % LANES, 1)
            packed = jnp.where(self.lane() // 32 == layer, jnp.where(cell < 16, first, last), packed)
        return packed

    def take_halo(self, ref, pack, from_left, from_right):
        cell = lax.broadcasted_iota(jnp.int32, (8, LANES), 1) % 32
        for part in range(4):
            rows = pl.ds(8 * part, 8)
            below = pltpu.roll(from_left, (LANES - 8 * part) % LANES, 1)
            above = pltpu.roll(from_right, 24 - 8 * part, 1) if part < 3 else from_right
            ref[pack, rows, :] = jnp.where(cell < 8, below, jnp.where(cell >= 24, above, ref[pack, rows, :]))

    def give_halo(self, ref, pack, side):
        cell = lax.broadcasted_iota(jnp.int32, (8, LANES), 1) % 32
        packed = None
        for part in range(4):
            shift = (8 * part - 8 - 8 * side) % LANES
            tile = ref[pack, pl.ds(8 * part, 8), :]
            tile = pltpu.roll(tile, shift, 1) if shift else tile
            packed = tile if part == 0 else jnp.where(cell // 8 == part, tile, packed)
        return packed

    def mend(self, tile, ref, at):
        packed, layer = ref[at // 4], at % 4
        first = pltpu.roll(packed, (LANES - 32 * layer - 8) % LANES, 1)
        last = pltpu.roll(packed, (LANES + 104 - 32 * layer) % LANES, 1)
        return jnp.where(self.lane() < 4, first, jnp.where(self.lane() >= LANES - 4, last, tile))


LEVEL_FIELDS = 9
LEVEL_SHAPES = ((1, 16, 32, LANES), (2, 14, 16, LANES), (1, 34, 8, LANES), (1, 15, 8, LANES))
RULER = 1024
SENDERS = 14 + 2 * (2 * REACH + 1)
GROUPS = 36 + 2 * (2 * REACH + 1)


def kernel(wide, narrow, rhs, coef, kept, added, *scratch):
    scratch = list(scratch)
    level_refs = []
    for _ in range(4):
        level_refs.append(scratch[:LEVEL_FIELDS])
        scratch = scratch[LEVEL_FIELDS:]
    strip_refs, scratch = scratch[:LEVEL_FIELDS], scratch[LEVEL_FIELDS:]
    (ps, zs, rz, rcn, kp, k1cx, k1c, sk, sp, k1x, k1p, k1z, rc2, s2m, rs2, rx1, rx1b, sb0, hx0, p1, p0, ruler,
     local_sem, send_sem, recv_sem) = scratch
    me_w = lax.axis_index("wide")
    me_n = lax.axis_index("narrow")

    def there(dw, dn):
        return (lax.rem(me_w + (dw + wide), wide), lax.rem(me_n + (dn + narrow), narrow))

    has = (me_w > 0, me_w < wide - 1)
    has_z = (me_n > 0, me_n < narrow - 1)
    reach = (jnp.minimum(me_w, REACH), jnp.minimum(wide - 1 - me_w, REACH))

    def for_far(first, body, last=REACH):
        for side in range(2):
            sign = 2 * side - 1

            def step(k, carry):
                body(REACH + sign * k, sign * k)
                return carry

            lax.fori_loop(first, jnp.minimum(reach[side], last) + 1, step, 0)

    def for_sides(body):
        for side in range(2):
            pl.when(has[side])(functools.partial(body, side, 2 * side - 1))

    def for_sides_z(body):
        for side in range(2):
            pl.when(has_z[side])(functools.partial(body, side, 2 * side - 1))

    def for_corners(body):
        for side in range(2):
            for side_z in range(2):
                pl.when(has[side] & has_z[side_z])(
                    functools.partial(body, side, side_z, 2 * side - 1, 2 * side_z - 1)
                )

    @pl.when((me_n == 0) | (me_n == narrow - 1))
    def clear_z():
        for ref in (rz, rcn, k1c, k1z, k1p):
            ref[...] = jnp.zeros(ref.shape, F32)

    @pl.when((me_w < REACH) | (me_w >= wide - REACH))
    def clear():
        def zero(ref):
            ref[...] = jnp.zeros(ref.shape, F32)

        for ref in (rcn, rx1, rx1b, hx0, rc2, rs2, k1cx, k1c, k1x, k1p):
            zero(ref)
        for side in range(2):
            for ref in level_refs[0][:2]:
                zero(ref.at[0, pl.ds(12 * side, 4)])
            zero(level_refs[1][0].at[0, 13 * side])

    def if_reach(least, body):
        for side in range(2):
            pl.when(reach[side] >= least)(functools.partial(body, side, 2 * side - 1))

    barrier = pltpu.get_barrier_semaphore()

    def greet(dw, dn):
        pl.semaphore_signal(barrier, inc=1, device_id=there(dw, dn), device_id_type=MESH_ID)

    for_far(1, lambda slot, dw: greet(dw, 0), HALF_REACH)
    for_sides_z(lambda side, dn: greet(0, dn))
    for_corners(lambda side, side_z, dw, dn: greet(dw, dn))

    c0, s0 = level_refs[0][0], level_refs[0][1]
    load_c = pltpu.make_async_copy(coef, c0.at[0, pl.ds(4, 8)], local_sem.at[0])
    load_s = pltpu.make_async_copy(rhs, s0.at[0, pl.ds(4, 8)], local_sem.at[1])
    load_c.start()
    load_s.start()
    beside_x = jnp.where(has[0], 1, 0) + jnp.where(has[1], 1, 0)
    beside_z = jnp.where(has_z[0], 1, 0) + jnp.where(has_z[1], 1, 0)
    greeted = beside_z + beside_x * beside_z
    for side in range(2):
        greeted = greeted + jnp.minimum(reach[side], HALF_REACH)

    left = jnp.where(me_n > 0, 1.0, 0.0).astype(F32)
    right = jnp.where(me_n < narrow - 1, 1.0, 0.0).astype(F32)

    def lanes(rows):
        return lax.broadcasted_iota(jnp.int32, (rows, LANES), 1)

    def edges(rows, until, low, since, high):
        at = lanes(rows)
        return jnp.where(at < until, low, jnp.where(at >= since, high, 0.0))

    def centred(rows):
        at = lanes(rows)
        return jnp.where((at >= 32) & (at < 96), 1.0, edges(rows, 32, left, 96, right))

    level_0 = Level(level_refs[0], 1.0, 32, 1, 1, 8 * me_w - 4, 8 * wide, [None])
    strips = Strips(strip_refs, 8 * me_w - 4, 8 * wide, left, right)
    level_1 = Level(
        level_refs[1], 0.25, 16, 1, 1, 4 * me_w - 5, 4 * wide, [centred(16), edges(16, 32, right, 96, left)]
    )
    level_2 = Level(level_refs[2], 0.0625, 8, 1, 2, 2 * me_w - 16, 2 * wide, [centred(8)])
    level_3 = Level(level_refs[3], 0.015625, 8, 2, 4, me_w - 7, wide, [centred(8)])

    sent = [0] * SENDERS

    def send(group, src, dst, dw, dn, rows, sender):
        if isinstance(sender, int):
            sent[sender] += rows
        pltpu.make_async_remote_copy(
            src_ref=src, dst_ref=dst, send_sem=send_sem.at[sender], recv_sem=recv_sem.at[group],
            device_id=there(dw, dn), device_id_type=MESH_ID,
        ).start()

    def ruled(rows, group, sender):
        span = ruler.at[pl.ds(0, rows)]
        return pltpu.make_async_remote_copy(
            src_ref=span, dst_ref=span, send_sem=send_sem.at[sender], recv_sem=recv_sem.at[group],
            device_id=there(0, 1), device_id_type=MESH_ID,
        )

    def receive(group, rows):
        ruled(rows, group, 0).wait_recv()

    def receive_sides(group, rows):
        for_sides(lambda side, dw: receive(group + side, rows))

    def receive_sides_z(group, rows):
        for_sides_z(lambda side, dn: receive(group + side, rows))

    def receive_corners(group, rows):
        for_corners(lambda side, side_z, dw, dn: receive(group + 2 * side + side_z, rows))

    def receive_far(group, last=REACH):
        for_far(1, lambda slot, dw: receive(group + slot, 8), last)

    def sends_done(sender):
        ruled(sent[sender], 0, sender).wait_send()

    from_z, from_s1z = 0, 2
    from_c_corner, from_k_corner, from_s1_corner = 4, 8, 12
    from_c, from_s, from_s_next, from_k, from_s1, from_c1b, from_x0, from_x1, from_x1b = range(16, 34, 2)
    from_four = 34
    from_c2 = 36
    from_s2 = from_c2 + 2 * REACH + 1
    sender_x, sender_x1, sender_x1b, sender_four, sender_z = range(0, 10, 2)
    sender_corner, sender_c2, sender_far = 10, 14, 14 + 2 * REACH + 1

    def restrict_0(ref):
        out = []
        for layer in range(4):
            total = None
            for dx in range(2):
                for dy in range(2):
                    term = ref[0, 4 + 2 * layer + dx, pl.ds(dy, 16, stride=2), :]
                    total = term if total is None else total + term
            total = total + pltpu.roll(total, LANES - 1, 1)
            out.append(0.125 * jnp.take_along_axis(total, (2 * lanes(16) + 64) % LANES, axis=1))
        return out

    odd_8 = lanes(8) % 2 == 1

    def pairs_1(ref):
        out = []
        for layer in range(2):
            total = None
            for dx in range(2):
                for dy in range(2):
                    term = ref[0, 5 + 2 * layer + dx, pl.ds(dy, 8, stride=2), :]
                    total = term if total is None else total + term
            total = total + jnp.where(odd_8, pltpu.roll(total, 1, 1), pltpu.roll(total, LANES - 1, 1))
            out.append(0.125 * total)
        return jnp.where(odd_8, out[1], out[0])

    def squeeze_1(layers, ref, row):
        for part in range(2):
            ref[pl.ds(row + 16 * part, 16), :] = jnp.where(lanes(16) < 64, layers[part], layers[part + 2])

    pl.semaphore_wait(barrier, greeted)

    @for_sides
    def send_faces(side, dw):
        send(from_c + 1 - side, coef.at[pl.ds(4 * side, 4)], c0.at[0, pl.ds(12 - 12 * side, 4)], dw, 0, 128, sender_x + side)
        send(from_s + 1 - side, rhs.at[7 * side], s0.at[0, 12 - 9 * side], dw, 0, 32, sender_x + side)

    def squeeze_halves(first, second):
        low_quarter = lanes(16) % 64 < 32
        return (
            jnp.where(low_quarter, pltpu.roll(first, 96, 1), second),
            jnp.where(low_quarter, first, pltpu.roll(second, 32, 1)),
        )

    load_c.wait()
    own_c1 = restrict_0(c0)
    for half in range(2):
        strips.c[1 + half] = strips.own(c0, 1 + half)
    for side in range(2):
        squeeze_1(own_c1, zs.at[side], 32)
        for half in range(2):
            zs[side, pl.ds(16 * half, 8), :] = strips.give_halo(strips.c, 1 + half, side)
    load_s.wait()
    for half in range(2):
        strips.s[1 + half] = strips.own(s0, 1 + half)
    for side in range(2):
        for half in range(2):
            zs[side, pl.ds(16 * half + 8, 8), :] = strips.give_halo(strips.s, 1 + half, side)

    for_sides_z(
        lambda side, dn: send(from_z + 1 - side, zs.at[side], rz.at[1 - side], 0, dn, 64, sender_z + side)
    )

    def send_corner(group, src, dst, rows, side, side_z):
        at = 2 * side + side_z
        send(group + 3 - at, src, dst, 2 * side - 1, 2 * side_z - 1, rows, sender_corner + at)

    @for_corners
    def send_c_corner(side, side_z, dw, dn):
        src = zs.at[side_z, pl.ds(16 * side, 16)]
        send_corner(from_c_corner, src, rcn.at[1 - side, 1 - side_z], 16, side, side_z)

    @for_sides
    def send_s_next(side, dw):
        src = rhs.at[pl.ds(1 + 4 * side, 2)]
        send(from_s_next + 1 - side, src, s0.at[0, pl.ds(13 - 12 * side, 2)], dw, 0, 64, sender_x + side)

    steps = cheb(3)
    sweep_a = (level_0.va, level_0.vb, 1, 1, steps[1], True)
    sweep_b = (level_0.vb, level_0.va, 1, 1, steps[2], False)
    level_0.setup(5, 10, 6, 1)
    level_0.start(5, 10, 6, 1, steps[0][1])
    over_layers(6, 9, 4, lambda at: level_0.sweep_at(at, *sweep_a))
    over_layers(7, 8, 2, lambda at: level_0.sweep_at(at, *sweep_b))

    def take_halos(field, ref, pack, got):
        rows = pl.ds(8 * field + (16 if pack == 2 else 0), 8)
        strips.take_halo(ref, pack, got[0, rows, :], got[1, rows, :])

    receive_sides_z(from_z, 64)
    for field, ref in enumerate((strips.c, strips.s)):
        for half in range(2):
            take_halos(field, ref, 1 + half, rz)

    def spread_1(ref, block):
        at_lane = lanes(16)
        low_half = at_lane < 64
        low_quarter = at_lane % 64 < 32
        for part in range(2):
            before, own, after = (block(dz, part) for dz in (-1, 0, 1))
            near = jnp.where(low_quarter, before, after)
            outer = jnp.where(low_quarter, after, before)
            own_r, near_r, outer_r = (pltpu.roll(t, 64, 1) for t in (own, near, outer))
            at = 5 + part
            for at, own_a, own_b, near_a, near_b, outer_a, outer_b in (
                (at, own, own_r, near, near_r, outer, outer_r),
                (at + 2, own_r, own, near_r, near, outer_r, outer),
            ):
                centre = jnp.where(low_half, own_a, own_b)
                ref[0, at] = jnp.where(at_lane < 32, near_a, jnp.where(at_lane < 96, centre, near_b))
                ref[1, at] = jnp.where(low_half, outer_a, outer_b)

    def coef_block(dz, part):
        rows = pl.ds(32 + 16 * part, 16)
        return zs[0, rows, :] if dz == 0 else rz[(1 + dz) // 2, rows, :]

    spread_1(level_1.c, coef_block)
    rc2[REACH] = pairs_1(level_1.c)

    for_far(
        1,
        lambda slot, dw: send(
            from_c2 + 2 * REACH - slot, rc2.at[REACH], rc2.at[2 * REACH - slot], dw, 0, 8, sender_c2 + slot
        ),
        HALF_REACH,
    )
    k1_own = zs.at[0, pl.ds(32, 32)]
    halves = squeeze_halves(zs[0, pl.ds(32, 16), :], zs[0, pl.ds(48, 16), :])
    at_lane = lanes(16)
    for side in range(2):
        near, far = (0, 3) if side == 0 else (3, 0)
        full = level_1.c[0, 5 + near]
        place = (32 * far + 31, 32 * far)
        cell = (64, 63)
        for side_z in range(2):
            moved = pltpu.roll(full, (place[side_z] - cell[side_z]) % LANES, 1)
            kp[side, side_z] = jnp.where(at_lane == place[side_z], moved, halves[side_z])
    for_sides(
        lambda side, dw: send(from_k + 1 - side, k1_own, k1cx.at[1 - side], dw, 0, 32, sender_x + side)
    )
    for_corners(
        lambda side, side_z, dw, dn: send_corner(
            from_k_corner, kp.at[side, side_z], k1c.at[1 - side, 1 - side_z], 16, side, side_z
        )
    )

    receive_sides(from_c, 128)
    receive_corners(from_c_corner, 16)
    for side in range(2):
        strips.c[3 * side] = strips.own(c0, 3 * side)
        take_halos(0, strips.c, 3 * side, rcn.at[side])
    level_0.setup_below(1, 1)
    over_sides(1, 11, 4, lambda at: level_0.setup_at(at, 1))
    strips.setup()
    receive_sides(from_s, 32)
    over_sides(3, 11, 2, lambda at: level_0.start_at(at, 1, steps[0][1]))
    over_sides(4, 10, 2, lambda at: level_0.sweep_at(at, *sweep_a))
    over_sides(5, 9, 2, lambda at: level_0.sweep_at(at, *sweep_b))
    over_layers(6, 9, 4, lambda at: level_0.residual_at(at, level_0.va, level_0.vb, 1))
    receive_sides(from_s_next, 64)
    for side in range(2):
        strips.s[3 * side] = strips.own(s0, 3 * side, range(1 - side, 4 - side))
        take_halos(1, strips.s, 3 * side, rcn.at[side])
    over_sides(1, 13, 2, lambda at: level_0.start_at(at, 1, steps[0][1]))
    strips.start(steps[0][1])
    over_sides(2, 12, 2, lambda at: level_0.sweep_at(at, *sweep_a))
    strips.sweep(strips.va, strips.vb, steps[1], fresh=True)
    over_sides(3, 11, 2, lambda at: level_0.sweep_at(at, *sweep_b))
    strips.sweep(strips.vb, strips.va, steps[2])
    over_sides(4, 10, 2, lambda at: level_0.residual_at(at, level_0.va, level_0.vb, 1))
    strips.residual(strips.va, strips.vb)
    for at in range(4, 12):
        level_0.vb[0, at] = strips.mend(level_0.vb[0, at], strips.vb, at)

    squeeze_1(restrict_0(level_0.vb), sk, 0)

    sp[0], sp[1] = squeeze_halves(sk[pl.ds(0, 16), :], sk[pl.ds(16, 16), :])

    for_sides(lambda side, dw: send(from_s1 + 1 - side, sk, k1x.at[1 - side], dw, 0, 32, sender_x + side))
    for_corners(
        lambda side, side_z, dw, dn: send_corner(
            from_s1_corner, sp.at[side_z], k1p.at[1 - side, 1 - side_z], 16, side, side_z
        )
    )
    for_sides_z(lambda side, dn: send(from_s1z + 1 - side, sk, k1z.at[1 - side], 0, dn, 32, sender_z + side))

    receive_far(from_c2, HALF_REACH)

    @functools.partial(if_reach, HALF_REACH)
    def send_four(side, sign):
        src, dst = rc2.at[pl.ds(9 - 5 * side, 4)], rc2.at[pl.ds(13 - 13 * side, 4)]
        send(from_four + 1 - side, src, dst, HALF_REACH * sign, 0, 32, sender_four + side)

    for at in range(3, 13):
        level_0.va[0, at] = strips.mend(level_0.va[0, at], strips.va, at)
    own_cell = (strips.lane() % 32 >= 8) & (strips.lane() % 32 < 24)
    for pack_at, layers in enumerate(((3,), range(4), range(4), (0,))):
        strips.va[pack_at] = jnp.where(own_cell, strips.own(level_0.va, pack_at, layers), strips.va[pack_at])
    for side in range(2):
        first = 9 if side == 0 else 5
        for layer in range(2):
            sb0[side, pl.ds(32 * layer, 32), :] = level_0.va[0, first + layer]
        packed = strips.va[2 - side]
        middle = (lanes(16) >= 32) & (lanes(16) < 96)
        sb0[side, pl.ds(64, 16), :] = jnp.where(middle, packed[:16], pltpu.roll(packed[16:], 64, 1))

    @for_sides
    def send_iterate_0(side, dw):
        send(from_x0 + 1 - side, sb0.at[1 - side], hx0.at[1 - side], dw, 0, 80, sender_x + side)

    def source_block(dz, part):
        rows = pl.ds(16 * part, 16)
        return sk[rows, :] if dz == 0 else k1z[(1 + dz) // 2, rows, :]

    def spread_beside(ref, blocks, packs):
        at_lane = lanes(16)
        low_half = at_lane < 64
        for side in range(2):
            for layer in range(4):
                own = blocks[side, pl.ds(16 * (layer % 2), 16), :]
                other = pltpu.roll(own, 64, 1)
                centre = jnp.where(low_half, own, other) if layer < 2 else jnp.where(low_half, other, own)
                before = pltpu.roll(packs[side, 0], (LANES - 32 * layer) % LANES, 1)
                after = pltpu.roll(packs[side, 1], (LANES + 96 - 32 * layer) % LANES, 1)
                ref[0, 1 + 8 * side + layer] = jnp.where(at_lane < 32, before, jnp.where(at_lane < 96, centre, after))

    receive_sides(from_k, 32)
    receive_corners(from_k_corner, 16)
    spread_beside(level_1.c, k1cx, k1c)
    for side in range(2):
        far = 3 if side == 1 else 0
        below, above = (pltpu.roll(k1c[side, side_z], (shift - 32 * far) % LANES, 1)
                        for side_z, shift in ((0, 127), (1, -31)))
        level_1.c[1, 4 + 5 * side] = jnp.where(lanes(16) < 64, above, below)

    @for_sides
    def send_coef_1(side, dw):
        send(from_c1b + 1 - side, level_1.c.at[0, 9 - 5 * side], level_1.c.at[0, 13 - 13 * side], dw, 0, 16, sender_x + side)

    level_1.setup_below(2, 1)
    over_sides(2, 10, 2, lambda at: level_1.setup_at(at, 1))
    over_layers(4, 9, 6, lambda at: level_1.setup_at(at, 2))

    receive_sides_z(from_s1z, 32)
    spread_1(level_1.s, source_block)
    receive_sides(from_s1, 32)
    receive_corners(from_s1_corner, 16)
    spread_beside(level_1.s, k1x, k1p)
    level_1.start(2, 11, 10, 1, steps[0][1])
    over_layers(5, 8, 4, lambda at: level_1.start_outer(at, steps[0][1]))
    over_sides(3, 9, 2, lambda at: level_1.sweep_at(at, level_1.va, level_1.vb, 1, 1, steps[1], True))
    over_layers(5, 8, 4, lambda at: level_1.sweep_at(at, level_1.va, level_1.vb, 2, 1, steps[1], True))
    level_1.sweep(level_1.vb, level_1.va, 4, 9, 6, 1, 1, steps[2])
    level_1.residual(level_1.va, level_1.vb, 5, 8, 4, 1)

    value = pairs_1(level_1.vb)
    s2m[...] = value
    rs2[REACH] = value

    def send_far(at, carry):
        for side in range(2):
            k = REACH - at
            slot, dw = REACH + (2 * side - 1) * k, (2 * side - 1) * k

            @pl.when(k <= reach[side])
            def send_one():
                send(from_s2 + 2 * REACH - slot, s2m, rs2.at[2 * REACH - slot], dw, 0, 8, sender_far + slot)

        return carry

    lax.fori_loop(0, REACH, send_far, 0)

    @for_sides
    def send_iterate_1(side, dw):
        send(from_x1 + 1 - side, level_1.va.at[0, pl.ds(6 - side, 3)], rx1.at[1 - side], dw, 0, 48, sender_x1 + side)

    for side in range(2):
        @pl.when(reach[side] >= 2)
        def send_next_1():
            layer = level_1.va.at[0, 5 + 3 * side]
            send(from_x1b + 1 - side, layer, rx1b.at[1 - side], 4 * side - 2, 0, 16, sender_x1b + side)

    receive_sides(from_c1b, 16)
    level_1.setup_below(1, 1)
    over_sides(1, 12, 1, lambda at: level_1.setup_at(at, 1))

    def spread_2(ref, blocks):
        for block in range(2 * REACH + 1):
            packed = blocks[block]
            ref[0, 2 * block] = jnp.where(odd_8, pltpu.roll(packed, 1, 1), packed)
            ref[0, 2 * block + 1] = jnp.where(odd_8, packed, pltpu.roll(packed, LANES - 1, 1))

    def restrict_2(ref, at):
        total = ref[0, 2 * at + 2] + ref[0, 2 * at + 3]
        odd_row = lax.broadcasted_iota(jnp.int32, (8, LANES), 0) % 2 == 1
        total = total + jnp.where(odd_row, pltpu.roll(total, 1, 0), pltpu.roll(total, 7, 0))
        second = lanes(8) % 4 >= 2
        total = total + jnp.where(second, pltpu.roll(total, 2, 1), pltpu.roll(total, LANES - 2, 1))
        return 0.125 * total

    if_reach(HALF_REACH, lambda side, sign: receive(from_four + side, 32))
    spread_2(level_2.c, rc2)
    level_2.setup(1, 32, 16, 1)
    for at in range(15):
        level_3.c[0, at] = restrict_2(level_2.c, at)
    level_3.setup(1, 13, 13, 1)

    for_sides(lambda side, dw: sends_done(sender_x + side))
    for_sides_z(lambda side, dn: sends_done(sender_z + side))
    for_corners(lambda side, side_z, dw, dn: sends_done(sender_corner + 2 * side + side_z))
    if_reach(HALF_REACH, lambda side, sign: sends_done(sender_four + side))
    for_far(1, lambda slot, dw: ruled(8, 0, sender_c2 + slot).wait_send(), HALF_REACH)
    for_far(1, lambda slot, dw: ruled(8, 0, sender_far + slot).wait_send())
    for side in range(2):
        pl.when(has[side])(functools.partial(sends_done, sender_x1 + side))
        pl.when(reach[side] >= 2)(functools.partial(sends_done, sender_x1b + side))

    receive_far(from_s2)
    spread_2(level_2.s, rs2)
    level_2.start(1, 32, 32, 1, steps[0][1])
    level_2.sweep(level_2.va, level_2.vb, 2, 31, 30, 1, 1, steps[1], fresh=True)
    level_2.sweep(level_2.vb, level_2.va, 3, 30, 28, 1, 1, steps[2])
    level_2.residual(level_2.va, level_2.vb, 4, 29, 26, 1)

    for at in range(1, 14):
        level_3.s[0, at] = restrict_2(level_2.vb, at)
    coarse = cheb(4)
    level_3.start(1, 13, 13, 1, coarse[0][1])
    level_3.sweep(level_3.va, level_3.vb, 2, 12, 11, 1, 1, coarse[1], fresh=True)
    level_3.sweep(level_3.vb, level_3.va, 3, 11, 9, 1, 1, coarse[2])
    level_3.sweep(level_3.va, level_3.vb, 4, 10, 7, 1, 1, coarse[3])

    for at in range(10, 24):
        level_2.vb[0, at] = level_2.va[0, at] + level_3.vb[0, (at - 2) // 2]
    level_2.sweep(level_2.vb, level_2.va, 11, 22, 12, 1, 1, steps[0], fresh=True)
    level_2.sweep(level_2.va, level_2.vb, 12, 21, 10, 1, 1, steps[1])
    level_2.sweep(level_2.vb, level_2.va, 13, 20, 8, 1, 1, steps[2])

    for at in range(8):
        value = level_2.va[0, 13 + at]
        for part in range(2):
            p1[at, pl.ds(part, 8, stride=2), :] = value
    receive_sides(from_x1, 48)
    for side in range(2):
        pl.when(reach[side] >= 2)(functools.partial(receive, from_x1b + side, 16))
    for at in range(14):
        if 4 <= at <= 9:
            before = level_1.va[0, at]
        else:
            before = rx1b[0] if at == 0 else rx1[0, at - 1] if at < 4 else rx1[1, at - 10] if at < 13 else rx1b[1]
        level_1.vb[0, at] = before + p1[(at + 1) // 2]
    level_1.sweep(level_1.vb, level_1.va, 1, 12, 12, 1, 1, steps[0], fresh=True)
    level_1.sweep(level_1.va, level_1.vb, 2, 11, 10, 1, 1, steps[1])
    level_1.sweep(level_1.vb, level_1.va, 3, 10, 8, 1, 1, steps[2])

    cell = lanes(16) % 32
    strip_lane = jnp.where(cell < 16, 28, 84) + cell // 2
    low_half = lanes(16) < 64
    fine = []
    for at in range(8):
        value = level_1.va[0, 3 + at]
        own = jnp.take_along_axis(value, lanes(16) // 2 + 32, axis=1)
        fine.append(jnp.take_along_axis(value, strip_lane, axis=1))
        for part in range(2):
            p0[at, pl.ds(part, 16, stride=2), :] = own
    for pack in range(4):
        value = jnp.where(low_half, fine[2 * pack], fine[2 * pack + 1])
        for part in range(2):
            ps[pack, pl.ds(part, 16, stride=2), :] = value
    receive_sides(from_x0, 80)
    for side in range(2):
        for layer in range(2):
            at = (1 if side == 0 else 13) + layer
            level_0.vb[0, at] = hx0[side, pl.ds(32 * layer, 32), :] + p0[at // 2]
        packed = hx0[side, pl.ds(64, 16), :]
        layer = lanes(16) // 32
        for part, value in enumerate((packed, pltpu.roll(packed, 64, 1))):
            rows = pl.ds(16 * part, 16)
            own = jnp.where(layer == (3 if side == 0 else 0), strips.va[3 * side, rows, :], 0.0)
            value = jnp.where((layer == 1) | (layer == 2), value, own)
            strips.vb[3 * side, rows, :] = value + ps[3 * side, rows, :]
    for pack in (1, 2):
        strips.vb[pack] = strips.va[pack] + ps[pack]

    def correct(at):
        level_0.vb[0, at] = level_0.va[0, at] + p0[at // 2]

    over_layers(3, 12, 10, correct)
    level_0.sweep(level_0.vb, level_0.va, 2, 13, 12, 1, 1, steps[0], fresh=True)
    strips.sweep(strips.vb, strips.va, steps[0], fresh=True)
    level_0.sweep(level_0.va, level_0.vb, 3, 12, 10, 1, 1, steps[1])
    strips.sweep(strips.va, strips.vb, steps[1])
    strips.sweep(strips.vb, strips.va, steps[2])
    inner = (strips.lane() >= 4) & (strips.lane() < LANES - 4)
    for at in range(4, 12):
        kept_here, added_here = level_0.last_at(at, level_0.vb, level_0.va, steps[2])
        kept[at - 4] = strips.mend(kept_here, strips.va, at)
        added[at - 4] = jnp.where(inner, added_here, 0.0)


def per_device(right_side, conductivity, wide, narrow):
    brick = (8, 32, LANES)
    scratch = []
    for shape in LEVEL_SHAPES:
        scratch += [pltpu.VMEM(shape, F32)] * LEVEL_FIELDS
    scratch += [pltpu.VMEM((4, 32, LANES), F32)] * LEVEL_FIELDS
    shapes = [
        (4, 32, LANES),
        (2, 64, LANES), (2, 64, LANES), (2, 2, 16, LANES),
        (2, 2, 16, LANES), (2, 32, LANES), (2, 2, 16, LANES),
        (32, LANES), (2, 16, LANES), (2, 32, LANES), (2, 2, 16, LANES), (2, 32, LANES),
        (2 * REACH + 1, 8, LANES), (8, LANES), (2 * REACH + 1, 8, LANES),
        (2, 3, 16, LANES), (2, 16, LANES),
        (2, 80, LANES), (2, 80, LANES),
        (8, 16, LANES), (8, 32, LANES),
        (RULER, LANES),
    ]
    scratch += [pltpu.VMEM(shape, F32) for shape in shapes]
    scratch += [pltpu.SemaphoreType.DMA((2,)), pltpu.SemaphoreType.DMA((SENDERS,)), pltpu.SemaphoreType.DMA((GROUPS,))]
    kept, added = pl.pallas_call(
        functools.partial(kernel, wide, narrow),
        out_shape=[jax.ShapeDtypeStruct(brick, F32)] * 2,
        in_specs=[pl.BlockSpec(memory_space=pltpu.HBM)] * 2,
        out_specs=[pl.BlockSpec(memory_space=pltpu.VMEM)] * 2,
        scratch_shapes=scratch,
        compiler_params=pltpu.CompilerParams(
            collective_id=0, has_side_effects=True, vmem_limit_bytes=32 * 1024 * 1024
        ),
    )(pltpu.with_memory_space_constraint(right_side, pltpu.HBM), pltpu.with_memory_space_constraint(conductivity, pltpu.HBM))
    return kept + added


def solution(mesh):
    spec = P("wide", None, "narrow")
    body = functools.partial(per_device, wide=mesh.shape["wide"], narrow=mesh.shape["narrow"])
    return jax.shard_map(body, mesh=mesh, in_specs=(spec, spec), out_specs=spec, check_vma=False)
```

```python
import functools

import jax
import jax.numpy as jnp
from jax import lax
from jax.experimental import pallas as pl
from jax.experimental.pallas import tpu as pltpu
from jax.sharding import PartitionSpec as P

CENTER = 1.125
HALF = 0.875
LANES = 128
REACH = 8
HALF_REACH = 4
GREET_REACH = 2
F32 = jnp.float32
MESH_ID = pl.DeviceIdType.MESH


def cheb(sweeps):
    sigma = CENTER / HALF
    steps = [(0.0, 1.0 / CENTER)]
    ratio = 1.0 / sigma
    for _ in range(sweeps - 1):
        ratio_next = 1.0 / (2.0 * sigma - ratio)
        steps.append((ratio_next * ratio, 2.0 * ratio_next / HALF))
        ratio = ratio_next
    return steps


def over_sides(first, second, count, body):
    for base in (first, second):
        for at in range(count):
            body(base + at)


def over_layers(low, high, unroll, body):
    count = high - low + 1
    if count == unroll:
        for at in range(low, high + 1):
            body(at)
        return

    def block(step, carry):
        for at in range(unroll):
            body(low + step * unroll + at)
        return carry

    lax.fori_loop(0, count // unroll, block, 0)


class Level:
    def __init__(self, refs, scale, rows, row_step, lane_step, base, extent, lane_mask):
        self.c, self.s, self.cx, self.cy, self.cz, self.iv, self.dg, self.va, self.vb = refs
        self.half = 0.5 * scale
        self.rows, self.row_step, self.lane_step = rows, row_step, lane_step
        self.base, self.extent, self.lane_mask = base, extent, lane_mask

    def inside(self, at):
        where_x = self.base + at
        return jnp.where((where_x >= 0) & (where_x < self.extent), 1.0, 0.0).astype(F32)

    def lane(self):
        return lax.broadcasted_iota(jnp.int32, (self.rows, LANES), 1)

    def row(self):
        return lax.broadcasted_iota(jnp.int32, (self.rows, LANES), 0)

    def y_up(self, tile):
        return pltpu.roll(tile, self.rows - self.row_step, 0)

    def y_down(self, tile):
        return pltpu.roll(tile, self.row_step, 0)

    def turned(self, tiles, shift, edge, count):
        out = [pltpu.roll(t, shift, 1) for t in tiles]
        if len(tiles) == 1:
            return out
        at_edge = self.lane() == edge
        return [jnp.where(at_edge, out[1 - k], out[k]) for k in range(count)]

    def z_up(self, tiles, count):
        return self.turned(tiles, LANES - self.lane_step, LANES - 1, count)

    def z_down(self, tiles, count):
        return self.turned(tiles, self.lane_step, 0, count)

    def masked(self, at, tiles):
        keep = self.inside(at) * self.half
        out = []
        for k in range(tiles):
            mask = self.lane_mask[k]
            out.append(self.c[k, at] * (keep if mask is None else mask * keep))
        return out

    def setup_below(self, low, tiles):
        first, second = self.masked(low - 1, tiles), self.masked(low, tiles)
        for k in range(tiles):
            self.cx[k, low - 1] = first[k] + second[k]

    def setup_at(self, at, tiles):
        before, here, after = self.masked(at - 1, tiles), self.masked(at, tiles), self.masked(at + 1, tiles)
        inside = self.inside(at)
        top = self.row() >= self.rows - self.row_step
        bottom = self.row() < self.row_step
        z_up, z_down = self.z_up(here, tiles), self.z_down(here, tiles)
        for k in range(tiles):
            own = here[k]
            x_low = before[k] + own
            x_high = own + after[k]
            y_low = own + jnp.where(bottom, 0.0, self.y_down(own))
            y_high = own + jnp.where(top, 0.0, self.y_up(own))
            z_low = own + z_down[k]
            z_high = own + z_up[k]
            diagonal = x_low + x_high + y_low + y_high + z_low + z_high
            keep = inside if self.lane_mask[k] is None else self.lane_mask[k] * inside
            self.cx[k, at] = x_high
            self.cy[k, at] = jnp.where(top, 0.0, y_high)
            self.cz[k, at] = z_high
            if k == 0:
                self.dg[0, at] = diagonal
            self.iv[k, at] = jnp.where(jnp.full_like(own, 0.0) + keep > 0.5, 1.0 / diagonal, 0.0)

    def setup(self, low, high, unroll, tiles):
        self.setup_below(low, tiles)
        over_layers(low, high, unroll, lambda at: self.setup_at(at, tiles))

    def start_at(self, at, tiles, beta):
        for k in range(tiles):
            self.va[k, at] = self.s[k, at] * self.iv[k, at] * beta

    def start_outer(self, at, beta):
        self.va[1, at] = self.s[1, at] * self.iv[1, at] * beta

    def start(self, low, high, unroll, tiles, beta):
        over_layers(low, high, unroll, lambda at: self.start_at(at, tiles, beta))

    def around(self, field, at, tiles, count):
        here = [field[k, at] for k in range(tiles)]
        cz = [self.cz[k, at] for k in range(tiles)]
        z_up = self.z_up(here, count)
        z_down = self.z_down([cz[k] * here[k] for k in range(tiles)], count)
        sums = []
        for k in range(count):
            cy = self.cy[k, at]
            total = self.cx[k, at] * field[k, at + 1] + self.cx[k, at - 1] * field[k, at - 1]
            total = total + (cy * self.y_up(here[k]) + self.y_down(cy * here[k]))
            total = total + (cz[k] * z_up[k] + z_down[k])
            sums.append(total + self.s[k, at])
        return here, sums

    def sweep_at(self, at, field, result, tiles, count, step, fresh):
        alpha, beta = step
        here, sums = self.around(field, at, tiles, count)
        for k in range(count):
            kept = (1.0 + alpha - beta) * here[k]
            if not fresh:
                kept = kept - alpha * result[k, at]
            result[k, at] = kept + (beta * self.iv[k, at]) * sums[k]

    def sweep(self, field, result, low, high, unroll, tiles, count, step, fresh=False):
        over_layers(low, high, unroll, lambda at: self.sweep_at(at, field, result, tiles, count, step, fresh))

    def residual_at(self, at, field, result, tiles):
        here, sums = self.around(field, at, tiles, 1)
        result[0, at] = sums[0] - self.dg[0, at] * here[0]

    def residual(self, field, result, low, high, unroll, tiles):
        over_layers(low, high, unroll, lambda at: self.residual_at(at, field, result, tiles))

    def last_at(self, at, field, older, step):
        alpha, beta = step
        here, sums = self.around(field, at, 1, 1)
        return (1.0 + alpha - beta) * here[0] - alpha * older[0, at], (beta * self.iv[0, at]) * sums[0]


class Strips:
    def __init__(self, refs, base, extent, left, right):
        self.c, self.s, self.cx, self.cy, self.cz, self.iv, self.dg, self.va, self.vb = refs
        self.base, self.extent, self.left, self.right = base, extent, left, right

    def lane(self):
        return lax.broadcasted_iota(jnp.int32, (32, LANES), 1)

    def mask(self, pack):
        where_x = self.base + 4 * pack + self.lane() // 32
        cell = self.lane() % 32
        keep = jnp.where(cell < 8, self.left, jnp.where(cell >= 24, self.right, 1.0))
        return jnp.where((where_x >= 0) & (where_x < self.extent), keep, 0.0)

    def x_up(self, tiles):
        turned = [pltpu.roll(t, LANES - 32, 1) for t in tiles]
        return [jnp.where(self.lane() < LANES - 32, turned[p], turned[min(p + 1, 3)]) for p in range(4)]

    def x_down(self, tiles):
        turned = [pltpu.roll(t, 32, 1) for t in tiles]
        return [jnp.where(self.lane() >= 32, turned[p], turned[max(p - 1, 0)]) for p in range(4)]

    def setup(self):
        row = lax.broadcasted_iota(jnp.int32, (32, LANES), 0)
        top, bottom = row == 31, row == 0
        masks = [self.mask(p) for p in range(4)]
        own = [self.c[p] * (0.5 * masks[p]) for p in range(4)]
        above = self.x_up(own)
        x_high = [own[p] + above[p] for p in range(4)]
        x_low = self.x_down(x_high)
        for p in range(4):
            y_high = own[p] + jnp.where(top, 0.0, pltpu.roll(own[p], 31, 0))
            y_low = jnp.where(bottom, own[p], pltpu.roll(y_high, 1, 0))
            z_high = own[p] + pltpu.roll(own[p], LANES - 1, 1)
            z_low = pltpu.roll(z_high, 1, 1)
            diagonal = x_low[p] + x_high[p] + y_low + y_high + z_low + z_high
            self.cx[p] = x_high[p]
            self.cy[p] = jnp.where(top, 0.0, y_high)
            self.cz[p] = z_high
            self.dg[p] = diagonal
            self.iv[p] = jnp.where(masks[p] > 0.5, 1.0 / diagonal, 0.0)

    def start(self, beta):
        for p in range(4):
            self.va[p] = self.s[p] * self.iv[p] * beta

    def around(self, field):
        here = [field[p] for p in range(4)]
        cx = [self.cx[p] for p in range(4)]
        x_up = self.x_up(here)
        x_down = self.x_down([cx[p] * here[p] for p in range(4)])
        sums = []
        for p in range(4):
            cy, cz = self.cy[p], self.cz[p]
            total = cx[p] * x_up[p] + x_down[p]
            total = total + (cy * pltpu.roll(here[p], 31, 0) + pltpu.roll(cy * here[p], 1, 0))
            total = total + (cz * pltpu.roll(here[p], LANES - 1, 1) + pltpu.roll(cz * here[p], 1, 1))
            sums.append(total + self.s[p])
        return here, sums

    def sweep(self, field, result, step, fresh=False):
        alpha, beta = step
        here, sums = self.around(field)
        for p in range(4):
            kept = (1.0 + alpha - beta) * here[p]
            if not fresh:
                kept = kept - alpha * result[p]
            result[p] = kept + (beta * self.iv[p]) * sums[p]

    def residual(self, field, result):
        here, sums = self.around(field)
        for p in range(4):
            result[p] = sums[p] - self.dg[p] * here[p]

    def own(self, ref, pack, layers=range(4)):
        cell = self.lane() % 32
        packed = jnp.zeros((32, LANES), F32)
        for layer in layers:
            tile = ref[0, 4 * pack + layer]
            first = pltpu.roll(tile, 32 * layer + 8, 1)
            last = pltpu.roll(tile, (32 * layer + 24) % LANES, 1)
            packed = jnp.where(self.lane() // 32 == layer, jnp.where(cell < 16, first, last), packed)
        return packed

    def take_halo(self, ref, pack, from_left, from_right):
        cell = lax.broadcasted_iota(jnp.int32, (8, LANES), 1) % 32
        for part in range(4):
            rows = pl.ds(8 * part, 8)
            below = pltpu.roll(from_left, (LANES - 8 * part) % LANES, 1)
            above = pltpu.roll(from_right, 24 - 8 * part, 1) if part < 3 else from_right
            ref[pack, rows, :] = jnp.where(cell < 8, below, jnp.where(cell >= 24, above, ref[pack, rows, :]))

    def give_halo(self, ref, pack, side):
        cell = lax.broadcasted_iota(jnp.int32, (8, LANES), 1) % 32
        packed = None
        for part in range(4):
            shift = (8 * part - 8 - 8 * side) % LANES
            tile = ref[pack, pl.ds(8 * part, 8), :]
            tile = pltpu.roll(tile, shift, 1) if shift else tile
            packed = tile if part == 0 else jnp.where(cell // 8 == part, tile, packed)
        return packed

    def mend(self, tile, ref, at):
        packed, layer = ref[at // 4], at % 4
        first = pltpu.roll(packed, (LANES - 32 * layer - 8) % LANES, 1)
        last = pltpu.roll(packed, (LANES + 104 - 32 * layer) % LANES, 1)
        return jnp.where(self.lane() < 4, first, jnp.where(self.lane() >= LANES - 4, last, tile))


LEVEL_FIELDS = 9
LEVEL_SHAPES = ((1, 16, 32, LANES), (2, 14, 16, LANES), (1, 34, 8, LANES), (1, 15, 8, LANES))
RULER = 1024
SENDERS = 14 + 2 * (2 * REACH + 1)
GROUPS = 36 + 2 * (2 * REACH + 1)


def kernel(wide, narrow, rhs, coef, kept, added, *scratch):
    scratch = list(scratch)
    level_refs = []
    for _ in range(4):
        level_refs.append(scratch[:LEVEL_FIELDS])
        scratch = scratch[LEVEL_FIELDS:]
    strip_refs, scratch = scratch[:LEVEL_FIELDS], scratch[LEVEL_FIELDS:]
    (ps, zs, rz, rcn, kp, k1cx, k1c, sk, sp, k1x, k1p, k1z, rc2, s2m, rs2, rx1, rx1b, sb0, hx0, p1, p0, ruler,
     local_sem, send_sem, recv_sem) = scratch
    me_w = lax.axis_index("wide")
    me_n = lax.axis_index("narrow")

    def there(dw, dn):
        return (lax.rem(me_w + (dw + wide), wide), lax.rem(me_n + (dn + narrow), narrow))

    has = (me_w > 0, me_w < wide - 1)
    has_z = (me_n > 0, me_n < narrow - 1)
    reach = (jnp.minimum(me_w, REACH), jnp.minimum(wide - 1 - me_w, REACH))

    def for_far(first, body, last=REACH):
        for side in range(2):
            sign = 2 * side - 1

            def step(k, carry):
                body(REACH + sign * k, sign * k)
                return carry

            lax.fori_loop(first, jnp.minimum(reach[side], last) + 1, step, 0)

    def for_all_far(body):
        inner = reach[0] + reach[1] == 2 * REACH

        @pl.when(inner)
        def straight():
            for k in range(REACH, 0, -1):
                for sign in (-1, 1):
                    body(REACH + sign * k, sign * k)

        pl.when(jnp.logical_not(inner))(functools.partial(for_far, 1, body))

    def for_sides(body):
        for side in range(2):
            pl.when(has[side])(functools.partial(body, side, 2 * side - 1))

    def for_sides_z(body):
        for side in range(2):
            pl.when(has_z[side])(functools.partial(body, side, 2 * side - 1))

    def for_corners(body):
        for side in range(2):
            for side_z in range(2):
                pl.when(has[side] & has_z[side_z])(
                    functools.partial(body, side, side_z, 2 * side - 1, 2 * side_z - 1)
                )

    @pl.when((me_n == 0) | (me_n == narrow - 1))
    def clear_z():
        for ref in (rz, rcn, k1c, k1z, k1p):
            ref[...] = jnp.zeros(ref.shape, F32)

    @pl.when((me_w < REACH) | (me_w >= wide - REACH))
    def clear():
        def zero(ref):
            ref[...] = jnp.zeros(ref.shape, F32)

        for ref in (rcn, rx1, rx1b, hx0, rc2, rs2, k1cx, k1c, k1x, k1p):
            zero(ref)
        for side in range(2):
            for ref in level_refs[0][:2]:
                zero(ref.at[0, pl.ds(12 * side, 4)])
            zero(level_refs[1][0].at[0, 13 * side])

    def if_reach(least, body):
        for side in range(2):
            pl.when(reach[side] >= least)(functools.partial(body, side, 2 * side - 1))

    barrier = pltpu.get_barrier_semaphore()

    def greet(dw, dn):
        pl.semaphore_signal(barrier, inc=1, device_id=there(dw, dn), device_id_type=MESH_ID)

    for_far(1, lambda slot, dw: greet(dw, 0), GREET_REACH)
    for_sides_z(lambda side, dn: greet(0, dn))
    for_corners(lambda side, side_z, dw, dn: greet(dw, dn))

    c0, s0 = level_refs[0][0], level_refs[0][1]
    load_c = pltpu.make_async_copy(coef, c0.at[0, pl.ds(4, 8)], local_sem.at[0])
    load_s = pltpu.make_async_copy(rhs, s0.at[0, pl.ds(4, 8)], local_sem.at[1])
    load_c.start()
    load_s.start()
    beside_x = jnp.where(has[0], 1, 0) + jnp.where(has[1], 1, 0)
    beside_z = jnp.where(has_z[0], 1, 0) + jnp.where(has_z[1], 1, 0)
    greeted = beside_z + beside_x * beside_z
    for side in range(2):
        greeted = greeted + jnp.minimum(reach[side], GREET_REACH)

    left = jnp.where(me_n > 0, 1.0, 0.0).astype(F32)
    right = jnp.where(me_n < narrow - 1, 1.0, 0.0).astype(F32)

    def lanes(rows):
        return lax.broadcasted_iota(jnp.int32, (rows, LANES), 1)

    def edges(rows, until, low, since, high):
        at = lanes(rows)
        return jnp.where(at < until, low, jnp.where(at >= since, high, 0.0))

    def centred(rows):
        at = lanes(rows)
        return jnp.where((at >= 32) & (at < 96), 1.0, edges(rows, 32, left, 96, right))

    level_0 = Level(level_refs[0], 1.0, 32, 1, 1, 8 * me_w - 4, 8 * wide, [None])
    strips = Strips(strip_refs, 8 * me_w - 4, 8 * wide, left, right)
    level_1 = Level(
        level_refs[1], 0.25, 16, 1, 1, 4 * me_w - 5, 4 * wide, [centred(16), edges(16, 32, right, 96, left)]
    )
    level_2 = Level(level_refs[2], 0.0625, 8, 1, 2, 2 * me_w - 16, 2 * wide, [centred(8)])
    level_3 = Level(level_refs[3], 0.015625, 8, 2, 4, me_w - 7, wide, [centred(8)])

    sent = [0] * SENDERS

    def send(group, src, dst, dw, dn, rows, sender):
        if isinstance(sender, int):
            sent[sender] += rows
        pltpu.make_async_remote_copy(
            src_ref=src, dst_ref=dst, send_sem=send_sem.at[sender], recv_sem=recv_sem.at[group],
            device_id=there(dw, dn), device_id_type=MESH_ID,
        ).start()

    def ruled(rows, group, sender):
        span = ruler.at[pl.ds(0, rows)]
        return pltpu.make_async_remote_copy(
            src_ref=span, dst_ref=span, send_sem=send_sem.at[sender], recv_sem=recv_sem.at[group],
            device_id=there(0, 1), device_id_type=MESH_ID,
        )

    def receive(group, rows):
        ruled(rows, group, 0).wait_recv()

    def receive_sides(group, rows):
        for_sides(lambda side, dw: receive(group + side, rows))

    def receive_sides_z(group, rows):
        for_sides_z(lambda side, dn: receive(group + side, rows))

    def receive_corners(group, rows):
        for_corners(lambda side, side_z, dw, dn: receive(group + 2 * side + side_z, rows))

    def receive_far(group, first, last):
        for_far(first, lambda slot, dw: receive(group + slot, 8), last)

    def sends_done(sender):
        ruled(sent[sender], 0, sender).wait_send()

    from_z, from_s1z = 0, 2
    from_c_corner, from_k_corner, from_s1_corner = 4, 8, 12
    from_c, from_s, from_s_next, from_k, from_s1, from_c1b, from_x0, from_x1, from_x1b = range(16, 34, 2)
    from_four = 34
    from_c2 = 36
    from_s2 = from_c2 + 2 * REACH + 1
    sender_x, sender_x1, sender_x1b, sender_four, sender_z = range(0, 10, 2)
    sender_corner, sender_c2, sender_far = 10, 14, 14 + 2 * REACH + 1

    def restrict_0(ref):
        out = []
        for layer in range(4):
            total = None
            for dx in range(2):
                for dy in range(2):
                    term = ref[0, 4 + 2 * layer + dx, pl.ds(dy, 16, stride=2), :]
                    total = term if total is None else total + term
            total = total + pltpu.roll(total, LANES - 1, 1)
            out.append(0.125 * jnp.take_along_axis(total, (2 * lanes(16) + 64) % LANES, axis=1))
        return out

    odd_8 = lanes(8) % 2 == 1

    def pairs_1(ref):
        out = []
        for layer in range(2):
            total = None
            for dx in range(2):
                for dy in range(2):
                    term = ref[0, 5 + 2 * layer + dx, pl.ds(dy, 8, stride=2), :]
                    total = term if total is None else total + term
            total = total + jnp.where(odd_8, pltpu.roll(total, 1, 1), pltpu.roll(total, LANES - 1, 1))
            out.append(0.125 * total)
        return jnp.where(odd_8, out[1], out[0])

    def squeeze_1(layers, ref, row):
        for part in range(2):
            ref[pl.ds(row + 16 * part, 16), :] = jnp.where(lanes(16) < 64, layers[part], layers[part + 2])

    pl.semaphore_wait(barrier, greeted)

    @for_sides
    def send_faces(side, dw):
        send(from_c + 1 - side, coef.at[pl.ds(4 * side, 4)], c0.at[0, pl.ds(12 - 12 * side, 4)], dw, 0, 128, sender_x + side)
        send(from_s + 1 - side, rhs.at[7 * side], s0.at[0, 12 - 9 * side], dw, 0, 32, sender_x + side)

    def squeeze_halves(first, second):
        low_quarter = lanes(16) % 64 < 32
        return (
            jnp.where(low_quarter, pltpu.roll(first, 96, 1), second),
            jnp.where(low_quarter, first, pltpu.roll(second, 32, 1)),
        )

    load_c.wait()
    own_c1 = restrict_0(c0)
    for half in range(2):
        strips.c[1 + half] = strips.own(c0, 1 + half)
    for side in range(2):
        squeeze_1(own_c1, zs.at[side], 32)
        for half in range(2):
            zs[side, pl.ds(16 * half, 8), :] = strips.give_halo(strips.c, 1 + half, side)
    load_s.wait()
    for half in range(2):
        strips.s[1 + half] = strips.own(s0, 1 + half)
    for side in range(2):
        for half in range(2):
            zs[side, pl.ds(16 * half + 8, 8), :] = strips.give_halo(strips.s, 1 + half, side)

    for_sides_z(
        lambda side, dn: send(from_z + 1 - side, zs.at[side], rz.at[1 - side], 0, dn, 64, sender_z + side)
    )

    def send_corner(group, src, dst, rows, side, side_z):
        at = 2 * side + side_z
        send(group + 3 - at, src, dst, 2 * side - 1, 2 * side_z - 1, rows, sender_corner + at)

    @for_corners
    def send_c_corner(side, side_z, dw, dn):
        src = zs.at[side_z, pl.ds(16 * side, 16)]
        send_corner(from_c_corner, src, rcn.at[1 - side, 1 - side_z], 16, side, side_z)

    @for_sides
    def send_s_next(side, dw):
        src = rhs.at[pl.ds(1 + 4 * side, 2)]
        send(from_s_next + 1 - side, src, s0.at[0, pl.ds(13 - 12 * side, 2)], dw, 0, 64, sender_x + side)

    steps = cheb(3)
    sweep_a = (level_0.va, level_0.vb, 1, 1, steps[1], True)
    sweep_b = (level_0.vb, level_0.va, 1, 1, steps[2], False)
    level_0.setup(5, 10, 6, 1)
    level_0.start(5, 10, 6, 1, steps[0][1])
    over_layers(6, 9, 4, lambda at: level_0.sweep_at(at, *sweep_a))
    over_layers(7, 8, 2, lambda at: level_0.sweep_at(at, *sweep_b))

    def take_halos(field, ref, pack, got):
        rows = pl.ds(8 * field + (16 if pack == 2 else 0), 8)
        strips.take_halo(ref, pack, got[0, rows, :], got[1, rows, :])

    receive_sides_z(from_z, 64)
    for field, ref in enumerate((strips.c, strips.s)):
        for half in range(2):
            take_halos(field, ref, 1 + half, rz)

    def spread_1(ref, block):
        at_lane = lanes(16)
        low_half = at_lane < 64
        low_quarter = at_lane % 64 < 32
        for part in range(2):
            before, own, after = (block(dz, part) for dz in (-1, 0, 1))
            near = jnp.where(low_quarter, before, after)
            outer = jnp.where(low_quarter, after, before)
            own_r, near_r, outer_r = (pltpu.roll(t, 64, 1) for t in (own, near, outer))
            at = 5 + part
            for at, own_a, own_b, near_a, near_b, outer_a, outer_b in (
                (at, own, own_r, near, near_r, outer, outer_r),
                (at + 2, own_r, own, near_r, near, outer_r, outer),
            ):
                centre = jnp.where(low_half, own_a, own_b)
                ref[0, at] = jnp.where(at_lane < 32, near_a, jnp.where(at_lane < 96, centre, near_b))
                ref[1, at] = jnp.where(low_half, outer_a, outer_b)

    def coef_block(dz, part):
        rows = pl.ds(32 + 16 * part, 16)
        return zs[0, rows, :] if dz == 0 else rz[(1 + dz) // 2, rows, :]

    spread_1(level_1.c, coef_block)
    rc2[REACH] = pairs_1(level_1.c)

    def send_block(slot, dw):
        send(from_c2 + 2 * REACH - slot, rc2.at[REACH], rc2.at[2 * REACH - slot], dw, 0, 8, sender_c2 + slot)

    for_far(1, send_block, GREET_REACH)
    k1_own = zs.at[0, pl.ds(32, 32)]
    halves = squeeze_halves(zs[0, pl.ds(32, 16), :], zs[0, pl.ds(48, 16), :])
    at_lane = lanes(16)
    for side in range(2):
        near, far = (0, 3) if side == 0 else (3, 0)
        full = level_1.c[0, 5 + near]
        place = (32 * far + 31, 32 * far)
        cell = (64, 63)
        for side_z in range(2):
            moved = pltpu.roll(full, (place[side_z] - cell[side_z]) % LANES, 1)
            kp[side, side_z] = jnp.where(at_lane == place[side_z], moved, halves[side_z])
    for_sides(
        lambda side, dw: send(from_k + 1 - side, k1_own, k1cx.at[1 - side], dw, 0, 32, sender_x + side)
    )
    for_corners(
        lambda side, side_z, dw, dn: send_corner(
            from_k_corner, kp.at[side, side_z], k1c.at[1 - side, 1 - side_z], 16, side, side_z
        )
    )

    receive_sides(from_c, 128)
    receive_corners(from_c_corner, 16)
    for side in range(2):
        strips.c[3 * side] = strips.own(c0, 3 * side)
        take_halos(0, strips.c, 3 * side, rcn.at[side])
    level_0.setup_below(1, 1)
    over_sides(1, 11, 4, lambda at: level_0.setup_at(at, 1))
    strips.setup()
    receive_sides(from_s, 32)
    over_sides(3, 11, 2, lambda at: level_0.start_at(at, 1, steps[0][1]))
    over_sides(4, 10, 2, lambda at: level_0.sweep_at(at, *sweep_a))
    over_sides(5, 9, 2, lambda at: level_0.sweep_at(at, *sweep_b))
    over_layers(6, 9, 4, lambda at: level_0.residual_at(at, level_0.va, level_0.vb, 1))
    receive_far(from_c2, 1, GREET_REACH)
    for_far(GREET_REACH + 1, send_block, HALF_REACH)
    receive_sides(from_s_next, 64)
    for side in range(2):
        strips.s[3 * side] = strips.own(s0, 3 * side, range(1 - side, 4 - side))
        take_halos(1, strips.s, 3 * side, rcn.at[side])
    over_sides(1, 13, 2, lambda at: level_0.start_at(at, 1, steps[0][1]))
    strips.start(steps[0][1])
    over_sides(2, 12, 2, lambda at: level_0.sweep_at(at, *sweep_a))
    strips.sweep(strips.va, strips.vb, steps[1], fresh=True)
    over_sides(3, 11, 2, lambda at: level_0.sweep_at(at, *sweep_b))
    strips.sweep(strips.vb, strips.va, steps[2])
    over_sides(4, 10, 2, lambda at: level_0.residual_at(at, level_0.va, level_0.vb, 1))
    strips.residual(strips.va, strips.vb)
    for at in range(4, 12):
        level_0.vb[0, at] = strips.mend(level_0.vb[0, at], strips.vb, at)

    squeeze_1(restrict_0(level_0.vb), sk, 0)

    sp[0], sp[1] = squeeze_halves(sk[pl.ds(0, 16), :], sk[pl.ds(16, 16), :])

    for_sides(lambda side, dw: send(from_s1 + 1 - side, sk, k1x.at[1 - side], dw, 0, 32, sender_x + side))
    for_corners(
        lambda side, side_z, dw, dn: send_corner(
            from_s1_corner, sp.at[side_z], k1p.at[1 - side, 1 - side_z], 16, side, side_z
        )
    )
    for_sides_z(lambda side, dn: send(from_s1z + 1 - side, sk, k1z.at[1 - side], 0, dn, 32, sender_z + side))

    receive_far(from_c2, GREET_REACH + 1, HALF_REACH)

    @functools.partial(if_reach, HALF_REACH)
    def send_four(side, sign):
        src, dst = rc2.at[pl.ds(9 - 5 * side, 4)], rc2.at[pl.ds(13 - 13 * side, 4)]
        send(from_four + 1 - side, src, dst, HALF_REACH * sign, 0, 32, sender_four + side)

    for at in range(3, 13):
        level_0.va[0, at] = strips.mend(level_0.va[0, at], strips.va, at)
    own_cell = (strips.lane() % 32 >= 8) & (strips.lane() % 32 < 24)
    for pack_at, layers in enumerate(((3,), range(4), range(4), (0,))):
        strips.va[pack_at] = jnp.where(own_cell, strips.own(level_0.va, pack_at, layers), strips.va[pack_at])
    for side in range(2):
        first = 9 if side == 0 else 5
        for layer in range(2):
            sb0[side, pl.ds(32 * layer, 32), :] = level_0.va[0, first + layer]
        packed = strips.va[2 - side]
        middle = (lanes(16) >= 32) & (lanes(16) < 96)
        sb0[side, pl.ds(64, 16), :] = jnp.where(middle, packed[:16], pltpu.roll(packed[16:], 64, 1))

    @for_sides
    def send_iterate_0(side, dw):
        send(from_x0 + 1 - side, sb0.at[1 - side], hx0.at[1 - side], dw, 0, 80, sender_x + side)

    def source_block(dz, part):
        rows = pl.ds(16 * part, 16)
        return sk[rows, :] if dz == 0 else k1z[(1 + dz) // 2, rows, :]

    def spread_beside(ref, blocks, packs):
        at_lane = lanes(16)
        low_half = at_lane < 64
        for side in range(2):
            for layer in range(4):
                own = blocks[side, pl.ds(16 * (layer % 2), 16), :]
                other = pltpu.roll(own, 64, 1)
                centre = jnp.where(low_half, own, other) if layer < 2 else jnp.where(low_half, other, own)
                before = pltpu.roll(packs[side, 0], (LANES - 32 * layer) % LANES, 1)
                after = pltpu.roll(packs[side, 1], (LANES + 96 - 32 * layer) % LANES, 1)
                ref[0, 1 + 8 * side + layer] = jnp.where(at_lane < 32, before, jnp.where(at_lane < 96, centre, after))

    receive_sides(from_k, 32)
    receive_corners(from_k_corner, 16)
    spread_beside(level_1.c, k1cx, k1c)
    for side in range(2):
        far = 3 if side == 1 else 0
        below, above = (pltpu.roll(k1c[side, side_z], (shift - 32 * far) % LANES, 1)
                        for side_z, shift in ((0, 127), (1, -31)))
        level_1.c[1, 4 + 5 * side] = jnp.where(lanes(16) < 64, above, below)

    @for_sides
    def send_coef_1(side, dw):
        send(from_c1b + 1 - side, level_1.c.at[0, 9 - 5 * side], level_1.c.at[0, 13 - 13 * side], dw, 0, 16, sender_x + side)

    level_1.setup_below(2, 1)
    over_sides(2, 10, 2, lambda at: level_1.setup_at(at, 1))
    over_layers(4, 9, 6, lambda at: level_1.setup_at(at, 2))

    receive_sides_z(from_s1z, 32)
    spread_1(level_1.s, source_block)
    receive_sides(from_s1, 32)
    receive_corners(from_s1_corner, 16)
    spread_beside(level_1.s, k1x, k1p)
    level_1.start(2, 11, 10, 1, steps[0][1])
    over_layers(5, 8, 4, lambda at: level_1.start_outer(at, steps[0][1]))
    over_sides(3, 9, 2, lambda at: level_1.sweep_at(at, level_1.va, level_1.vb, 1, 1, steps[1], True))
    over_layers(5, 8, 4, lambda at: level_1.sweep_at(at, level_1.va, level_1.vb, 2, 1, steps[1], True))
    level_1.sweep(level_1.vb, level_1.va, 4, 9, 6, 1, 1, steps[2])
    level_1.residual(level_1.va, level_1.vb, 5, 8, 4, 1)

    value = pairs_1(level_1.vb)
    s2m[...] = value
    rs2[REACH] = value

    for_all_far(
        lambda slot, dw: send(
            from_s2 + 2 * REACH - slot, s2m, rs2.at[2 * REACH - slot], dw, 0, 8, sender_far + slot
        )
    )

    @for_sides
    def send_iterate_1(side, dw):
        send(from_x1 + 1 - side, level_1.va.at[0, pl.ds(6 - side, 3)], rx1.at[1 - side], dw, 0, 48, sender_x1 + side)

    for side in range(2):
        @pl.when(reach[side] >= 2)
        def send_next_1():
            layer = level_1.va.at[0, 5 + 3 * side]
            send(from_x1b + 1 - side, layer, rx1b.at[1 - side], 4 * side - 2, 0, 16, sender_x1b + side)

    receive_sides(from_c1b, 16)
    level_1.setup_below(1, 1)
    over_sides(1, 12, 1, lambda at: level_1.setup_at(at, 1))

    def spread_2(ref, blocks):
        for block in range(2 * REACH + 1):
            packed = blocks[block]
            ref[0, 2 * block] = jnp.where(odd_8, pltpu.roll(packed, 1, 1), packed)
            ref[0, 2 * block + 1] = jnp.where(odd_8, packed, pltpu.roll(packed, LANES - 1, 1))

    def restrict_2(ref, at):
        total = ref[0, 2 * at + 2] + ref[0, 2 * at + 3]
        odd_row = lax.broadcasted_iota(jnp.int32, (8, LANES), 0) % 2 == 1
        total = total + jnp.where(odd_row, pltpu.roll(total, 1, 0), pltpu.roll(total, 7, 0))
        second = lanes(8) % 4 >= 2
        total = total + jnp.where(second, pltpu.roll(total, 2, 1), pltpu.roll(total, LANES - 2, 1))
        return 0.125 * total

    if_reach(HALF_REACH, lambda side, sign: receive(from_four + side, 32))
    spread_2(level_2.c, rc2)
    level_2.setup(1, 32, 16, 1)
    for at in range(15):
        level_3.c[0, at] = restrict_2(level_2.c, at)
    level_3.setup(1, 13, 13, 1)

    for_sides(lambda side, dw: sends_done(sender_x + side))
    for_sides_z(lambda side, dn: sends_done(sender_z + side))
    for_corners(lambda side, side_z, dw, dn: sends_done(sender_corner + 2 * side + side_z))
    if_reach(HALF_REACH, lambda side, sign: sends_done(sender_four + side))
    for_far(1, lambda slot, dw: ruled(8, 0, sender_c2 + slot).wait_send(), HALF_REACH)
    for_all_far(lambda slot, dw: ruled(8, 0, sender_far + slot).wait_send())
    for side in range(2):
        pl.when(has[side])(functools.partial(sends_done, sender_x1 + side))
        pl.when(reach[side] >= 2)(functools.partial(sends_done, sender_x1b + side))

    for_all_far(lambda slot, dw: receive(from_s2 + slot, 8))
    spread_2(level_2.s, rs2)
    level_2.start(1, 32, 32, 1, steps[0][1])
    level_2.sweep(level_2.va, level_2.vb, 2, 31, 30, 1, 1, steps[1], fresh=True)
    level_2.sweep(level_2.vb, level_2.va, 3, 30, 28, 1, 1, steps[2])
    level_2.residual(level_2.va, level_2.vb, 4, 29, 26, 1)

    for at in range(1, 14):
        level_3.s[0, at] = restrict_2(level_2.vb, at)
    coarse = cheb(4)
    level_3.start(1, 13, 13, 1, coarse[0][1])
    level_3.sweep(level_3.va, level_3.vb, 2, 12, 11, 1, 1, coarse[1], fresh=True)
    level_3.sweep(level_3.vb, level_3.va, 3, 11, 9, 1, 1, coarse[2])
    level_3.sweep(level_3.va, level_3.vb, 4, 10, 7, 1, 1, coarse[3])

    for at in range(10, 24):
        level_2.vb[0, at] = level_2.va[0, at] + level_3.vb[0, (at - 2) // 2]
    level_2.sweep(level_2.vb, level_2.va, 11, 22, 12, 1, 1, steps[0], fresh=True)
    level_2.sweep(level_2.va, level_2.vb, 12, 21, 10, 1, 1, steps[1])
    level_2.sweep(level_2.vb, level_2.va, 13, 20, 8, 1, 1, steps[2])

    for at in range(8):
        value = level_2.va[0, 13 + at]
        for part in range(2):
            p1[at, pl.ds(part, 8, stride=2), :] = value
    receive_sides(from_x1, 48)
    for side in range(2):
        pl.when(reach[side] >= 2)(functools.partial(receive, from_x1b + side, 16))
    for at in range(14):
        if 4 <= at <= 9:
            before = level_1.va[0, at]
        else:
            before = rx1b[0] if at == 0 else rx1[0, at - 1] if at < 4 else rx1[1, at - 10] if at < 13 else rx1b[1]
        level_1.vb[0, at] = before + p1[(at + 1) // 2]
    level_1.sweep(level_1.vb, level_1.va, 1, 12, 12, 1, 1, steps[0], fresh=True)
    level_1.sweep(level_1.va, level_1.vb, 2, 11, 10, 1, 1, steps[1])
    level_1.sweep(level_1.vb, level_1.va, 3, 10, 8, 1, 1, steps[2])

    cell = lanes(16) % 32
    strip_lane = jnp.where(cell < 16, 28, 84) + cell // 2
    low_half = lanes(16) < 64
    fine = []
    for at in range(8):
        value = level_1.va[0, 3 + at]
        own = jnp.take_along_axis(value, lanes(16) // 2 + 32, axis=1)
        fine.append(jnp.take_along_axis(value, strip_lane, axis=1))
        for part in range(2):
            p0[at, pl.ds(part, 16, stride=2), :] = own
    for pack in range(4):
        value = jnp.where(low_half, fine[2 * pack], fine[2 * pack + 1])
        for part in range(2):
            ps[pack, pl.ds(part, 16, stride=2), :] = value
    receive_sides(from_x0, 80)
    for side in range(2):
        for layer in range(2):
            at = (1 if side == 0 else 13) + layer
            level_0.vb[0, at] = hx0[side, pl.ds(32 * layer, 32), :] + p0[at // 2]
        packed = hx0[side, pl.ds(64, 16), :]
        layer = lanes(16) // 32
        for part, value in enumerate((packed, pltpu.roll(packed, 64, 1))):
            rows = pl.ds(16 * part, 16)
            own = jnp.where(layer == (3 if side == 0 else 0), strips.va[3 * side, rows, :], 0.0)
            value = jnp.where((layer == 1) | (layer == 2), value, own)
            strips.vb[3 * side, rows, :] = value + ps[3 * side, rows, :]
    for pack in (1, 2):
        strips.vb[pack] = strips.va[pack] + ps[pack]

    def correct(at):
        level_0.vb[0, at] = level_0.va[0, at] + p0[at // 2]

    over_layers(3, 12, 10, correct)
    level_0.sweep(level_0.vb, level_0.va, 2, 13, 12, 1, 1, steps[0], fresh=True)
    strips.sweep(strips.vb, strips.va, steps[0], fresh=True)
    level_0.sweep(level_0.va, level_0.vb, 3, 12, 10, 1, 1, steps[1])
    strips.sweep(strips.va, strips.vb, steps[1])
    strips.sweep(strips.vb, strips.va, steps[2])
    inner = (strips.lane() >= 4) & (strips.lane() < LANES - 4)
    for at in range(4, 12):
        kept_here, added_here = level_0.last_at(at, level_0.vb, level_0.va, steps[2])
        kept[at - 4] = strips.mend(kept_here, strips.va, at)
        added[at - 4] = jnp.where(inner, added_here, 0.0)


def per_device(right_side, conductivity, wide, narrow):
    brick = (8, 32, LANES)
    scratch = []
    for shape in LEVEL_SHAPES:
        scratch += [pltpu.VMEM(shape, F32)] * LEVEL_FIELDS
    scratch += [pltpu.VMEM((4, 32, LANES), F32)] * LEVEL_FIELDS
    shapes = [
        (4, 32, LANES),
        (2, 64, LANES), (2, 64, LANES), (2, 2, 16, LANES),
        (2, 2, 16, LANES), (2, 32, LANES), (2, 2, 16, LANES),
        (32, LANES), (2, 16, LANES), (2, 32, LANES), (2, 2, 16, LANES), (2, 32, LANES),
        (2 * REACH + 1, 8, LANES), (8, LANES), (2 * REACH + 1, 8, LANES),
        (2, 3, 16, LANES), (2, 16, LANES),
        (2, 80, LANES), (2, 80, LANES),
        (8, 16, LANES), (8, 32, LANES),
        (RULER, LANES),
    ]
    scratch += [pltpu.VMEM(shape, F32) for shape in shapes]
    scratch += [pltpu.SemaphoreType.DMA((2,)), pltpu.SemaphoreType.DMA((SENDERS,)), pltpu.SemaphoreType.DMA((GROUPS,))]
    kept, added = pl.pallas_call(
        functools.partial(kernel, wide, narrow),
        out_shape=[jax.ShapeDtypeStruct(brick, F32)] * 2,
        in_specs=[pl.BlockSpec(memory_space=pltpu.HBM)] * 2,
        out_specs=[pl.BlockSpec(memory_space=pltpu.VMEM)] * 2,
        scratch_shapes=scratch,
        compiler_params=pltpu.CompilerParams(
            collective_id=0, has_side_effects=True, vmem_limit_bytes=32 * 1024 * 1024
        ),
    )(pltpu.with_memory_space_constraint(right_side, pltpu.HBM), pltpu.with_memory_space_constraint(conductivity, pltpu.HBM))
    return kept + added


def solution(mesh):
    spec = P("wide", None, "narrow")
    body = functools.partial(per_device, wide=mesh.shape["wide"], narrow=mesh.shape["narrow"])
    return jax.shard_map(body, mesh=mesh, in_specs=(spec, spec), out_specs=spec, check_vma=False)
```

```python
import functools

import jax
import jax.numpy as jnp
from jax import lax
from jax.experimental import pallas as pl
from jax.experimental.pallas import tpu as pltpu
from jax.sharding import PartitionSpec as P

CENTER = 1.125
HALF = 0.875
LANES = 128
REACH = 8
HALF_REACH = 4
GREET_REACH = 2
F32 = jnp.float32
MESH_ID = pl.DeviceIdType.MESH


def cheb(sweeps):
    sigma = CENTER / HALF
    steps = [(0.0, 1.0 / CENTER)]
    ratio = 1.0 / sigma
    for _ in range(sweeps - 1):
        ratio_next = 1.0 / (2.0 * sigma - ratio)
        steps.append((ratio_next * ratio, 2.0 * ratio_next / HALF))
        ratio = ratio_next
    return steps


def over_sides(first, second, count, body):
    for base in (first, second):
        for at in range(count):
            body(base + at)


def over_layers(low, high, unroll, body):
    count = high - low + 1
    if count == unroll:
        for at in range(low, high + 1):
            body(at)
        return

    def block(step, carry):
        for at in range(unroll):
            body(low + step * unroll + at)
        return carry

    lax.fori_loop(0, count // unroll, block, 0)


class Level:
    def __init__(self, refs, scale, rows, row_step, lane_step, base, extent, lane_mask):
        self.c, self.s, self.cx, self.cy, self.cz, self.iv, self.dg, self.va, self.vb = refs
        self.half = 0.5 * scale
        self.rows, self.row_step, self.lane_step = rows, row_step, lane_step
        self.base, self.extent, self.lane_mask = base, extent, lane_mask

    def inside(self, at):
        where_x = self.base + at
        return jnp.where((where_x >= 0) & (where_x < self.extent), 1.0, 0.0).astype(F32)

    def lane(self):
        return lax.broadcasted_iota(jnp.int32, (self.rows, LANES), 1)

    def row(self):
        return lax.broadcasted_iota(jnp.int32, (self.rows, LANES), 0)

    def y_up(self, tile):
        return pltpu.roll(tile, self.rows - self.row_step, 0)

    def y_down(self, tile):
        return pltpu.roll(tile, self.row_step, 0)

    def turned(self, tiles, shift, edge, count):
        out = [pltpu.roll(t, shift, 1) for t in tiles]
        if len(tiles) == 1:
            return out
        at_edge = self.lane() == edge
        return [jnp.where(at_edge, out[1 - k], out[k]) for k in range(count)]

    def z_up(self, tiles, count):
        return self.turned(tiles, LANES - self.lane_step, LANES - 1, count)

    def z_down(self, tiles, count):
        return self.turned(tiles, self.lane_step, 0, count)

    def masked(self, at, tiles):
        keep = self.inside(at) * self.half
        out = []
        for k in range(tiles):
            mask = self.lane_mask[k]
            out.append(self.c[k, at] * (keep if mask is None else mask * keep))
        return out

    def setup_below(self, low, tiles):
        first, second = self.masked(low - 1, tiles), self.masked(low, tiles)
        for k in range(tiles):
            self.cx[k, low - 1] = first[k] + second[k]

    def setup_at(self, at, tiles):
        before, here, after = self.masked(at - 1, tiles), self.masked(at, tiles), self.masked(at + 1, tiles)
        inside = self.inside(at)
        top = self.row() >= self.rows - self.row_step
        bottom = self.row() < self.row_step
        z_up, z_down = self.z_up(here, tiles), self.z_down(here, tiles)
        for k in range(tiles):
            own = here[k]
            x_low = before[k] + own
            x_high = own + after[k]
            y_low = own + jnp.where(bottom, 0.0, self.y_down(own))
            y_high = own + jnp.where(top, 0.0, self.y_up(own))
            z_low = own + z_down[k]
            z_high = own + z_up[k]
            diagonal = x_low + x_high + y_low + y_high + z_low + z_high
            keep = inside if self.lane_mask[k] is None else self.lane_mask[k] * inside
            self.cx[k, at] = x_high
            self.cy[k, at] = jnp.where(top, 0.0, y_high)
            self.cz[k, at] = z_high
            if k == 0:
                self.dg[0, at] = diagonal
            self.iv[k, at] = jnp.where(jnp.full_like(own, 0.0) + keep > 0.5, 1.0 / diagonal, 0.0)

    def setup(self, low, high, unroll, tiles):
        self.setup_below(low, tiles)
        over_layers(low, high, unroll, lambda at: self.setup_at(at, tiles))

    def start_at(self, at, tiles, beta):
        for k in range(tiles):
            self.va[k, at] = self.s[k, at] * self.iv[k, at] * beta

    def start_outer(self, at, beta):
        self.va[1, at] = self.s[1, at] * self.iv[1, at] * beta

    def start(self, low, high, unroll, tiles, beta):
        over_layers(low, high, unroll, lambda at: self.start_at(at, tiles, beta))

    def around(self, field, at, tiles, count):
        here = [field[k, at] for k in range(tiles)]
        cz = [self.cz[k, at] for k in range(tiles)]
        z_up = self.z_up(here, count)
        z_down = self.z_down([cz[k] * here[k] for k in range(tiles)], count)
        sums = []
        for k in range(count):
            cy = self.cy[k, at]
            total = self.cx[k, at] * field[k, at + 1] + self.cx[k, at - 1] * field[k, at - 1]
            total = total + (cy * self.y_up(here[k]) + self.y_down(cy * here[k]))
            total = total + (cz[k] * z_up[k] + z_down[k])
            sums.append(total + self.s[k, at])
        return here, sums

    def sweep_at(self, at, field, result, tiles, count, step, fresh):
        alpha, beta = step
        here, sums = self.around(field, at, tiles, count)
        for k in range(count):
            kept = (1.0 + alpha - beta) * here[k]
            if not fresh:
                kept = kept - alpha * result[k, at]
            result[k, at] = kept + (beta * self.iv[k, at]) * sums[k]

    def sweep(self, field, result, low, high, unroll, tiles, count, step, fresh=False):
        over_layers(low, high, unroll, lambda at: self.sweep_at(at, field, result, tiles, count, step, fresh))

    def residual_at(self, at, field, result, tiles):
        here, sums = self.around(field, at, tiles, 1)
        result[0, at] = sums[0] - self.dg[0, at] * here[0]

    def residual(self, field, result, low, high, unroll, tiles):
        over_layers(low, high, unroll, lambda at: self.residual_at(at, field, result, tiles))

    def last_at(self, at, field, older, step):
        alpha, beta = step
        here, sums = self.around(field, at, 1, 1)
        return (1.0 + alpha - beta) * here[0] - alpha * older[0, at], (beta * self.iv[0, at]) * sums[0]


class Strips:
    def __init__(self, refs, base, extent, left, right):
        self.c, self.s, self.cx, self.cy, self.cz, self.iv, self.dg, self.va, self.vb = refs
        self.base, self.extent, self.left, self.right = base, extent, left, right

    def lane(self):
        return lax.broadcasted_iota(jnp.int32, (32, LANES), 1)

    def mask(self, pack):
        where_x = self.base + 4 * pack + self.lane() // 32
        cell = self.lane() % 32
        keep = jnp.where(cell < 8, self.left, jnp.where(cell >= 24, self.right, 1.0))
        return jnp.where((where_x >= 0) & (where_x < self.extent), keep, 0.0)

    def x_up(self, tiles):
        turned = [pltpu.roll(t, LANES - 32, 1) for t in tiles]
        return [jnp.where(self.lane() < LANES - 32, turned[p], turned[min(p + 1, 3)]) for p in range(4)]

    def x_down(self, tiles):
        turned = [pltpu.roll(t, 32, 1) for t in tiles]
        return [jnp.where(self.lane() >= 32, turned[p], turned[max(p - 1, 0)]) for p in range(4)]

    def setup(self):
        row = lax.broadcasted_iota(jnp.int32, (32, LANES), 0)
        top, bottom = row == 31, row == 0
        masks = [self.mask(p) for p in range(4)]
        own = [self.c[p] * (0.5 * masks[p]) for p in range(4)]
        above = self.x_up(own)
        x_high = [own[p] + above[p] for p in range(4)]
        x_low = self.x_down(x_high)
        for p in range(4):
            y_high = own[p] + jnp.where(top, 0.0, pltpu.roll(own[p], 31, 0))
            y_low = jnp.where(bottom, own[p], pltpu.roll(y_high, 1, 0))
            z_high = own[p] + pltpu.roll(own[p], LANES - 1, 1)
            z_low = pltpu.roll(z_high, 1, 1)
            diagonal = x_low[p] + x_high[p] + y_low + y_high + z_low + z_high
            self.cx[p] = x_high[p]
            self.cy[p] = jnp.where(top, 0.0, y_high)
            self.cz[p] = z_high
            self.dg[p] = diagonal
            self.iv[p] = jnp.where(masks[p] > 0.5, 1.0 / diagonal, 0.0)

    def start(self, beta):
        for p in range(4):
            self.va[p] = self.s[p] * self.iv[p] * beta

    def around(self, field):
        here = [field[p] for p in range(4)]
        cx = [self.cx[p] for p in range(4)]
        x_up = self.x_up(here)
        x_down = self.x_down([cx[p] * here[p] for p in range(4)])
        sums = []
        for p in range(4):
            cy, cz = self.cy[p], self.cz[p]
            total = cx[p] * x_up[p] + x_down[p]
            total = total + (cy * pltpu.roll(here[p], 31, 0) + pltpu.roll(cy * here[p], 1, 0))
            total = total + (cz * pltpu.roll(here[p], LANES - 1, 1) + pltpu.roll(cz * here[p], 1, 1))
            sums.append(total + self.s[p])
        return here, sums

    def sweep(self, field, result, step, fresh=False):
        alpha, beta = step
        here, sums = self.around(field)
        for p in range(4):
            kept = (1.0 + alpha - beta) * here[p]
            if not fresh:
                kept = kept - alpha * result[p]
            result[p] = kept + (beta * self.iv[p]) * sums[p]

    def residual(self, field, result):
        here, sums = self.around(field)
        for p in range(4):
            result[p] = sums[p] - self.dg[p] * here[p]

    def own(self, ref, pack, layers=range(4)):
        cell = self.lane() % 32
        packed = jnp.zeros((32, LANES), F32)
        for layer in layers:
            tile = ref[0, 4 * pack + layer]
            first = pltpu.roll(tile, 32 * layer + 8, 1)
            last = pltpu.roll(tile, (32 * layer + 24) % LANES, 1)
            packed = jnp.where(self.lane() // 32 == layer, jnp.where(cell < 16, first, last), packed)
        return packed

    def take_halo(self, ref, pack, from_left, from_right):
        cell = lax.broadcasted_iota(jnp.int32, (8, LANES), 1) % 32
        for part in range(4):
            rows = pl.ds(8 * part, 8)
            below = pltpu.roll(from_left, (LANES - 8 * part) % LANES, 1)
            above = pltpu.roll(from_right, 24 - 8 * part, 1) if part < 3 else from_right
            ref[pack, rows, :] = jnp.where(cell < 8, below, jnp.where(cell >= 24, above, ref[pack, rows, :]))

    def give_halo(self, ref, pack, side):
        cell = lax.broadcasted_iota(jnp.int32, (8, LANES), 1) % 32
        packed = None
        for part in range(4):
            shift = (8 * part - 8 - 8 * side) % LANES
            tile = ref[pack, pl.ds(8 * part, 8), :]
            tile = pltpu.roll(tile, shift, 1) if shift else tile
            packed = tile if part == 0 else jnp.where(cell // 8 == part, tile, packed)
        return packed

    def mend(self, tile, ref, at):
        packed, layer = ref[at // 4], at % 4
        first = pltpu.roll(packed, (LANES - 32 * layer - 8) % LANES, 1)
        last = pltpu.roll(packed, (LANES + 104 - 32 * layer) % LANES, 1)
        return jnp.where(self.lane() < 4, first, jnp.where(self.lane() >= LANES - 4, last, tile))


LEVEL_FIELDS = 9
LEVEL_SHAPES = ((1, 16, 32, LANES), (2, 14, 16, LANES), (1, 34, 8, LANES), (1, 15, 8, LANES))
RULER = 1024
SENDERS = 14 + 2 * (2 * REACH + 1)
GROUPS = 36 + 2 * (2 * REACH + 1)


def kernel(wide, narrow, rhs, coef, kept, added, *scratch):
    scratch = list(scratch)
    level_refs = []
    for _ in range(4):
        level_refs.append(scratch[:LEVEL_FIELDS])
        scratch = scratch[LEVEL_FIELDS:]
    strip_refs, scratch = scratch[:LEVEL_FIELDS], scratch[LEVEL_FIELDS:]
    (ps, zs, rz, rcn, kp, k1cx, k1c, sk, sp, k1x, k1p, k1z, rc2, s2m, rs2, rx1, rx1b, sb0, hx0, p1, p0, ruler,
     local_sem, send_sem, recv_sem) = scratch
    me_w = lax.axis_index("wide")
    me_n = lax.axis_index("narrow")

    def there(dw, dn):
        return (lax.rem(me_w + (dw + wide), wide), lax.rem(me_n + (dn + narrow), narrow))

    has = (me_w > 0, me_w < wide - 1)
    has_z = (me_n > 0, me_n < narrow - 1)
    reach = (jnp.minimum(me_w, REACH), jnp.minimum(wide - 1 - me_w, REACH))

    def for_far(first, body, last=REACH):
        for side in range(2):
            sign = 2 * side - 1

            def step(k, carry):
                body(REACH + sign * k, sign * k)
                return carry

            lax.fori_loop(first, jnp.minimum(reach[side], last) + 1, step, 0)

    def for_all_far(body):
        inner = reach[0] + reach[1] == 2 * REACH

        @pl.when(inner)
        def straight():
            for k in range(REACH, 0, -1):
                for sign in (-1, 1):
                    body(REACH + sign * k, sign * k)

        pl.when(jnp.logical_not(inner))(functools.partial(for_far, 1, body))

    def for_sides(body):
        for side in range(2):
            pl.when(has[side])(functools.partial(body, side, 2 * side - 1))

    def for_sides_z(body):
        for side in range(2):
            pl.when(has_z[side])(functools.partial(body, side, 2 * side - 1))

    def for_corners(body):
        for side in range(2):
            for side_z in range(2):
                pl.when(has[side] & has_z[side_z])(
                    functools.partial(body, side, side_z, 2 * side - 1, 2 * side_z - 1)
                )

    @pl.when((me_n == 0) | (me_n == narrow - 1))
    def clear_z():
        for ref in (rz, rcn, k1c, k1z, k1p):
            ref[...] = jnp.zeros(ref.shape, F32)

    @pl.when((me_w < REACH) | (me_w >= wide - REACH))
    def clear():
        def zero(ref):
            ref[...] = jnp.zeros(ref.shape, F32)

        for ref in (rcn, rx1, rx1b, hx0, rc2, rs2, k1cx, k1c, k1x, k1p):
            zero(ref)
        for side in range(2):
            for ref in level_refs[0][:2]:
                zero(ref.at[0, pl.ds(12 * side, 4)])
            zero(level_refs[1][0].at[0, 13 * side])

    def if_reach(least, body):
        for side in range(2):
            pl.when(reach[side] >= least)(functools.partial(body, side, 2 * side - 1))

    barrier = pltpu.get_barrier_semaphore()

    def greet(dw, dn):
        pl.semaphore_signal(barrier, inc=1, device_id=there(dw, dn), device_id_type=MESH_ID)

    for_far(1, lambda slot, dw: greet(dw, 0), GREET_REACH)
    for_sides_z(lambda side, dn: greet(0, dn))
    for_corners(lambda side, side_z, dw, dn: greet(dw, dn))

    c0, s0 = level_refs[0][0], level_refs[0][1]
    load_c = pltpu.make_async_copy(coef, c0.at[0, pl.ds(4, 8)], local_sem.at[0])
    load_s = pltpu.make_async_copy(rhs, s0.at[0, pl.ds(4, 8)], local_sem.at[1])
    load_c.start()
    load_s.start()
    beside_x = jnp.where(has[0], 1, 0) + jnp.where(has[1], 1, 0)
    beside_z = jnp.where(has_z[0], 1, 0) + jnp.where(has_z[1], 1, 0)
    greeted = beside_z + beside_x * beside_z
    for side in range(2):
        greeted = greeted + jnp.minimum(reach[side], GREET_REACH)

    left = jnp.where(me_n > 0, 1.0, 0.0).astype(F32)
    right = jnp.where(me_n < narrow - 1, 1.0, 0.0).astype(F32)

    def lanes(rows):
        return lax.broadcasted_iota(jnp.int32, (rows, LANES), 1)

    def edges(rows, until, low, since, high):
        at = lanes(rows)
        return jnp.where(at < until, low, jnp.where(at >= since, high, 0.0))

    def centred(rows):
        at = lanes(rows)
        return jnp.where((at >= 32) & (at < 96), 1.0, edges(rows, 32, left, 96, right))

    level_0 = Level(level_refs[0], 1.0, 32, 1, 1, 8 * me_w - 4, 8 * wide, [None])
    strips = Strips(strip_refs, 8 * me_w - 4, 8 * wide, left, right)
    level_1 = Level(
        level_refs[1], 0.25, 16, 1, 1, 4 * me_w - 5, 4 * wide, [centred(16), edges(16, 32, right, 96, left)]
    )
    level_2 = Level(level_refs[2], 0.0625, 8, 1, 2, 2 * me_w - 16, 2 * wide, [centred(8)])
    level_3 = Level(level_refs[3], 0.015625, 8, 2, 4, me_w - 7, wide, [centred(8)])

    sent = [0] * SENDERS

    def send(group, src, dst, dw, dn, rows, sender):
        if isinstance(sender, int):
            sent[sender] += rows
        pltpu.make_async_remote_copy(
            src_ref=src, dst_ref=dst, send_sem=send_sem.at[sender], recv_sem=recv_sem.at[group],
            device_id=there(dw, dn), device_id_type=MESH_ID,
        ).start()

    def ruled(rows, group, sender):
        span = ruler.at[pl.ds(0, rows)]
        return pltpu.make_async_remote_copy(
            src_ref=span, dst_ref=span, send_sem=send_sem.at[sender], recv_sem=recv_sem.at[group],
            device_id=there(0, 1), device_id_type=MESH_ID,
        )

    def receive(group, rows):
        ruled(rows, group, 0).wait_recv()

    def receive_sides(group, rows):
        for_sides(lambda side, dw: receive(group + side, rows))

    def receive_sides_z(group, rows):
        for_sides_z(lambda side, dn: receive(group + side, rows))

    def receive_corners(group, rows):
        for_corners(lambda side, side_z, dw, dn: receive(group + 2 * side + side_z, rows))

    def receive_far(group, first, last):
        for_far(first, lambda slot, dw: receive(group + slot, 8), last)

    def sends_done(sender):
        ruled(sent[sender], 0, sender).wait_send()

    from_z, from_s1z = 0, 2
    from_c_corner, from_k_corner, from_s1_corner = 4, 8, 12
    from_c, from_s, from_s_next, from_k, from_s1, from_c1b, from_x0, from_x1, from_x1b = range(16, 34, 2)
    from_four = 34
    from_c2 = 36
    from_s2 = from_c2 + 2 * REACH + 1
    sender_x, sender_x1, sender_x1b, sender_four, sender_z = range(0, 10, 2)
    sender_corner, sender_c2, sender_far = 10, 14, 14 + 2 * REACH + 1

    def restrict_0(ref):
        out = []
        for layer in range(4):
            total = None
            for dx in range(2):
                for dy in range(2):
                    term = ref[0, 4 + 2 * layer + dx, pl.ds(dy, 16, stride=2), :]
                    total = term if total is None else total + term
            total = total + pltpu.roll(total, LANES - 1, 1)
            out.append(0.125 * jnp.take_along_axis(total, (2 * lanes(16) + 64) % LANES, axis=1))
        return out

    odd_8 = lanes(8) % 2 == 1

    def pairs_1(ref):
        out = []
        for layer in range(2):
            total = None
            for dx in range(2):
                for dy in range(2):
                    term = ref[0, 5 + 2 * layer + dx, pl.ds(dy, 8, stride=2), :]
                    total = term if total is None else total + term
            total = total + jnp.where(odd_8, pltpu.roll(total, 1, 1), pltpu.roll(total, LANES - 1, 1))
            out.append(0.125 * total)
        return jnp.where(odd_8, out[1], out[0])

    def squeeze_1(layers, ref, row):
        for part in range(2):
            ref[pl.ds(row + 16 * part, 16), :] = jnp.where(lanes(16) < 64, layers[part], layers[part + 2])

    pl.semaphore_wait(barrier, greeted)

    @for_sides
    def send_faces(side, dw):
        send(from_c + 1 - side, coef.at[pl.ds(4 * side, 4)], c0.at[0, pl.ds(12 - 12 * side, 4)], dw, 0, 128, sender_x + side)
        send(from_s + 1 - side, rhs.at[7 * side], s0.at[0, 12 - 9 * side], dw, 0, 32, sender_x + side)

    def squeeze_halves(first, second):
        low_quarter = lanes(16) % 64 < 32
        return (
            jnp.where(low_quarter, pltpu.roll(first, 96, 1), second),
            jnp.where(low_quarter, first, pltpu.roll(second, 32, 1)),
        )

    load_c.wait()
    own_c1 = restrict_0(c0)
    for half in range(2):
        strips.c[1 + half] = strips.own(c0, 1 + half)
    for side in range(2):
        squeeze_1(own_c1, zs.at[side], 32)
        for half in range(2):
            zs[side, pl.ds(16 * half, 8), :] = strips.give_halo(strips.c, 1 + half, side)
    load_s.wait()
    for half in range(2):
        strips.s[1 + half] = strips.own(s0, 1 + half)
    for side in range(2):
        for half in range(2):
            zs[side, pl.ds(16 * half + 8, 8), :] = strips.give_halo(strips.s, 1 + half, side)

    for_sides_z(
        lambda side, dn: send(from_z + 1 - side, zs.at[side], rz.at[1 - side], 0, dn, 64, sender_z + side)
    )

    def send_corner(group, src, dst, rows, side, side_z):
        at = 2 * side + side_z
        send(group + 3 - at, src, dst, 2 * side - 1, 2 * side_z - 1, rows, sender_corner + at)

    @for_corners
    def send_c_corner(side, side_z, dw, dn):
        src = zs.at[side_z, pl.ds(16 * side, 16)]
        send_corner(from_c_corner, src, rcn.at[1 - side, 1 - side_z], 16, side, side_z)

    @for_sides
    def send_s_next(side, dw):
        src = rhs.at[pl.ds(1 + 4 * side, 2)]
        send(from_s_next + 1 - side, src, s0.at[0, pl.ds(13 - 12 * side, 2)], dw, 0, 64, sender_x + side)

    steps = cheb(3)
    sweep_a = (level_0.va, level_0.vb, 1, 1, steps[1], True)
    sweep_b = (level_0.vb, level_0.va, 1, 1, steps[2], False)
    level_0.setup(5, 10, 6, 1)
    level_0.start(5, 10, 6, 1, steps[0][1])
    over_layers(6, 9, 4, lambda at: level_0.sweep_at(at, *sweep_a))
    over_layers(7, 8, 2, lambda at: level_0.sweep_at(at, *sweep_b))

    def take_halos(field, ref, pack, got):
        rows = pl.ds(8 * field + (16 if pack == 2 else 0), 8)
        strips.take_halo(ref, pack, got[0, rows, :], got[1, rows, :])

    receive_sides_z(from_z, 64)
    for field, ref in enumerate((strips.c, strips.s)):
        for half in range(2):
            take_halos(field, ref, 1 + half, rz)

    def spread_1(ref, block):
        at_lane = lanes(16)
        low_half = at_lane < 64
        low_quarter = at_lane % 64 < 32
        for part in range(2):
            before, own, after = (block(dz, part) for dz in (-1, 0, 1))
            near = jnp.where(low_quarter, before, after)
            outer = jnp.where(low_quarter, after, before)
            own_r, near_r, outer_r = (pltpu.roll(t, 64, 1) for t in (own, near, outer))
            at = 5 + part
            for at, own_a, own_b, near_a, near_b, outer_a, outer_b in (
                (at, own, own_r, near, near_r, outer, outer_r),
                (at + 2, own_r, own, near_r, near, outer_r, outer),
            ):
                centre = jnp.where(low_half, own_a, own_b)
                ref[0, at] = jnp.where(at_lane < 32, near_a, jnp.where(at_lane < 96, centre, near_b))
                ref[1, at] = jnp.where(low_half, outer_a, outer_b)

    def coef_block(dz, part):
        rows = pl.ds(32 + 16 * part, 16)
        return zs[0, rows, :] if dz == 0 else rz[(1 + dz) // 2, rows, :]

    spread_1(level_1.c, coef_block)
    rc2[REACH] = pairs_1(level_1.c)

    def send_block(slot, dw):
        send(from_c2 + 2 * REACH - slot, rc2.at[REACH], rc2.at[2 * REACH - slot], dw, 0, 8, sender_c2 + slot)

    for_far(1, send_block, GREET_REACH)
    k1_own = zs.at[0, pl.ds(32, 32)]
    halves = squeeze_halves(zs[0, pl.ds(32, 16), :], zs[0, pl.ds(48, 16), :])
    at_lane = lanes(16)
    for side in range(2):
        near, far = (0, 3) if side == 0 else (3, 0)
        full = level_1.c[0, 5 + near]
        place = (32 * far + 31, 32 * far)
        cell = (64, 63)
        for side_z in range(2):
            moved = pltpu.roll(full, (place[side_z] - cell[side_z]) % LANES, 1)
            kp[side, side_z] = jnp.where(at_lane == place[side_z], moved, halves[side_z])
    for_sides(
        lambda side, dw: send(from_k + 1 - side, k1_own, k1cx.at[1 - side], dw, 0, 32, sender_x + side)
    )
    for_corners(
        lambda side, side_z, dw, dn: send_corner(
            from_k_corner, kp.at[side, side_z], k1c.at[1 - side, 1 - side_z], 16, side, side_z
        )
    )

    receive_sides(from_c, 128)
    receive_corners(from_c_corner, 16)
    for side in range(2):
        strips.c[3 * side] = strips.own(c0, 3 * side)
        take_halos(0, strips.c, 3 * side, rcn.at[side])
    level_0.setup_below(1, 1)
    over_sides(1, 11, 4, lambda at: level_0.setup_at(at, 1))
    strips.setup()
    receive_sides(from_s, 32)
    over_sides(3, 11, 2, lambda at: level_0.start_at(at, 1, steps[0][1]))
    over_sides(4, 10, 2, lambda at: level_0.sweep_at(at, *sweep_a))
    over_sides(5, 9, 2, lambda at: level_0.sweep_at(at, *sweep_b))
    over_layers(6, 9, 4, lambda at: level_0.residual_at(at, level_0.va, level_0.vb, 1))
    receive_sides(from_s_next, 64)
    for side in range(2):
        strips.s[3 * side] = strips.own(s0, 3 * side, range(1 - side, 4 - side))
        take_halos(1, strips.s, 3 * side, rcn.at[side])
    over_sides(1, 13, 2, lambda at: level_0.start_at(at, 1, steps[0][1]))
    strips.start(steps[0][1])
    over_sides(2, 12, 2, lambda at: level_0.sweep_at(at, *sweep_a))
    strips.sweep(strips.va, strips.vb, steps[1], fresh=True)
    over_sides(3, 11, 2, lambda at: level_0.sweep_at(at, *sweep_b))
    strips.sweep(strips.vb, strips.va, steps[2])
    over_sides(4, 10, 2, lambda at: level_0.residual_at(at, level_0.va, level_0.vb, 1))
    strips.residual(strips.va, strips.vb)
    for at in range(4, 12):
        level_0.vb[0, at] = strips.mend(level_0.vb[0, at], strips.vb, at)

    squeeze_1(restrict_0(level_0.vb), sk, 0)

    sp[0], sp[1] = squeeze_halves(sk[pl.ds(0, 16), :], sk[pl.ds(16, 16), :])

    for_sides(lambda side, dw: send(from_s1 + 1 - side, sk, k1x.at[1 - side], dw, 0, 32, sender_x + side))
    for_corners(
        lambda side, side_z, dw, dn: send_corner(
            from_s1_corner, sp.at[side_z], k1p.at[1 - side, 1 - side_z], 16, side, side_z
        )
    )
    for_sides_z(lambda side, dn: send(from_s1z + 1 - side, sk, k1z.at[1 - side], 0, dn, 32, sender_z + side))

    receive_far(from_c2, 1, GREET_REACH)
    for_far(GREET_REACH + 1, send_block, HALF_REACH)

    for at in range(3, 13):
        level_0.va[0, at] = strips.mend(level_0.va[0, at], strips.va, at)
    own_cell = (strips.lane() % 32 >= 8) & (strips.lane() % 32 < 24)
    for pack_at, layers in enumerate(((3,), range(4), range(4), (0,))):
        strips.va[pack_at] = jnp.where(own_cell, strips.own(level_0.va, pack_at, layers), strips.va[pack_at])
    for side in range(2):
        first = 9 if side == 0 else 5
        for layer in range(2):
            sb0[side, pl.ds(32 * layer, 32), :] = level_0.va[0, first + layer]
        packed = strips.va[2 - side]
        middle = (lanes(16) >= 32) & (lanes(16) < 96)
        sb0[side, pl.ds(64, 16), :] = jnp.where(middle, packed[:16], pltpu.roll(packed[16:], 64, 1))

    @for_sides
    def send_iterate_0(side, dw):
        send(from_x0 + 1 - side, sb0.at[1 - side], hx0.at[1 - side], dw, 0, 80, sender_x + side)

    def source_block(dz, part):
        rows = pl.ds(16 * part, 16)
        return sk[rows, :] if dz == 0 else k1z[(1 + dz) // 2, rows, :]

    def spread_beside(ref, blocks, packs):
        at_lane = lanes(16)
        low_half = at_lane < 64
        for side in range(2):
            for layer in range(4):
                own = blocks[side, pl.ds(16 * (layer % 2), 16), :]
                other = pltpu.roll(own, 64, 1)
                centre = jnp.where(low_half, own, other) if layer < 2 else jnp.where(low_half, other, own)
                before = pltpu.roll(packs[side, 0], (LANES - 32 * layer) % LANES, 1)
                after = pltpu.roll(packs[side, 1], (LANES + 96 - 32 * layer) % LANES, 1)
                ref[0, 1 + 8 * side + layer] = jnp.where(at_lane < 32, before, jnp.where(at_lane < 96, centre, after))

    receive_sides(from_k, 32)
    receive_corners(from_k_corner, 16)
    spread_beside(level_1.c, k1cx, k1c)
    for side in range(2):
        far = 3 if side == 1 else 0
        below, above = (pltpu.roll(k1c[side, side_z], (shift - 32 * far) % LANES, 1)
                        for side_z, shift in ((0, 127), (1, -31)))
        level_1.c[1, 4 + 5 * side] = jnp.where(lanes(16) < 64, above, below)

    @for_sides
    def send_coef_1(side, dw):
        send(from_c1b + 1 - side, level_1.c.at[0, 9 - 5 * side], level_1.c.at[0, 13 - 13 * side], dw, 0, 16, sender_x + side)

    level_1.setup_below(2, 1)
    over_sides(2, 10, 2, lambda at: level_1.setup_at(at, 1))
    over_layers(4, 9, 6, lambda at: level_1.setup_at(at, 2))

    receive_sides_z(from_s1z, 32)
    spread_1(level_1.s, source_block)
    receive_sides(from_s1, 32)
    receive_corners(from_s1_corner, 16)
    spread_beside(level_1.s, k1x, k1p)
    level_1.start(2, 11, 10, 1, steps[0][1])
    over_layers(5, 8, 4, lambda at: level_1.start_outer(at, steps[0][1]))
    over_sides(3, 9, 2, lambda at: level_1.sweep_at(at, level_1.va, level_1.vb, 1, 1, steps[1], True))
    over_layers(5, 8, 4, lambda at: level_1.sweep_at(at, level_1.va, level_1.vb, 2, 1, steps[1], True))
    level_1.sweep(level_1.vb, level_1.va, 4, 9, 6, 1, 1, steps[2])
    level_1.residual(level_1.va, level_1.vb, 5, 8, 4, 1)

    value = pairs_1(level_1.vb)
    s2m[...] = value
    rs2[REACH] = value

    receive_far(from_c2, GREET_REACH + 1, HALF_REACH)
    for_all_far(
        lambda slot, dw: send(
            from_s2 + 2 * REACH - slot, s2m, rs2.at[2 * REACH - slot], dw, 0, 8, sender_far + slot
        )
    )

    @functools.partial(if_reach, HALF_REACH)
    def send_four(side, sign):
        src, dst = rc2.at[pl.ds(9 - 5 * side, 4)], rc2.at[pl.ds(13 - 13 * side, 4)]
        send(from_four + 1 - side, src, dst, HALF_REACH * sign, 0, 32, sender_four + side)

    @for_sides
    def send_iterate_1(side, dw):
        send(from_x1 + 1 - side, level_1.va.at[0, pl.ds(6 - side, 3)], rx1.at[1 - side], dw, 0, 48, sender_x1 + side)

    for side in range(2):
        @pl.when(reach[side] >= 2)
        def send_next_1():
            layer = level_1.va.at[0, 5 + 3 * side]
            send(from_x1b + 1 - side, layer, rx1b.at[1 - side], 4 * side - 2, 0, 16, sender_x1b + side)

    receive_sides(from_c1b, 16)
    level_1.setup_below(1, 1)
    over_sides(1, 12, 1, lambda at: level_1.setup_at(at, 1))

    def spread_2(ref, blocks):
        for block in range(2 * REACH + 1):
            packed = blocks[block]
            ref[0, 2 * block] = jnp.where(odd_8, pltpu.roll(packed, 1, 1), packed)
            ref[0, 2 * block + 1] = jnp.where(odd_8, packed, pltpu.roll(packed, LANES - 1, 1))

    def restrict_2(ref, at):
        total = ref[0, 2 * at + 2] + ref[0, 2 * at + 3]
        odd_row = lax.broadcasted_iota(jnp.int32, (8, LANES), 0) % 2 == 1
        total = total + jnp.where(odd_row, pltpu.roll(total, 1, 0), pltpu.roll(total, 7, 0))
        second = lanes(8) % 4 >= 2
        total = total + jnp.where(second, pltpu.roll(total, 2, 1), pltpu.roll(total, LANES - 2, 1))
        return 0.125 * total

    if_reach(HALF_REACH, lambda side, sign: receive(from_four + side, 32))
    spread_2(level_2.c, rc2)
    level_2.setup(1, 32, 16, 1)
    for at in range(15):
        level_3.c[0, at] = restrict_2(level_2.c, at)
    level_3.setup(1, 13, 13, 1)

    for_sides(lambda side, dw: sends_done(sender_x + side))
    for_sides_z(lambda side, dn: sends_done(sender_z + side))
    for_corners(lambda side, side_z, dw, dn: sends_done(sender_corner + 2 * side + side_z))
    if_reach(HALF_REACH, lambda side, sign: sends_done(sender_four + side))
    for_far(1, lambda slot, dw: ruled(8, 0, sender_c2 + slot).wait_send(), HALF_REACH)
    for_all_far(lambda slot, dw: ruled(8, 0, sender_far + slot).wait_send())
    for side in range(2):
        pl.when(has[side])(functools.partial(sends_done, sender_x1 + side))
        pl.when(reach[side] >= 2)(functools.partial(sends_done, sender_x1b + side))

    for_all_far(lambda slot, dw: receive(from_s2 + slot, 8))
    spread_2(level_2.s, rs2)
    level_2.start(1, 32, 32, 1, steps[0][1])
    level_2.sweep(level_2.va, level_2.vb, 2, 31, 30, 1, 1, steps[1], fresh=True)
    level_2.sweep(level_2.vb, level_2.va, 3, 30, 28, 1, 1, steps[2])
    level_2.residual(level_2.va, level_2.vb, 4, 29, 26, 1)

    for at in range(1, 14):
        level_3.s[0, at] = restrict_2(level_2.vb, at)
    coarse = cheb(4)
    level_3.start(1, 13, 13, 1, coarse[0][1])
    level_3.sweep(level_3.va, level_3.vb, 2, 12, 11, 1, 1, coarse[1], fresh=True)
    level_3.sweep(level_3.vb, level_3.va, 3, 11, 9, 1, 1, coarse[2])
    level_3.sweep(level_3.va, level_3.vb, 4, 10, 7, 1, 1, coarse[3])

    for at in range(10, 24):
        level_2.vb[0, at] = level_2.va[0, at] + level_3.vb[0, (at - 2) // 2]
    level_2.sweep(level_2.vb, level_2.va, 11, 22, 12, 1, 1, steps[0], fresh=True)
    level_2.sweep(level_2.va, level_2.vb, 12, 21, 10, 1, 1, steps[1])
    level_2.sweep(level_2.vb, level_2.va, 13, 20, 8, 1, 1, steps[2])

    for at in range(8):
        value = level_2.va[0, 13 + at]
        for part in range(2):
            p1[at, pl.ds(part, 8, stride=2), :] = value
    receive_sides(from_x1, 48)
    for side in range(2):
        pl.when(reach[side] >= 2)(functools.partial(receive, from_x1b + side, 16))
    for at in range(14):
        if 4 <= at <= 9:
            before = level_1.va[0, at]
        else:
            before = rx1b[0] if at == 0 else rx1[0, at - 1] if at < 4 else rx1[1, at - 10] if at < 13 else rx1b[1]
        level_1.vb[0, at] = before + p1[(at + 1) // 2]
    level_1.sweep(level_1.vb, level_1.va, 1, 12, 12, 1, 1, steps[0], fresh=True)
    level_1.sweep(level_1.va, level_1.vb, 2, 11, 10, 1, 1, steps[1])
    level_1.sweep(level_1.vb, level_1.va, 3, 10, 8, 1, 1, steps[2])

    cell = lanes(16) % 32
    strip_lane = jnp.where(cell < 16, 28, 84) + cell // 2
    low_half = lanes(16) < 64
    fine = []
    for at in range(8):
        value = level_1.va[0, 3 + at]
        own = jnp.take_along_axis(value, lanes(16) // 2 + 32, axis=1)
        fine.append(jnp.take_along_axis(value, strip_lane, axis=1))
        for part in range(2):
            p0[at, pl.ds(part, 16, stride=2), :] = own
    for pack in range(4):
        value = jnp.where(low_half, fine[2 * pack], fine[2 * pack + 1])
        for part in range(2):
            ps[pack, pl.ds(part, 16, stride=2), :] = value
    receive_sides(from_x0, 80)
    for side in range(2):
        for layer in range(2):
            at = (1 if side == 0 else 13) + layer
            level_0.vb[0, at] = hx0[side, pl.ds(32 * layer, 32), :] + p0[at // 2]
        packed = hx0[side, pl.ds(64, 16), :]
        layer = lanes(16) // 32
        for part, value in enumerate((packed, pltpu.roll(packed, 64, 1))):
            rows = pl.ds(16 * part, 16)
            own = jnp.where(layer == (3 if side == 0 else 0), strips.va[3 * side, rows, :], 0.0)
            value = jnp.where((layer == 1) | (layer == 2), value, own)
            strips.vb[3 * side, rows, :] = value + ps[3 * side, rows, :]
    for pack in (1, 2):
        strips.vb[pack] = strips.va[pack] + ps[pack]

    def correct(at):
        level_0.vb[0, at] = level_0.va[0, at] + p0[at // 2]

    over_layers(3, 12, 10, correct)
    level_0.sweep(level_0.vb, level_0.va, 2, 13, 12, 1, 1, steps[0], fresh=True)
    strips.sweep(strips.vb, strips.va, steps[0], fresh=True)
    level_0.sweep(level_0.va, level_0.vb, 3, 12, 10, 1, 1, steps[1])
    strips.sweep(strips.va, strips.vb, steps[1])
    strips.sweep(strips.vb, strips.va, steps[2])
    inner = (strips.lane() >= 4) & (strips.lane() < LANES - 4)
    for at in range(4, 12):
        kept_here, added_here = level_0.last_at(at, level_0.vb, level_0.va, steps[2])
        kept[at - 4] = strips.mend(kept_here, strips.va, at)
        added[at - 4] = jnp.where(inner, added_here, 0.0)


def per_device(right_side, conductivity, wide, narrow):
    brick = (8, 32, LANES)
    scratch = []
    for shape in LEVEL_SHAPES:
        scratch += [pltpu.VMEM(shape, F32)] * LEVEL_FIELDS
    scratch += [pltpu.VMEM((4, 32, LANES), F32)] * LEVEL_FIELDS
    shapes = [
        (4, 32, LANES),
        (2, 64, LANES), (2, 64, LANES), (2, 2, 16, LANES),
        (2, 2, 16, LANES), (2, 32, LANES), (2, 2, 16, LANES),
        (32, LANES), (2, 16, LANES), (2, 32, LANES), (2, 2, 16, LANES), (2, 32, LANES),
        (2 * REACH + 1, 8, LANES), (8, LANES), (2 * REACH + 1, 8, LANES),
        (2, 3, 16, LANES), (2, 16, LANES),
        (2, 80, LANES), (2, 80, LANES),
        (8, 16, LANES), (8, 32, LANES),
        (RULER, LANES),
    ]
    scratch += [pltpu.VMEM(shape, F32) for shape in shapes]
    scratch += [pltpu.SemaphoreType.DMA((2,)), pltpu.SemaphoreType.DMA((SENDERS,)), pltpu.SemaphoreType.DMA((GROUPS,))]
    kept, added = pl.pallas_call(
        functools.partial(kernel, wide, narrow),
        out_shape=[jax.ShapeDtypeStruct(brick, F32)] * 2,
        in_specs=[pl.BlockSpec(memory_space=pltpu.HBM)] * 2,
        out_specs=[pl.BlockSpec(memory_space=pltpu.VMEM)] * 2,
        scratch_shapes=scratch,
        compiler_params=pltpu.CompilerParams(
            collective_id=0, has_side_effects=True, vmem_limit_bytes=32 * 1024 * 1024
        ),
    )(pltpu.with_memory_space_constraint(right_side, pltpu.HBM), pltpu.with_memory_space_constraint(conductivity, pltpu.HBM))
    return kept + added


def solution(mesh):
    spec = P("wide", None, "narrow")
    body = functools.partial(per_device, wide=mesh.shape["wide"], narrow=mesh.shape["narrow"])
    return jax.shard_map(body, mesh=mesh, in_specs=(spec, spec), out_specs=spec, check_vma=False)
```

```python
import functools

import jax
import jax.numpy as jnp
from jax import lax
from jax.experimental import pallas as pl
from jax.experimental.pallas import tpu as pltpu
from jax.sharding import PartitionSpec as P

CENTER = 1.125
HALF = 0.875
LANES = 128
REACH = 8
HALF_REACH = 4
F32 = jnp.float32
MESH_ID = pl.DeviceIdType.MESH


def cheb(sweeps):
    sigma = CENTER / HALF
    steps = [(0.0, 1.0 / CENTER)]
    ratio = 1.0 / sigma
    for _ in range(sweeps - 1):
        ratio_next = 1.0 / (2.0 * sigma - ratio)
        steps.append((ratio_next * ratio, 2.0 * ratio_next / HALF))
        ratio = ratio_next
    return steps


def over_sides(first, second, count, body):
    for base in (first, second):
        for at in range(count):
            body(base + at)


def over_layers(low, high, unroll, body):
    count = high - low + 1
    if count == unroll:
        for at in range(low, high + 1):
            body(at)
        return

    def block(step, carry):
        for at in range(unroll):
            body(low + step * unroll + at)
        return carry

    lax.fori_loop(0, count // unroll, block, 0)


class Level:
    def __init__(self, refs, scale, rows, row_step, lane_step, base, extent, lane_mask):
        self.c, self.s, self.cx, self.cy, self.cz, self.iv, self.dg, self.va, self.vb = refs
        self.half = 0.5 * scale
        self.rows, self.row_step, self.lane_step = rows, row_step, lane_step
        self.base, self.extent, self.lane_mask = base, extent, lane_mask

    def inside(self, at):
        where_x = self.base + at
        return jnp.where((where_x >= 0) & (where_x < self.extent), 1.0, 0.0).astype(F32)

    def lane(self):
        return lax.broadcasted_iota(jnp.int32, (self.rows, LANES), 1)

    def row(self):
        return lax.broadcasted_iota(jnp.int32, (self.rows, LANES), 0)

    def y_up(self, tile):
        return pltpu.roll(tile, self.rows - self.row_step, 0)

    def y_down(self, tile):
        return pltpu.roll(tile, self.row_step, 0)

    def turned(self, tiles, shift, edge, count):
        out = [pltpu.roll(t, shift, 1) for t in tiles]
        if len(tiles) == 1:
            return out
        at_edge = self.lane() == edge
        return [jnp.where(at_edge, out[1 - k], out[k]) for k in range(count)]

    def z_up(self, tiles, count):
        return self.turned(tiles, LANES - self.lane_step, LANES - 1, count)

    def z_down(self, tiles, count):
        return self.turned(tiles, self.lane_step, 0, count)

    def masked(self, at, tiles):
        keep = self.inside(at) * self.half
        out = []
        for k in range(tiles):
            mask = self.lane_mask[k]
            out.append(self.c[k, at] * (keep if mask is None else mask * keep))
        return out

    def setup_below(self, low, tiles):
        first, second = self.masked(low - 1, tiles), self.masked(low, tiles)
        for k in range(tiles):
            self.cx[k, low - 1] = first[k] + second[k]

    def setup_at(self, at, tiles):
        before, here, after = self.masked(at - 1, tiles), self.masked(at, tiles), self.masked(at + 1, tiles)
        inside = self.inside(at)
        top = self.row() >= self.rows - self.row_step
        bottom = self.row() < self.row_step
        z_up, z_down = self.z_up(here, tiles), self.z_down(here, tiles)
        for k in range(tiles):
            own = here[k]
            x_low = before[k] + own
            x_high = own + after[k]
            y_low = own + jnp.where(bottom, 0.0, self.y_down(own))
            y_high = own + jnp.where(top, 0.0, self.y_up(own))
            z_low = own + z_down[k]
            z_high = own + z_up[k]
            diagonal = x_low + x_high + y_low + y_high + z_low + z_high
            keep = inside if self.lane_mask[k] is None else self.lane_mask[k] * inside
            self.cx[k, at] = x_high
            self.cy[k, at] = jnp.where(top, 0.0, y_high)
            self.cz[k, at] = z_high
            if k == 0:
                self.dg[0, at] = diagonal
            self.iv[k, at] = jnp.where(jnp.full_like(own, 0.0) + keep > 0.5, 1.0 / diagonal, 0.0)

    def setup(self, low, high, unroll, tiles):
        self.setup_below(low, tiles)
        over_layers(low, high, unroll, lambda at: self.setup_at(at, tiles))

    def start_at(self, at, tiles, beta):
        for k in range(tiles):
            self.va[k, at] = self.s[k, at] * self.iv[k, at] * beta

    def start_outer(self, at, beta):
        self.va[1, at] = self.s[1, at] * self.iv[1, at] * beta

    def start(self, low, high, unroll, tiles, beta):
        over_layers(low, high, unroll, lambda at: self.start_at(at, tiles, beta))

    def around(self, field, at, tiles, count):
        here = [field[k, at] for k in range(tiles)]
        cz = [self.cz[k, at] for k in range(tiles)]
        z_up = self.z_up(here, count)
        z_down = self.z_down([cz[k] * here[k] for k in range(tiles)], count)
        sums = []
        for k in range(count):
            cy = self.cy[k, at]
            total = self.cx[k, at] * field[k, at + 1] + self.cx[k, at - 1] * field[k, at - 1]
            total = total + (cy * self.y_up(here[k]) + self.y_down(cy * here[k]))
            total = total + (cz[k] * z_up[k] + z_down[k])
            sums.append(total + self.s[k, at])
        return here, sums

    def sweep_at(self, at, field, result, tiles, count, step, fresh):
        alpha, beta = step
        here, sums = self.around(field, at, tiles, count)
        for k in range(count):
            kept = (1.0 + alpha - beta) * here[k]
            if not fresh:
                kept = kept - alpha * result[k, at]
            result[k, at] = kept + (beta * self.iv[k, at]) * sums[k]

    def sweep(self, field, result, low, high, unroll, tiles, count, step, fresh=False):
        over_layers(low, high, unroll, lambda at: self.sweep_at(at, field, result, tiles, count, step, fresh))

    def residual_at(self, at, field, result, tiles):
        here, sums = self.around(field, at, tiles, 1)
        result[0, at] = sums[0] - self.dg[0, at] * here[0]

    def residual(self, field, result, low, high, unroll, tiles):
        over_layers(low, high, unroll, lambda at: self.residual_at(at, field, result, tiles))

    def last_at(self, at, field, older, step):
        alpha, beta = step
        here, sums = self.around(field, at, 1, 1)
        return (1.0 + alpha - beta) * here[0] - alpha * older[0, at], (beta * self.iv[0, at]) * sums[0]


class Strips:
    def __init__(self, refs, base, extent, left, right):
        self.c, self.s, self.cx, self.cy, self.cz, self.iv, self.dg, self.va, self.vb = refs
        self.base, self.extent, self.left, self.right = base, extent, left, right

    def lane(self):
        return lax.broadcasted_iota(jnp.int32, (32, LANES), 1)

    def mask(self, pack):
        where_x = self.base + 4 * pack + self.lane() // 32
        cell = self.lane() % 32
        keep = jnp.where(cell < 8, self.left, jnp.where(cell >= 24, self.right, 1.0))
        return jnp.where((where_x >= 0) & (where_x < self.extent), keep, 0.0)

    def x_up(self, tiles):
        turned = [pltpu.roll(t, LANES - 32, 1) for t in tiles]
        return [jnp.where(self.lane() < LANES - 32, turned[p], turned[min(p + 1, 3)]) for p in range(4)]

    def x_down(self, tiles):
        turned = [pltpu.roll(t, 32, 1) for t in tiles]
        return [jnp.where(self.lane() >= 32, turned[p], turned[max(p - 1, 0)]) for p in range(4)]

    def setup(self):
        row = lax.broadcasted_iota(jnp.int32, (32, LANES), 0)
        top, bottom = row == 31, row == 0
        masks = [self.mask(p) for p in range(4)]
        own = [self.c[p] * (0.5 * masks[p]) for p in range(4)]
        above = self.x_up(own)
        x_high = [own[p] + above[p] for p in range(4)]
        x_low = self.x_down(x_high)
        for p in range(4):
            y_high = own[p] + jnp.where(top, 0.0, pltpu.roll(own[p], 31, 0))
            y_low = jnp.where(bottom, own[p], pltpu.roll(y_high, 1, 0))
            z_high = own[p] + pltpu.roll(own[p], LANES - 1, 1)
            z_low = pltpu.roll(z_high, 1, 1)
            diagonal = x_low[p] + x_high[p] + y_low + y_high + z_low + z_high
            self.cx[p] = x_high[p]
            self.cy[p] = jnp.where(top, 0.0, y_high)
            self.cz[p] = z_high
            self.dg[p] = diagonal
            self.iv[p] = jnp.where(masks[p] > 0.5, 1.0 / diagonal, 0.0)

    def start(self, beta):
        for p in range(4):
            self.va[p] = self.s[p] * self.iv[p] * beta

    def around(self, field):
        here = [field[p] for p in range(4)]
        cx = [self.cx[p] for p in range(4)]
        x_up = self.x_up(here)
        x_down = self.x_down([cx[p] * here[p] for p in range(4)])
        sums = []
        for p in range(4):
            cy, cz = self.cy[p], self.cz[p]
            total = cx[p] * x_up[p] + x_down[p]
            total = total + (cy * pltpu.roll(here[p], 31, 0) + pltpu.roll(cy * here[p], 1, 0))
            total = total + (cz * pltpu.roll(here[p], LANES - 1, 1) + pltpu.roll(cz * here[p], 1, 1))
            sums.append(total + self.s[p])
        return here, sums

    def sweep(self, field, result, step, fresh=False):
        alpha, beta = step
        here, sums = self.around(field)
        for p in range(4):
            kept = (1.0 + alpha - beta) * here[p]
            if not fresh:
                kept = kept - alpha * result[p]
            result[p] = kept + (beta * self.iv[p]) * sums[p]

    def residual(self, field, result):
        here, sums = self.around(field)
        for p in range(4):
            result[p] = sums[p] - self.dg[p] * here[p]

    def own(self, ref, pack, layers=range(4)):
        cell = self.lane() % 32
        packed = jnp.zeros((32, LANES), F32)
        for layer in layers:
            tile = ref[0, 4 * pack + layer]
            first = pltpu.roll(tile, 32 * layer + 8, 1)
            last = pltpu.roll(tile, (32 * layer + 24) % LANES, 1)
            packed = jnp.where(self.lane() // 32 == layer, jnp.where(cell < 16, first, last), packed)
        return packed

    def take_halo(self, ref, pack, from_left, from_right):
        cell = lax.broadcasted_iota(jnp.int32, (8, LANES), 1) % 32
        for part in range(4):
            rows = pl.ds(8 * part, 8)
            below = pltpu.roll(from_left, (LANES - 8 * part) % LANES, 1)
            above = pltpu.roll(from_right, 24 - 8 * part, 1) if part < 3 else from_right
            ref[pack, rows, :] = jnp.where(cell < 8, below, jnp.where(cell >= 24, above, ref[pack, rows, :]))

    def give_halo(self, ref, pack, side):
        cell = lax.broadcasted_iota(jnp.int32, (8, LANES), 1) % 32
        packed = None
        for part in range(4):
            shift = (8 * part - 8 - 8 * side) % LANES
            tile = ref[pack, pl.ds(8 * part, 8), :]
            tile = pltpu.roll(tile, shift, 1) if shift else tile
            packed = tile if part == 0 else jnp.where(cell // 8 == part, tile, packed)
        return packed

    def mend(self, tile, ref, at):
        packed, layer = ref[at // 4], at % 4
        first = pltpu.roll(packed, (LANES - 32 * layer - 8) % LANES, 1)
        last = pltpu.roll(packed, (LANES + 104 - 32 * layer) % LANES, 1)
        return jnp.where(self.lane() < 4, first, jnp.where(self.lane() >= LANES - 4, last, tile))


LEVEL_FIELDS = 9
LEVEL_SHAPES = ((1, 16, 32, LANES), (2, 14, 16, LANES), (1, 34, 8, LANES), (1, 15, 8, LANES))
RULER = 1024
SENDERS = 10 + 2 * (2 * REACH + 1)
GROUPS = 34 + 2 * (2 * REACH + 1)


def kernel(wide, narrow, rhs, coef, kept, added, *scratch):
    scratch = list(scratch)
    level_refs = []
    for _ in range(4):
        level_refs.append(scratch[:LEVEL_FIELDS])
        scratch = scratch[LEVEL_FIELDS:]
    strip_refs, scratch = scratch[:LEVEL_FIELDS], scratch[LEVEL_FIELDS:]
    (ps, zs, rz, rcn, kp, k1cx, k1c, sk, sp, k1x, k1p, k1z, rc2, s2m, rs2, rx1, sb0, hx0, p1, p0, ruler,
     local_sem, send_sem, recv_sem) = scratch
    me_w = lax.axis_index("wide")
    me_n = lax.axis_index("narrow")

    def there(dw, dn):
        return (lax.rem(me_w + (dw + wide), wide), lax.rem(me_n + (dn + narrow), narrow))

    has = (me_w > 0, me_w < wide - 1)
    has_z = (me_n > 0, me_n < narrow - 1)
    reach = (jnp.minimum(me_w, REACH), jnp.minimum(wide - 1 - me_w, REACH))

    def for_far(first, body, last=REACH):
        for side in range(2):
            sign = 2 * side - 1

            def step(k, carry):
                body(REACH + sign * k, sign * k)
                return carry

            lax.fori_loop(first, jnp.minimum(reach[side], last) + 1, step, 0)

    def for_all_far(body):
        inner = reach[0] + reach[1] == 2 * REACH

        @pl.when(inner)
        def straight():
            for k in range(REACH, 0, -1):
                for sign in (-1, 1):
                    body(REACH + sign * k, sign * k)

        pl.when(jnp.logical_not(inner))(functools.partial(for_far, 1, body))

    def for_sides(body):
        for side in range(2):
            pl.when(has[side])(functools.partial(body, side, 2 * side - 1))

    def for_sides_z(body):
        for side in range(2):
            pl.when(has_z[side])(functools.partial(body, side, 2 * side - 1))

    def for_corners(body):
        for side in range(2):
            for side_z in range(2):
                pl.when(has[side] & has_z[side_z])(
                    functools.partial(body, side, side_z, 2 * side - 1, 2 * side_z - 1)
                )

    @pl.when((me_n == 0) | (me_n == narrow - 1))
    def clear_z():
        for ref in (rz, rcn, k1c, k1z, k1p):
            ref[...] = jnp.zeros(ref.shape, F32)

    @pl.when((me_w < REACH) | (me_w >= wide - REACH))
    def clear():
        def zero(ref):
            ref[...] = jnp.zeros(ref.shape, F32)

        for ref in (rcn, rx1, hx0, rc2, rs2, k1cx, k1c, k1x, k1p):
            zero(ref)
        for side in range(2):
            for ref in level_refs[0][:2]:
                zero(ref.at[0, pl.ds(12 * side, 4)])
            zero(level_refs[1][0].at[0, 13 * side])

    def if_reach(least, body):
        for side in range(2):
            pl.when(reach[side] >= least)(functools.partial(body, side, 2 * side - 1))

    barrier = pltpu.get_barrier_semaphore()

    def greet(dw, dn):
        pl.semaphore_signal(barrier, inc=1, device_id=there(dw, dn), device_id_type=MESH_ID)

    for_far(1, lambda slot, dw: greet(dw, 0), HALF_REACH)
    for_sides_z(lambda side, dn: greet(0, dn))
    for_corners(lambda side, side_z, dw, dn: greet(dw, dn))

    c0, s0 = level_refs[0][0], level_refs[0][1]
    load_c = pltpu.make_async_copy(coef, c0.at[0, pl.ds(4, 8)], local_sem.at[0])
    load_s = pltpu.make_async_copy(rhs, s0.at[0, pl.ds(4, 8)], local_sem.at[1])
    load_c.start()
    load_s.start()
    beside_x = jnp.where(has[0], 1, 0) + jnp.where(has[1], 1, 0)
    beside_z = jnp.where(has_z[0], 1, 0) + jnp.where(has_z[1], 1, 0)
    greeted = beside_z + beside_x * beside_z
    for side in range(2):
        greeted = greeted + jnp.minimum(reach[side], HALF_REACH)

    left = jnp.where(me_n > 0, 1.0, 0.0).astype(F32)
    right = jnp.where(me_n < narrow - 1, 1.0, 0.0).astype(F32)

    def lanes(rows):
        return lax.broadcasted_iota(jnp.int32, (rows, LANES), 1)

    def edges(rows, until, low, since, high):
        at = lanes(rows)
        return jnp.where(at < until, low, jnp.where(at >= since, high, 0.0))

    def centred(rows):
        at = lanes(rows)
        return jnp.where((at >= 32) & (at < 96), 1.0, edges(rows, 32, left, 96, right))

    level_0 = Level(level_refs[0], 1.0, 32, 1, 1, 8 * me_w - 4, 8 * wide, [None])
    strips = Strips(strip_refs, 8 * me_w - 4, 8 * wide, left, right)
    level_1 = Level(
        level_refs[1], 0.25, 16, 1, 1, 4 * me_w - 5, 4 * wide, [centred(16), edges(16, 32, right, 96, left)]
    )
    level_2 = Level(level_refs[2], 0.0625, 8, 1, 2, 2 * me_w - 16, 2 * wide, [centred(8)])
    level_3 = Level(level_refs[3], 0.015625, 8, 2, 4, me_w - 7, wide, [centred(8)])

    sent = [0] * SENDERS

    def send(group, src, dst, dw, dn, rows, sender):
        if isinstance(sender, int):
            sent[sender] += rows
        pltpu.make_async_remote_copy(
            src_ref=src, dst_ref=dst, send_sem=send_sem.at[sender], recv_sem=recv_sem.at[group],
            device_id=there(dw, dn), device_id_type=MESH_ID,
        ).start()

    def ruled(rows, group, sender):
        span = ruler.at[pl.ds(0, rows)]
        return pltpu.make_async_remote_copy(
            src_ref=span, dst_ref=span, send_sem=send_sem.at[sender], recv_sem=recv_sem.at[group],
            device_id=there(0, 1), device_id_type=MESH_ID,
        )

    def receive(group, rows):
        ruled(rows, group, 0).wait_recv()

    def receive_sides(group, rows):
        for_sides(lambda side, dw: receive(group + side, rows))

    def receive_sides_z(group, rows):
        for_sides_z(lambda side, dn: receive(group + side, rows))

    def receive_corners(group, rows):
        for_corners(lambda side, side_z, dw, dn: receive(group + 2 * side + side_z, rows))

    def receive_far(group, last=REACH):
        for_far(1, lambda slot, dw: receive(group + slot, 8), last)

    def sends_done(sender):
        ruled(sent[sender], 0, sender).wait_send()

    from_z, from_s1z = 0, 2
    from_c_corner, from_k_corner, from_s1_corner = 4, 8, 12
    from_c, from_s, from_s_next, from_k, from_s1, from_c1b, from_x0, from_x1 = range(16, 32, 2)
    from_four = 32
    from_c2 = 34
    from_s2 = from_c2 + 2 * REACH + 1
    sender_x, sender_four, sender_z = range(0, 6, 2)
    sender_corner, sender_c2, sender_far = 6, 10, 10 + 2 * REACH + 1

    def restrict_0(ref):
        out = []
        for layer in range(4):
            total = None
            for dx in range(2):
                for dy in range(2):
                    term = ref[0, 4 + 2 * layer + dx, pl.ds(dy, 16, stride=2), :]
                    total = term if total is None else total + term
            total = total + pltpu.roll(total, LANES - 1, 1)
            out.append(0.125 * jnp.take_along_axis(total, (2 * lanes(16) + 64) % LANES, axis=1))
        return out

    odd_8 = lanes(8) % 2 == 1

    def pairs_1(ref):
        out = []
        for layer in range(2):
            total = None
            for dx in range(2):
                for dy in range(2):
                    term = ref[0, 5 + 2 * layer + dx, pl.ds(dy, 8, stride=2), :]
                    total = term if total is None else total + term
            total = total + jnp.where(odd_8, pltpu.roll(total, 1, 1), pltpu.roll(total, LANES - 1, 1))
            out.append(0.125 * total)
        return jnp.where(odd_8, out[1], out[0])

    def squeeze_1(layers, ref, row):
        for part in range(2):
            ref[pl.ds(row + 16 * part, 16), :] = jnp.where(lanes(16) < 64, layers[part], layers[part + 2])

    pl.semaphore_wait(barrier, greeted)

    @for_sides
    def send_faces(side, dw):
        send(from_c + 1 - side, coef.at[pl.ds(4 * side, 4)], c0.at[0, pl.ds(12 - 12 * side, 4)], dw, 0, 128, sender_x + side)
        send(from_s + 1 - side, rhs.at[7 * side], s0.at[0, 12 - 9 * side], dw, 0, 32, sender_x + side)

    def squeeze_halves(first, second):
        low_quarter = lanes(16) % 64 < 32
        return (
            jnp.where(low_quarter, pltpu.roll(first, 96, 1), second),
            jnp.where(low_quarter, first, pltpu.roll(second, 32, 1)),
        )

    load_c.wait()
    own_c1 = restrict_0(c0)
    for half in range(2):
        strips.c[1 + half] = strips.own(c0, 1 + half)
    for side in range(2):
        squeeze_1(own_c1, zs.at[side], 32)
        for half in range(2):
            zs[side, pl.ds(16 * half, 8), :] = strips.give_halo(strips.c, 1 + half, side)
    load_s.wait()
    for half in range(2):
        strips.s[1 + half] = strips.own(s0, 1 + half)
    for side in range(2):
        for half in range(2):
            zs[side, pl.ds(16 * half + 8, 8), :] = strips.give_halo(strips.s, 1 + half, side)

    for_sides_z(
        lambda side, dn: send(from_z + 1 - side, zs.at[side], rz.at[1 - side], 0, dn, 64, sender_z + side)
    )

    def send_corner(group, src, dst, rows, side, side_z):
        at = 2 * side + side_z
        send(group + 3 - at, src, dst, 2 * side - 1, 2 * side_z - 1, rows, sender_corner + at)

    @for_corners
    def send_c_corner(side, side_z, dw, dn):
        src = zs.at[side_z, pl.ds(16 * side, 16)]
        send_corner(from_c_corner, src, rcn.at[1 - side, 1 - side_z], 16, side, side_z)

    @for_sides
    def send_s_next(side, dw):
        src = rhs.at[pl.ds(1 + 4 * side, 2)]
        send(from_s_next + 1 - side, src, s0.at[0, pl.ds(13 - 12 * side, 2)], dw, 0, 64, sender_x + side)

    steps = cheb(3)
    sweep_a = (level_0.va, level_0.vb, 1, 1, steps[1], True)
    sweep_b = (level_0.vb, level_0.va, 1, 1, steps[2], False)
    level_0.setup(5, 10, 6, 1)
    level_0.start(5, 10, 6, 1, steps[0][1])
    over_layers(6, 9, 4, lambda at: level_0.sweep_at(at, *sweep_a))
    over_layers(7, 8, 2, lambda at: level_0.sweep_at(at, *sweep_b))

    def take_halos(field, ref, pack, got):
        rows = pl.ds(8 * field + (16 if pack == 2 else 0), 8)
        strips.take_halo(ref, pack, got[0, rows, :], got[1, rows, :])

    receive_sides_z(from_z, 64)
    for field, ref in enumerate((strips.c, strips.s)):
        for half in range(2):
            take_halos(field, ref, 1 + half, rz)

    def spread_1(ref, block):
        at_lane = lanes(16)
        low_half = at_lane < 64
        low_quarter = at_lane % 64 < 32
        for part in range(2):
            before, own, after = (block(dz, part) for dz in (-1, 0, 1))
            near = jnp.where(low_quarter, before, after)
            outer = jnp.where(low_quarter, after, before)
            own_r, near_r, outer_r = (pltpu.roll(t, 64, 1) for t in (own, near, outer))
            at = 5 + part
            for at, own_a, own_b, near_a, near_b, outer_a, outer_b in (
                (at, own, own_r, near, near_r, outer, outer_r),
                (at + 2, own_r, own, near_r, near, outer_r, outer),
            ):
                centre = jnp.where(low_half, own_a, own_b)
                ref[0, at] = jnp.where(at_lane < 32, near_a, jnp.where(at_lane < 96, centre, near_b))
                ref[1, at] = jnp.where(low_half, outer_a, outer_b)

    def coef_block(dz, part):
        rows = pl.ds(32 + 16 * part, 16)
        return zs[0, rows, :] if dz == 0 else rz[(1 + dz) // 2, rows, :]

    spread_1(level_1.c, coef_block)
    rc2[REACH] = pairs_1(level_1.c)

    for_far(
        1,
        lambda slot, dw: send(
            from_c2 + 2 * REACH - slot, rc2.at[REACH], rc2.at[2 * REACH - slot], dw, 0, 8, sender_c2 + slot
        ),
        HALF_REACH,
    )
    k1_own = zs.at[0, pl.ds(32, 32)]
    halves = squeeze_halves(zs[0, pl.ds(32, 16), :], zs[0, pl.ds(48, 16), :])
    at_lane = lanes(16)
    for side in range(2):
        near, far = (0, 3) if side == 0 else (3, 0)
        full = level_1.c[0, 5 + near]
        place = (32 * far + 31, 32 * far)
        cell = (64, 63)
        for side_z in range(2):
            moved = pltpu.roll(full, (place[side_z] - cell[side_z]) % LANES, 1)
            kp[side, side_z] = jnp.where(at_lane == place[side_z], moved, halves[side_z])
    for_sides(
        lambda side, dw: send(from_k + 1 - side, k1_own, k1cx.at[1 - side], dw, 0, 32, sender_x + side)
    )
    for_corners(
        lambda side, side_z, dw, dn: send_corner(
            from_k_corner, kp.at[side, side_z], k1c.at[1 - side, 1 - side_z], 16, side, side_z
        )
    )

    receive_sides(from_c, 128)
    receive_corners(from_c_corner, 16)
    for side in range(2):
        strips.c[3 * side] = strips.own(c0, 3 * side)
        take_halos(0, strips.c, 3 * side, rcn.at[side])
    level_0.setup_below(1, 1)
    over_sides(1, 11, 4, lambda at: level_0.setup_at(at, 1))
    strips.setup()
    receive_sides(from_s, 32)
    over_sides(3, 11, 2, lambda at: level_0.start_at(at, 1, steps[0][1]))
    over_sides(4, 10, 2, lambda at: level_0.sweep_at(at, *sweep_a))
    over_sides(5, 9, 2, lambda at: level_0.sweep_at(at, *sweep_b))
    over_layers(6, 9, 4, lambda at: level_0.residual_at(at, level_0.va, level_0.vb, 1))
    receive_sides(from_s_next, 64)
    for side in range(2):
        strips.s[3 * side] = strips.own(s0, 3 * side, range(1 - side, 4 - side))
        take_halos(1, strips.s, 3 * side, rcn.at[side])
    over_sides(1, 13, 2, lambda at: level_0.start_at(at, 1, steps[0][1]))
    strips.start(steps[0][1])
    over_sides(2, 12, 2, lambda at: level_0.sweep_at(at, *sweep_a))
    strips.sweep(strips.va, strips.vb, steps[1], fresh=True)
    over_sides(3, 11, 2, lambda at: level_0.sweep_at(at, *sweep_b))
    strips.sweep(strips.vb, strips.va, steps[2])
    over_sides(4, 10, 2, lambda at: level_0.residual_at(at, level_0.va, level_0.vb, 1))
    strips.residual(strips.va, strips.vb)
    for at in range(4, 12):
        level_0.vb[0, at] = strips.mend(level_0.vb[0, at], strips.vb, at)

    squeeze_1(restrict_0(level_0.vb), sk, 0)

    sp[0], sp[1] = squeeze_halves(sk[pl.ds(0, 16), :], sk[pl.ds(16, 16), :])

    for_sides(lambda side, dw: send(from_s1 + 1 - side, sk, k1x.at[1 - side], dw, 0, 32, sender_x + side))
    for_corners(
        lambda side, side_z, dw, dn: send_corner(
            from_s1_corner, sp.at[side_z], k1p.at[1 - side, 1 - side_z], 16, side, side_z
        )
    )
    for_sides_z(lambda side, dn: send(from_s1z + 1 - side, sk, k1z.at[1 - side], 0, dn, 32, sender_z + side))

    receive_far(from_c2, HALF_REACH)

    @functools.partial(if_reach, HALF_REACH)
    def send_four(side, sign):
        src, dst = rc2.at[pl.ds(9 - 5 * side, 4)], rc2.at[pl.ds(13 - 13 * side, 4)]
        send(from_four + 1 - side, src, dst, HALF_REACH * sign, 0, 32, sender_four + side)

    for at in range(3, 13):
        level_0.va[0, at] = strips.mend(level_0.va[0, at], strips.va, at)
    own_cell = (strips.lane() % 32 >= 8) & (strips.lane() % 32 < 24)
    for pack_at, layers in enumerate(((3,), range(4), range(4), (0,))):
        strips.va[pack_at] = jnp.where(own_cell, strips.own(level_0.va, pack_at, layers), strips.va[pack_at])
    for side in range(2):
        first = 9 if side == 0 else 5
        for layer in range(2):
            sb0[side, pl.ds(32 * layer, 32), :] = level_0.va[0, first + layer]
        packed = strips.va[2 - side]
        middle = (lanes(16) >= 32) & (lanes(16) < 96)
        sb0[side, pl.ds(64, 16), :] = jnp.where(middle, packed[:16], pltpu.roll(packed[16:], 64, 1))

    @for_sides
    def send_iterate_0(side, dw):
        send(from_x0 + 1 - side, sb0.at[1 - side], hx0.at[1 - side], dw, 0, 80, sender_x + side)

    def source_block(dz, part):
        rows = pl.ds(16 * part, 16)
        return sk[rows, :] if dz == 0 else k1z[(1 + dz) // 2, rows, :]

    def spread_beside(ref, blocks, packs):
        at_lane = lanes(16)
        low_half = at_lane < 64
        for side in range(2):
            for layer in range(4):
                own = blocks[side, pl.ds(16 * (layer % 2), 16), :]
                other = pltpu.roll(own, 64, 1)
                centre = jnp.where(low_half, own, other) if layer < 2 else jnp.where(low_half, other, own)
                before = pltpu.roll(packs[side, 0], (LANES - 32 * layer) % LANES, 1)
                after = pltpu.roll(packs[side, 1], (LANES + 96 - 32 * layer) % LANES, 1)
                ref[0, 1 + 8 * side + layer] = jnp.where(at_lane < 32, before, jnp.where(at_lane < 96, centre, after))

    receive_sides(from_k, 32)
    receive_corners(from_k_corner, 16)
    spread_beside(level_1.c, k1cx, k1c)
    for side in range(2):
        far = 3 if side == 1 else 0
        below, above = (pltpu.roll(k1c[side, side_z], (shift - 32 * far) % LANES, 1)
                        for side_z, shift in ((0, 127), (1, -31)))
        level_1.c[1, 4 + 5 * side] = jnp.where(lanes(16) < 64, above, below)

    @for_sides
    def send_coef_1(side, dw):
        send(from_c1b + 1 - side, level_1.c.at[0, 9 - 5 * side], level_1.c.at[0, 13 - 13 * side], dw, 0, 16, sender_x + side)

    level_1.setup_below(2, 1)
    over_sides(2, 10, 2, lambda at: level_1.setup_at(at, 1))
    over_layers(4, 9, 6, lambda at: level_1.setup_at(at, 2))

    receive_sides_z(from_s1z, 32)
    spread_1(level_1.s, source_block)
    receive_sides(from_s1, 32)
    receive_corners(from_s1_corner, 16)
    spread_beside(level_1.s, k1x, k1p)
    level_1.start(2, 11, 10, 1, steps[0][1])
    over_layers(5, 8, 4, lambda at: level_1.start_outer(at, steps[0][1]))
    over_sides(3, 9, 2, lambda at: level_1.sweep_at(at, level_1.va, level_1.vb, 1, 1, steps[1], True))
    over_layers(5, 8, 4, lambda at: level_1.sweep_at(at, level_1.va, level_1.vb, 2, 1, steps[1], True))
    level_1.sweep(level_1.vb, level_1.va, 4, 9, 6, 1, 1, steps[2])
    level_1.residual(level_1.va, level_1.vb, 5, 8, 4, 1)

    value = pairs_1(level_1.vb)
    s2m[...] = value
    rs2[REACH] = value

    for_all_far(
        lambda slot, dw: send(
            from_s2 + 2 * REACH - slot, s2m, rs2.at[2 * REACH - slot], dw, 0, 8, sender_far + slot
        )
    )

    @for_sides
    def send_iterate_1(side, dw):
        layers = level_1.va.at[0, pl.ds(6 - 2 * side, 4)]
        send(from_x1 + 1 - side, layers, rx1.at[1 - side], dw, 0, 64, sender_x + side)

    receive_sides(from_c1b, 16)
    level_1.setup_below(1, 1)
    over_sides(1, 12, 1, lambda at: level_1.setup_at(at, 1))

    def spread_2(ref, blocks):
        for block in range(2 * REACH + 1):
            packed = blocks[block]
            ref[0, 2 * block] = jnp.where(odd_8, pltpu.roll(packed, 1, 1), packed)
            ref[0, 2 * block + 1] = jnp.where(odd_8, packed, pltpu.roll(packed, LANES - 1, 1))

    def restrict_2(ref, at):
        total = ref[0, 2 * at + 2] + ref[0, 2 * at + 3]
        odd_row = lax.broadcasted_iota(jnp.int32, (8, LANES), 0) % 2 == 1
        total = total + jnp.where(odd_row, pltpu.roll(total, 1, 0), pltpu.roll(total, 7, 0))
        second = lanes(8) % 4 >= 2
        total = total + jnp.where(second, pltpu.roll(total, 2, 1), pltpu.roll(total, LANES - 2, 1))
        return 0.125 * total

    if_reach(HALF_REACH, lambda side, sign: receive(from_four + side, 32))
    spread_2(level_2.c, rc2)
    level_2.setup(1, 32, 16, 1)
    for at in range(15):
        level_3.c[0, at] = restrict_2(level_2.c, at)
    level_3.setup(1, 13, 13, 1)

    for_sides(lambda side, dw: sends_done(sender_x + side))
    for_sides_z(lambda side, dn: sends_done(sender_z + side))
    for_corners(lambda side, side_z, dw, dn: sends_done(sender_corner + 2 * side + side_z))
    if_reach(HALF_REACH, lambda side, sign: sends_done(sender_four + side))
    for_far(1, lambda slot, dw: ruled(8, 0, sender_c2 + slot).wait_send(), HALF_REACH)
    for_all_far(lambda slot, dw: ruled(8, 0, sender_far + slot).wait_send())

    for_all_far(lambda slot, dw: receive(from_s2 + slot, 8))
    spread_2(level_2.s, rs2)
    level_2.start(1, 32, 32, 1, steps[0][1])
    level_2.sweep(level_2.va, level_2.vb, 2, 31, 30, 1, 1, steps[1], fresh=True)
    level_2.sweep(level_2.vb, level_2.va, 3, 30, 28, 1, 1, steps[2])
    level_2.residual(level_2.va, level_2.vb, 4, 29, 26, 1)

    for at in range(1, 14):
        level_3.s[0, at] = restrict_2(level_2.vb, at)
    coarse = cheb(4)
    level_3.start(1, 13, 13, 1, coarse[0][1])
    level_3.sweep(level_3.va, level_3.vb, 2, 12, 11, 1, 1, coarse[1], fresh=True)
    level_3.sweep(level_3.vb, level_3.va, 3, 11, 9, 1, 1, coarse[2])
    level_3.sweep(level_3.va, level_3.vb, 4, 10, 7, 1, 1, coarse[3])

    for at in range(10, 24):
        level_2.vb[0, at] = level_2.va[0, at] + level_3.vb[0, (at - 2) // 2]
    level_2.sweep(level_2.vb, level_2.va, 11, 22, 12, 1, 1, steps[0], fresh=True)
    level_2.sweep(level_2.va, level_2.vb, 12, 21, 10, 1, 1, steps[1])
    level_2.sweep(level_2.vb, level_2.va, 13, 20, 8, 1, 1, steps[2])

    for at in range(8):
        value = level_2.va[0, 13 + at]
        for part in range(2):
            p1[at, pl.ds(part, 8, stride=2), :] = value
    receive_sides(from_x1, 64)
    for at in range(14):
        if 4 <= at <= 9:
            before = level_1.va[0, at]
        else:
            before = rx1[0, at] if at < 4 else rx1[1, at - 10]
        level_1.vb[0, at] = before + p1[(at + 1) // 2]
    level_1.sweep(level_1.vb, level_1.va, 1, 12, 12, 1, 1, steps[0], fresh=True)
    level_1.sweep(level_1.va, level_1.vb, 2, 11, 10, 1, 1, steps[1])
    level_1.sweep(level_1.vb, level_1.va, 3, 10, 8, 1, 1, steps[2])

    cell = lanes(16) % 32
    strip_lane = jnp.where(cell < 16, 28, 84) + cell // 2
    low_half = lanes(16) < 64
    fine = []
    for at in range(8):
        value = level_1.va[0, 3 + at]
        own = jnp.take_along_axis(value, lanes(16) // 2 + 32, axis=1)
        fine.append(jnp.take_along_axis(value, strip_lane, axis=1))
        for part in range(2):
            p0[at, pl.ds(part, 16, stride=2), :] = own
    for pack in range(4):
        value = jnp.where(low_half, fine[2 * pack], fine[2 * pack + 1])
        for part in range(2):
            ps[pack, pl.ds(part, 16, stride=2), :] = value
    receive_sides(from_x0, 80)
    for side in range(2):
        for layer in range(2):
            at = (1 if side == 0 else 13) + layer
            level_0.vb[0, at] = hx0[side, pl.ds(32 * layer, 32), :] + p0[at // 2]
        packed = hx0[side, pl.ds(64, 16), :]
        layer = lanes(16) // 32
        for part, value in enumerate((packed, pltpu.roll(packed, 64, 1))):
            rows = pl.ds(16 * part, 16)
            own = jnp.where(layer == (3 if side == 0 else 0), strips.va[3 * side, rows, :], 0.0)
            value = jnp.where((layer == 1) | (layer == 2), value, own)
            strips.vb[3 * side, rows, :] = value + ps[3 * side, rows, :]
    for pack in (1, 2):
        strips.vb[pack] = strips.va[pack] + ps[pack]

    def correct(at):
        level_0.vb[0, at] = level_0.va[0, at] + p0[at // 2]

    over_layers(3, 12, 10, correct)
    level_0.sweep(level_0.vb, level_0.va, 2, 13, 12, 1, 1, steps[0], fresh=True)
    strips.sweep(strips.vb, strips.va, steps[0], fresh=True)
    level_0.sweep(level_0.va, level_0.vb, 3, 12, 10, 1, 1, steps[1])
    strips.sweep(strips.va, strips.vb, steps[1])
    strips.sweep(strips.vb, strips.va, steps[2])
    inner = (strips.lane() >= 4) & (strips.lane() < LANES - 4)
    for at in range(4, 12):
        kept_here, added_here = level_0.last_at(at, level_0.vb, level_0.va, steps[2])
        kept[at - 4] = strips.mend(kept_here, strips.va, at)
        added[at - 4] = jnp.where(inner, added_here, 0.0)


def per_device(right_side, conductivity, wide, narrow):
    brick = (8, 32, LANES)
    scratch = []
    for shape in LEVEL_SHAPES:
        scratch += [pltpu.VMEM(shape, F32)] * LEVEL_FIELDS
    scratch += [pltpu.VMEM((4, 32, LANES), F32)] * LEVEL_FIELDS
    shapes = [
        (4, 32, LANES),
        (2, 64, LANES), (2, 64, LANES), (2, 2, 16, LANES),
        (2, 2, 16, LANES), (2, 32, LANES), (2, 2, 16, LANES),
        (32, LANES), (2, 16, LANES), (2, 32, LANES), (2, 2, 16, LANES), (2, 32, LANES),
        (2 * REACH + 1, 8, LANES), (8, LANES), (2 * REACH + 1, 8, LANES),
        (2, 4, 16, LANES),
        (2, 80, LANES), (2, 80, LANES),
        (8, 16, LANES), (8, 32, LANES),
        (RULER, LANES),
    ]
    scratch += [pltpu.VMEM(shape, F32) for shape in shapes]
    scratch += [pltpu.SemaphoreType.DMA((2,)), pltpu.SemaphoreType.DMA((SENDERS,)), pltpu.SemaphoreType.DMA((GROUPS,))]
    kept, added = pl.pallas_call(
        functools.partial(kernel, wide, narrow),
        out_shape=[jax.ShapeDtypeStruct(brick, F32)] * 2,
        in_specs=[pl.BlockSpec(memory_space=pltpu.HBM)] * 2,
        out_specs=[pl.BlockSpec(memory_space=pltpu.VMEM)] * 2,
        scratch_shapes=scratch,
        compiler_params=pltpu.CompilerParams(
            collective_id=0, has_side_effects=True, vmem_limit_bytes=32 * 1024 * 1024
        ),
    )(pltpu.with_memory_space_constraint(right_side, pltpu.HBM), pltpu.with_memory_space_constraint(conductivity, pltpu.HBM))
    return kept + added


def solution(mesh):
    spec = P("wide", None, "narrow")
    body = functools.partial(per_device, wide=mesh.shape["wide"], narrow=mesh.shape["narrow"])
    return jax.shard_map(body, mesh=mesh, in_specs=(spec, spec), out_specs=spec, check_vma=False)
```

```python
import functools

import jax
import jax.numpy as jnp
from jax import lax
from jax.experimental import pallas as pl
from jax.experimental.pallas import tpu as pltpu
from jax.sharding import PartitionSpec as P

CENTER = 1.125
HALF = 0.875
LANES = 128
REACH = 8
HALF_REACH = 4
F32 = jnp.float32
MESH_ID = pl.DeviceIdType.MESH


def cheb(sweeps):
    sigma = CENTER / HALF
    steps = [(0.0, 1.0 / CENTER)]
    ratio = 1.0 / sigma
    for _ in range(sweeps - 1):
        ratio_next = 1.0 / (2.0 * sigma - ratio)
        steps.append((ratio_next * ratio, 2.0 * ratio_next / HALF))
        ratio = ratio_next
    return steps


def over_sides(first, second, count, body):
    for base in (first, second):
        for at in range(count):
            body(base + at)


def over_layers(low, high, unroll, body):
    count = high - low + 1
    if count == unroll:
        for at in range(low, high + 1):
            body(at)
        return

    def block(step, carry):
        for at in range(unroll):
            body(low + step * unroll + at)
        return carry

    lax.fori_loop(0, count // unroll, block, 0)


class Level:
    def __init__(self, refs, scale, rows, row_step, lane_step, base, extent, lane_mask):
        self.c, self.s, self.cx, self.cy, self.cz, self.iv, self.dg, self.va, self.vb = refs
        self.half = 0.5 * scale
        self.rows, self.row_step, self.lane_step = rows, row_step, lane_step
        self.base, self.extent, self.lane_mask = base, extent, lane_mask

    def inside(self, at):
        where_x = self.base + at
        return jnp.where((where_x >= 0) & (where_x < self.extent), 1.0, 0.0).astype(F32)

    def lane(self):
        return lax.broadcasted_iota(jnp.int32, (self.rows, LANES), 1)

    def row(self):
        return lax.broadcasted_iota(jnp.int32, (self.rows, LANES), 0)

    def y_up(self, tile):
        return pltpu.roll(tile, self.rows - self.row_step, 0)

    def y_down(self, tile):
        return pltpu.roll(tile, self.row_step, 0)

    def turned(self, tiles, shift, edge, count):
        out = [pltpu.roll(t, shift, 1) for t in tiles]
        if len(tiles) == 1:
            return out
        at_edge = self.lane() == edge
        return [jnp.where(at_edge, out[1 - k], out[k]) for k in range(count)]

    def z_up(self, tiles, count):
        return self.turned(tiles, LANES - self.lane_step, LANES - 1, count)

    def z_down(self, tiles, count):
        return self.turned(tiles, self.lane_step, 0, count)

    def masked(self, at, tiles):
        keep = self.inside(at) * self.half
        out = []
        for k in range(tiles):
            mask = self.lane_mask[k]
            out.append(self.c[k, at] * (keep if mask is None else mask * keep))
        return out

    def setup_below(self, low, tiles):
        first, second = self.masked(low - 1, tiles), self.masked(low, tiles)
        for k in range(tiles):
            self.cx[k, low - 1] = first[k] + second[k]

    def setup_at(self, at, tiles):
        before, here, after = self.masked(at - 1, tiles), self.masked(at, tiles), self.masked(at + 1, tiles)
        inside = self.inside(at)
        top = self.row() >= self.rows - self.row_step
        bottom = self.row() < self.row_step
        z_up, z_down = self.z_up(here, tiles), self.z_down(here, tiles)
        for k in range(tiles):
            own = here[k]
            x_low = before[k] + own
            x_high = own + after[k]
            y_low = own + jnp.where(bottom, 0.0, self.y_down(own))
            y_high = own + jnp.where(top, 0.0, self.y_up(own))
            z_low = own + z_down[k]
            z_high = own + z_up[k]
            diagonal = x_low + x_high + y_low + y_high + z_low + z_high
            keep = inside if self.lane_mask[k] is None else self.lane_mask[k] * inside
            self.cx[k, at] = x_high
            self.cy[k, at] = jnp.where(top, 0.0, y_high)
            self.cz[k, at] = z_high
            if k == 0:
                self.dg[0, at] = diagonal
            self.iv[k, at] = jnp.where(jnp.full_like(own, 0.0) + keep > 0.5, 1.0 / diagonal, 0.0)

    def setup(self, low, high, unroll, tiles):
        self.setup_below(low, tiles)
        over_layers(low, high, unroll, lambda at: self.setup_at(at, tiles))

    def start_at(self, at, tiles, beta):
        for k in range(tiles):
            self.va[k, at] = self.s[k, at] * self.iv[k, at] * beta

    def start_outer(self, at, beta):
        self.va[1, at] = self.s[1, at] * self.iv[1, at] * beta

    def start(self, low, high, unroll, tiles, beta):
        over_layers(low, high, unroll, lambda at: self.start_at(at, tiles, beta))

    def around(self, field, at, tiles, count):
        here = [field[k, at] for k in range(tiles)]
        cz = [self.cz[k, at] for k in range(tiles)]
        z_up = self.z_up(here, count)
        z_down = self.z_down([cz[k] * here[k] for k in range(tiles)], count)
        sums = []
        for k in range(count):
            cy = self.cy[k, at]
            total = self.cx[k, at] * field[k, at + 1] + self.cx[k, at - 1] * field[k, at - 1]
            total = total + (cy * self.y_up(here[k]) + self.y_down(cy * here[k]))
            total = total + (cz[k] * z_up[k] + z_down[k])
            sums.append(total + self.s[k, at])
        return here, sums

    def sweep_at(self, at, field, result, tiles, count, step, fresh):
        alpha, beta = step
        here, sums = self.around(field, at, tiles, count)
        for k in range(count):
            kept = (1.0 + alpha - beta) * here[k]
            if not fresh:
                kept = kept - alpha * result[k, at]
            result[k, at] = kept + (beta * self.iv[k, at]) * sums[k]

    def sweep(self, field, result, low, high, unroll, tiles, count, step, fresh=False):
        over_layers(low, high, unroll, lambda at: self.sweep_at(at, field, result, tiles, count, step, fresh))

    def residual_at(self, at, field, result, tiles):
        here, sums = self.around(field, at, tiles, 1)
        result[0, at] = sums[0] - self.dg[0, at] * here[0]

    def residual(self, field, result, low, high, unroll, tiles):
        over_layers(low, high, unroll, lambda at: self.residual_at(at, field, result, tiles))

    def last_at(self, at, field, older, step):
        alpha, beta = step
        here, sums = self.around(field, at, 1, 1)
        return (1.0 + alpha - beta) * here[0] - alpha * older[0, at], (beta * self.iv[0, at]) * sums[0]


class Strips:
    def __init__(self, refs, base, extent, left, right):
        self.c, self.s, self.cx, self.cy, self.cz, self.iv, self.dg, self.va, self.vb = refs
        self.base, self.extent, self.left, self.right = base, extent, left, right

    def lane(self):
        return lax.broadcasted_iota(jnp.int32, (32, LANES), 1)

    def mask(self, pack):
        where_x = self.base + 4 * pack + self.lane() // 32
        cell = self.lane() % 32
        keep = jnp.where(cell < 8, self.left, jnp.where(cell >= 24, self.right, 1.0))
        return jnp.where((where_x >= 0) & (where_x < self.extent), keep, 0.0)

    def x_up(self, tiles):
        turned = [pltpu.roll(t, LANES - 32, 1) for t in tiles]
        return [jnp.where(self.lane() < LANES - 32, turned[p], turned[min(p + 1, 3)]) for p in range(4)]

    def x_down(self, tiles):
        turned = [pltpu.roll(t, 32, 1) for t in tiles]
        return [jnp.where(self.lane() >= 32, turned[p], turned[max(p - 1, 0)]) for p in range(4)]

    def setup(self):
        row = lax.broadcasted_iota(jnp.int32, (32, LANES), 0)
        top, bottom = row == 31, row == 0
        masks = [self.mask(p) for p in range(4)]
        own = [self.c[p] * (0.5 * masks[p]) for p in range(4)]
        above = self.x_up(own)
        x_high = [own[p] + above[p] for p in range(4)]
        x_low = self.x_down(x_high)
        for p in range(4):
            y_high = own[p] + jnp.where(top, 0.0, pltpu.roll(own[p], 31, 0))
            y_low = jnp.where(bottom, own[p], pltpu.roll(y_high, 1, 0))
            z_high = own[p] + pltpu.roll(own[p], LANES - 1, 1)
            z_low = pltpu.roll(z_high, 1, 1)
            diagonal = x_low[p] + x_high[p] + y_low + y_high + z_low + z_high
            self.cx[p] = x_high[p]
            self.cy[p] = jnp.where(top, 0.0, y_high)
            self.cz[p] = z_high
            self.dg[p] = diagonal
            self.iv[p] = jnp.where(masks[p] > 0.5, 1.0 / diagonal, 0.0)

    def start(self, beta):
        for p in range(4):
            self.va[p] = self.s[p] * self.iv[p] * beta

    def around(self, field):
        here = [field[p] for p in range(4)]
        cx = [self.cx[p] for p in range(4)]
        x_up = self.x_up(here)
        x_down = self.x_down([cx[p] * here[p] for p in range(4)])
        sums = []
        for p in range(4):
            cy, cz = self.cy[p], self.cz[p]
            total = cx[p] * x_up[p] + x_down[p]
            total = total + (cy * pltpu.roll(here[p], 31, 0) + pltpu.roll(cy * here[p], 1, 0))
            total = total + (cz * pltpu.roll(here[p], LANES - 1, 1) + pltpu.roll(cz * here[p], 1, 1))
            sums.append(total + self.s[p])
        return here, sums

    def sweep(self, field, result, step, fresh=False):
        alpha, beta = step
        here, sums = self.around(field)
        for p in range(4):
            kept = (1.0 + alpha - beta) * here[p]
            if not fresh:
                kept = kept - alpha * result[p]
            result[p] = kept + (beta * self.iv[p]) * sums[p]

    def residual(self, field, result):
        here, sums = self.around(field)
        for p in range(4):
            result[p] = sums[p] - self.dg[p] * here[p]

    def own(self, ref, pack, layers=range(4)):
        cell = self.lane() % 32
        packed = jnp.zeros((32, LANES), F32)
        for layer in layers:
            tile = ref[0, 4 * pack + layer]
            first = pltpu.roll(tile, 32 * layer + 8, 1)
            last = pltpu.roll(tile, (32 * layer + 24) % LANES, 1)
            packed = jnp.where(self.lane() // 32 == layer, jnp.where(cell < 16, first, last), packed)
        return packed

    def take_halo(self, ref, pack, from_left, from_right):
        cell = lax.broadcasted_iota(jnp.int32, (8, LANES), 1) % 32
        for part in range(4):
            rows = pl.ds(8 * part, 8)
            below = pltpu.roll(from_left, (LANES - 8 * part) % LANES, 1)
            above = pltpu.roll(from_right, 24 - 8 * part, 1) if part < 3 else from_right
            ref[pack, rows, :] = jnp.where(cell < 8, below, jnp.where(cell >= 24, above, ref[pack, rows, :]))

    def give_halo(self, ref, pack, side):
        cell = lax.broadcasted_iota(jnp.int32, (8, LANES), 1) % 32
        packed = None
        for part in range(4):
            shift = (8 * part - 8 - 8 * side) % LANES
            tile = ref[pack, pl.ds(8 * part, 8), :]
            tile = pltpu.roll(tile, shift, 1) if shift else tile
            packed = tile if part == 0 else jnp.where(cell // 8 == part, tile, packed)
        return packed

    def mend(self, tile, ref, at):
        packed, layer = ref[at // 4], at % 4
        first = pltpu.roll(packed, (LANES - 32 * layer - 8) % LANES, 1)
        last = pltpu.roll(packed, (LANES + 104 - 32 * layer) % LANES, 1)
        return jnp.where(self.lane() < 4, first, jnp.where(self.lane() >= LANES - 4, last, tile))


LEVEL_FIELDS = 9
LEVEL_SHAPES = ((1, 16, 32, LANES), (2, 14, 16, LANES), (1, 34, 8, LANES), (1, 15, 8, LANES))
RULER = 1024
SENDERS = 10 + 2 * (2 * REACH + 1)
GROUPS = 34 + 2 * (2 * REACH + 1)


def kernel(wide, narrow, rhs, coef, kept, added, *scratch):
    scratch = list(scratch)
    level_refs = []
    for _ in range(4):
        level_refs.append(scratch[:LEVEL_FIELDS])
        scratch = scratch[LEVEL_FIELDS:]
    strip_refs, scratch = scratch[:LEVEL_FIELDS], scratch[LEVEL_FIELDS:]
    (ps, zs, rz, rcn, kp, k1cx, k1c, sk, sp, k1x, k1p, k1z, rc2, s2m, rs2, rx1, sb0, hx0, p1, p0, ruler,
     local_sem, send_sem, recv_sem) = scratch
    me_w = lax.axis_index("wide")
    me_n = lax.axis_index("narrow")

    def there(dw, dn):
        return (lax.rem(me_w + (dw + wide), wide), lax.rem(me_n + (dn + narrow), narrow))

    has = (me_w > 0, me_w < wide - 1)
    has_z = (me_n > 0, me_n < narrow - 1)
    reach = (jnp.minimum(me_w, REACH), jnp.minimum(wide - 1 - me_w, REACH))

    def for_far(first, body, last=REACH):
        for side in range(2):
            sign = 2 * side - 1

            def step(k, carry):
                body(REACH + sign * k, sign * k)
                return carry

            lax.fori_loop(first, jnp.minimum(reach[side], last) + 1, step, 0)

    def for_all_far(body):
        inner = reach[0] + reach[1] == 2 * REACH

        @pl.when(inner)
        def straight():
            for k in range(REACH, 0, -1):
                for sign in (-1, 1):
                    body(REACH + sign * k, sign * k)

        pl.when(jnp.logical_not(inner))(functools.partial(for_far, 1, body))

    def for_sides(body):
        for side in range(2):
            pl.when(has[side])(functools.partial(body, side, 2 * side - 1))

    def for_sides_z(body):
        for side in range(2):
            pl.when(has_z[side])(functools.partial(body, side, 2 * side - 1))

    def for_corners(body):
        for side in range(2):
            for side_z in range(2):
                pl.when(has[side] & has_z[side_z])(
                    functools.partial(body, side, side_z, 2 * side - 1, 2 * side_z - 1)
                )

    @pl.when((me_n == 0) | (me_n == narrow - 1))
    def clear_z():
        for ref in (rz, rcn, k1c, k1z, k1p):
            ref[...] = jnp.zeros(ref.shape, F32)

    @pl.when((me_w < REACH) | (me_w >= wide - REACH))
    def clear():
        def zero(ref):
            ref[...] = jnp.zeros(ref.shape, F32)

        for ref in (rcn, rx1, hx0, rc2, rs2, k1cx, k1c, k1x, k1p):
            zero(ref)
        for side in range(2):
            for ref in level_refs[0][:2]:
                zero(ref.at[0, pl.ds(12 * side, 4)])
            zero(level_refs[1][0].at[0, 13 * side])

    def if_reach(least, body):
        for side in range(2):
            pl.when(reach[side] >= least)(functools.partial(body, side, 2 * side - 1))

    barrier = pltpu.get_barrier_semaphore()

    def greet(dw, dn):
        pl.semaphore_signal(barrier, inc=1, device_id=there(dw, dn), device_id_type=MESH_ID)

    for_far(1, lambda slot, dw: greet(dw, 0), HALF_REACH)
    for_sides_z(lambda side, dn: greet(0, dn))
    for_corners(lambda side, side_z, dw, dn: greet(dw, dn))

    c0, s0 = level_refs[0][0], level_refs[0][1]
    load_c = pltpu.make_async_copy(coef, c0.at[0, pl.ds(4, 8)], local_sem.at[0])
    load_s = pltpu.make_async_copy(rhs, s0.at[0, pl.ds(4, 8)], local_sem.at[1])
    load_c.start()
    load_s.start()
    beside_x = jnp.where(has[0], 1, 0) + jnp.where(has[1], 1, 0)
    beside_z = jnp.where(has_z[0], 1, 0) + jnp.where(has_z[1], 1, 0)
    greeted = beside_z + beside_x * beside_z
    for side in range(2):
        greeted = greeted + jnp.minimum(reach[side], HALF_REACH)

    left = jnp.where(me_n > 0, 1.0, 0.0).astype(F32)
    right = jnp.where(me_n < narrow - 1, 1.0, 0.0).astype(F32)

    def lanes(rows):
        return lax.broadcasted_iota(jnp.int32, (rows, LANES), 1)

    def edges(rows, until, low, since, high):
        at = lanes(rows)
        return jnp.where(at < until, low, jnp.where(at >= since, high, 0.0))

    def centred(rows):
        at = lanes(rows)
        return jnp.where((at >= 32) & (at < 96), 1.0, edges(rows, 32, left, 96, right))

    level_0 = Level(level_refs[0], 1.0, 32, 1, 1, 8 * me_w - 4, 8 * wide, [None])
    strips = Strips(strip_refs, 8 * me_w - 4, 8 * wide, left, right)
    level_1 = Level(
        level_refs[1], 0.25, 16, 1, 1, 4 * me_w - 5, 4 * wide, [centred(16), edges(16, 32, right, 96, left)]
    )
    level_2 = Level(level_refs[2], 0.0625, 8, 1, 2, 2 * me_w - 16, 2 * wide, [centred(8)])
    level_3 = Level(level_refs[3], 0.015625, 8, 2, 4, me_w - 7, wide, [centred(8)])

    sent = [0] * SENDERS

    def send(group, src, dst, dw, dn, rows, sender):
        if isinstance(sender, int):
            sent[sender] += rows
        pltpu.make_async_remote_copy(
            src_ref=src, dst_ref=dst, send_sem=send_sem.at[sender], recv_sem=recv_sem.at[group],
            device_id=there(dw, dn), device_id_type=MESH_ID,
        ).start()

    def ruled(rows, group, sender):
        span = ruler.at[pl.ds(0, rows)]
        return pltpu.make_async_remote_copy(
            src_ref=span, dst_ref=span, send_sem=send_sem.at[sender], recv_sem=recv_sem.at[group],
            device_id=there(0, 1), device_id_type=MESH_ID,
        )

    def receive(group, rows):
        ruled(rows, group, 0).wait_recv()

    def receive_sides(group, rows):
        for_sides(lambda side, dw: receive(group + side, rows))

    def receive_sides_z(group, rows):
        for_sides_z(lambda side, dn: receive(group + side, rows))

    def receive_corners(group, rows):
        for_corners(lambda side, side_z, dw, dn: receive(group + 2 * side + side_z, rows))

    def receive_far(group, last=REACH):
        for_far(1, lambda slot, dw: receive(group + slot, 8), last)

    def sends_done(sender):
        ruled(sent[sender], 0, sender).wait_send()

    from_z, from_s1z = 0, 2
    from_c_corner, from_k_corner, from_s1_corner = 4, 8, 12
    from_c, from_s, from_s_next, from_k, from_s1, from_c1b, from_x0, from_x1 = range(16, 32, 2)
    from_four = 32
    from_c2 = 34
    from_s2 = from_c2 + 2 * REACH + 1
    sender_x, sender_four, sender_z = range(0, 6, 2)
    sender_corner, sender_c2, sender_far = 6, 10, 10 + 2 * REACH + 1

    def restrict_0(ref):
        out = []
        for layer in range(4):
            total = None
            for dx in range(2):
                for dy in range(2):
                    term = ref[0, 4 + 2 * layer + dx, pl.ds(dy, 16, stride=2), :]
                    total = term if total is None else total + term
            total = total + pltpu.roll(total, LANES - 1, 1)
            out.append(0.125 * jnp.take_along_axis(total, (2 * lanes(16) + 64) % LANES, axis=1))
        return out

    odd_8 = lanes(8) % 2 == 1

    def pairs_1(ref):
        out = []
        for layer in range(2):
            total = None
            for dx in range(2):
                for dy in range(2):
                    term = ref[0, 5 + 2 * layer + dx, pl.ds(dy, 8, stride=2), :]
                    total = term if total is None else total + term
            total = total + jnp.where(odd_8, pltpu.roll(total, 1, 1), pltpu.roll(total, LANES - 1, 1))
            out.append(0.125 * total)
        return jnp.where(odd_8, out[1], out[0])

    def squeeze_1(layers, ref, row):
        for part in range(2):
            ref[pl.ds(row + 16 * part, 16), :] = jnp.where(lanes(16) < 64, layers[part], layers[part + 2])

    load_c.wait()
    load_s.wait()
    pl.semaphore_wait(barrier, greeted)

    @for_sides
    def send_faces(side, dw):
        src, dst = c0.at[0, pl.ds(4 + 4 * side, 4)], c0.at[0, pl.ds(12 - 12 * side, 4)]
        send(from_c + 1 - side, src, dst, dw, 0, 128, sender_x + side)

    @for_sides
    def send_nearest(side, dw):
        send(from_s + 1 - side, s0.at[0, 4 + 7 * side], s0.at[0, 12 - 9 * side], dw, 0, 32, sender_x + side)

    def squeeze_halves(first, second):
        low_quarter = lanes(16) % 64 < 32
        return (
            jnp.where(low_quarter, pltpu.roll(first, 96, 1), second),
            jnp.where(low_quarter, first, pltpu.roll(second, 32, 1)),
        )

    own_c1 = restrict_0(c0)
    for half in range(2):
        strips.c[1 + half] = strips.own(c0, 1 + half)
    for side in range(2):
        squeeze_1(own_c1, zs.at[side], 32)
        for half in range(2):
            zs[side, pl.ds(16 * half, 8), :] = strips.give_halo(strips.c, 1 + half, side)
    for half in range(2):
        strips.s[1 + half] = strips.own(s0, 1 + half)
    for side in range(2):
        for half in range(2):
            zs[side, pl.ds(16 * half + 8, 8), :] = strips.give_halo(strips.s, 1 + half, side)

    for_sides_z(
        lambda side, dn: send(from_z + 1 - side, zs.at[side], rz.at[1 - side], 0, dn, 64, sender_z + side)
    )

    def send_corner(group, src, dst, rows, side, side_z):
        at = 2 * side + side_z
        send(group + 3 - at, src, dst, 2 * side - 1, 2 * side_z - 1, rows, sender_corner + at)

    @for_corners
    def send_c_corner(side, side_z, dw, dn):
        src = zs.at[side_z, pl.ds(16 * side, 16)]
        send_corner(from_c_corner, src, rcn.at[1 - side, 1 - side_z], 16, side, side_z)

    @for_sides
    def send_s_next(side, dw):
        src = s0.at[0, pl.ds(5 + 4 * side, 2)]
        send(from_s_next + 1 - side, src, s0.at[0, pl.ds(13 - 12 * side, 2)], dw, 0, 64, sender_x + side)

    steps = cheb(3)
    sweep_a = (level_0.va, level_0.vb, 1, 1, steps[1], True)
    sweep_b = (level_0.vb, level_0.va, 1, 1, steps[2], False)
    level_0.setup(5, 10, 6, 1)
    level_0.start(5, 10, 6, 1, steps[0][1])
    over_layers(6, 9, 4, lambda at: level_0.sweep_at(at, *sweep_a))
    over_layers(7, 8, 2, lambda at: level_0.sweep_at(at, *sweep_b))

    def take_halos(field, ref, pack, got):
        rows = pl.ds(8 * field + (16 if pack == 2 else 0), 8)
        strips.take_halo(ref, pack, got[0, rows, :], got[1, rows, :])

    receive_sides_z(from_z, 64)
    for field, ref in enumerate((strips.c, strips.s)):
        for half in range(2):
            take_halos(field, ref, 1 + half, rz)

    def spread_1(ref, block):
        at_lane = lanes(16)
        low_half = at_lane < 64
        low_quarter = at_lane % 64 < 32
        for part in range(2):
            before, own, after = (block(dz, part) for dz in (-1, 0, 1))
            near = jnp.where(low_quarter, before, after)
            outer = jnp.where(low_quarter, after, before)
            own_r, near_r, outer_r = (pltpu.roll(t, 64, 1) for t in (own, near, outer))
            at = 5 + part
            for at, own_a, own_b, near_a, near_b, outer_a, outer_b in (
                (at, own, own_r, near, near_r, outer, outer_r),
                (at + 2, own_r, own, near_r, near, outer_r, outer),
            ):
                centre = jnp.where(low_half, own_a, own_b)
                ref[0, at] = jnp.where(at_lane < 32, near_a, jnp.where(at_lane < 96, centre, near_b))
                ref[1, at] = jnp.where(low_half, outer_a, outer_b)

    def coef_block(dz, part):
        rows = pl.ds(32 + 16 * part, 16)
        return zs[0, rows, :] if dz == 0 else rz[(1 + dz) // 2, rows, :]

    spread_1(level_1.c, coef_block)
    rc2[REACH] = pairs_1(level_1.c)

    for_far(
        1,
        lambda slot, dw: send(
            from_c2 + 2 * REACH - slot, rc2.at[REACH], rc2.at[2 * REACH - slot], dw, 0, 8, sender_c2 + slot
        ),
        HALF_REACH,
    )
    k1_own = zs.at[0, pl.ds(32, 32)]
    halves = squeeze_halves(zs[0, pl.ds(32, 16), :], zs[0, pl.ds(48, 16), :])
    at_lane = lanes(16)
    for side in range(2):
        near, far = (0, 3) if side == 0 else (3, 0)
        full = level_1.c[0, 5 + near]
        place = (32 * far + 31, 32 * far)
        cell = (64, 63)
        for side_z in range(2):
            moved = pltpu.roll(full, (place[side_z] - cell[side_z]) % LANES, 1)
            kp[side, side_z] = jnp.where(at_lane == place[side_z], moved, halves[side_z])
    for_sides(
        lambda side, dw: send(from_k + 1 - side, k1_own, k1cx.at[1 - side], dw, 0, 32, sender_x + side)
    )
    for_corners(
        lambda side, side_z, dw, dn: send_corner(
            from_k_corner, kp.at[side, side_z], k1c.at[1 - side, 1 - side_z], 16, side, side_z
        )
    )

    receive_sides(from_c, 128)
    receive_corners(from_c_corner, 16)
    for side in range(2):
        strips.c[3 * side] = strips.own(c0, 3 * side)
        take_halos(0, strips.c, 3 * side, rcn.at[side])
    level_0.setup_below(1, 1)
    over_sides(1, 11, 4, lambda at: level_0.setup_at(at, 1))
    strips.setup()
    receive_sides(from_s, 32)
    over_sides(3, 11, 2, lambda at: level_0.start_at(at, 1, steps[0][1]))
    over_sides(4, 10, 2, lambda at: level_0.sweep_at(at, *sweep_a))
    over_sides(5, 9, 2, lambda at: level_0.sweep_at(at, *sweep_b))
    over_layers(6, 9, 4, lambda at: level_0.residual_at(at, level_0.va, level_0.vb, 1))
    receive_sides(from_s_next, 64)
    for side in range(2):
        strips.s[3 * side] = strips.own(s0, 3 * side, range(1 - side, 4 - side))
        take_halos(1, strips.s, 3 * side, rcn.at[side])
    over_sides(1, 13, 2, lambda at: level_0.start_at(at, 1, steps[0][1]))
    strips.start(steps[0][1])
    over_sides(2, 12, 2, lambda at: level_0.sweep_at(at, *sweep_a))
    strips.sweep(strips.va, strips.vb, steps[1], fresh=True)
    over_sides(3, 11, 2, lambda at: level_0.sweep_at(at, *sweep_b))
    strips.sweep(strips.vb, strips.va, steps[2])
    over_sides(4, 10, 2, lambda at: level_0.residual_at(at, level_0.va, level_0.vb, 1))
    strips.residual(strips.va, strips.vb)
    for at in range(4, 12):
        level_0.vb[0, at] = strips.mend(level_0.vb[0, at], strips.vb, at)

    squeeze_1(restrict_0(level_0.vb), sk, 0)

    sp[0], sp[1] = squeeze_halves(sk[pl.ds(0, 16), :], sk[pl.ds(16, 16), :])

    for_sides(lambda side, dw: send(from_s1 + 1 - side, sk, k1x.at[1 - side], dw, 0, 32, sender_x + side))
    for_corners(
        lambda side, side_z, dw, dn: send_corner(
            from_s1_corner, sp.at[side_z], k1p.at[1 - side, 1 - side_z], 16, side, side_z
        )
    )
    for_sides_z(lambda side, dn: send(from_s1z + 1 - side, sk, k1z.at[1 - side], 0, dn, 32, sender_z + side))

    receive_far(from_c2, HALF_REACH)

    @functools.partial(if_reach, HALF_REACH)
    def send_four(side, sign):
        src, dst = rc2.at[pl.ds(9 - 5 * side, 4)], rc2.at[pl.ds(13 - 13 * side, 4)]
        send(from_four + 1 - side, src, dst, HALF_REACH * sign, 0, 32, sender_four + side)

    for at in range(3, 13):
        level_0.va[0, at] = strips.mend(level_0.va[0, at], strips.va, at)
    own_cell = (strips.lane() % 32 >= 8) & (strips.lane() % 32 < 24)
    for pack_at, layers in enumerate(((3,), range(4), range(4), (0,))):
        strips.va[pack_at] = jnp.where(own_cell, strips.own(level_0.va, pack_at, layers), strips.va[pack_at])
    for side in range(2):
        first = 9 if side == 0 else 5
        for layer in range(2):
            sb0[side, pl.ds(32 * layer, 32), :] = level_0.va[0, first + layer]
        packed = strips.va[2 - side]
        middle = (lanes(16) >= 32) & (lanes(16) < 96)
        sb0[side, pl.ds(64, 16), :] = jnp.where(middle, packed[:16], pltpu.roll(packed[16:], 64, 1))

    @for_sides
    def send_iterate_0(side, dw):
        send(from_x0 + 1 - side, sb0.at[1 - side], hx0.at[1 - side], dw, 0, 80, sender_x + side)

    def source_block(dz, part):
        rows = pl.ds(16 * part, 16)
        return sk[rows, :] if dz == 0 else k1z[(1 + dz) // 2, rows, :]

    def spread_beside(ref, blocks, packs):
        at_lane = lanes(16)
        low_half = at_lane < 64
        for side in range(2):
            for layer in range(4):
                own = blocks[side, pl.ds(16 * (layer % 2), 16), :]
                other = pltpu.roll(own, 64, 1)
                centre = jnp.where(low_half, own, other) if layer < 2 else jnp.where(low_half, other, own)
                before = pltpu.roll(packs[side, 0], (LANES - 32 * layer) % LANES, 1)
                after = pltpu.roll(packs[side, 1], (LANES + 96 - 32 * layer) % LANES, 1)
                ref[0, 1 + 8 * side + layer] = jnp.where(at_lane < 32, before, jnp.where(at_lane < 96, centre, after))

    receive_sides(from_k, 32)
    receive_corners(from_k_corner, 16)
    spread_beside(level_1.c, k1cx, k1c)
    for side in range(2):
        far = 3 if side == 1 else 0
        below, above = (pltpu.roll(k1c[side, side_z], (shift - 32 * far) % LANES, 1)
                        for side_z, shift in ((0, 127), (1, -31)))
        level_1.c[1, 4 + 5 * side] = jnp.where(lanes(16) < 64, above, below)

    @for_sides
    def send_coef_1(side, dw):
        send(from_c1b + 1 - side, level_1.c.at[0, 9 - 5 * side], level_1.c.at[0, 13 - 13 * side], dw, 0, 16, sender_x + side)

    level_1.setup_below(2, 1)
    over_sides(2, 10, 2, lambda at: level_1.setup_at(at, 1))
    over_layers(4, 9, 6, lambda at: level_1.setup_at(at, 2))

    receive_sides_z(from_s1z, 32)
    spread_1(level_1.s, source_block)
    receive_sides(from_s1, 32)
    receive_corners(from_s1_corner, 16)
    spread_beside(level_1.s, k1x, k1p)
    level_1.start(2, 11, 10, 1, steps[0][1])
    over_layers(5, 8, 4, lambda at: level_1.start_outer(at, steps[0][1]))
    over_sides(3, 9, 2, lambda at: level_1.sweep_at(at, level_1.va, level_1.vb, 1, 1, steps[1], True))
    over_layers(5, 8, 4, lambda at: level_1.sweep_at(at, level_1.va, level_1.vb, 2, 1, steps[1], True))
    level_1.sweep(level_1.vb, level_1.va, 4, 9, 6, 1, 1, steps[2])
    level_1.residual(level_1.va, level_1.vb, 5, 8, 4, 1)

    value = pairs_1(level_1.vb)
    s2m[...] = value
    rs2[REACH] = value

    for_all_far(
        lambda slot, dw: send(
            from_s2 + 2 * REACH - slot, s2m, rs2.at[2 * REACH - slot], dw, 0, 8, sender_far + slot
        )
    )

    @for_sides
    def send_iterate_1(side, dw):
        layers = level_1.va.at[0, pl.ds(6 - 2 * side, 4)]
        send(from_x1 + 1 - side, layers, rx1.at[1 - side], dw, 0, 64, sender_x + side)

    receive_sides(from_c1b, 16)
    level_1.setup_below(1, 1)
    over_sides(1, 12, 1, lambda at: level_1.setup_at(at, 1))

    def spread_2(ref, blocks):
        for block in range(2 * REACH + 1):
            packed = blocks[block]
            ref[0, 2 * block] = jnp.where(odd_8, pltpu.roll(packed, 1, 1), packed)
            ref[0, 2 * block + 1] = jnp.where(odd_8, packed, pltpu.roll(packed, LANES - 1, 1))

    def restrict_2(ref, at):
        total = ref[0, 2 * at + 2] + ref[0, 2 * at + 3]
        odd_row = lax.broadcasted_iota(jnp.int32, (8, LANES), 0) % 2 == 1
        total = total + jnp.where(odd_row, pltpu.roll(total, 1, 0), pltpu.roll(total, 7, 0))
        second = lanes(8) % 4 >= 2
        total = total + jnp.where(second, pltpu.roll(total, 2, 1), pltpu.roll(total, LANES - 2, 1))
        return 0.125 * total

    if_reach(HALF_REACH, lambda side, sign: receive(from_four + side, 32))
    spread_2(level_2.c, rc2)
    level_2.setup(1, 32, 16, 1)
    for at in range(15):
        level_3.c[0, at] = restrict_2(level_2.c, at)
    level_3.setup(1, 13, 13, 1)

    for_sides(lambda side, dw: sends_done(sender_x + side))
    for_sides_z(lambda side, dn: sends_done(sender_z + side))
    for_corners(lambda side, side_z, dw, dn: sends_done(sender_corner + 2 * side + side_z))
    if_reach(HALF_REACH, lambda side, sign: sends_done(sender_four + side))
    for_far(1, lambda slot, dw: ruled(8, 0, sender_c2 + slot).wait_send(), HALF_REACH)
    for_all_far(lambda slot, dw: ruled(8, 0, sender_far + slot).wait_send())

    for_all_far(lambda slot, dw: receive(from_s2 + slot, 8))
    spread_2(level_2.s, rs2)
    level_2.start(1, 32, 32, 1, steps[0][1])
    level_2.sweep(level_2.va, level_2.vb, 2, 31, 30, 1, 1, steps[1], fresh=True)
    level_2.sweep(level_2.vb, level_2.va, 3, 30, 28, 1, 1, steps[2])
    level_2.residual(level_2.va, level_2.vb, 4, 29, 26, 1)

    for at in range(1, 14):
        level_3.s[0, at] = restrict_2(level_2.vb, at)
    coarse = cheb(4)
    level_3.start(1, 13, 13, 1, coarse[0][1])
    level_3.sweep(level_3.va, level_3.vb, 2, 12, 11, 1, 1, coarse[1], fresh=True)
    level_3.sweep(level_3.vb, level_3.va, 3, 11, 9, 1, 1, coarse[2])
    level_3.sweep(level_3.va, level_3.vb, 4, 10, 7, 1, 1, coarse[3])

    for at in range(10, 24):
        level_2.vb[0, at] = level_2.va[0, at] + level_3.vb[0, (at - 2) // 2]
    level_2.sweep(level_2.vb, level_2.va, 11, 22, 12, 1, 1, steps[0], fresh=True)
    level_2.sweep(level_2.va, level_2.vb, 12, 21, 10, 1, 1, steps[1])
    level_2.sweep(level_2.vb, level_2.va, 13, 20, 8, 1, 1, steps[2])

    for at in range(8):
        value = level_2.va[0, 13 + at]
        for part in range(2):
            p1[at, pl.ds(part, 8, stride=2), :] = value
    receive_sides(from_x1, 64)
    for at in range(14):
        if 4 <= at <= 9:
            before = level_1.va[0, at]
        else:
            before = rx1[0, at] if at < 4 else rx1[1, at - 10]
        level_1.vb[0, at] = before + p1[(at + 1) // 2]
    level_1.sweep(level_1.vb, level_1.va, 1, 12, 12, 1, 1, steps[0], fresh=True)
    level_1.sweep(level_1.va, level_1.vb, 2, 11, 10, 1, 1, steps[1])
    level_1.sweep(level_1.vb, level_1.va, 3, 10, 8, 1, 1, steps[2])

    cell = lanes(16) % 32
    strip_lane = jnp.where(cell < 16, 28, 84) + cell // 2
    low_half = lanes(16) < 64
    fine = []
    for at in range(8):
        value = level_1.va[0, 3 + at]
        own = jnp.take_along_axis(value, lanes(16) // 2 + 32, axis=1)
        fine.append(jnp.take_along_axis(value, strip_lane, axis=1))
        for part in range(2):
            p0[at, pl.ds(part, 16, stride=2), :] = own
    for pack in range(4):
        value = jnp.where(low_half, fine[2 * pack], fine[2 * pack + 1])
        for part in range(2):
            ps[pack, pl.ds(part, 16, stride=2), :] = value
    receive_sides(from_x0, 80)
    for side in range(2):
        for layer in range(2):
            at = (1 if side == 0 else 13) + layer
            level_0.vb[0, at] = hx0[side, pl.ds(32 * layer, 32), :] + p0[at // 2]
        packed = hx0[side, pl.ds(64, 16), :]
        layer = lanes(16) // 32
        for part, value in enumerate((packed, pltpu.roll(packed, 64, 1))):
            rows = pl.ds(16 * part, 16)
            own = jnp.where(layer == (3 if side == 0 else 0), strips.va[3 * side, rows, :], 0.0)
            value = jnp.where((layer == 1) | (layer == 2), value, own)
            strips.vb[3 * side, rows, :] = value + ps[3 * side, rows, :]
    for pack in (1, 2):
        strips.vb[pack] = strips.va[pack] + ps[pack]

    def correct(at):
        level_0.vb[0, at] = level_0.va[0, at] + p0[at // 2]

    over_layers(3, 12, 10, correct)
    level_0.sweep(level_0.vb, level_0.va, 2, 13, 12, 1, 1, steps[0], fresh=True)
    strips.sweep(strips.vb, strips.va, steps[0], fresh=True)
    level_0.sweep(level_0.va, level_0.vb, 3, 12, 10, 1, 1, steps[1])
    strips.sweep(strips.va, strips.vb, steps[1])
    strips.sweep(strips.vb, strips.va, steps[2])
    inner = (strips.lane() >= 4) & (strips.lane() < LANES - 4)
    for at in range(4, 12):
        kept_here, added_here = level_0.last_at(at, level_0.vb, level_0.va, steps[2])
        kept[at - 4] = strips.mend(kept_here, strips.va, at)
        added[at - 4] = jnp.where(inner, added_here, 0.0)


def per_device(right_side, conductivity, wide, narrow):
    brick = (8, 32, LANES)
    scratch = []
    for shape in LEVEL_SHAPES:
        scratch += [pltpu.VMEM(shape, F32)] * LEVEL_FIELDS
    scratch += [pltpu.VMEM((4, 32, LANES), F32)] * LEVEL_FIELDS
    shapes = [
        (4, 32, LANES),
        (2, 64, LANES), (2, 64, LANES), (2, 2, 16, LANES),
        (2, 2, 16, LANES), (2, 32, LANES), (2, 2, 16, LANES),
        (32, LANES), (2, 16, LANES), (2, 32, LANES), (2, 2, 16, LANES), (2, 32, LANES),
        (2 * REACH + 1, 8, LANES), (8, LANES), (2 * REACH + 1, 8, LANES),
        (2, 4, 16, LANES),
        (2, 80, LANES), (2, 80, LANES),
        (8, 16, LANES), (8, 32, LANES),
        (RULER, LANES),
    ]
    scratch += [pltpu.VMEM(shape, F32) for shape in shapes]
    scratch += [pltpu.SemaphoreType.DMA((2,)), pltpu.SemaphoreType.DMA((SENDERS,)), pltpu.SemaphoreType.DMA((GROUPS,))]
    kept, added = pl.pallas_call(
        functools.partial(kernel, wide, narrow),
        out_shape=[jax.ShapeDtypeStruct(brick, F32)] * 2,
        in_specs=[pl.BlockSpec(memory_space=pltpu.HBM)] * 2,
        out_specs=[pl.BlockSpec(memory_space=pltpu.VMEM)] * 2,
        scratch_shapes=scratch,
        compiler_params=pltpu.CompilerParams(
            collective_id=0, has_side_effects=True, vmem_limit_bytes=32 * 1024 * 1024
        ),
    )(pltpu.with_memory_space_constraint(right_side, pltpu.HBM), pltpu.with_memory_space_constraint(conductivity, pltpu.HBM))
    return kept + added


def solution(mesh):
    spec = P("wide", None, "narrow")
    body = functools.partial(per_device, wide=mesh.shape["wide"], narrow=mesh.shape["narrow"])
    return jax.shard_map(body, mesh=mesh, in_specs=(spec, spec), out_specs=spec, check_vma=False)
```

```python
import functools

import jax
import jax.numpy as jnp
from jax import lax
from jax.experimental import pallas as pl
from jax.experimental.pallas import tpu as pltpu
from jax.sharding import PartitionSpec as P

CENTER = 1.125
HALF = 0.875
LANES = 128
REACH = 8
HALF_REACH = 4
F32 = jnp.float32
MESH_ID = pl.DeviceIdType.MESH


def cheb(sweeps):
    sigma = CENTER / HALF
    steps = [(0.0, 1.0 / CENTER)]
    ratio = 1.0 / sigma
    for _ in range(sweeps - 1):
        ratio_next = 1.0 / (2.0 * sigma - ratio)
        steps.append((ratio_next * ratio, 2.0 * ratio_next / HALF))
        ratio = ratio_next
    return steps


def over_sides(first, second, count, body):
    for base in (first, second):
        for at in range(count):
            body(base + at)


def over_layers(low, high, unroll, body):
    count = high - low + 1
    if count == unroll:
        for at in range(low, high + 1):
            body(at)
        return

    def block(step, carry):
        for at in range(unroll):
            body(low + step * unroll + at)
        return carry

    lax.fori_loop(0, count // unroll, block, 0)


class Level:
    def __init__(self, refs, scale, rows, row_step, lane_step, base, extent, lane_mask):
        self.c, self.s, self.cx, self.cy, self.cz, self.iv, self.dg, self.va, self.vb = refs
        self.half = 0.5 * scale
        self.rows, self.row_step, self.lane_step = rows, row_step, lane_step
        self.base, self.extent, self.lane_mask = base, extent, lane_mask

    def inside(self, at):
        where_x = self.base + at
        return jnp.where((where_x >= 0) & (where_x < self.extent), 1.0, 0.0).astype(F32)

    def lane(self):
        return lax.broadcasted_iota(jnp.int32, (self.rows, LANES), 1)

    def row(self):
        return lax.broadcasted_iota(jnp.int32, (self.rows, LANES), 0)

    def y_up(self, tile):
        return pltpu.roll(tile, self.rows - self.row_step, 0)

    def y_down(self, tile):
        return pltpu.roll(tile, self.row_step, 0)

    def turned(self, tiles, shift, edge, count):
        out = [pltpu.roll(t, shift, 1) for t in tiles]
        if len(tiles) == 1:
            return out
        at_edge = self.lane() == edge
        return [jnp.where(at_edge, out[1 - k], out[k]) for k in range(count)]

    def z_up(self, tiles, count):
        return self.turned(tiles, LANES - self.lane_step, LANES - 1, count)

    def z_down(self, tiles, count):
        return self.turned(tiles, self.lane_step, 0, count)

    def masked(self, at, tiles):
        keep = self.inside(at) * self.half
        out = []
        for k in range(tiles):
            mask = self.lane_mask[k]
            out.append(self.c[k, at] * (keep if mask is None else mask * keep))
        return out

    def setup_below(self, low, tiles):
        first, second = self.masked(low - 1, tiles), self.masked(low, tiles)
        for k in range(tiles):
            self.cx[k, low - 1] = first[k] + second[k]

    def setup_at(self, at, tiles):
        before, here, after = self.masked(at - 1, tiles), self.masked(at, tiles), self.masked(at + 1, tiles)
        inside = self.inside(at)
        top = self.row() >= self.rows - self.row_step
        bottom = self.row() < self.row_step
        z_up, z_down = self.z_up(here, tiles), self.z_down(here, tiles)
        for k in range(tiles):
            own = here[k]
            x_low = before[k] + own
            x_high = own + after[k]
            y_low = own + jnp.where(bottom, 0.0, self.y_down(own))
            y_high = own + jnp.where(top, 0.0, self.y_up(own))
            z_low = own + z_down[k]
            z_high = own + z_up[k]
            diagonal = x_low + x_high + y_low + y_high + z_low + z_high
            keep = inside if self.lane_mask[k] is None else self.lane_mask[k] * inside
            self.cx[k, at] = x_high
            self.cy[k, at] = jnp.where(top, 0.0, y_high)
            self.cz[k, at] = z_high
            if k == 0:
                self.dg[0, at] = diagonal
            self.iv[k, at] = jnp.where(jnp.full_like(own, 0.0) + keep > 0.5, 1.0 / diagonal, 0.0)

    def setup(self, low, high, unroll, tiles):
        self.setup_below(low, tiles)
        over_layers(low, high, unroll, lambda at: self.setup_at(at, tiles))

    def start_at(self, at, tiles, beta):
        for k in range(tiles):
            self.va[k, at] = self.s[k, at] * self.iv[k, at] * beta

    def start_outer(self, at, beta):
        self.va[1, at] = self.s[1, at] * self.iv[1, at] * beta

    def start(self, low, high, unroll, tiles, beta):
        over_layers(low, high, unroll, lambda at: self.start_at(at, tiles, beta))

    def around(self, field, at, tiles, count):
        here = [field[k, at] for k in range(tiles)]
        cz = [self.cz[k, at] for k in range(tiles)]
        z_up = self.z_up(here, count)
        z_down = self.z_down([cz[k] * here[k] for k in range(tiles)], count)
        sums = []
        for k in range(count):
            cy = self.cy[k, at]
            total = self.cx[k, at] * field[k, at + 1] + self.cx[k, at - 1] * field[k, at - 1]
            total = total + (cy * self.y_up(here[k]) + self.y_down(cy * here[k]))
            total = total + (cz[k] * z_up[k] + z_down[k])
            sums.append(total + self.s[k, at])
        return here, sums

    def sweep_at(self, at, field, result, tiles, count, step, fresh):
        alpha, beta = step
        here, sums = self.around(field, at, tiles, count)
        for k in range(count):
            kept = (1.0 + alpha - beta) * here[k]
            if not fresh:
                kept = kept - alpha * result[k, at]
            result[k, at] = kept + (beta * self.iv[k, at]) * sums[k]

    def sweep(self, field, result, low, high, unroll, tiles, count, step, fresh=False):
        over_layers(low, high, unroll, lambda at: self.sweep_at(at, field, result, tiles, count, step, fresh))

    def residual_at(self, at, field, result, tiles):
        here, sums = self.around(field, at, tiles, 1)
        result[0, at] = sums[0] - self.dg[0, at] * here[0]

    def residual(self, field, result, low, high, unroll, tiles):
        over_layers(low, high, unroll, lambda at: self.residual_at(at, field, result, tiles))

    def last_at(self, at, field, older, step):
        alpha, beta = step
        here, sums = self.around(field, at, 1, 1)
        return (1.0 + alpha - beta) * here[0] - alpha * older[0, at], (beta * self.iv[0, at]) * sums[0]


class Strips:
    def __init__(self, refs, base, extent, left, right):
        self.c, self.s, self.cx, self.cy, self.cz, self.iv, self.dg, self.va, self.vb = refs
        self.base, self.extent, self.left, self.right = base, extent, left, right

    def lane(self):
        return lax.broadcasted_iota(jnp.int32, (32, LANES), 1)

    def mask(self, pack):
        where_x = self.base + 4 * pack + self.lane() // 32
        cell = self.lane() % 32
        keep = jnp.where(cell < 8, self.left, jnp.where(cell >= 24, self.right, 1.0))
        return jnp.where((where_x >= 0) & (where_x < self.extent), keep, 0.0)

    def x_up(self, tiles):
        turned = [pltpu.roll(t, LANES - 32, 1) for t in tiles]
        return [jnp.where(self.lane() < LANES - 32, turned[p], turned[min(p + 1, 3)]) for p in range(4)]

    def x_down(self, tiles):
        turned = [pltpu.roll(t, 32, 1) for t in tiles]
        return [jnp.where(self.lane() >= 32, turned[p], turned[max(p - 1, 0)]) for p in range(4)]

    def setup(self):
        row = lax.broadcasted_iota(jnp.int32, (32, LANES), 0)
        top, bottom = row == 31, row == 0
        masks = [self.mask(p) for p in range(4)]
        own = [self.c[p] * (0.5 * masks[p]) for p in range(4)]
        above = self.x_up(own)
        x_high = [own[p] + above[p] for p in range(4)]
        x_low = self.x_down(x_high)
        for p in range(4):
            y_high = own[p] + jnp.where(top, 0.0, pltpu.roll(own[p], 31, 0))
            y_low = jnp.where(bottom, own[p], pltpu.roll(y_high, 1, 0))
            z_high = own[p] + pltpu.roll(own[p], LANES - 1, 1)
            z_low = pltpu.roll(z_high, 1, 1)
            diagonal = x_low[p] + x_high[p] + y_low + y_high + z_low + z_high
            self.cx[p] = x_high[p]
            self.cy[p] = jnp.where(top, 0.0, y_high)
            self.cz[p] = z_high
            self.dg[p] = diagonal
            self.iv[p] = jnp.where(masks[p] > 0.5, 1.0 / diagonal, 0.0)

    def start(self, beta):
        for p in range(4):
            self.va[p] = self.s[p] * self.iv[p] * beta

    def around(self, field):
        here = [field[p] for p in range(4)]
        cx = [self.cx[p] for p in range(4)]
        x_up = self.x_up(here)
        x_down = self.x_down([cx[p] * here[p] for p in range(4)])
        sums = []
        for p in range(4):
            cy, cz = self.cy[p], self.cz[p]
            total = cx[p] * x_up[p] + x_down[p]
            total = total + (cy * pltpu.roll(here[p], 31, 0) + pltpu.roll(cy * here[p], 1, 0))
            total = total + (cz * pltpu.roll(here[p], LANES - 1, 1) + pltpu.roll(cz * here[p], 1, 1))
            sums.append(total + self.s[p])
        return here, sums

    def sweep(self, field, result, step, fresh=False):
        alpha, beta = step
        here, sums = self.around(field)
        for p in range(4):
            kept = (1.0 + alpha - beta) * here[p]
            if not fresh:
                kept = kept - alpha * result[p]
            result[p] = kept + (beta * self.iv[p]) * sums[p]

    def residual(self, field, result):
        here, sums = self.around(field)
        for p in range(4):
            result[p] = sums[p] - self.dg[p] * here[p]

    def own(self, ref, pack, layers=range(4)):
        cell = self.lane() % 32
        packed = jnp.zeros((32, LANES), F32)
        for layer in layers:
            tile = ref[0, 4 * pack + layer]
            first = pltpu.roll(tile, 32 * layer + 8, 1)
            last = pltpu.roll(tile, (32 * layer + 24) % LANES, 1)
            packed = jnp.where(self.lane() // 32 == layer, jnp.where(cell < 16, first, last), packed)
        return packed

    def take_halo(self, ref, pack, from_left, from_right):
        cell = lax.broadcasted_iota(jnp.int32, (8, LANES), 1) % 32
        for part in range(4):
            rows = pl.ds(8 * part, 8)
            below = pltpu.roll(from_left, (LANES - 8 * part) % LANES, 1)
            above = pltpu.roll(from_right, 24 - 8 * part, 1) if part < 3 else from_right
            ref[pack, rows, :] = jnp.where(cell < 8, below, jnp.where(cell >= 24, above, ref[pack, rows, :]))

    def give_halo(self, ref, pack, side):
        cell = lax.broadcasted_iota(jnp.int32, (8, LANES), 1) % 32
        packed = None
        for part in range(4):
            shift = (8 * part - 8 - 8 * side) % LANES
            tile = ref[pack, pl.ds(8 * part, 8), :]
            tile = pltpu.roll(tile, shift, 1) if shift else tile
            packed = tile if part == 0 else jnp.where(cell // 8 == part, tile, packed)
        return packed

    def mend(self, tile, ref, at):
        packed, layer = ref[at // 4], at % 4
        first = pltpu.roll(packed, (LANES - 32 * layer - 8) % LANES, 1)
        last = pltpu.roll(packed, (LANES + 104 - 32 * layer) % LANES, 1)
        return jnp.where(self.lane() < 4, first, jnp.where(self.lane() >= LANES - 4, last, tile))


LEVEL_FIELDS = 9
LEVEL_SHAPES = ((1, 16, 32, LANES), (2, 14, 16, LANES), (1, 34, 8, LANES), (1, 15, 8, LANES))
RULER = 1024
SENDERS = 10 + 2 * (2 * REACH + 1)
GROUPS = 34 + 2 * (2 * REACH + 1)


def kernel(wide, narrow, rhs, coef, kept, added, *scratch):
    scratch = list(scratch)
    level_refs = []
    for _ in range(4):
        level_refs.append(scratch[:LEVEL_FIELDS])
        scratch = scratch[LEVEL_FIELDS:]
    strip_refs, scratch = scratch[:LEVEL_FIELDS], scratch[LEVEL_FIELDS:]
    (ps, zs, rz, rcn, kp, k1cx, k1c, sk, sp, k1x, k1p, k1z, rc2, s2m, rs2, rx1, sb0, hx0, p1, p0, ruler,
     local_sem, send_sem, recv_sem) = scratch
    me_w = lax.axis_index("wide")
    me_n = lax.axis_index("narrow")

    def there(dw, dn):
        return (lax.rem(me_w + (dw + wide), wide), lax.rem(me_n + (dn + narrow), narrow))

    has = (me_w > 0, me_w < wide - 1)
    has_z = (me_n > 0, me_n < narrow - 1)
    reach = (jnp.minimum(me_w, REACH), jnp.minimum(wide - 1 - me_w, REACH))

    def for_far(first, body, last=REACH):
        for side in range(2):
            sign = 2 * side - 1

            def step(k, carry):
                body(REACH + sign * k, sign * k)
                return carry

            lax.fori_loop(first, jnp.minimum(reach[side], last) + 1, step, 0)

    def for_all_far(body):
        inner = reach[0] + reach[1] == 2 * REACH

        @pl.when(inner)
        def straight():
            for k in range(REACH, 0, -1):
                for sign in (-1, 1):
                    body(REACH + sign * k, sign * k)

        pl.when(jnp.logical_not(inner))(functools.partial(for_far, 1, body))

    def for_sides(body):
        for side in range(2):
            pl.when(has[side])(functools.partial(body, side, 2 * side - 1))

    def for_sides_z(body):
        for side in range(2):
            pl.when(has_z[side])(functools.partial(body, side, 2 * side - 1))

    def for_corners(body):
        for side in range(2):
            for side_z in range(2):
                pl.when(has[side] & has_z[side_z])(
                    functools.partial(body, side, side_z, 2 * side - 1, 2 * side_z - 1)
                )

    @pl.when((me_n == 0) | (me_n == narrow - 1))
    def clear_z():
        for ref in (rz, rcn, k1c, k1z, k1p):
            ref[...] = jnp.zeros(ref.shape, F32)

    @pl.when((me_w < REACH) | (me_w >= wide - REACH))
    def clear():
        def zero(ref):
            ref[...] = jnp.zeros(ref.shape, F32)

        for ref in (rcn, rx1, hx0, rc2, rs2, k1cx, k1c, k1x, k1p):
            zero(ref)
        for side in range(2):
            for ref in level_refs[0][:2]:
                zero(ref.at[0, pl.ds(12 * side, 4)])
            zero(level_refs[1][0].at[0, 13 * side])

    def if_reach(least, body):
        for side in range(2):
            pl.when(reach[side] >= least)(functools.partial(body, side, 2 * side - 1))

    barrier = pltpu.get_barrier_semaphore()

    def greet(dw, dn):
        pl.semaphore_signal(barrier, inc=1, device_id=there(dw, dn), device_id_type=MESH_ID)

    for_far(1, lambda slot, dw: greet(dw, 0), HALF_REACH)
    for_sides_z(lambda side, dn: greet(0, dn))
    for_corners(lambda side, side_z, dw, dn: greet(dw, dn))

    c0, s0 = level_refs[0][0], level_refs[0][1]
    load_c = pltpu.make_async_copy(coef, c0.at[0, pl.ds(4, 8)], local_sem.at[0])
    load_s = pltpu.make_async_copy(rhs, s0.at[0, pl.ds(4, 8)], local_sem.at[1])
    load_c.start()
    load_s.start()
    beside_x = jnp.where(has[0], 1, 0) + jnp.where(has[1], 1, 0)
    beside_z = jnp.where(has_z[0], 1, 0) + jnp.where(has_z[1], 1, 0)
    greeted = beside_z + beside_x * beside_z
    for side in range(2):
        greeted = greeted + jnp.minimum(reach[side], HALF_REACH)

    left = jnp.where(me_n > 0, 1.0, 0.0).astype(F32)
    right = jnp.where(me_n < narrow - 1, 1.0, 0.0).astype(F32)

    def lanes(rows):
        return lax.broadcasted_iota(jnp.int32, (rows, LANES), 1)

    def edges(rows, until, low, since, high):
        at = lanes(rows)
        return jnp.where(at < until, low, jnp.where(at >= since, high, 0.0))

    def centred(rows):
        at = lanes(rows)
        return jnp.where((at >= 32) & (at < 96), 1.0, edges(rows, 32, left, 96, right))

    level_0 = Level(level_refs[0], 1.0, 32, 1, 1, 8 * me_w - 4, 8 * wide, [None])
    strips = Strips(strip_refs, 8 * me_w - 4, 8 * wide, left, right)
    level_1 = Level(
        level_refs[1], 0.25, 16, 1, 1, 4 * me_w - 5, 4 * wide, [centred(16), edges(16, 32, right, 96, left)]
    )
    level_2 = Level(level_refs[2], 0.0625, 8, 1, 2, 2 * me_w - 16, 2 * wide, [centred(8)])
    level_3 = Level(level_refs[3], 0.015625, 8, 2, 4, me_w - 7, wide, [centred(8)])

    sent = [0] * SENDERS

    def send(group, src, dst, dw, dn, rows, sender):
        if isinstance(sender, int):
            sent[sender] += rows
        pltpu.make_async_remote_copy(
            src_ref=src, dst_ref=dst, send_sem=send_sem.at[sender], recv_sem=recv_sem.at[group],
            device_id=there(dw, dn), device_id_type=MESH_ID,
        ).start()

    def ruled(rows, group, sender):
        span = ruler.at[pl.ds(0, rows)]
        return pltpu.make_async_remote_copy(
            src_ref=span, dst_ref=span, send_sem=send_sem.at[sender], recv_sem=recv_sem.at[group],
            device_id=there(0, 1), device_id_type=MESH_ID,
        )

    def receive(group, rows):
        ruled(rows, group, 0).wait_recv()

    def receive_sides(group, rows):
        for_sides(lambda side, dw: receive(group + side, rows))

    def receive_sides_z(group, rows):
        for_sides_z(lambda side, dn: receive(group + side, rows))

    def receive_corners(group, rows):
        for_corners(lambda side, side_z, dw, dn: receive(group + 2 * side + side_z, rows))

    def receive_far(group, last=REACH):
        for_far(1, lambda slot, dw: receive(group + slot, 8), last)

    def sends_done(sender):
        ruled(sent[sender], 0, sender).wait_send()

    from_z, from_s1z = 0, 2
    from_c_corner, from_k_corner, from_s1_corner = 4, 8, 12
    from_c, from_s, from_s_next, from_k, from_s1, from_c1b, from_x0, from_x1 = range(16, 32, 2)
    from_four = 32
    from_c2 = 34
    from_s2 = from_c2 + 2 * REACH + 1
    sender_x, sender_four, sender_z = range(0, 6, 2)
    sender_corner, sender_c2, sender_far = 6, 10, 10 + 2 * REACH + 1

    def restrict_0(ref):
        out = []
        for layer in range(4):
            total = None
            for dx in range(2):
                for dy in range(2):
                    term = ref[0, 4 + 2 * layer + dx, pl.ds(dy, 16, stride=2), :]
                    total = term if total is None else total + term
            total = total + pltpu.roll(total, LANES - 1, 1)
            out.append(0.125 * jnp.take_along_axis(total, (2 * lanes(16) + 64) % LANES, axis=1))
        return out

    odd_8 = lanes(8) % 2 == 1

    def pairs_1(ref):
        out = []
        for layer in range(2):
            total = None
            for dx in range(2):
                for dy in range(2):
                    term = ref[0, 5 + 2 * layer + dx, pl.ds(dy, 8, stride=2), :]
                    total = term if total is None else total + term
            total = total + jnp.where(odd_8, pltpu.roll(total, 1, 1), pltpu.roll(total, LANES - 1, 1))
            out.append(0.125 * total)
        return jnp.where(odd_8, out[1], out[0])

    def squeeze_1(layers, ref, row):
        for part in range(2):
            ref[pl.ds(row + 16 * part, 16), :] = jnp.where(lanes(16) < 64, layers[part], layers[part + 2])

    def squeeze_halves(first, second):
        low_quarter = lanes(16) % 64 < 32
        return (
            jnp.where(low_quarter, pltpu.roll(first, 96, 1), second),
            jnp.where(low_quarter, first, pltpu.roll(second, 32, 1)),
        )

    load_c.wait()
    own_c1 = restrict_0(c0)
    for half in range(2):
        strips.c[1 + half] = strips.own(c0, 1 + half)
    for side in range(2):
        squeeze_1(own_c1, zs.at[side], 32)
        for half in range(2):
            zs[side, pl.ds(16 * half, 8), :] = strips.give_halo(strips.c, 1 + half, side)
    load_s.wait()
    for half in range(2):
        strips.s[1 + half] = strips.own(s0, 1 + half)
    for side in range(2):
        for half in range(2):
            zs[side, pl.ds(16 * half + 8, 8), :] = strips.give_halo(strips.s, 1 + half, side)

    pl.semaphore_wait(barrier, greeted)

    @for_sides
    def send_faces(side, dw):
        src, dst = c0.at[0, pl.ds(4 + 4 * side, 4)], c0.at[0, pl.ds(12 - 12 * side, 4)]
        send(from_c + 1 - side, src, dst, dw, 0, 128, sender_x + side)

    @for_sides
    def send_nearest(side, dw):
        send(from_s + 1 - side, s0.at[0, 4 + 7 * side], s0.at[0, 12 - 9 * side], dw, 0, 32, sender_x + side)

    for_sides_z(
        lambda side, dn: send(from_z + 1 - side, zs.at[side], rz.at[1 - side], 0, dn, 64, sender_z + side)
    )

    def send_corner(group, src, dst, rows, side, side_z):
        at = 2 * side + side_z
        send(group + 3 - at, src, dst, 2 * side - 1, 2 * side_z - 1, rows, sender_corner + at)

    @for_corners
    def send_c_corner(side, side_z, dw, dn):
        src = zs.at[side_z, pl.ds(16 * side, 16)]
        send_corner(from_c_corner, src, rcn.at[1 - side, 1 - side_z], 16, side, side_z)

    @for_sides
    def send_s_next(side, dw):
        src = s0.at[0, pl.ds(5 + 4 * side, 2)]
        send(from_s_next + 1 - side, src, s0.at[0, pl.ds(13 - 12 * side, 2)], dw, 0, 64, sender_x + side)

    steps = cheb(3)
    sweep_a = (level_0.va, level_0.vb, 1, 1, steps[1], True)
    sweep_b = (level_0.vb, level_0.va, 1, 1, steps[2], False)
    level_0.setup(5, 10, 6, 1)
    level_0.start(5, 10, 6, 1, steps[0][1])
    over_layers(6, 9, 4, lambda at: level_0.sweep_at(at, *sweep_a))
    over_layers(7, 8, 2, lambda at: level_0.sweep_at(at, *sweep_b))

    def take_halos(field, ref, pack, got):
        rows = pl.ds(8 * field + (16 if pack == 2 else 0), 8)
        strips.take_halo(ref, pack, got[0, rows, :], got[1, rows, :])

    receive_sides_z(from_z, 64)
    for field, ref in enumerate((strips.c, strips.s)):
        for half in range(2):
            take_halos(field, ref, 1 + half, rz)

    def spread_1(ref, block):
        at_lane = lanes(16)
        low_half = at_lane < 64
        low_quarter = at_lane % 64 < 32
        for part in range(2):
            before, own, after = (block(dz, part) for dz in (-1, 0, 1))
            near = jnp.where(low_quarter, before, after)
            outer = jnp.where(low_quarter, after, before)
            own_r, near_r, outer_r = (pltpu.roll(t, 64, 1) for t in (own, near, outer))
            at = 5 + part
            for at, own_a, own_b, near_a, near_b, outer_a, outer_b in (
                (at, own, own_r, near, near_r, outer, outer_r),
                (at + 2, own_r, own, near_r, near, outer_r, outer),
            ):
                centre = jnp.where(low_half, own_a, own_b)
                ref[0, at] = jnp.where(at_lane < 32, near_a, jnp.where(at_lane < 96, centre, near_b))
                ref[1, at] = jnp.where(low_half, outer_a, outer_b)

    def coef_block(dz, part):
        rows = pl.ds(32 + 16 * part, 16)
        return zs[0, rows, :] if dz == 0 else rz[(1 + dz) // 2, rows, :]

    spread_1(level_1.c, coef_block)
    rc2[REACH] = pairs_1(level_1.c)

    for_far(
        1,
        lambda slot, dw: send(
            from_c2 + 2 * REACH - slot, rc2.at[REACH], rc2.at[2 * REACH - slot], dw, 0, 8, sender_c2 + slot
        ),
        HALF_REACH,
    )
    k1_own = zs.at[0, pl.ds(32, 32)]
    halves = squeeze_halves(zs[0, pl.ds(32, 16), :], zs[0, pl.ds(48, 16), :])
    at_lane = lanes(16)
    for side in range(2):
        near, far = (0, 3) if side == 0 else (3, 0)
        full = level_1.c[0, 5 + near]
        place = (32 * far + 31, 32 * far)
        cell = (64, 63)
        for side_z in range(2):
            moved = pltpu.roll(full, (place[side_z] - cell[side_z]) % LANES, 1)
            kp[side, side_z] = jnp.where(at_lane == place[side_z], moved, halves[side_z])
    for_sides(
        lambda side, dw: send(from_k + 1 - side, k1_own, k1cx.at[1 - side], dw, 0, 32, sender_x + side)
    )
    for_corners(
        lambda side, side_z, dw, dn: send_corner(
            from_k_corner, kp.at[side, side_z], k1c.at[1 - side, 1 - side_z], 16, side, side_z
        )
    )

    receive_sides(from_c, 128)
    receive_corners(from_c_corner, 16)
    for side in range(2):
        strips.c[3 * side] = strips.own(c0, 3 * side)
        take_halos(0, strips.c, 3 * side, rcn.at[side])
    level_0.setup_below(1, 1)
    over_sides(1, 11, 4, lambda at: level_0.setup_at(at, 1))
    strips.setup()
    receive_sides(from_s, 32)
    over_sides(3, 11, 2, lambda at: level_0.start_at(at, 1, steps[0][1]))
    over_sides(4, 10, 2, lambda at: level_0.sweep_at(at, *sweep_a))
    over_sides(5, 9, 2, lambda at: level_0.sweep_at(at, *sweep_b))
    over_layers(6, 9, 4, lambda at: level_0.residual_at(at, level_0.va, level_0.vb, 1))
    receive_sides(from_s_next, 64)
    for side in range(2):
        strips.s[3 * side] = strips.own(s0, 3 * side, range(1 - side, 4 - side))
        take_halos(1, strips.s, 3 * side, rcn.at[side])
    over_sides(1, 13, 2, lambda at: level_0.start_at(at, 1, steps[0][1]))
    strips.start(steps[0][1])
    over_sides(2, 12, 2, lambda at: level_0.sweep_at(at, *sweep_a))
    strips.sweep(strips.va, strips.vb, steps[1], fresh=True)
    over_sides(3, 11, 2, lambda at: level_0.sweep_at(at, *sweep_b))
    strips.sweep(strips.vb, strips.va, steps[2])
    over_sides(4, 10, 2, lambda at: level_0.residual_at(at, level_0.va, level_0.vb, 1))
    strips.residual(strips.va, strips.vb)
    for at in range(4, 12):
        level_0.vb[0, at] = strips.mend(level_0.vb[0, at], strips.vb, at)

    squeeze_1(restrict_0(level_0.vb), sk, 0)

    sp[0], sp[1] = squeeze_halves(sk[pl.ds(0, 16), :], sk[pl.ds(16, 16), :])

    for_sides(lambda side, dw: send(from_s1 + 1 - side, sk, k1x.at[1 - side], dw, 0, 32, sender_x + side))
    for_corners(
        lambda side, side_z, dw, dn: send_corner(
            from_s1_corner, sp.at[side_z], k1p.at[1 - side, 1 - side_z], 16, side, side_z
        )
    )
    for_sides_z(lambda side, dn: send(from_s1z + 1 - side, sk, k1z.at[1 - side], 0, dn, 32, sender_z + side))

    receive_far(from_c2, HALF_REACH)

    @functools.partial(if_reach, HALF_REACH)
    def send_four(side, sign):
        src, dst = rc2.at[pl.ds(9 - 5 * side, 4)], rc2.at[pl.ds(13 - 13 * side, 4)]
        send(from_four + 1 - side, src, dst, HALF_REACH * sign, 0, 32, sender_four + side)

    for at in range(3, 13):
        level_0.va[0, at] = strips.mend(level_0.va[0, at], strips.va, at)
    own_cell = (strips.lane() % 32 >= 8) & (strips.lane() % 32 < 24)
    for pack_at, layers in enumerate(((3,), range(4), range(4), (0,))):
        strips.va[pack_at] = jnp.where(own_cell, strips.own(level_0.va, pack_at, layers), strips.va[pack_at])
    for side in range(2):
        first = 9 if side == 0 else 5
        for layer in range(2):
            sb0[side, pl.ds(32 * layer, 32), :] = level_0.va[0, first + layer]
        packed = strips.va[2 - side]
        middle = (lanes(16) >= 32) & (lanes(16) < 96)
        sb0[side, pl.ds(64, 16), :] = jnp.where(middle, packed[:16], pltpu.roll(packed[16:], 64, 1))

    @for_sides
    def send_iterate_0(side, dw):
        send(from_x0 + 1 - side, sb0.at[1 - side], hx0.at[1 - side], dw, 0, 80, sender_x + side)

    def source_block(dz, part):
        rows = pl.ds(16 * part, 16)
        return sk[rows, :] if dz == 0 else k1z[(1 + dz) // 2, rows, :]

    def spread_beside(ref, blocks, packs):
        at_lane = lanes(16)
        low_half = at_lane < 64
        for side in range(2):
            for layer in range(4):
                own = blocks[side, pl.ds(16 * (layer % 2), 16), :]
                other = pltpu.roll(own, 64, 1)
                centre = jnp.where(low_half, own, other) if layer < 2 else jnp.where(low_half, other, own)
                before = pltpu.roll(packs[side, 0], (LANES - 32 * layer) % LANES, 1)
                after = pltpu.roll(packs[side, 1], (LANES + 96 - 32 * layer) % LANES, 1)
                ref[0, 1 + 8 * side + layer] = jnp.where(at_lane < 32, before, jnp.where(at_lane < 96, centre, after))

    receive_sides(from_k, 32)
    receive_corners(from_k_corner, 16)
    spread_beside(level_1.c, k1cx, k1c)
    for side in range(2):
        far = 3 if side == 1 else 0
        below, above = (pltpu.roll(k1c[side, side_z], (shift - 32 * far) % LANES, 1)
                        for side_z, shift in ((0, 127), (1, -31)))
        level_1.c[1, 4 + 5 * side] = jnp.where(lanes(16) < 64, above, below)

    @for_sides
    def send_coef_1(side, dw):
        send(from_c1b + 1 - side, level_1.c.at[0, 9 - 5 * side], level_1.c.at[0, 13 - 13 * side], dw, 0, 16, sender_x + side)

    level_1.setup_below(2, 1)
    over_sides(2, 10, 2, lambda at: level_1.setup_at(at, 1))
    over_layers(4, 9, 6, lambda at: level_1.setup_at(at, 2))

    receive_sides_z(from_s1z, 32)
    spread_1(level_1.s, source_block)
    receive_sides(from_s1, 32)
    receive_corners(from_s1_corner, 16)
    spread_beside(level_1.s, k1x, k1p)
    level_1.start(2, 11, 10, 1, steps[0][1])
    over_layers(5, 8, 4, lambda at: level_1.start_outer(at, steps[0][1]))
    over_sides(3, 9, 2, lambda at: level_1.sweep_at(at, level_1.va, level_1.vb, 1, 1, steps[1], True))
    over_layers(5, 8, 4, lambda at: level_1.sweep_at(at, level_1.va, level_1.vb, 2, 1, steps[1], True))
    level_1.sweep(level_1.vb, level_1.va, 4, 9, 6, 1, 1, steps[2])
    level_1.residual(level_1.va, level_1.vb, 5, 8, 4, 1)

    value = pairs_1(level_1.vb)
    s2m[...] = value
    rs2[REACH] = value

    for_all_far(
        lambda slot, dw: send(
            from_s2 + 2 * REACH - slot, s2m, rs2.at[2 * REACH - slot], dw, 0, 8, sender_far + slot
        )
    )

    @for_sides
    def send_iterate_1(side, dw):
        layers = level_1.va.at[0, pl.ds(6 - 2 * side, 4)]
        send(from_x1 + 1 - side, layers, rx1.at[1 - side], dw, 0, 64, sender_x + side)

    receive_sides(from_c1b, 16)
    level_1.setup_below(1, 1)
    over_sides(1, 12, 1, lambda at: level_1.setup_at(at, 1))

    def spread_2(ref, blocks):
        for block in range(2 * REACH + 1):
            packed = blocks[block]
            ref[0, 2 * block] = jnp.where(odd_8, pltpu.roll(packed, 1, 1), packed)
            ref[0, 2 * block + 1] = jnp.where(odd_8, packed, pltpu.roll(packed, LANES - 1, 1))

    def restrict_2(ref, at):
        total = ref[0, 2 * at + 2] + ref[0, 2 * at + 3]
        odd_row = lax.broadcasted_iota(jnp.int32, (8, LANES), 0) % 2 == 1
        total = total + jnp.where(odd_row, pltpu.roll(total, 1, 0), pltpu.roll(total, 7, 0))
        second = lanes(8) % 4 >= 2
        total = total + jnp.where(second, pltpu.roll(total, 2, 1), pltpu.roll(total, LANES - 2, 1))
        return 0.125 * total

    if_reach(HALF_REACH, lambda side, sign: receive(from_four + side, 32))
    spread_2(level_2.c, rc2)
    level_2.setup(1, 32, 16, 1)
    for at in range(15):
        level_3.c[0, at] = restrict_2(level_2.c, at)
    level_3.setup(1, 13, 13, 1)

    for_sides(lambda side, dw: sends_done(sender_x + side))
    for_sides_z(lambda side, dn: sends_done(sender_z + side))
    for_corners(lambda side, side_z, dw, dn: sends_done(sender_corner + 2 * side + side_z))
    if_reach(HALF_REACH, lambda side, sign: sends_done(sender_four + side))
    for_far(1, lambda slot, dw: ruled(8, 0, sender_c2 + slot).wait_send(), HALF_REACH)
    for_all_far(lambda slot, dw: ruled(8, 0, sender_far + slot).wait_send())

    for_all_far(lambda slot, dw: receive(from_s2 + slot, 8))
    spread_2(level_2.s, rs2)
    level_2.start(1, 32, 32, 1, steps[0][1])
    level_2.sweep(level_2.va, level_2.vb, 2, 31, 30, 1, 1, steps[1], fresh=True)
    level_2.sweep(level_2.vb, level_2.va, 3, 30, 28, 1, 1, steps[2])
    level_2.residual(level_2.va, level_2.vb, 4, 29, 26, 1)

    for at in range(1, 14):
        level_3.s[0, at] = restrict_2(level_2.vb, at)
    coarse = cheb(4)
    level_3.start(1, 13, 13, 1, coarse[0][1])
    level_3.sweep(level_3.va, level_3.vb, 2, 12, 11, 1, 1, coarse[1], fresh=True)
    level_3.sweep(level_3.vb, level_3.va, 3, 11, 9, 1, 1, coarse[2])
    level_3.sweep(level_3.va, level_3.vb, 4, 10, 7, 1, 1, coarse[3])

    for at in range(10, 24):
        level_2.vb[0, at] = level_2.va[0, at] + level_3.vb[0, (at - 2) // 2]
    level_2.sweep(level_2.vb, level_2.va, 11, 22, 12, 1, 1, steps[0], fresh=True)
    level_2.sweep(level_2.va, level_2.vb, 12, 21, 10, 1, 1, steps[1])
    level_2.sweep(level_2.vb, level_2.va, 13, 20, 8, 1, 1, steps[2])

    for at in range(8):
        value = level_2.va[0, 13 + at]
        for part in range(2):
            p1[at, pl.ds(part, 8, stride=2), :] = value
    receive_sides(from_x1, 64)
    for at in range(14):
        if 4 <= at <= 9:
            before = level_1.va[0, at]
        else:
            before = rx1[0, at] if at < 4 else rx1[1, at - 10]
        level_1.vb[0, at] = before + p1[(at + 1) // 2]
    level_1.sweep(level_1.vb, level_1.va, 1, 12, 12, 1, 1, steps[0], fresh=True)
    level_1.sweep(level_1.va, level_1.vb, 2, 11, 10, 1, 1, steps[1])
    level_1.sweep(level_1.vb, level_1.va, 3, 10, 8, 1, 1, steps[2])

    cell = lanes(16) % 32
    strip_lane = jnp.where(cell < 16, 28, 84) + cell // 2
    low_half = lanes(16) < 64
    fine = []
    for at in range(8):
        value = level_1.va[0, 3 + at]
        own = jnp.take_along_axis(value, lanes(16) // 2 + 32, axis=1)
        fine.append(jnp.take_along_axis(value, strip_lane, axis=1))
        for part in range(2):
            p0[at, pl.ds(part, 16, stride=2), :] = own
    for pack in range(4):
        value = jnp.where(low_half, fine[2 * pack], fine[2 * pack + 1])
        for part in range(2):
            ps[pack, pl.ds(part, 16, stride=2), :] = value
    receive_sides(from_x0, 80)
    for side in range(2):
        for layer in range(2):
            at = (1 if side == 0 else 13) + layer
            level_0.vb[0, at] = hx0[side, pl.ds(32 * layer, 32), :] + p0[at // 2]
        packed = hx0[side, pl.ds(64, 16), :]
        layer = lanes(16) // 32
        for part, value in enumerate((packed, pltpu.roll(packed, 64, 1))):
            rows = pl.ds(16 * part, 16)
            own = jnp.where(layer == (3 if side == 0 else 0), strips.va[3 * side, rows, :], 0.0)
            value = jnp.where((layer == 1) | (layer == 2), value, own)
            strips.vb[3 * side, rows, :] = value + ps[3 * side, rows, :]
    for pack in (1, 2):
        strips.vb[pack] = strips.va[pack] + ps[pack]

    def correct(at):
        level_0.vb[0, at] = level_0.va[0, at] + p0[at // 2]

    over_layers(3, 12, 10, correct)
    level_0.sweep(level_0.vb, level_0.va, 2, 13, 12, 1, 1, steps[0], fresh=True)
    strips.sweep(strips.vb, strips.va, steps[0], fresh=True)
    level_0.sweep(level_0.va, level_0.vb, 3, 12, 10, 1, 1, steps[1])
    strips.sweep(strips.va, strips.vb, steps[1])
    strips.sweep(strips.vb, strips.va, steps[2])
    inner = (strips.lane() >= 4) & (strips.lane() < LANES - 4)
    for at in range(4, 12):
        kept_here, added_here = level_0.last_at(at, level_0.vb, level_0.va, steps[2])
        kept[at - 4] = strips.mend(kept_here, strips.va, at)
        added[at - 4] = jnp.where(inner, added_here, 0.0)


def per_device(right_side, conductivity, wide, narrow):
    brick = (8, 32, LANES)
    scratch = []
    for shape in LEVEL_SHAPES:
        scratch += [pltpu.VMEM(shape, F32)] * LEVEL_FIELDS
    scratch += [pltpu.VMEM((4, 32, LANES), F32)] * LEVEL_FIELDS
    shapes = [
        (4, 32, LANES),
        (2, 64, LANES), (2, 64, LANES), (2, 2, 16, LANES),
        (2, 2, 16, LANES), (2, 32, LANES), (2, 2, 16, LANES),
        (32, LANES), (2, 16, LANES), (2, 32, LANES), (2, 2, 16, LANES), (2, 32, LANES),
        (2 * REACH + 1, 8, LANES), (8, LANES), (2 * REACH + 1, 8, LANES),
        (2, 4, 16, LANES),
        (2, 80, LANES), (2, 80, LANES),
        (8, 16, LANES), (8, 32, LANES),
        (RULER, LANES),
    ]
    scratch += [pltpu.VMEM(shape, F32) for shape in shapes]
    scratch += [pltpu.SemaphoreType.DMA((2,)), pltpu.SemaphoreType.DMA((SENDERS,)), pltpu.SemaphoreType.DMA((GROUPS,))]
    kept, added = pl.pallas_call(
        functools.partial(kernel, wide, narrow),
        out_shape=[jax.ShapeDtypeStruct(brick, F32)] * 2,
        in_specs=[pl.BlockSpec(memory_space=pltpu.HBM)] * 2,
        out_specs=[pl.BlockSpec(memory_space=pltpu.VMEM)] * 2,
        scratch_shapes=scratch,
        compiler_params=pltpu.CompilerParams(
            collective_id=0, has_side_effects=True, vmem_limit_bytes=32 * 1024 * 1024
        ),
    )(pltpu.with_memory_space_constraint(right_side, pltpu.HBM), pltpu.with_memory_space_constraint(conductivity, pltpu.HBM))
    return kept + added


def solution(mesh):
    spec = P("wide", None, "narrow")
    body = functools.partial(per_device, wide=mesh.shape["wide"], narrow=mesh.shape["narrow"])
    return jax.shard_map(body, mesh=mesh, in_specs=(spec, spec), out_specs=spec, check_vma=False)
```

```python
import functools

import jax
import jax.numpy as jnp
from jax import lax
from jax.experimental import pallas as pl
from jax.experimental.pallas import tpu as pltpu
from jax.sharding import PartitionSpec as P

CENTER = 1.125
HALF = 0.875
LANES = 128
REACH = 8
HALF_REACH = 4
F32 = jnp.float32
MESH_ID = pl.DeviceIdType.MESH


def cheb(sweeps):
    sigma = CENTER / HALF
    steps = [(0.0, 1.0 / CENTER)]
    ratio = 1.0 / sigma
    for _ in range(sweeps - 1):
        ratio_next = 1.0 / (2.0 * sigma - ratio)
        steps.append((ratio_next * ratio, 2.0 * ratio_next / HALF))
        ratio = ratio_next
    return steps


def over_sides(first, second, count, body):
    for base in (first, second):
        for at in range(count):
            body(base + at)


def over_layers(low, high, unroll, body):
    count = high - low + 1
    if count == unroll:
        for at in range(low, high + 1):
            body(at)
        return

    def block(step, carry):
        for at in range(unroll):
            body(low + step * unroll + at)
        return carry

    lax.fori_loop(0, count // unroll, block, 0)


class Level:
    def __init__(self, refs, scale, rows, row_step, lane_step, base, extent, lane_mask):
        self.c, self.s, self.cx, self.cy, self.cz, self.iv, self.dg, self.va, self.vb = refs
        self.half = 0.5 * scale
        self.rows, self.row_step, self.lane_step = rows, row_step, lane_step
        self.base, self.extent, self.lane_mask = base, extent, lane_mask

    def inside(self, at):
        where_x = self.base + at
        return jnp.where((where_x >= 0) & (where_x < self.extent), 1.0, 0.0).astype(F32)

    def lane(self):
        return lax.broadcasted_iota(jnp.int32, (self.rows, LANES), 1)

    def row(self):
        return lax.broadcasted_iota(jnp.int32, (self.rows, LANES), 0)

    def y_up(self, tile):
        return pltpu.roll(tile, self.rows - self.row_step, 0)

    def y_down(self, tile):
        return pltpu.roll(tile, self.row_step, 0)

    def turned(self, tiles, shift, edge, count):
        out = [pltpu.roll(t, shift, 1) for t in tiles]
        if len(tiles) == 1:
            return out
        at_edge = self.lane() == edge
        return [jnp.where(at_edge, out[1 - k], out[k]) for k in range(count)]

    def z_up(self, tiles, count):
        return self.turned(tiles, LANES - self.lane_step, LANES - 1, count)

    def z_down(self, tiles, count):
        return self.turned(tiles, self.lane_step, 0, count)

    def masked(self, at, tiles):
        keep = self.inside(at) * self.half
        out = []
        for k in range(tiles):
            mask = self.lane_mask[k]
            out.append(self.c[k, at] * (keep if mask is None else mask * keep))
        return out

    def setup_below(self, low, tiles):
        first, second = self.masked(low - 1, tiles), self.masked(low, tiles)
        for k in range(tiles):
            self.cx[k, low - 1] = first[k] + second[k]

    def setup_at(self, at, tiles):
        before, here, after = self.masked(at - 1, tiles), self.masked(at, tiles), self.masked(at + 1, tiles)
        inside = self.inside(at)
        top = self.row() >= self.rows - self.row_step
        bottom = self.row() < self.row_step
        z_up, z_down = self.z_up(here, tiles), self.z_down(here, tiles)
        for k in range(tiles):
            own = here[k]
            x_low = before[k] + own
            x_high = own + after[k]
            y_low = own + jnp.where(bottom, 0.0, self.y_down(own))
            y_high = own + jnp.where(top, 0.0, self.y_up(own))
            z_low = own + z_down[k]
            z_high = own + z_up[k]
            diagonal = x_low + x_high + y_low + y_high + z_low + z_high
            keep = inside if self.lane_mask[k] is None else self.lane_mask[k] * inside
            self.cx[k, at] = x_high
            self.cy[k, at] = jnp.where(top, 0.0, y_high)
            self.cz[k, at] = z_high
            if k == 0:
                self.dg[0, at] = diagonal
            self.iv[k, at] = jnp.where(jnp.full_like(own, 0.0) + keep > 0.5, 1.0 / diagonal, 0.0)

    def setup(self, low, high, unroll, tiles):
        self.setup_below(low, tiles)
        over_layers(low, high, unroll, lambda at: self.setup_at(at, tiles))

    def start_at(self, at, tiles, beta):
        for k in range(tiles):
            self.va[k, at] = self.s[k, at] * self.iv[k, at] * beta

    def start_outer(self, at, beta):
        self.va[1, at] = self.s[1, at] * self.iv[1, at] * beta

    def start(self, low, high, unroll, tiles, beta):
        over_layers(low, high, unroll, lambda at: self.start_at(at, tiles, beta))

    def around(self, field, at, tiles, count):
        here = [field[k, at] for k in range(tiles)]
        cz = [self.cz[k, at] for k in range(tiles)]
        z_up = self.z_up(here, count)
        z_down = self.z_down([cz[k] * here[k] for k in range(tiles)], count)
        sums = []
        for k in range(count):
            cy = self.cy[k, at]
            total = self.cx[k, at] * field[k, at + 1] + self.cx[k, at - 1] * field[k, at - 1]
            total = total + (cy * self.y_up(here[k]) + self.y_down(cy * here[k]))
            total = total + (cz[k] * z_up[k] + z_down[k])
            sums.append(total + self.s[k, at])
        return here, sums

    def sweep_at(self, at, field, result, tiles, count, step, fresh):
        alpha, beta = step
        here, sums = self.around(field, at, tiles, count)
        for k in range(count):
            kept = (1.0 + alpha - beta) * here[k]
            if not fresh:
                kept = kept - alpha * result[k, at]
            result[k, at] = kept + (beta * self.iv[k, at]) * sums[k]

    def sweep(self, field, result, low, high, unroll, tiles, count, step, fresh=False):
        over_layers(low, high, unroll, lambda at: self.sweep_at(at, field, result, tiles, count, step, fresh))

    def residual_at(self, at, field, result, tiles):
        here, sums = self.around(field, at, tiles, 1)
        result[0, at] = sums[0] - self.dg[0, at] * here[0]

    def residual(self, field, result, low, high, unroll, tiles):
        over_layers(low, high, unroll, lambda at: self.residual_at(at, field, result, tiles))

    def last_at(self, at, field, older, step):
        alpha, beta = step
        here, sums = self.around(field, at, 1, 1)
        return (1.0 + alpha - beta) * here[0] - alpha * older[0, at], (beta * self.iv[0, at]) * sums[0]


class Strips:
    def __init__(self, refs, base, extent, left, right):
        self.c, self.s, self.cx, self.cy, self.cz, self.iv, self.dg, self.va, self.vb = refs
        self.base, self.extent, self.left, self.right = base, extent, left, right

    def lane(self):
        return lax.broadcasted_iota(jnp.int32, (32, LANES), 1)

    def mask(self, pack):
        where_x = self.base + 4 * pack + self.lane() // 32
        cell = self.lane() % 32
        keep = jnp.where(cell < 8, self.left, jnp.where(cell >= 24, self.right, 1.0))
        return jnp.where((where_x >= 0) & (where_x < self.extent), keep, 0.0)

    def x_up(self, tiles):
        turned = [pltpu.roll(t, LANES - 32, 1) for t in tiles]
        return [jnp.where(self.lane() < LANES - 32, turned[p], turned[min(p + 1, 3)]) for p in range(4)]

    def x_down(self, tiles):
        turned = [pltpu.roll(t, 32, 1) for t in tiles]
        return [jnp.where(self.lane() >= 32, turned[p], turned[max(p - 1, 0)]) for p in range(4)]

    def setup(self):
        row = lax.broadcasted_iota(jnp.int32, (32, LANES), 0)
        top, bottom = row == 31, row == 0
        masks = [self.mask(p) for p in range(4)]
        own = [self.c[p] * (0.5 * masks[p]) for p in range(4)]
        above = self.x_up(own)
        x_high = [own[p] + above[p] for p in range(4)]
        x_low = self.x_down(x_high)
        for p in range(4):
            y_high = own[p] + jnp.where(top, 0.0, pltpu.roll(own[p], 31, 0))
            y_low = jnp.where(bottom, own[p], pltpu.roll(y_high, 1, 0))
            z_high = own[p] + pltpu.roll(own[p], LANES - 1, 1)
            z_low = pltpu.roll(z_high, 1, 1)
            diagonal = x_low[p] + x_high[p] + y_low + y_high + z_low + z_high
            self.cx[p] = x_high[p]
            self.cy[p] = jnp.where(top, 0.0, y_high)
            self.cz[p] = z_high
            self.dg[p] = diagonal
            self.iv[p] = jnp.where(masks[p] > 0.5, 1.0 / diagonal, 0.0)

    def start(self, beta):
        for p in range(4):
            self.va[p] = self.s[p] * self.iv[p] * beta

    def around(self, field):
        here = [field[p] for p in range(4)]
        cx = [self.cx[p] for p in range(4)]
        x_up = self.x_up(here)
        x_down = self.x_down([cx[p] * here[p] for p in range(4)])
        sums = []
        for p in range(4):
            cy, cz = self.cy[p], self.cz[p]
            total = cx[p] * x_up[p] + x_down[p]
            total = total + (cy * pltpu.roll(here[p], 31, 0) + pltpu.roll(cy * here[p], 1, 0))
            total = total + (cz * pltpu.roll(here[p], LANES - 1, 1) + pltpu.roll(cz * here[p], 1, 1))
            sums.append(total + self.s[p])
        return here, sums

    def sweep(self, field, result, step, fresh=False):
        alpha, beta = step
        here, sums = self.around(field)
        for p in range(4):
            kept = (1.0 + alpha - beta) * here[p]
            if not fresh:
                kept = kept - alpha * result[p]
            result[p] = kept + (beta * self.iv[p]) * sums[p]

    def residual(self, field, result):
        here, sums = self.around(field)
        for p in range(4):
            result[p] = sums[p] - self.dg[p] * here[p]

    def own(self, ref, pack, layers=range(4)):
        cell = self.lane() % 32
        packed = jnp.zeros((32, LANES), F32)
        for layer in layers:
            tile = ref[0, 4 * pack + layer]
            first = pltpu.roll(tile, 32 * layer + 8, 1)
            last = pltpu.roll(tile, (32 * layer + 24) % LANES, 1)
            packed = jnp.where(self.lane() // 32 == layer, jnp.where(cell < 16, first, last), packed)
        return packed

    def take_halo(self, ref, pack, from_left, from_right):
        cell = lax.broadcasted_iota(jnp.int32, (8, LANES), 1) % 32
        for part in range(4):
            rows = pl.ds(8 * part, 8)
            below = pltpu.roll(from_left, (LANES - 8 * part) % LANES, 1)
            above = pltpu.roll(from_right, 24 - 8 * part, 1) if part < 3 else from_right
            ref[pack, rows, :] = jnp.where(cell < 8, below, jnp.where(cell >= 24, above, ref[pack, rows, :]))

    def give_halo(self, ref, pack, side):
        cell = lax.broadcasted_iota(jnp.int32, (8, LANES), 1) % 32
        packed = None
        for part in range(4):
            shift = (8 * part - 8 - 8 * side) % LANES
            tile = ref[pack, pl.ds(8 * part, 8), :]
            tile = pltpu.roll(tile, shift, 1) if shift else tile
            packed = tile if part == 0 else jnp.where(cell // 8 == part, tile, packed)
        return packed

    def mend(self, tile, ref, at):
        packed, layer = ref[at // 4], at % 4
        first = pltpu.roll(packed, (LANES - 32 * layer - 8) % LANES, 1)
        last = pltpu.roll(packed, (LANES + 104 - 32 * layer) % LANES, 1)
        return jnp.where(self.lane() < 4, first, jnp.where(self.lane() >= LANES - 4, last, tile))


LEVEL_FIELDS = 9
LEVEL_SHAPES = ((1, 16, 32, LANES), (2, 14, 16, LANES), (1, 34, 8, LANES), (1, 15, 8, LANES))
RULER = 1024
SENDERS = 10 + 2 * (2 * REACH + 1)
GROUPS = 34 + 2 * (2 * REACH + 1)


def kernel(wide, narrow, rhs, coef, kept, added, *scratch):
    scratch = list(scratch)
    level_refs = []
    for _ in range(4):
        level_refs.append(scratch[:LEVEL_FIELDS])
        scratch = scratch[LEVEL_FIELDS:]
    strip_refs, scratch = scratch[:LEVEL_FIELDS], scratch[LEVEL_FIELDS:]
    (ps, zs, rz, rcn, kp, k1cx, k1c, sk, sp, k1x, k1p, k1z, rc2, s2m, rs2, rx1, sb0, hx0, p1, p0, ruler,
     local_sem, send_sem, recv_sem) = scratch
    me_w = lax.axis_index("wide")
    me_n = lax.axis_index("narrow")

    def there(dw, dn):
        return (lax.rem(me_w + (dw + wide), wide), lax.rem(me_n + (dn + narrow), narrow))

    has = (me_w > 0, me_w < wide - 1)
    has_z = (me_n > 0, me_n < narrow - 1)
    reach = (jnp.minimum(me_w, REACH), jnp.minimum(wide - 1 - me_w, REACH))

    def for_far(first, body, last=REACH):
        for side in range(2):
            sign = 2 * side - 1

            def step(k, carry):
                body(REACH + sign * k, sign * k)
                return carry

            lax.fori_loop(first, jnp.minimum(reach[side], last) + 1, step, 0)

    def for_all_far(body):
        inner = reach[0] + reach[1] == 2 * REACH

        @pl.when(inner)
        def straight():
            for k in range(REACH, 0, -1):
                for sign in (-1, 1):
                    body(REACH + sign * k, sign * k)

        pl.when(jnp.logical_not(inner))(functools.partial(for_far, 1, body))

    def for_sides(body):
        for side in range(2):
            pl.when(has[side])(functools.partial(body, side, 2 * side - 1))

    def for_sides_z(body):
        for side in range(2):
            pl.when(has_z[side])(functools.partial(body, side, 2 * side - 1))

    def for_corners(body):
        for side in range(2):
            for side_z in range(2):
                pl.when(has[side] & has_z[side_z])(
                    functools.partial(body, side, side_z, 2 * side - 1, 2 * side_z - 1)
                )

    @pl.when((me_n == 0) | (me_n == narrow - 1))
    def clear_z():
        for ref in (rz, rcn, k1c, k1z, k1p):
            ref[...] = jnp.zeros(ref.shape, F32)

    @pl.when((me_w < REACH) | (me_w >= wide - REACH))
    def clear():
        def zero(ref):
            ref[...] = jnp.zeros(ref.shape, F32)

        for ref in (rcn, rx1, hx0, rc2, rs2, k1cx, k1c, k1x, k1p):
            zero(ref)
        for side in range(2):
            for ref in level_refs[0][:2]:
                zero(ref.at[0, pl.ds(12 * side, 4)])
            zero(level_refs[1][0].at[0, 13 * side])

    def if_reach(least, body):
        for side in range(2):
            pl.when(reach[side] >= least)(functools.partial(body, side, 2 * side - 1))

    barrier = pltpu.get_barrier_semaphore()

    def greet(dw, dn):
        pl.semaphore_signal(barrier, inc=1, device_id=there(dw, dn), device_id_type=MESH_ID)

    for_far(1, lambda slot, dw: greet(dw, 0), HALF_REACH)
    for_sides_z(lambda side, dn: greet(0, dn))
    for_corners(lambda side, side_z, dw, dn: greet(dw, dn))

    c0, s0 = level_refs[0][0], level_refs[0][1]
    load_c = pltpu.make_async_copy(coef, c0.at[0, pl.ds(4, 8)], local_sem.at[0])
    load_s = pltpu.make_async_copy(rhs, s0.at[0, pl.ds(4, 8)], local_sem.at[1])
    load_c.start()
    load_s.start()
    beside_x = jnp.where(has[0], 1, 0) + jnp.where(has[1], 1, 0)
    beside_z = jnp.where(has_z[0], 1, 0) + jnp.where(has_z[1], 1, 0)
    greeted = beside_z + beside_x * beside_z
    for side in range(2):
        greeted = greeted + jnp.minimum(reach[side], HALF_REACH)

    left = jnp.where(me_n > 0, 1.0, 0.0).astype(F32)
    right = jnp.where(me_n < narrow - 1, 1.0, 0.0).astype(F32)

    def lanes(rows):
        return lax.broadcasted_iota(jnp.int32, (rows, LANES), 1)

    def edges(rows, until, low, since, high):
        at = lanes(rows)
        return jnp.where(at < until, low, jnp.where(at >= since, high, 0.0))

    def centred(rows):
        at = lanes(rows)
        return jnp.where((at >= 32) & (at < 96), 1.0, edges(rows, 32, left, 96, right))

    level_0 = Level(level_refs[0], 1.0, 32, 1, 1, 8 * me_w - 4, 8 * wide, [None])
    strips = Strips(strip_refs, 8 * me_w - 4, 8 * wide, left, right)
    level_1 = Level(
        level_refs[1], 0.25, 16, 1, 1, 4 * me_w - 5, 4 * wide, [centred(16), edges(16, 32, right, 96, left)]
    )
    level_2 = Level(level_refs[2], 0.0625, 8, 1, 2, 2 * me_w - 16, 2 * wide, [centred(8)])
    level_3 = Level(level_refs[3], 0.015625, 8, 2, 4, me_w - 7, wide, [centred(8)])

    sent = [0] * SENDERS

    def send(group, src, dst, dw, dn, rows, sender):
        if isinstance(sender, int):
            sent[sender] += rows
        pltpu.make_async_remote_copy(
            src_ref=src, dst_ref=dst, send_sem=send_sem.at[sender], recv_sem=recv_sem.at[group],
            device_id=there(dw, dn), device_id_type=MESH_ID,
        ).start()

    def ruled(rows, group, sender):
        span = ruler.at[pl.ds(0, rows)]
        return pltpu.make_async_remote_copy(
            src_ref=span, dst_ref=span, send_sem=send_sem.at[sender], recv_sem=recv_sem.at[group],
            device_id=there(0, 1), device_id_type=MESH_ID,
        )

    def receive(group, rows):
        ruled(rows, group, 0).wait_recv()

    def receive_sides(group, rows):
        for_sides(lambda side, dw: receive(group + side, rows))

    def receive_sides_z(group, rows):
        for_sides_z(lambda side, dn: receive(group + side, rows))

    def receive_corners(group, rows):
        for_corners(lambda side, side_z, dw, dn: receive(group + 2 * side + side_z, rows))

    def receive_far(group, last=REACH):
        for_far(1, lambda slot, dw: receive(group + slot, 8), last)

    def sends_done(sender):
        ruled(sent[sender], 0, sender).wait_send()

    from_z, from_s1z = 0, 2
    from_c_corner, from_k_corner, from_s1_corner = 4, 8, 12
    from_c, from_s, from_s_next, from_k, from_s1, from_c1b, from_x0, from_x1 = range(16, 32, 2)
    from_four = 32
    from_c2 = 34
    from_s2 = from_c2 + 2 * REACH + 1
    sender_x, sender_four, sender_z = range(0, 6, 2)
    sender_corner, sender_c2, sender_far = 6, 10, 10 + 2 * REACH + 1

    def restrict_0(ref):
        out = []
        for layer in range(4):
            total = None
            for dx in range(2):
                for dy in range(2):
                    term = ref[0, 4 + 2 * layer + dx, pl.ds(dy, 16, stride=2), :]
                    total = term if total is None else total + term
            total = total + pltpu.roll(total, LANES - 1, 1)
            out.append(0.125 * jnp.take_along_axis(total, (2 * lanes(16) + 64) % LANES, axis=1))
        return out

    odd_8 = lanes(8) % 2 == 1

    def pairs_1(ref):
        out = []
        for layer in range(2):
            total = None
            for dx in range(2):
                for dy in range(2):
                    term = ref[0, 5 + 2 * layer + dx, pl.ds(dy, 8, stride=2), :]
                    total = term if total is None else total + term
            total = total + jnp.where(odd_8, pltpu.roll(total, 1, 1), pltpu.roll(total, LANES - 1, 1))
            out.append(0.125 * total)
        return jnp.where(odd_8, out[1], out[0])

    def squeeze_1(layers, ref, row):
        for part in range(2):
            ref[pl.ds(row + 16 * part, 16), :] = jnp.where(lanes(16) < 64, layers[part], layers[part + 2])

    def squeeze_halves(first, second):
        low_quarter = lanes(16) % 64 < 32
        return (
            jnp.where(low_quarter, pltpu.roll(first, 96, 1), second),
            jnp.where(low_quarter, first, pltpu.roll(second, 32, 1)),
        )

    load_c.wait()
    own_c1 = restrict_0(c0)
    for half in range(2):
        strips.c[1 + half] = strips.own(c0, 1 + half)
    for side in range(2):
        squeeze_1(own_c1, zs.at[side], 32)
        for half in range(2):
            zs[side, pl.ds(16 * half, 8), :] = strips.give_halo(strips.c, 1 + half, side)
    load_s.wait()
    for half in range(2):
        strips.s[1 + half] = strips.own(s0, 1 + half)
    for side in range(2):
        for half in range(2):
            zs[side, pl.ds(16 * half + 8, 8), :] = strips.give_halo(strips.s, 1 + half, side)

    pl.semaphore_wait(barrier, greeted)

    @for_sides
    def send_faces(side, dw):
        for part in range(2):
            first = 2 * part if side == 0 else 2 - 2 * part
            src, dst = c0.at[0, pl.ds(4 + 4 * side + first, 2)], c0.at[0, pl.ds(12 - 12 * side + first, 2)]
            send(from_c + 1 - side, src, dst, dw, 0, 64, sender_x + side)

    @for_sides
    def send_nearest(side, dw):
        send(from_s + 1 - side, s0.at[0, 4 + 7 * side], s0.at[0, 12 - 9 * side], dw, 0, 32, sender_x + side)

    for_sides_z(
        lambda side, dn: send(from_z + 1 - side, zs.at[side], rz.at[1 - side], 0, dn, 64, sender_z + side)
    )

    def send_corner(group, src, dst, rows, side, side_z):
        at = 2 * side + side_z
        send(group + 3 - at, src, dst, 2 * side - 1, 2 * side_z - 1, rows, sender_corner + at)

    @for_corners
    def send_c_corner(side, side_z, dw, dn):
        src = zs.at[side_z, pl.ds(16 * side, 16)]
        send_corner(from_c_corner, src, rcn.at[1 - side, 1 - side_z], 16, side, side_z)

    @for_sides
    def send_s_next(side, dw):
        src = s0.at[0, pl.ds(5 + 4 * side, 2)]
        send(from_s_next + 1 - side, src, s0.at[0, pl.ds(13 - 12 * side, 2)], dw, 0, 64, sender_x + side)

    steps = cheb(3)
    sweep_a = (level_0.va, level_0.vb, 1, 1, steps[1], True)
    sweep_b = (level_0.vb, level_0.va, 1, 1, steps[2], False)
    level_0.setup(5, 10, 6, 1)
    level_0.start(5, 10, 6, 1, steps[0][1])
    over_layers(6, 9, 4, lambda at: level_0.sweep_at(at, *sweep_a))
    over_layers(7, 8, 2, lambda at: level_0.sweep_at(at, *sweep_b))

    def take_halos(field, ref, pack, got):
        rows = pl.ds(8 * field + (16 if pack == 2 else 0), 8)
        strips.take_halo(ref, pack, got[0, rows, :], got[1, rows, :])

    receive_sides_z(from_z, 64)
    for field, ref in enumerate((strips.c, strips.s)):
        for half in range(2):
            take_halos(field, ref, 1 + half, rz)

    def spread_1(ref, block):
        at_lane = lanes(16)
        low_half = at_lane < 64
        low_quarter = at_lane % 64 < 32
        for part in range(2):
            before, own, after = (block(dz, part) for dz in (-1, 0, 1))
            near = jnp.where(low_quarter, before, after)
            outer = jnp.where(low_quarter, after, before)
            own_r, near_r, outer_r = (pltpu.roll(t, 64, 1) for t in (own, near, outer))
            at = 5 + part
            for at, own_a, own_b, near_a, near_b, outer_a, outer_b in (
                (at, own, own_r, near, near_r, outer, outer_r),
                (at + 2, own_r, own, near_r, near, outer_r, outer),
            ):
                centre = jnp.where(low_half, own_a, own_b)
                ref[0, at] = jnp.where(at_lane < 32, near_a, jnp.where(at_lane < 96, centre, near_b))
                ref[1, at] = jnp.where(low_half, outer_a, outer_b)

    def coef_block(dz, part):
        rows = pl.ds(32 + 16 * part, 16)
        return zs[0, rows, :] if dz == 0 else rz[(1 + dz) // 2, rows, :]

    spread_1(level_1.c, coef_block)
    rc2[REACH] = pairs_1(level_1.c)

    for_far(
        1,
        lambda slot, dw: send(
            from_c2 + 2 * REACH - slot, rc2.at[REACH], rc2.at[2 * REACH - slot], dw, 0, 8, sender_c2 + slot
        ),
        HALF_REACH,
    )
    k1_own = zs.at[0, pl.ds(32, 32)]
    halves = squeeze_halves(zs[0, pl.ds(32, 16), :], zs[0, pl.ds(48, 16), :])
    at_lane = lanes(16)
    for side in range(2):
        near, far = (0, 3) if side == 0 else (3, 0)
        full = level_1.c[0, 5 + near]
        place = (32 * far + 31, 32 * far)
        cell = (64, 63)
        for side_z in range(2):
            moved = pltpu.roll(full, (place[side_z] - cell[side_z]) % LANES, 1)
            kp[side, side_z] = jnp.where(at_lane == place[side_z], moved, halves[side_z])
    for_sides(
        lambda side, dw: send(from_k + 1 - side, k1_own, k1cx.at[1 - side], dw, 0, 32, sender_x + side)
    )
    for_corners(
        lambda side, side_z, dw, dn: send_corner(
            from_k_corner, kp.at[side, side_z], k1c.at[1 - side, 1 - side_z], 16, side, side_z
        )
    )

    receive_sides(from_c, 128)
    receive_corners(from_c_corner, 16)
    for side in range(2):
        strips.c[3 * side] = strips.own(c0, 3 * side)
        take_halos(0, strips.c, 3 * side, rcn.at[side])
    level_0.setup_below(1, 1)
    over_sides(1, 11, 4, lambda at: level_0.setup_at(at, 1))
    strips.setup()
    receive_sides(from_s, 32)
    over_sides(3, 11, 2, lambda at: level_0.start_at(at, 1, steps[0][1]))
    over_sides(4, 10, 2, lambda at: level_0.sweep_at(at, *sweep_a))
    over_sides(5, 9, 2, lambda at: level_0.sweep_at(at, *sweep_b))
    over_layers(6, 9, 4, lambda at: level_0.residual_at(at, level_0.va, level_0.vb, 1))
    receive_sides(from_s_next, 64)
    for side in range(2):
        strips.s[3 * side] = strips.own(s0, 3 * side, range(1 - side, 4 - side))
        take_halos(1, strips.s, 3 * side, rcn.at[side])
    over_sides(1, 13, 2, lambda at: level_0.start_at(at, 1, steps[0][1]))
    strips.start(steps[0][1])
    over_sides(2, 12, 2, lambda at: level_0.sweep_at(at, *sweep_a))
    strips.sweep(strips.va, strips.vb, steps[1], fresh=True)
    over_sides(3, 11, 2, lambda at: level_0.sweep_at(at, *sweep_b))
    strips.sweep(strips.vb, strips.va, steps[2])
    over_sides(4, 10, 2, lambda at: level_0.residual_at(at, level_0.va, level_0.vb, 1))
    strips.residual(strips.va, strips.vb)
    for at in range(4, 12):
        level_0.vb[0, at] = strips.mend(level_0.vb[0, at], strips.vb, at)

    squeeze_1(restrict_0(level_0.vb), sk, 0)

    sp[0], sp[1] = squeeze_halves(sk[pl.ds(0, 16), :], sk[pl.ds(16, 16), :])

    for_sides(lambda side, dw: send(from_s1 + 1 - side, sk, k1x.at[1 - side], dw, 0, 32, sender_x + side))
    for_corners(
        lambda side, side_z, dw, dn: send_corner(
            from_s1_corner, sp.at[side_z], k1p.at[1 - side, 1 - side_z], 16, side, side_z
        )
    )
    for_sides_z(lambda side, dn: send(from_s1z + 1 - side, sk, k1z.at[1 - side], 0, dn, 32, sender_z + side))

    receive_far(from_c2, HALF_REACH)

    @functools.partial(if_reach, HALF_REACH)
    def send_four(side, sign):
        src, dst = rc2.at[pl.ds(9 - 5 * side, 4)], rc2.at[pl.ds(13 - 13 * side, 4)]
        send(from_four + 1 - side, src, dst, HALF_REACH * sign, 0, 32, sender_four + side)

    for at in range(3, 13):
        level_0.va[0, at] = strips.mend(level_0.va[0, at], strips.va, at)
    own_cell = (strips.lane() % 32 >= 8) & (strips.lane() % 32 < 24)
    for pack_at, layers in enumerate(((3,), range(4), range(4), (0,))):
        strips.va[pack_at] = jnp.where(own_cell, strips.own(level_0.va, pack_at, layers), strips.va[pack_at])
    for side in range(2):
        first = 9 if side == 0 else 5
        for layer in range(2):
            sb0[side, pl.ds(32 * layer, 32), :] = level_0.va[0, first + layer]
        packed = strips.va[2 - side]
        middle = (lanes(16) >= 32) & (lanes(16) < 96)
        sb0[side, pl.ds(64, 16), :] = jnp.where(middle, packed[:16], pltpu.roll(packed[16:], 64, 1))

    @for_sides
    def send_iterate_0(side, dw):
        send(from_x0 + 1 - side, sb0.at[1 - side], hx0.at[1 - side], dw, 0, 80, sender_x + side)

    def source_block(dz, part):
        rows = pl.ds(16 * part, 16)
        return sk[rows, :] if dz == 0 else k1z[(1 + dz) // 2, rows, :]

    def spread_beside(ref, blocks, packs):
        at_lane = lanes(16)
        low_half = at_lane < 64
        for side in range(2):
            for layer in range(4):
                own = blocks[side, pl.ds(16 * (layer % 2), 16), :]
                other = pltpu.roll(own, 64, 1)
                centre = jnp.where(low_half, own, other) if layer < 2 else jnp.where(low_half, other, own)
                before = pltpu.roll(packs[side, 0], (LANES - 32 * layer) % LANES, 1)
                after = pltpu.roll(packs[side, 1], (LANES + 96 - 32 * layer) % LANES, 1)
                ref[0, 1 + 8 * side + layer] = jnp.where(at_lane < 32, before, jnp.where(at_lane < 96, centre, after))

    receive_sides(from_k, 32)
    receive_corners(from_k_corner, 16)
    spread_beside(level_1.c, k1cx, k1c)
    for side in range(2):
        far = 3 if side == 1 else 0
        below, above = (pltpu.roll(k1c[side, side_z], (shift - 32 * far) % LANES, 1)
                        for side_z, shift in ((0, 127), (1, -31)))
        level_1.c[1, 4 + 5 * side] = jnp.where(lanes(16) < 64, above, below)

    @for_sides
    def send_coef_1(side, dw):
        send(from_c1b + 1 - side, level_1.c.at[0, 9 - 5 * side], level_1.c.at[0, 13 - 13 * side], dw, 0, 16, sender_x + side)

    level_1.setup_below(2, 1)
    over_sides(2, 10, 2, lambda at: level_1.setup_at(at, 1))
    over_layers(4, 9, 6, lambda at: level_1.setup_at(at, 2))

    receive_sides_z(from_s1z, 32)
    spread_1(level_1.s, source_block)
    receive_sides(from_s1, 32)
    receive_corners(from_s1_corner, 16)
    spread_beside(level_1.s, k1x, k1p)
    level_1.start(2, 11, 10, 1, steps[0][1])
    over_layers(5, 8, 4, lambda at: level_1.start_outer(at, steps[0][1]))
    over_sides(3, 9, 2, lambda at: level_1.sweep_at(at, level_1.va, level_1.vb, 1, 1, steps[1], True))
    over_layers(5, 8, 4, lambda at: level_1.sweep_at(at, level_1.va, level_1.vb, 2, 1, steps[1], True))
    level_1.sweep(level_1.vb, level_1.va, 4, 9, 6, 1, 1, steps[2])
    level_1.residual(level_1.va, level_1.vb, 5, 8, 4, 1)

    value = pairs_1(level_1.vb)
    s2m[...] = value
    rs2[REACH] = value

    for_all_far(
        lambda slot, dw: send(
            from_s2 + 2 * REACH - slot, s2m, rs2.at[2 * REACH - slot], dw, 0, 8, sender_far + slot
        )
    )

    @for_sides
    def send_iterate_1(side, dw):
        layers = level_1.va.at[0, pl.ds(6 - 2 * side, 4)]
        send(from_x1 + 1 - side, layers, rx1.at[1 - side], dw, 0, 64, sender_x + side)

    receive_sides(from_c1b, 16)
    level_1.setup_below(1, 1)
    over_sides(1, 12, 1, lambda at: level_1.setup_at(at, 1))

    def spread_2(ref, blocks):
        for block in range(2 * REACH + 1):
            packed = blocks[block]
            ref[0, 2 * block] = jnp.where(odd_8, pltpu.roll(packed, 1, 1), packed)
            ref[0, 2 * block + 1] = jnp.where(odd_8, packed, pltpu.roll(packed, LANES - 1, 1))

    def restrict_2(ref, at):
        total = ref[0, 2 * at + 2] + ref[0, 2 * at + 3]
        odd_row = lax.broadcasted_iota(jnp.int32, (8, LANES), 0) % 2 == 1
        total = total + jnp.where(odd_row, pltpu.roll(total, 1, 0), pltpu.roll(total, 7, 0))
        second = lanes(8) % 4 >= 2
        total = total + jnp.where(second, pltpu.roll(total, 2, 1), pltpu.roll(total, LANES - 2, 1))
        return 0.125 * total

    if_reach(HALF_REACH, lambda side, sign: receive(from_four + side, 32))
    spread_2(level_2.c, rc2)
    level_2.setup(1, 32, 16, 1)
    for at in range(15):
        level_3.c[0, at] = restrict_2(level_2.c, at)
    level_3.setup(1, 13, 13, 1)

    for_sides(lambda side, dw: sends_done(sender_x + side))
    for_sides_z(lambda side, dn: sends_done(sender_z + side))
    for_corners(lambda side, side_z, dw, dn: sends_done(sender_corner + 2 * side + side_z))
    if_reach(HALF_REACH, lambda side, sign: sends_done(sender_four + side))
    for_far(1, lambda slot, dw: ruled(8, 0, sender_c2 + slot).wait_send(), HALF_REACH)
    for_all_far(lambda slot, dw: ruled(8, 0, sender_far + slot).wait_send())

    for_all_far(lambda slot, dw: receive(from_s2 + slot, 8))
    spread_2(level_2.s, rs2)
    level_2.start(1, 32, 32, 1, steps[0][1])
    level_2.sweep(level_2.va, level_2.vb, 2, 31, 30, 1, 1, steps[1], fresh=True)
    level_2.sweep(level_2.vb, level_2.va, 3, 30, 28, 1, 1, steps[2])
    level_2.residual(level_2.va, level_2.vb, 4, 29, 26, 1)

    for at in range(1, 14):
        level_3.s[0, at] = restrict_2(level_2.vb, at)
    coarse = cheb(4)
    level_3.start(1, 13, 13, 1, coarse[0][1])
    level_3.sweep(level_3.va, level_3.vb, 2, 12, 11, 1, 1, coarse[1], fresh=True)
    level_3.sweep(level_3.vb, level_3.va, 3, 11, 9, 1, 1, coarse[2])
    level_3.sweep(level_3.va, level_3.vb, 4, 10, 7, 1, 1, coarse[3])

    for at in range(10, 24):
        level_2.vb[0, at] = level_2.va[0, at] + level_3.vb[0, (at - 2) // 2]
    level_2.sweep(level_2.vb, level_2.va, 11, 22, 12, 1, 1, steps[0], fresh=True)
    level_2.sweep(level_2.va, level_2.vb, 12, 21, 10, 1, 1, steps[1])
    level_2.sweep(level_2.vb, level_2.va, 13, 20, 8, 1, 1, steps[2])

    for at in range(8):
        value = level_2.va[0, 13 + at]
        for part in range(2):
            p1[at, pl.ds(part, 8, stride=2), :] = value
    receive_sides(from_x1, 64)
    for at in range(14):
        if 4 <= at <= 9:
            before = level_1.va[0, at]
        else:
            before = rx1[0, at] if at < 4 else rx1[1, at - 10]
        level_1.vb[0, at] = before + p1[(at + 1) // 2]
    level_1.sweep(level_1.vb, level_1.va, 1, 12, 12, 1, 1, steps[0], fresh=True)
    level_1.sweep(level_1.va, level_1.vb, 2, 11, 10, 1, 1, steps[1])
    level_1.sweep(level_1.vb, level_1.va, 3, 10, 8, 1, 1, steps[2])

    cell = lanes(16) % 32
    strip_lane = jnp.where(cell < 16, 28, 84) + cell // 2
    low_half = lanes(16) < 64
    fine = []
    for at in range(8):
        value = level_1.va[0, 3 + at]
        own = jnp.take_along_axis(value, lanes(16) // 2 + 32, axis=1)
        fine.append(jnp.take_along_axis(value, strip_lane, axis=1))
        for part in range(2):
            p0[at, pl.ds(part, 16, stride=2), :] = own
    for pack in range(4):
        value = jnp.where(low_half, fine[2 * pack], fine[2 * pack + 1])
        for part in range(2):
            ps[pack, pl.ds(part, 16, stride=2), :] = value
    receive_sides(from_x0, 80)
    for side in range(2):
        for layer in range(2):
            at = (1 if side == 0 else 13) + layer
            level_0.vb[0, at] = hx0[side, pl.ds(32 * layer, 32), :] + p0[at // 2]
        packed = hx0[side, pl.ds(64, 16), :]
        layer = lanes(16) // 32
        for part, value in enumerate((packed, pltpu.roll(packed, 64, 1))):
            rows = pl.ds(16 * part, 16)
            own = jnp.where(layer == (3 if side == 0 else 0), strips.va[3 * side, rows, :], 0.0)
            value = jnp.where((layer == 1) | (layer == 2), value, own)
            strips.vb[3 * side, rows, :] = value + ps[3 * side, rows, :]
    for pack in (1, 2):
        strips.vb[pack] = strips.va[pack] + ps[pack]

    def correct(at):
        level_0.vb[0, at] = level_0.va[0, at] + p0[at // 2]

    over_layers(3, 12, 10, correct)
    level_0.sweep(level_0.vb, level_0.va, 2, 13, 12, 1, 1, steps[0], fresh=True)
    strips.sweep(strips.vb, strips.va, steps[0], fresh=True)
    level_0.sweep(level_0.va, level_0.vb, 3, 12, 10, 1, 1, steps[1])
    strips.sweep(strips.va, strips.vb, steps[1])
    strips.sweep(strips.vb, strips.va, steps[2])
    inner = (strips.lane() >= 4) & (strips.lane() < LANES - 4)
    for at in range(4, 12):
        kept_here, added_here = level_0.last_at(at, level_0.vb, level_0.va, steps[2])
        kept[at - 4] = strips.mend(kept_here, strips.va, at)
        added[at - 4] = jnp.where(inner, added_here, 0.0)


def per_device(right_side, conductivity, wide, narrow):
    brick = (8, 32, LANES)
    scratch = []
    for shape in LEVEL_SHAPES:
        scratch += [pltpu.VMEM(shape, F32)] * LEVEL_FIELDS
    scratch += [pltpu.VMEM((4, 32, LANES), F32)] * LEVEL_FIELDS
    shapes = [
        (4, 32, LANES),
        (2, 64, LANES), (2, 64, LANES), (2, 2, 16, LANES),
        (2, 2, 16, LANES), (2, 32, LANES), (2, 2, 16, LANES),
        (32, LANES), (2, 16, LANES), (2, 32, LANES), (2, 2, 16, LANES), (2, 32, LANES),
        (2 * REACH + 1, 8, LANES), (8, LANES), (2 * REACH + 1, 8, LANES),
        (2, 4, 16, LANES),
        (2, 80, LANES), (2, 80, LANES),
        (8, 16, LANES), (8, 32, LANES),
        (RULER, LANES),
    ]
    scratch += [pltpu.VMEM(shape, F32) for shape in shapes]
    scratch += [pltpu.SemaphoreType.DMA((2,)), pltpu.SemaphoreType.DMA((SENDERS,)), pltpu.SemaphoreType.DMA((GROUPS,))]
    kept, added = pl.pallas_call(
        functools.partial(kernel, wide, narrow),
        out_shape=[jax.ShapeDtypeStruct(brick, F32)] * 2,
        in_specs=[pl.BlockSpec(memory_space=pltpu.HBM)] * 2,
        out_specs=[pl.BlockSpec(memory_space=pltpu.VMEM)] * 2,
        scratch_shapes=scratch,
        compiler_params=pltpu.CompilerParams(
            collective_id=0, has_side_effects=True, vmem_limit_bytes=32 * 1024 * 1024
        ),
    )(pltpu.with_memory_space_constraint(right_side, pltpu.HBM), pltpu.with_memory_space_constraint(conductivity, pltpu.HBM))
    return kept + added


def solution(mesh):
    spec = P("wide", None, "narrow")
    body = functools.partial(per_device, wide=mesh.shape["wide"], narrow=mesh.shape["narrow"])
    return jax.shard_map(body, mesh=mesh, in_specs=(spec, spec), out_specs=spec, check_vma=False)
```

```python
import functools

import jax
import jax.numpy as jnp
from jax import lax
from jax.experimental import pallas as pl
from jax.experimental.pallas import tpu as pltpu
from jax.sharding import PartitionSpec as P

CENTER = 1.125
HALF = 0.875
LANES = 128
REACH = 8
HALF_REACH = 4
F32 = jnp.float32
MESH_ID = pl.DeviceIdType.MESH


def cheb(sweeps):
    sigma = CENTER / HALF
    steps = [(0.0, 1.0 / CENTER)]
    ratio = 1.0 / sigma
    for _ in range(sweeps - 1):
        ratio_next = 1.0 / (2.0 * sigma - ratio)
        steps.append((ratio_next * ratio, 2.0 * ratio_next / HALF))
        ratio = ratio_next
    return steps


def over_sides(first, second, count, body):
    for base in (first, second):
        for at in range(count):
            body(base + at)


def over_layers(low, high, unroll, body):
    count = high - low + 1
    if count == unroll:
        for at in range(low, high + 1):
            body(at)
        return

    def block(step, carry):
        for at in range(unroll):
            body(low + step * unroll + at)
        return carry

    lax.fori_loop(0, count // unroll, block, 0)


class Level:
    def __init__(self, refs, scale, rows, row_step, lane_step, base, extent, lane_mask):
        self.c, self.s, self.cx, self.cy, self.cz, self.iv, self.dg, self.va, self.vb = refs
        self.half = 0.5 * scale
        self.rows, self.row_step, self.lane_step = rows, row_step, lane_step
        self.base, self.extent, self.lane_mask = base, extent, lane_mask

    def inside(self, at):
        where_x = self.base + at
        return jnp.where((where_x >= 0) & (where_x < self.extent), 1.0, 0.0).astype(F32)

    def lane(self):
        return lax.broadcasted_iota(jnp.int32, (self.rows, LANES), 1)

    def row(self):
        return lax.broadcasted_iota(jnp.int32, (self.rows, LANES), 0)

    def y_up(self, tile):
        return pltpu.roll(tile, self.rows - self.row_step, 0)

    def y_down(self, tile):
        return pltpu.roll(tile, self.row_step, 0)

    def turned(self, tiles, shift, edge, count):
        out = [pltpu.roll(t, shift, 1) for t in tiles]
        if len(tiles) == 1:
            return out
        at_edge = self.lane() == edge
        return [jnp.where(at_edge, out[1 - k], out[k]) for k in range(count)]

    def z_up(self, tiles, count):
        return self.turned(tiles, LANES - self.lane_step, LANES - 1, count)

    def z_down(self, tiles, count):
        return self.turned(tiles, self.lane_step, 0, count)

    def masked(self, at, tiles):
        keep = self.inside(at) * self.half
        out = []
        for k in range(tiles):
            mask = self.lane_mask[k]
            out.append(self.c[k, at] * (keep if mask is None else mask * keep))
        return out

    def setup_below(self, low, tiles):
        first, second = self.masked(low - 1, tiles), self.masked(low, tiles)
        for k in range(tiles):
            self.cx[k, low - 1] = first[k] + second[k]

    def setup_at(self, at, tiles):
        before, here, after = self.masked(at - 1, tiles), self.masked(at, tiles), self.masked(at + 1, tiles)
        inside = self.inside(at)
        top = self.row() >= self.rows - self.row_step
        bottom = self.row() < self.row_step
        z_up, z_down = self.z_up(here, tiles), self.z_down(here, tiles)
        for k in range(tiles):
            own = here[k]
            x_low = before[k] + own
            x_high = own + after[k]
            y_low = own + jnp.where(bottom, 0.0, self.y_down(own))
            y_high = own + jnp.where(top, 0.0, self.y_up(own))
            z_low = own + z_down[k]
            z_high = own + z_up[k]
            diagonal = x_low + x_high + y_low + y_high + z_low + z_high
            keep = inside if self.lane_mask[k] is None else self.lane_mask[k] * inside
            self.cx[k, at] = x_high
            self.cy[k, at] = jnp.where(top, 0.0, y_high)
            self.cz[k, at] = z_high
            if k == 0:
                self.dg[0, at] = diagonal
            self.iv[k, at] = jnp.where(jnp.full_like(own, 0.0) + keep > 0.5, 1.0 / diagonal, 0.0)

    def setup(self, low, high, unroll, tiles):
        self.setup_below(low, tiles)
        over_layers(low, high, unroll, lambda at: self.setup_at(at, tiles))

    def start_at(self, at, tiles, beta):
        for k in range(tiles):
            self.va[k, at] = self.s[k, at] * self.iv[k, at] * beta

    def start_outer(self, at, beta):
        self.va[1, at] = self.s[1, at] * self.iv[1, at] * beta

    def start(self, low, high, unroll, tiles, beta):
        over_layers(low, high, unroll, lambda at: self.start_at(at, tiles, beta))

    def around(self, field, at, tiles, count):
        here = [field[k, at] for k in range(tiles)]
        cz = [self.cz[k, at] for k in range(tiles)]
        z_up = self.z_up(here, count)
        z_down = self.z_down([cz[k] * here[k] for k in range(tiles)], count)
        sums = []
        for k in range(count):
            cy = self.cy[k, at]
            total = self.cx[k, at] * field[k, at + 1] + self.cx[k, at - 1] * field[k, at - 1]
            total = total + (cy * self.y_up(here[k]) + self.y_down(cy * here[k]))
            total = total + (cz[k] * z_up[k] + z_down[k])
            sums.append(total + self.s[k, at])
        return here, sums

    def sweep_at(self, at, field, result, tiles, count, step, fresh):
        alpha, beta = step
        here, sums = self.around(field, at, tiles, count)
        for k in range(count):
            kept = (1.0 + alpha - beta) * here[k]
            if not fresh:
                kept = kept - alpha * result[k, at]
            result[k, at] = kept + (beta * self.iv[k, at]) * sums[k]

    def sweep(self, field, result, low, high, unroll, tiles, count, step, fresh=False):
        over_layers(low, high, unroll, lambda at: self.sweep_at(at, field, result, tiles, count, step, fresh))

    def residual_at(self, at, field, result, tiles):
        here, sums = self.around(field, at, tiles, 1)
        result[0, at] = sums[0] - self.dg[0, at] * here[0]

    def residual(self, field, result, low, high, unroll, tiles):
        over_layers(low, high, unroll, lambda at: self.residual_at(at, field, result, tiles))

    def last_at(self, at, field, older, step):
        alpha, beta = step
        here, sums = self.around(field, at, 1, 1)
        return (1.0 + alpha - beta) * here[0] - alpha * older[0, at], (beta * self.iv[0, at]) * sums[0]


class Strips:
    def __init__(self, refs, base, extent, left, right):
        self.c, self.s, self.cx, self.cy, self.cz, self.iv, self.dg, self.va, self.vb = refs
        self.base, self.extent, self.left, self.right = base, extent, left, right

    def lane(self):
        return lax.broadcasted_iota(jnp.int32, (32, LANES), 1)

    def mask(self, pack):
        where_x = self.base + 4 * pack + self.lane() // 32
        cell = self.lane() % 32
        keep = jnp.where(cell < 8, self.left, jnp.where(cell >= 24, self.right, 1.0))
        return jnp.where((where_x >= 0) & (where_x < self.extent), keep, 0.0)

    def x_up(self, tiles):
        turned = [pltpu.roll(t, LANES - 32, 1) for t in tiles]
        return [jnp.where(self.lane() < LANES - 32, turned[p], turned[min(p + 1, 3)]) for p in range(4)]

    def x_down(self, tiles):
        turned = [pltpu.roll(t, 32, 1) for t in tiles]
        return [jnp.where(self.lane() >= 32, turned[p], turned[max(p - 1, 0)]) for p in range(4)]

    def setup(self):
        row = lax.broadcasted_iota(jnp.int32, (32, LANES), 0)
        top, bottom = row == 31, row == 0
        masks = [self.mask(p) for p in range(4)]
        own = [self.c[p] * (0.5 * masks[p]) for p in range(4)]
        above = self.x_up(own)
        x_high = [own[p] + above[p] for p in range(4)]
        x_low = self.x_down(x_high)
        for p in range(4):
            y_high = own[p] + jnp.where(top, 0.0, pltpu.roll(own[p], 31, 0))
            y_low = jnp.where(bottom, own[p], pltpu.roll(y_high, 1, 0))
            z_high = own[p] + pltpu.roll(own[p], LANES - 1, 1)
            z_low = pltpu.roll(z_high, 1, 1)
            diagonal = x_low[p] + x_high[p] + y_low + y_high + z_low + z_high
            self.cx[p] = x_high[p]
            self.cy[p] = jnp.where(top, 0.0, y_high)
            self.cz[p] = z_high
            self.dg[p] = diagonal
            self.iv[p] = jnp.where(masks[p] > 0.5, 1.0 / diagonal, 0.0)

    def start(self, beta):
        for p in range(4):
            self.va[p] = self.s[p] * self.iv[p] * beta

    def around(self, field):
        here = [field[p] for p in range(4)]
        cx = [self.cx[p] for p in range(4)]
        x_up = self.x_up(here)
        x_down = self.x_down([cx[p] * here[p] for p in range(4)])
        sums = []
        for p in range(4):
            cy, cz = self.cy[p], self.cz[p]
            total = cx[p] * x_up[p] + x_down[p]
            total = total + (cy * pltpu.roll(here[p], 31, 0) + pltpu.roll(cy * here[p], 1, 0))
            total = total + (cz * pltpu.roll(here[p], LANES - 1, 1) + pltpu.roll(cz * here[p], 1, 1))
            sums.append(total + self.s[p])
        return here, sums

    def sweep(self, field, result, step, fresh=False):
        alpha, beta = step
        here, sums = self.around(field)
        for p in range(4):
            kept = (1.0 + alpha - beta) * here[p]
            if not fresh:
                kept = kept - alpha * result[p]
            result[p] = kept + (beta * self.iv[p]) * sums[p]

    def residual(self, field, result):
        here, sums = self.around(field)
        for p in range(4):
            result[p] = sums[p] - self.dg[p] * here[p]

    def own(self, ref, pack, layers=range(4)):
        cell = self.lane() % 32
        packed = jnp.zeros((32, LANES), F32)
        for layer in layers:
            tile = ref[0, 4 * pack + layer]
            first = pltpu.roll(tile, 32 * layer + 8, 1)
            last = pltpu.roll(tile, (32 * layer + 24) % LANES, 1)
            packed = jnp.where(self.lane() // 32 == layer, jnp.where(cell < 16, first, last), packed)
        return packed

    def take_halo(self, ref, pack, from_left, from_right):
        cell = lax.broadcasted_iota(jnp.int32, (8, LANES), 1) % 32
        for part in range(4):
            rows = pl.ds(8 * part, 8)
            below = pltpu.roll(from_left, (LANES - 8 * part) % LANES, 1)
            above = pltpu.roll(from_right, 24 - 8 * part, 1) if part < 3 else from_right
            ref[pack, rows, :] = jnp.where(cell < 8, below, jnp.where(cell >= 24, above, ref[pack, rows, :]))

    def give_halo(self, ref, pack, side):
        cell = lax.broadcasted_iota(jnp.int32, (8, LANES), 1) % 32
        packed = None
        for part in range(4):
            shift = (8 * part - 8 - 8 * side) % LANES
            tile = ref[pack, pl.ds(8 * part, 8), :]
            tile = pltpu.roll(tile, shift, 1) if shift else tile
            packed = tile if part == 0 else jnp.where(cell // 8 == part, tile, packed)
        return packed

    def mend(self, tile, ref, at):
        packed, layer = ref[at // 4], at % 4
        first = pltpu.roll(packed, (LANES - 32 * layer - 8) % LANES, 1)
        last = pltpu.roll(packed, (LANES + 104 - 32 * layer) % LANES, 1)
        return jnp.where(self.lane() < 4, first, jnp.where(self.lane() >= LANES - 4, last, tile))


LEVEL_FIELDS = 9
LEVEL_SHAPES = ((1, 16, 32, LANES), (2, 14, 16, LANES), (1, 34, 8, LANES), (1, 15, 8, LANES))
RULER = 1024
SENDERS = 10 + 2 * (2 * REACH + 1)
GROUPS = 34 + 2 * (2 * REACH + 1)


def kernel(wide, narrow, rhs, coef, kept, added, *scratch):
    scratch = list(scratch)
    level_refs = []
    for _ in range(4):
        level_refs.append(scratch[:LEVEL_FIELDS])
        scratch = scratch[LEVEL_FIELDS:]
    strip_refs, scratch = scratch[:LEVEL_FIELDS], scratch[LEVEL_FIELDS:]
    (ps, zs, rz, rcn, kp, k1cx, k1c, sk, sp, k1x, k1p, k1z, rc2, s2m, rs2, rx1, sb0, hx0, p1, p0, ruler,
     local_sem, send_sem, recv_sem) = scratch
    me_w = lax.axis_index("wide")
    me_n = lax.axis_index("narrow")

    def there(dw, dn):
        return (lax.rem(me_w + (dw + wide), wide), lax.rem(me_n + (dn + narrow), narrow))

    has = (me_w > 0, me_w < wide - 1)
    has_z = (me_n > 0, me_n < narrow - 1)
    reach = (jnp.minimum(me_w, REACH), jnp.minimum(wide - 1 - me_w, REACH))

    def for_far(first, body, last=REACH):
        for side in range(2):
            sign = 2 * side - 1

            def step(k, carry):
                body(REACH + sign * k, sign * k)
                return carry

            lax.fori_loop(first, jnp.minimum(reach[side], last) + 1, step, 0)

    def for_all_far(body):
        inner = reach[0] + reach[1] == 2 * REACH

        @pl.when(inner)
        def straight():
            for k in range(REACH, 0, -1):
                for sign in (-1, 1):
                    body(REACH + sign * k, sign * k)

        pl.when(jnp.logical_not(inner))(functools.partial(for_far, 1, body))

    def for_sides(body):
        for side in range(2):
            pl.when(has[side])(functools.partial(body, side, 2 * side - 1))

    def for_sides_z(body):
        for side in range(2):
            pl.when(has_z[side])(functools.partial(body, side, 2 * side - 1))

    def for_corners(body):
        for side in range(2):
            for side_z in range(2):
                pl.when(has[side] & has_z[side_z])(
                    functools.partial(body, side, side_z, 2 * side - 1, 2 * side_z - 1)
                )

    @pl.when((me_n == 0) | (me_n == narrow - 1))
    def clear_z():
        for ref in (rz, rcn, k1c, k1z, k1p):
            ref[...] = jnp.zeros(ref.shape, F32)

    @pl.when((me_w < REACH) | (me_w >= wide - REACH))
    def clear():
        def zero(ref):
            ref[...] = jnp.zeros(ref.shape, F32)

        for ref in (rcn, rx1, hx0, rc2, rs2, k1cx, k1c, k1x, k1p):
            zero(ref)
        for side in range(2):
            for ref in level_refs[0][:2]:
                zero(ref.at[0, pl.ds(12 * side, 4)])
            zero(level_refs[1][0].at[0, 13 * side])

    def if_reach(least, body):
        for side in range(2):
            pl.when(reach[side] >= least)(functools.partial(body, side, 2 * side - 1))

    barrier = pltpu.get_barrier_semaphore()

    def greet(dw, dn):
        pl.semaphore_signal(barrier, inc=1, device_id=there(dw, dn), device_id_type=MESH_ID)

    for_far(1, lambda slot, dw: greet(dw, 0), HALF_REACH)
    for_sides_z(lambda side, dn: greet(0, dn))
    for_corners(lambda side, side_z, dw, dn: greet(dw, dn))

    c0, s0 = level_refs[0][0], level_refs[0][1]
    load_c = pltpu.make_async_copy(coef, c0.at[0, pl.ds(4, 8)], local_sem.at[0])
    load_s = pltpu.make_async_copy(rhs, s0.at[0, pl.ds(4, 8)], local_sem.at[1])
    load_c.start()
    load_s.start()
    beside_x = jnp.where(has[0], 1, 0) + jnp.where(has[1], 1, 0)
    beside_z = jnp.where(has_z[0], 1, 0) + jnp.where(has_z[1], 1, 0)
    greeted = beside_z + beside_x * beside_z
    for side in range(2):
        greeted = greeted + jnp.minimum(reach[side], HALF_REACH)

    left = jnp.where(me_n > 0, 1.0, 0.0).astype(F32)
    right = jnp.where(me_n < narrow - 1, 1.0, 0.0).astype(F32)

    def lanes(rows):
        return lax.broadcasted_iota(jnp.int32, (rows, LANES), 1)

    def edges(rows, until, low, since, high):
        at = lanes(rows)
        return jnp.where(at < until, low, jnp.where(at >= since, high, 0.0))

    def centred(rows):
        at = lanes(rows)
        return jnp.where((at >= 32) & (at < 96), 1.0, edges(rows, 32, left, 96, right))

    level_0 = Level(level_refs[0], 1.0, 32, 1, 1, 8 * me_w - 4, 8 * wide, [None])
    strips = Strips(strip_refs, 8 * me_w - 4, 8 * wide, left, right)
    level_1 = Level(
        level_refs[1], 0.25, 16, 1, 1, 4 * me_w - 5, 4 * wide, [centred(16), edges(16, 32, right, 96, left)]
    )
    level_2 = Level(level_refs[2], 0.0625, 8, 1, 2, 2 * me_w - 16, 2 * wide, [centred(8)])
    level_3 = Level(level_refs[3], 0.015625, 8, 2, 4, me_w - 7, wide, [centred(8)])

    sent = [0] * SENDERS

    def send(group, src, dst, dw, dn, rows, sender):
        if isinstance(sender, int):
            sent[sender] += rows
        pltpu.make_async_remote_copy(
            src_ref=src, dst_ref=dst, send_sem=send_sem.at[sender], recv_sem=recv_sem.at[group],
            device_id=there(dw, dn), device_id_type=MESH_ID,
        ).start()

    def ruled(rows, group, sender):
        span = ruler.at[pl.ds(0, rows)]
        return pltpu.make_async_remote_copy(
            src_ref=span, dst_ref=span, send_sem=send_sem.at[sender], recv_sem=recv_sem.at[group],
            device_id=there(0, 1), device_id_type=MESH_ID,
        )

    def receive(group, rows):
        ruled(rows, group, 0).wait_recv()

    def receive_sides(group, rows):
        for_sides(lambda side, dw: receive(group + side, rows))

    def receive_sides_z(group, rows):
        for_sides_z(lambda side, dn: receive(group + side, rows))

    def receive_corners(group, rows):
        for_corners(lambda side, side_z, dw, dn: receive(group + 2 * side + side_z, rows))

    def receive_far(group, last=REACH):
        for_far(1, lambda slot, dw: receive(group + slot, 8), last)

    def sends_done(sender):
        ruled(sent[sender], 0, sender).wait_send()

    from_z, from_s1z = 0, 2
    from_c_corner, from_k_corner, from_s1_corner = 4, 8, 12
    from_c, from_s, from_s_next, from_k, from_s1, from_c1b, from_x0, from_x1 = range(16, 32, 2)
    from_four = 32
    from_c2 = 34
    from_s2 = from_c2 + 2 * REACH + 1
    sender_x, sender_four, sender_z = range(0, 6, 2)
    sender_corner, sender_c2, sender_far = 6, 10, 10 + 2 * REACH + 1

    def restrict_0(ref):
        out = []
        for layer in range(4):
            total = None
            for dx in range(2):
                for dy in range(2):
                    term = ref[0, 4 + 2 * layer + dx, pl.ds(dy, 16, stride=2), :]
                    total = term if total is None else total + term
            total = total + pltpu.roll(total, LANES - 1, 1)
            out.append(0.125 * jnp.take_along_axis(total, (2 * lanes(16) + 64) % LANES, axis=1))
        return out

    odd_8 = lanes(8) % 2 == 1

    def pairs_1(ref):
        out = []
        for layer in range(2):
            total = None
            for dx in range(2):
                for dy in range(2):
                    term = ref[0, 5 + 2 * layer + dx, pl.ds(dy, 8, stride=2), :]
                    total = term if total is None else total + term
            total = total + jnp.where(odd_8, pltpu.roll(total, 1, 1), pltpu.roll(total, LANES - 1, 1))
            out.append(0.125 * total)
        return jnp.where(odd_8, out[1], out[0])

    def squeeze_1(layers, ref, row):
        for part in range(2):
            ref[pl.ds(row + 16 * part, 16), :] = jnp.where(lanes(16) < 64, layers[part], layers[part + 2])

    def squeeze_halves(first, second):
        low_quarter = lanes(16) % 64 < 32
        return (
            jnp.where(low_quarter, pltpu.roll(first, 96, 1), second),
            jnp.where(low_quarter, first, pltpu.roll(second, 32, 1)),
        )

    load_c.wait()
    own_c1 = restrict_0(c0)
    for half in range(2):
        strips.c[1 + half] = strips.own(c0, 1 + half)
    for side in range(2):
        squeeze_1(own_c1, zs.at[side], 32)
        for half in range(2):
            zs[side, pl.ds(16 * half, 8), :] = strips.give_halo(strips.c, 1 + half, side)
    load_s.wait()
    for half in range(2):
        strips.s[1 + half] = strips.own(s0, 1 + half)
    for side in range(2):
        for half in range(2):
            zs[side, pl.ds(16 * half + 8, 8), :] = strips.give_halo(strips.s, 1 + half, side)

    pl.semaphore_wait(barrier, greeted)

    @for_sides
    def send_faces(side, dw):
        for part in range(2):
            first = 2 * part if side == 0 else 2 - 2 * part
            src, dst = c0.at[0, pl.ds(4 + 4 * side + first, 2)], c0.at[0, pl.ds(12 - 12 * side + first, 2)]
            send(from_c + 1 - side, src, dst, dw, 0, 64, sender_x + side)

    @for_sides
    def send_nearest(side, dw):
        send(from_s + 1 - side, s0.at[0, 4 + 7 * side], s0.at[0, 12 - 9 * side], dw, 0, 32, sender_x + side)

    for_sides_z(
        lambda side, dn: send(from_z + 1 - side, zs.at[side], rz.at[1 - side], 0, dn, 64, sender_z + side)
    )

    def send_corner(group, src, dst, rows, side, side_z):
        at = 2 * side + side_z
        send(group + 3 - at, src, dst, 2 * side - 1, 2 * side_z - 1, rows, sender_corner + at)

    @for_corners
    def send_c_corner(side, side_z, dw, dn):
        src = zs.at[side_z, pl.ds(16 * side, 16)]
        send_corner(from_c_corner, src, rcn.at[1 - side, 1 - side_z], 16, side, side_z)

    @for_sides
    def send_s_next(side, dw):
        for part in range(2):
            layer = part if side == 0 else 1 - part
            src, dst = s0.at[0, 5 + 4 * side + layer], s0.at[0, 13 - 12 * side + layer]
            send(from_s_next + 1 - side, src, dst, dw, 0, 32, sender_x + side)

    steps = cheb(3)
    sweep_a = (level_0.va, level_0.vb, 1, 1, steps[1], True)
    sweep_b = (level_0.vb, level_0.va, 1, 1, steps[2], False)
    level_0.setup(5, 10, 6, 1)
    level_0.start(5, 10, 6, 1, steps[0][1])
    over_layers(6, 9, 4, lambda at: level_0.sweep_at(at, *sweep_a))
    over_layers(7, 8, 2, lambda at: level_0.sweep_at(at, *sweep_b))

    def take_halos(field, ref, pack, got):
        rows = pl.ds(8 * field + (16 if pack == 2 else 0), 8)
        strips.take_halo(ref, pack, got[0, rows, :], got[1, rows, :])

    receive_sides_z(from_z, 64)
    for field, ref in enumerate((strips.c, strips.s)):
        for half in range(2):
            take_halos(field, ref, 1 + half, rz)

    def spread_1(ref, block):
        at_lane = lanes(16)
        low_half = at_lane < 64
        low_quarter = at_lane % 64 < 32
        for part in range(2):
            before, own, after = (block(dz, part) for dz in (-1, 0, 1))
            near = jnp.where(low_quarter, before, after)
            outer = jnp.where(low_quarter, after, before)
            own_r, near_r, outer_r = (pltpu.roll(t, 64, 1) for t in (own, near, outer))
            at = 5 + part
            for at, own_a, own_b, near_a, near_b, outer_a, outer_b in (
                (at, own, own_r, near, near_r, outer, outer_r),
                (at + 2, own_r, own, near_r, near, outer_r, outer),
            ):
                centre = jnp.where(low_half, own_a, own_b)
                ref[0, at] = jnp.where(at_lane < 32, near_a, jnp.where(at_lane < 96, centre, near_b))
                ref[1, at] = jnp.where(low_half, outer_a, outer_b)

    def coef_block(dz, part):
        rows = pl.ds(32 + 16 * part, 16)
        return zs[0, rows, :] if dz == 0 else rz[(1 + dz) // 2, rows, :]

    spread_1(level_1.c, coef_block)
    rc2[REACH] = pairs_1(level_1.c)

    for_far(
        1,
        lambda slot, dw: send(
            from_c2 + 2 * REACH - slot, rc2.at[REACH], rc2.at[2 * REACH - slot], dw, 0, 8, sender_c2 + slot
        ),
        HALF_REACH,
    )
    k1_own = zs.at[0, pl.ds(32, 32)]
    halves = squeeze_halves(zs[0, pl.ds(32, 16), :], zs[0, pl.ds(48, 16), :])
    at_lane = lanes(16)
    for side in range(2):
        near, far = (0, 3) if side == 0 else (3, 0)
        full = level_1.c[0, 5 + near]
        place = (32 * far + 31, 32 * far)
        cell = (64, 63)
        for side_z in range(2):
            moved = pltpu.roll(full, (place[side_z] - cell[side_z]) % LANES, 1)
            kp[side, side_z] = jnp.where(at_lane == place[side_z], moved, halves[side_z])
    for_sides(
        lambda side, dw: send(from_k + 1 - side, k1_own, k1cx.at[1 - side], dw, 0, 32, sender_x + side)
    )
    for_corners(
        lambda side, side_z, dw, dn: send_corner(
            from_k_corner, kp.at[side, side_z], k1c.at[1 - side, 1 - side_z], 16, side, side_z
        )
    )

    receive_sides(from_c, 128)
    receive_corners(from_c_corner, 16)
    for side in range(2):
        strips.c[3 * side] = strips.own(c0, 3 * side)
        take_halos(0, strips.c, 3 * side, rcn.at[side])
    level_0.setup_below(1, 1)
    over_sides(1, 11, 4, lambda at: level_0.setup_at(at, 1))
    strips.setup()
    receive_sides(from_s, 32)
    over_sides(3, 11, 2, lambda at: level_0.start_at(at, 1, steps[0][1]))
    over_sides(4, 10, 2, lambda at: level_0.sweep_at(at, *sweep_a))
    over_sides(5, 9, 2, lambda at: level_0.sweep_at(at, *sweep_b))
    over_layers(6, 9, 4, lambda at: level_0.residual_at(at, level_0.va, level_0.vb, 1))
    receive_sides(from_s_next, 64)
    for side in range(2):
        strips.s[3 * side] = strips.own(s0, 3 * side, range(1 - side, 4 - side))
        take_halos(1, strips.s, 3 * side, rcn.at[side])
    over_sides(1, 13, 2, lambda at: level_0.start_at(at, 1, steps[0][1]))
    strips.start(steps[0][1])
    over_sides(2, 12, 2, lambda at: level_0.sweep_at(at, *sweep_a))
    strips.sweep(strips.va, strips.vb, steps[1], fresh=True)
    over_sides(3, 11, 2, lambda at: level_0.sweep_at(at, *sweep_b))
    strips.sweep(strips.vb, strips.va, steps[2])
    over_sides(4, 10, 2, lambda at: level_0.residual_at(at, level_0.va, level_0.vb, 1))
    strips.residual(strips.va, strips.vb)
    for at in range(4, 12):
        level_0.vb[0, at] = strips.mend(level_0.vb[0, at], strips.vb, at)

    squeeze_1(restrict_0(level_0.vb), sk, 0)

    sp[0], sp[1] = squeeze_halves(sk[pl.ds(0, 16), :], sk[pl.ds(16, 16), :])

    @for_sides
    def send_source(side, dw):
        for part in range(2):
            rows = pl.ds(16 * part, 16)
            send(from_s1 + 1 - side, sk.at[rows], k1x.at[1 - side, rows], dw, 0, 16, sender_x + side)

    for_corners(
        lambda side, side_z, dw, dn: send_corner(
            from_s1_corner, sp.at[side_z], k1p.at[1 - side, 1 - side_z], 16, side, side_z
        )
    )
    for_sides_z(lambda side, dn: send(from_s1z + 1 - side, sk, k1z.at[1 - side], 0, dn, 32, sender_z + side))

    receive_far(from_c2, HALF_REACH)

    @functools.partial(if_reach, HALF_REACH)
    def send_four(side, sign):
        src, dst = rc2.at[pl.ds(9 - 5 * side, 4)], rc2.at[pl.ds(13 - 13 * side, 4)]
        send(from_four + 1 - side, src, dst, HALF_REACH * sign, 0, 32, sender_four + side)

    for at in range(3, 13):
        level_0.va[0, at] = strips.mend(level_0.va[0, at], strips.va, at)
    own_cell = (strips.lane() % 32 >= 8) & (strips.lane() % 32 < 24)
    for pack_at, layers in enumerate(((3,), range(4), range(4), (0,))):
        strips.va[pack_at] = jnp.where(own_cell, strips.own(level_0.va, pack_at, layers), strips.va[pack_at])
    for side in range(2):
        first = 9 if side == 0 else 5
        for layer in range(2):
            sb0[side, pl.ds(32 * layer, 32), :] = level_0.va[0, first + layer]
        packed = strips.va[2 - side]
        middle = (lanes(16) >= 32) & (lanes(16) < 96)
        sb0[side, pl.ds(64, 16), :] = jnp.where(middle, packed[:16], pltpu.roll(packed[16:], 64, 1))

    @for_sides
    def send_iterate_0(side, dw):
        send(from_x0 + 1 - side, sb0.at[1 - side], hx0.at[1 - side], dw, 0, 80, sender_x + side)

    def source_block(dz, part):
        rows = pl.ds(16 * part, 16)
        return sk[rows, :] if dz == 0 else k1z[(1 + dz) // 2, rows, :]

    def spread_beside(ref, blocks, packs):
        at_lane = lanes(16)
        low_half = at_lane < 64
        for side in range(2):
            for layer in range(4):
                own = blocks[side, pl.ds(16 * (layer % 2), 16), :]
                other = pltpu.roll(own, 64, 1)
                centre = jnp.where(low_half, own, other) if layer < 2 else jnp.where(low_half, other, own)
                before = pltpu.roll(packs[side, 0], (LANES - 32 * layer) % LANES, 1)
                after = pltpu.roll(packs[side, 1], (LANES + 96 - 32 * layer) % LANES, 1)
                ref[0, 1 + 8 * side + layer] = jnp.where(at_lane < 32, before, jnp.where(at_lane < 96, centre, after))

    receive_sides(from_k, 32)
    receive_corners(from_k_corner, 16)
    spread_beside(level_1.c, k1cx, k1c)
    for side in range(2):
        far = 3 if side == 1 else 0
        below, above = (pltpu.roll(k1c[side, side_z], (shift - 32 * far) % LANES, 1)
                        for side_z, shift in ((0, 127), (1, -31)))
        level_1.c[1, 4 + 5 * side] = jnp.where(lanes(16) < 64, above, below)

    @for_sides
    def send_coef_1(side, dw):
        send(from_c1b + 1 - side, level_1.c.at[0, 9 - 5 * side], level_1.c.at[0, 13 - 13 * side], dw, 0, 16, sender_x + side)

    level_1.setup_below(2, 1)
    over_sides(2, 10, 2, lambda at: level_1.setup_at(at, 1))
    over_layers(4, 9, 6, lambda at: level_1.setup_at(at, 2))

    receive_sides_z(from_s1z, 32)
    spread_1(level_1.s, source_block)
    receive_sides(from_s1, 32)
    receive_corners(from_s1_corner, 16)
    spread_beside(level_1.s, k1x, k1p)
    level_1.start(2, 11, 10, 1, steps[0][1])
    over_layers(5, 8, 4, lambda at: level_1.start_outer(at, steps[0][1]))
    over_sides(3, 9, 2, lambda at: level_1.sweep_at(at, level_1.va, level_1.vb, 1, 1, steps[1], True))
    over_layers(5, 8, 4, lambda at: level_1.sweep_at(at, level_1.va, level_1.vb, 2, 1, steps[1], True))
    level_1.sweep(level_1.vb, level_1.va, 4, 9, 6, 1, 1, steps[2])
    level_1.residual(level_1.va, level_1.vb, 5, 8, 4, 1)

    value = pairs_1(level_1.vb)
    s2m[...] = value
    rs2[REACH] = value

    for_all_far(
        lambda slot, dw: send(
            from_s2 + 2 * REACH - slot, s2m, rs2.at[2 * REACH - slot], dw, 0, 8, sender_far + slot
        )
    )

    @for_sides
    def send_iterate_1(side, dw):
        layers = level_1.va.at[0, pl.ds(6 - 2 * side, 4)]
        send(from_x1 + 1 - side, layers, rx1.at[1 - side], dw, 0, 64, sender_x + side)

    receive_sides(from_c1b, 16)
    level_1.setup_below(1, 1)
    over_sides(1, 12, 1, lambda at: level_1.setup_at(at, 1))

    def spread_2(ref, blocks):
        for block in range(2 * REACH + 1):
            packed = blocks[block]
            ref[0, 2 * block] = jnp.where(odd_8, pltpu.roll(packed, 1, 1), packed)
            ref[0, 2 * block + 1] = jnp.where(odd_8, packed, pltpu.roll(packed, LANES - 1, 1))

    def restrict_2(ref, at):
        total = ref[0, 2 * at + 2] + ref[0, 2 * at + 3]
        odd_row = lax.broadcasted_iota(jnp.int32, (8, LANES), 0) % 2 == 1
        total = total + jnp.where(odd_row, pltpu.roll(total, 1, 0), pltpu.roll(total, 7, 0))
        second = lanes(8) % 4 >= 2
        total = total + jnp.where(second, pltpu.roll(total, 2, 1), pltpu.roll(total, LANES - 2, 1))
        return 0.125 * total

    if_reach(HALF_REACH, lambda side, sign: receive(from_four + side, 32))
    spread_2(level_2.c, rc2)
    level_2.setup(1, 32, 16, 1)
    for at in range(15):
        level_3.c[0, at] = restrict_2(level_2.c, at)
    level_3.setup(1, 13, 13, 1)

    for_sides(lambda side, dw: sends_done(sender_x + side))
    for_sides_z(lambda side, dn: sends_done(sender_z + side))
    for_corners(lambda side, side_z, dw, dn: sends_done(sender_corner + 2 * side + side_z))
    if_reach(HALF_REACH, lambda side, sign: sends_done(sender_four + side))
    for_far(1, lambda slot, dw: ruled(8, 0, sender_c2 + slot).wait_send(), HALF_REACH)
    for_all_far(lambda slot, dw: ruled(8, 0, sender_far + slot).wait_send())

    for_all_far(lambda slot, dw: receive(from_s2 + slot, 8))
    spread_2(level_2.s, rs2)
    level_2.start(1, 32, 32, 1, steps[0][1])
    level_2.sweep(level_2.va, level_2.vb, 2, 31, 30, 1, 1, steps[1], fresh=True)
    level_2.sweep(level_2.vb, level_2.va, 3, 30, 28, 1, 1, steps[2])
    level_2.residual(level_2.va, level_2.vb, 4, 29, 26, 1)

    for at in range(1, 14):
        level_3.s[0, at] = restrict_2(level_2.vb, at)
    coarse = cheb(4)
    level_3.start(1, 13, 13, 1, coarse[0][1])
    level_3.sweep(level_3.va, level_3.vb, 2, 12, 11, 1, 1, coarse[1], fresh=True)
    level_3.sweep(level_3.vb, level_3.va, 3, 11, 9, 1, 1, coarse[2])
    level_3.sweep(level_3.va, level_3.vb, 4, 10, 7, 1, 1, coarse[3])

    for at in range(10, 24):
        level_2.vb[0, at] = level_2.va[0, at] + level_3.vb[0, (at - 2) // 2]
    level_2.sweep(level_2.vb, level_2.va, 11, 22, 12, 1, 1, steps[0], fresh=True)
    level_2.sweep(level_2.va, level_2.vb, 12, 21, 10, 1, 1, steps[1])
    level_2.sweep(level_2.vb, level_2.va, 13, 20, 8, 1, 1, steps[2])

    for at in range(8):
        value = level_2.va[0, 13 + at]
        for part in range(2):
            p1[at, pl.ds(part, 8, stride=2), :] = value
    receive_sides(from_x1, 64)
    for at in range(14):
        if 4 <= at <= 9:
            before = level_1.va[0, at]
        else:
            before = rx1[0, at] if at < 4 else rx1[1, at - 10]
        level_1.vb[0, at] = before + p1[(at + 1) // 2]
    level_1.sweep(level_1.vb, level_1.va, 1, 12, 12, 1, 1, steps[0], fresh=True)
    level_1.sweep(level_1.va, level_1.vb, 2, 11, 10, 1, 1, steps[1])
    level_1.sweep(level_1.vb, level_1.va, 3, 10, 8, 1, 1, steps[2])

    cell = lanes(16) % 32
    strip_lane = jnp.where(cell < 16, 28, 84) + cell // 2
    low_half = lanes(16) < 64
    fine = []
    for at in range(8):
        value = level_1.va[0, 3 + at]
        own = jnp.take_along_axis(value, lanes(16) // 2 + 32, axis=1)
        fine.append(jnp.take_along_axis(value, strip_lane, axis=1))
        for part in range(2):
            p0[at, pl.ds(part, 16, stride=2), :] = own
    for pack in range(4):
        value = jnp.where(low_half, fine[2 * pack], fine[2 * pack + 1])
        for part in range(2):
            ps[pack, pl.ds(part, 16, stride=2), :] = value
    receive_sides(from_x0, 80)
    for side in range(2):
        for layer in range(2):
            at = (1 if side == 0 else 13) + layer
            level_0.vb[0, at] = hx0[side, pl.ds(32 * layer, 32), :] + p0[at // 2]
        packed = hx0[side, pl.ds(64, 16), :]
        layer = lanes(16) // 32
        for part, value in enumerate((packed, pltpu.roll(packed, 64, 1))):
            rows = pl.ds(16 * part, 16)
            own = jnp.where(layer == (3 if side == 0 else 0), strips.va[3 * side, rows, :], 0.0)
            value = jnp.where((layer == 1) | (layer == 2), value, own)
            strips.vb[3 * side, rows, :] = value + ps[3 * side, rows, :]
    for pack in (1, 2):
        strips.vb[pack] = strips.va[pack] + ps[pack]

    def correct(at):
        level_0.vb[0, at] = level_0.va[0, at] + p0[at // 2]

    over_layers(3, 12, 10, correct)
    level_0.sweep(level_0.vb, level_0.va, 2, 13, 12, 1, 1, steps[0], fresh=True)
    strips.sweep(strips.vb, strips.va, steps[0], fresh=True)
    level_0.sweep(level_0.va, level_0.vb, 3, 12, 10, 1, 1, steps[1])
    strips.sweep(strips.va, strips.vb, steps[1])
    strips.sweep(strips.vb, strips.va, steps[2])
    inner = (strips.lane() >= 4) & (strips.lane() < LANES - 4)
    for at in range(4, 12):
        kept_here, added_here = level_0.last_at(at, level_0.vb, level_0.va, steps[2])
        kept[at - 4] = strips.mend(kept_here, strips.va, at)
        added[at - 4] = jnp.where(inner, added_here, 0.0)


def per_device(right_side, conductivity, wide, narrow):
    brick = (8, 32, LANES)
    scratch = []
    for shape in LEVEL_SHAPES:
        scratch += [pltpu.VMEM(shape, F32)] * LEVEL_FIELDS
    scratch += [pltpu.VMEM((4, 32, LANES), F32)] * LEVEL_FIELDS
    shapes = [
        (4, 32, LANES),
        (2, 64, LANES), (2, 64, LANES), (2, 2, 16, LANES),
        (2, 2, 16, LANES), (2, 32, LANES), (2, 2, 16, LANES),
        (32, LANES), (2, 16, LANES), (2, 32, LANES), (2, 2, 16, LANES), (2, 32, LANES),
        (2 * REACH + 1, 8, LANES), (8, LANES), (2 * REACH + 1, 8, LANES),
        (2, 4, 16, LANES),
        (2, 80, LANES), (2, 80, LANES),
        (8, 16, LANES), (8, 32, LANES),
        (RULER, LANES),
    ]
    scratch += [pltpu.VMEM(shape, F32) for shape in shapes]
    scratch += [pltpu.SemaphoreType.DMA((2,)), pltpu.SemaphoreType.DMA((SENDERS,)), pltpu.SemaphoreType.DMA((GROUPS,))]
    kept, added = pl.pallas_call(
        functools.partial(kernel, wide, narrow),
        out_shape=[jax.ShapeDtypeStruct(brick, F32)] * 2,
        in_specs=[pl.BlockSpec(memory_space=pltpu.HBM)] * 2,
        out_specs=[pl.BlockSpec(memory_space=pltpu.VMEM)] * 2,
        scratch_shapes=scratch,
        compiler_params=pltpu.CompilerParams(
            collective_id=0, has_side_effects=True, vmem_limit_bytes=32 * 1024 * 1024
        ),
    )(pltpu.with_memory_space_constraint(right_side, pltpu.HBM), pltpu.with_memory_space_constraint(conductivity, pltpu.HBM))
    return kept + added


def solution(mesh):
    spec = P("wide", None, "narrow")
    body = functools.partial(per_device, wide=mesh.shape["wide"], narrow=mesh.shape["narrow"])
    return jax.shard_map(body, mesh=mesh, in_specs=(spec, spec), out_specs=spec, check_vma=False)
```
